32 devices in a mesh: dp: 16 (over z, y, x), mp: 2 (over core).
Axes of the slice: x: 2, y: 2, z: 4, core: 2. Of those that a mesh axis runs over, the one named last changes fastest.
Arguments:
- tokens: float32 [32768, 384], P(('dp', 'mp')), may hold values from -12 to 12
- condition: float32 [128, 384], P('dp'), may hold values from -12 to 12
- cotangent: float32 [32768, 384], P(('dp', 'mp')), may hold values from -12 to 12
- routes: int32 [32768, 2], P('dp'), may hold values from 0 to 7, as said below
- w_ada: float32 [384, 2304], P('dp'), may hold values from -0.3125 to 0.3125
- ada_first: float32 [384, 2304], P('dp'), may hold values from -1 to 1
- ada_second: float32 [384, 2304], P('dp'), may hold values from 0 to 1, as said below
- w_gate: float32 [384, 8], P('dp'), may hold values from -0.15625 to 0.15625
- gate_first: float32 [384, 8], P('dp'), may hold values from -1 to 1
- gate_second: float32 [384, 8], P('dp'), may hold values from 0 to 1, as said below
- w_attn: float32 [4, 384, 384], P(None, 'dp', 'mp'), may hold values from -4 to 4
- attn_first: float32 [4, 384, 384], P(None, 'dp', 'mp'), may hold values from -1 to 1
- attn_second: float32 [4, 384, 384], P(None, 'dp', 'mp'), may hold values from 0 to 1, as said below
- w_expert: float32 [2, 10, 384, 1536], P(None, None, 'dp', 'mp'), may hold values from -4 to 4
- expert_first: float32 [2, 10, 384, 1536], P(None, None, 'dp', 'mp'), may hold values from -1 to 1
- expert_second: float32 [2, 10, 384, 1536], P(None, None, 'dp', 'mp'), may hold values from 0 to 1, as said below
Outputs:
- output: float32 [32768, 384], P(('dp', 'mp'))
- grad_tokens: float32 [32768, 384], P(('dp', 'mp'))
- grad_norm: float32 [], replicated
- ada_new: float32 [384, 2304], P('dp')
- ada_first_new: float32 [384, 2304], P('dp')
- ada_second_new: float32 [384, 2304], P('dp')
- gate_new: float32 [384, 8], P('dp')
- gate_first_new: float32 [384, 8], P('dp')
- gate_second_new: float32 [384, 8], P('dp')
- attn_new: float32 [4, 384, 384], P(None, 'dp', 'mp')
- attn_first_new: float32 [4, 384, 384], P(None, 'dp', 'mp')
- attn_second_new: float32 [4, 384, 384], P(None, 'dp', 'mp')
- expert_new: float32 [2, 10, 384, 1536], P(None, None, 'dp', 'mp')
- expert_first_new: float32 [2, 10, 384, 1536], P(None, None, 'dp', 'mp')
- expert_second_new: float32 [2, 10, 384, 1536], P(None, None, 'dp', 'mp')
The draws below stay inside these ranges and needn't reach their ends.
Inputs may be any that keep to these rules, and one draw needn't show every extreme that they name: `routes`: each token names two different routed experts; loads differ from expert to expert and from group to group of 2048 tokens. `ada_second`: positive. `gate_second`: positive. `attn_second`: positive. `expert_second`: positive.
All inputs are finite; a program needn't handle non-finite values.
Results may differ from the reference program's by a relative error of at most 0.015.
The reference program's roundings to bfloat16 on the way count: a program that leaves them out, or rounds other values in their place, can miss the bound.
Values may be sent and summed in bfloat16 or wider, within the bound.
A program may use at most 256 MiB of HBM per device.

```python
import math
import jax
import jax.numpy as jnp
from jax import lax

D = 384
HEADS = 6
HD = 64
FF = 1536
SHARED = 2
E = 8
TOPK = 2
PATCH = 256
STEP = 10
IMG_DEV = 8
TOK_GRP = 2048
IMAGES = 128
TOKENS = 32768


def kind_rates():
    routed = math.sqrt(TOPK / E)
    return (11.4, 190.0, 25.0, 11.6, 1.44, 2.52 * routed, 0.55 * routed, 2.1, 3.75)


def kind_scales():
    rates = kind_rates()
    sizes_each = (6 * D * D, D * E, 2 * D * D, D * D, D * D, E * D * FF, E * D * FF, SHARED * D * FF, SHARED * D * FF)
    total = math.sqrt(sum((count_one * rate_one * rate_one for count_one, rate_one in zip(sizes_each, rates))))
    return tuple((0.05 * rate_one / total for rate_one in rates))


def attn_levels():
    levels = kind_scales()
    return jnp.array([levels[2], levels[2], levels[3], levels[4]], jnp.float32)[:, None, None]


def expert_levels():
    levels = kind_scales()
    upper = [levels[5]] * E + [levels[7]] * SHARED
    lower = [levels[6]] * E + [levels[8]] * SHARED
    return jnp.array([upper, lower], jnp.float32)[:, :, None, None]


def first_moment(key, shape, level):
    base = jax.random.truncated_normal(key, -3.0, 3.0, shape, jnp.float32)
    return base * (0.1 / 0.9 * level)


def second_moment(key, shape, level):
    factor = jnp.exp(jax.random.uniform(key, shape, jnp.float32, math.log(0.5), math.log(2.0)))
    return factor * (0.05 / 0.95 * level * level)


def draw_tokens(key, part):
    key = jax.random.fold_in(key, 11)
    columns = jnp.arange(D, dtype=jnp.float32) / (D - 1)
    base = jax.random.truncated_normal(key, -4.0, 4.0, (TOKENS, D), jnp.float32)
    return base * jnp.power(3.0, columns)[None, :]


def draw_condition(key, part):
    key = jax.random.fold_in(key, 12)
    columns = jnp.arange(D, dtype=jnp.float32) / (D - 1)
    base = jax.random.truncated_normal(key, -4.0, 4.0, (IMAGES, D), jnp.float32)
    return base * jnp.power(3.0, columns)[None, :]


def draw_cotangent(key, part):
    key = jax.random.fold_in(key, 13)
    columns = jnp.arange(D, dtype=jnp.float32) / (D - 1)
    base = jax.random.truncated_normal(key, -4.0, 4.0, (TOKENS, D), jnp.float32)
    return base * jnp.power(3.0, columns)[None, :]


def draw_routes(key, part):
    key = jax.random.fold_in(key, 21)
    groups = TOKENS // TOK_GRP
    key_level, key_pick, key_second = jax.random.split(key, 3)
    levels = jnp.power(2, jax.random.randint(key_level, (groups, E), 0, 4)).astype(jnp.int32)
    bounds = jnp.cumsum(levels, axis=1)
    pick = jax.random.randint(key_pick, (groups, TOK_GRP), 0, bounds[:, -1:])
    first = jnp.sum((bounds[:, None, :] <= pick[:, :, None]).astype(jnp.int32), axis=-1)
    first = first.at[:, 0].set(E - 1)
    second = (first + 1 + jax.random.randint(key_second, (groups, TOK_GRP), 0, E - 1)) % E
    return jnp.stack([first, second], axis=-1).reshape(TOKENS, TOPK).astype(jnp.int32)


def draw_w_attn(key, part):
    key = jax.random.fold_in(key, 31)
    base = jax.random.truncated_normal(key, -4.0, 4.0, (4, D, D), jnp.float32)
    narrow = 0.5 * D ** (-0.5)
    inner = D ** (-0.5)
    outer = math.sqrt(max(PATCH // 4, 1) / D)
    scales = jnp.array([narrow, narrow, inner, outer], jnp.float32)
    return base * scales[:, None, None]


def draw_w_expert(key, part):
    key = jax.random.fold_in(key, 32)
    base = jax.random.truncated_normal(key, -4.0, 4.0, (2, E + SHARED, D, FF), jnp.float32)
    up_scale = jnp.full((E + SHARED,), D ** (-0.5), jnp.float32)
    down_scale = jnp.concatenate([jnp.full((E,), max(FF // 64, 1) ** (-0.5), jnp.float32), jnp.full((SHARED,), FF ** (-0.5), jnp.float32)])
    scales = jnp.stack([up_scale, down_scale])
    return base * scales[:, :, None, None]


def draw_ada_first(key, part):
    key = jax.random.fold_in(key, 41)
    return first_moment(key, (D, 6 * D), kind_scales()[0])


def draw_ada_second(key, part):
    key = jax.random.fold_in(key, 42)
    return second_moment(key, (D, 6 * D), kind_scales()[0])


def draw_gate_first(key, part):
    key = jax.random.fold_in(key, 43)
    return first_moment(key, (D, E), kind_scales()[1])


def draw_gate_second(key, part):
    key = jax.random.fold_in(key, 44)
    return second_moment(key, (D, E), kind_scales()[1])


def draw_attn_first(key, part):
    key = jax.random.fold_in(key, 45)
    return first_moment(key, (4, D, D), attn_levels())


def draw_attn_second(key, part):
    key = jax.random.fold_in(key, 46)
    return second_moment(key, (4, D, D), attn_levels())


def draw_expert_first(key, part):
    key = jax.random.fold_in(key, 47)
    return first_moment(key, (2, E + SHARED, D, FF), expert_levels())


def draw_expert_second(key, part):
    key = jax.random.fold_in(key, 48)
    return second_moment(key, (2, E + SHARED, D, FF), expert_levels())


def block_scale(key, shape, cuts, smallest, high):
    gain, own = 1.0, jax.random.fold_in(key, 6)
    for axis_at, blocks in cuts:
        heights = jnp.exp(jax.random.uniform(jax.random.fold_in(own, axis_at), (blocks,), jnp.float32, smallest / len(cuts), high / len(cuts)))
        gain = gain * jnp.repeat(heights, shape[axis_at] // blocks).reshape([-1 if axis == axis_at else 1 for axis in range(len(shape))])
    return gain


def noise(own_key, extent, width, most, cuts=(), kind=jnp.bfloat16):
    values = width * jax.random.normal(own_key, extent, jnp.float32)
    if cuts:
        values = values * block_scale(own_key, extent, cuts, -0.22, 0.18)
    return jnp.clip(values, -most, most).astype(kind)


def setup_inputs(seed: int = 0) -> dict:
    streams_of = jax.random.split(jax.random.key(seed), 17)
    return {
        "tokens": draw_tokens(jax.random.fold_in(streams_of[16], 71), 0),
        "condition": draw_condition(jax.random.fold_in(streams_of[16], 71), 0),
        "cotangent": draw_cotangent(jax.random.fold_in(streams_of[16], 71), 0),
        "routes": draw_routes(jax.random.fold_in(streams_of[16], 71), 0),
        "w_ada": noise(streams_of[4], (D, 6 * D), D ** -0.5, 0.3125, ((0, 16),), jnp.float32),
        "ada_first": draw_ada_first(jax.random.fold_in(streams_of[16], 71), 0),
        "ada_second": draw_ada_second(jax.random.fold_in(streams_of[16], 71), 0),
        "w_gate": noise(streams_of[7], (D, E), (4 * D) ** -0.5, 0.15625, ((0, 16),), jnp.float32),
        "gate_first": draw_gate_first(jax.random.fold_in(streams_of[16], 71), 0),
        "gate_second": draw_gate_second(jax.random.fold_in(streams_of[16], 71), 0),
        "w_attn": draw_w_attn(jax.random.fold_in(streams_of[16], 71), 0),
        "attn_first": draw_attn_first(jax.random.fold_in(streams_of[16], 71), 0),
        "attn_second": draw_attn_second(jax.random.fold_in(streams_of[16], 71), 0),
        "w_expert": draw_w_expert(jax.random.fold_in(streams_of[16], 71), 0),
        "expert_first": draw_expert_first(jax.random.fold_in(streams_of[16], 71), 0),
        "expert_second": draw_expert_second(jax.random.fold_in(streams_of[16], 71), 0),
    }


@jax.custom_vjp
def low(v):
    return lax.optimization_barrier(v.astype(jnp.bfloat16)).astype(jnp.float32)

@jax.custom_vjp
def low_back(v):
    return v

def low_keep(v):
    return (low(v), None)

def low_pass(kept, grad):
    return (grad,)

def back_keep(v):
    return (v, None)

def back_low(kept, grad):
    return (low(grad),)
low.defvjp(low_keep, low_pass)
low_back.defvjp(back_keep, back_low)
EPS_NORM = 1e-06
CLIP_NORM = 0.1
RATE = 0.08
BETA_ONE = 0.9
BETA_TWO = 0.95
ADAM_EPS = 1e-08
DECAY = 0.01
HIGH = lax.Precision.HIGHEST

def layer_norm(value):
    center = value - lax.optimization_barrier(jnp.mean(value, axis=-1, keepdims=True))
    spread = lax.optimization_barrier(jnp.mean(center * center, axis=-1, keepdims=True))
    return center * lax.rsqrt(spread + EPS_NORM)

def rounded(value):
    return low(low_back(value))

def group_forward(lowered, rows, cond_rows, route_rows):
    w_ada, w_gate, w_attn, w_expert = lowered
    images = cond_rows.shape[0]
    modulation = low_back(jnp.dot(low(jax.nn.silu(cond_rows)), w_ada, precision=HIGH))
    modulation = modulation.reshape(images, 6, 1, D)
    x_img = rows.reshape(images, PATCH, D)
    h_one = low(layer_norm(x_img) * (1.0 + modulation[:, 1]) + modulation[:, 0])
    triple = rounded(jnp.einsum('ipd,jde->jipe', h_one, w_attn[:3], precision=HIGH))
    heads = triple.reshape(3, images, PATCH, HEADS, HD)
    scores = low_back(jnp.einsum('iqhc,ikhc->ihqk', heads[0], heads[1], precision=HIGH) * HD ** (-0.5))
    soft = jax.nn.softmax(scores, axis=-1)
    mixed = rounded(jnp.einsum('ihqk,ikhc->iqhc', low(soft), heads[2], precision=HIGH))
    mixed = mixed.reshape(images, PATCH, D)
    attention = low_back(jnp.einsum('ipc,jc->ipj', mixed, w_attn[3], precision=HIGH))
    x_one = x_img + modulation[:, 2] * attention
    h_two = low(layer_norm(x_one) * (1.0 + modulation[:, 4]) + modulation[:, 3]).reshape(images * PATCH, D)
    logits = low_back(jnp.dot(h_two, w_gate, precision=HIGH))
    router = jax.nn.softmax(logits, axis=-1)
    iota = jnp.arange(E, dtype=jnp.int32)
    chosen = lax.optimization_barrier(jnp.sum((route_rows[:, :, None] == iota[None, None, :]).astype(jnp.float32), axis=1))
    gate_table = router * chosen
    branch = jnp.zeros((images * PATCH, D), jnp.float32)
    for expert in range(E + SHARED):
        preact = low_back(jnp.dot(h_two, w_expert[0, expert], precision=HIGH))
        active = low(jax.nn.gelu(preact))
        result = jnp.einsum('tf,df->td', active, w_expert[1, expert], precision=HIGH)
        if expert < E:
            branch = branch + gate_table[:, expert:expert + 1] * low_back(result)
        else:
            branch = branch + result
    branch = low_back(branch).reshape(images, PATCH, D)
    return (x_one + modulation[:, 5] * branch).reshape(images * PATCH, D)

def adam(master, first, second, grad):
    first_new = BETA_ONE * first + (1.0 - BETA_ONE) * grad
    second_new = BETA_TWO * second + (1.0 - BETA_TWO) * grad * grad
    fix_one = 1.0 - BETA_ONE ** STEP
    fix_two = 1.0 - BETA_TWO ** STEP
    update = first_new / fix_one / (jnp.sqrt(second_new / fix_two) + ADAM_EPS) + DECAY * master
    return (master - RATE * update, first_new, second_new)

def reference(tokens, condition, cotangent, routes, w_ada, ada_first, ada_second, w_gate, gate_first, gate_second, w_attn, attn_first, attn_second, w_expert, expert_first, expert_second):
    groups = TOKENS // TOK_GRP
    cond_groups = condition.reshape(groups, IMG_DEV, D)
    route_groups = routes.reshape(groups, TOK_GRP, TOPK)
    checked = jax.checkpoint(group_forward)

    def forward(rows_all, ada, gate, attn, expert):
        lowered = (low(ada), low(gate), low(attn), low(expert))

        def advance(carry, inputs):
            return (carry, checked(lowered, inputs[0], inputs[1], inputs[2]))
        _, stacked = lax.scan(advance, jnp.zeros((), jnp.float32), (rows_all.reshape(groups, TOK_GRP, D), cond_groups, route_groups))
        return stacked.reshape(TOKENS, D)
    output, pullback = jax.vjp(forward, tokens, w_ada, w_gate, w_attn, w_expert)
    grad_tokens, grad_ada, grad_gate, grad_attn, grad_expert = pullback(cotangent)
    total = jnp.sum(grad_ada * grad_ada) + jnp.sum(grad_gate * grad_gate)
    total = total + jnp.sum(grad_attn * grad_attn) + jnp.sum(grad_expert * grad_expert)
    grad_norm = jnp.sqrt(total)
    factor = jnp.minimum(1.0, CLIP_NORM / (grad_norm + 1e-06))
    ada_new, ada_first_new, ada_second_new = adam(w_ada, ada_first, ada_second, grad_ada * factor)
    gate_new, gate_first_new, gate_second_new = adam(w_gate, gate_first, gate_second, grad_gate * factor)
    attn_new, attn_first_new, attn_second_new = adam(w_attn, attn_first, attn_second, grad_attn * factor)
    expert_new, expert_first_new, expert_second_new = adam(w_expert, expert_first, expert_second, grad_expert * factor)
    return (output, grad_tokens, grad_norm, ada_new, ada_first_new, ada_second_new, gate_new, gate_first_new, gate_second_new, attn_new, attn_first_new, attn_second_new, expert_new, expert_first_new, expert_second_new)
```

```python
import functools

import jax
import jax.numpy as jnp
from jax import lax
from jax.experimental import pallas as pl
from jax.experimental.pallas import tpu as pltpu
from jax.sharding import PartitionSpec as P

HD = 64
PATCH = 256
STEP = 10
LANES = 128
SUB = 16
TILE = 512

EPS_NORM = 1e-06
CLIP_NORM = 0.1
RATE = 0.08
BETA_ONE = 0.9
BETA_TWO = 0.95
ADAM_EPS = 1e-08
DECAY = 0.01
GELU_LIN = 0.7978845608
GELU_CUBE = 0.7978845608 * 0.044715

MESH = pl.DeviceIdType.MESH
VMEM_BYTES = 62 * 1024 * 1024
bf16 = jnp.bfloat16
f32 = jnp.float32
NN = (((1,), (0,)), ((), ()))
NT = (((1,), (1,)), ((), ()))
TN = (((0,), (0,)), ((), ()))


def mxu(left, right, dims=NN):
    return lax.dot_general(left, right, dims, preferred_element_type=f32)


def layer_norm(value):
    center = value - jnp.mean(value, axis=-1, keepdims=True)
    inverse = lax.rsqrt(jnp.mean(center * center, axis=-1, keepdims=True) + EPS_NORM)
    return (center * inverse, inverse)


def norm_back(grad, normed, inverse):
    mean_grad = jnp.mean(grad, axis=-1, keepdims=True)
    mean_proj = jnp.mean(grad * normed, axis=-1, keepdims=True)
    return inverse * (grad - mean_grad - normed * mean_proj)


def adam(master, first, second, grad):
    first_new = BETA_ONE * first + (1.0 - BETA_ONE) * grad
    second_new = BETA_TWO * second + (1.0 - BETA_TWO) * grad * grad
    fix_one = 1.0 - BETA_ONE**STEP
    fix_two = 1.0 - BETA_TWO**STEP
    update = first_new / fix_one / (jnp.sqrt(second_new / fix_two) + ADAM_EPS) + DECAY * master
    return (master - RATE * update, first_new, second_new)


def gelu_both(value):
    square = value * value
    tanh = jnp.tanh(value * (GELU_CUBE * square + GELU_LIN))
    half = 0.5 * tanh + 0.5
    act = value * half
    slope = half + act * (1.0 - tanh) * (3.0 * GELU_CUBE * square + GELU_LIN)
    return act, slope


def dp_sizes(count):
    side = 4 if count >= 64 else 2
    return count // (side * side), side


class Place:
    def __init__(self, count):
        self.count = count
        self.depth, self.side = dp_sizes(count)
        self.dp = lax.axis_index("dp")
        self.mp = lax.axis_index("mp")
        side = self.side
        self.z = self.dp // (side * side)
        y = (self.dp // side) % side
        x = self.dp % side
        self.a = jnp.where(self.mp == 0, y, x)
        self.b = jnp.where(self.mp == 0, x, y)
        self.slot = self.slot_at(self.a, self.b, self.z)

    def slot_at(self, a, b, z):
        return (a * self.side + b) * self.depth + z

    def device(self, a, b, z):
        side = self.side
        dp = jnp.where(self.mp == 0, (z * side + a) * side + b, (z * side + b) * side + a)
        return (dp, self.mp)

    def slot_of(self, dp):
        side = self.side
        z, y, x = dp // (side * side), (dp // side) % side, dp % side
        return jnp.where(self.mp == 0, self.slot_at(y, x, z), self.slot_at(x, y, z))

    def peers_z(self):
        return [self.device(self.a, self.b, (self.z + k) % self.depth) for k in range(1, self.depth)]

    def peers_b(self):
        return [self.device(self.a, (self.b + k) % self.side, self.z) for k in range(1, self.side)]

    def peers_a(self):
        return [self.device((self.a + k) % self.side, self.b, self.z) for k in range(1, self.side)]

    def other_core(self):
        return (self.dp, 1 - self.mp)

    def greet(self):
        peers = self.peers_z() + self.peers_b() + self.peers_a() + [self.other_core()]
        barrier = pltpu.get_barrier_semaphore()
        for peer in peers:
            pl.semaphore_signal(barrier, inc=1, device_id=peer, device_id_type=MESH)
        pl.semaphore_wait(barrier, len(peers))


def remote(src, dst, send, recv, peer):
    return pltpu.make_async_remote_copy(
        src_ref=src, dst_ref=dst, send_sem=send, recv_sem=recv, device_id=peer, device_id_type=MESH
    )


class Gather:
    def __init__(self, place, buf, send, recv):
        self.p, self.buf, self.send, self.recv = place, buf, send, recv

    def copies(self, stage, e):
        p = self.p
        if stage == 0:
            src = self.buf.at[e, pl.ds(p.slot, 1)]
            peers, base = p.peers_z(), 0
        elif stage == 1:
            src = self.buf.at[e, pl.ds(p.slot_at(p.a, p.b, 0), p.depth)]
            peers, base = p.peers_b(), p.depth - 1
        else:
            src = self.buf.at[e, pl.ds(p.slot_at(p.a, 0, 0), p.depth * p.side)]
            peers, base = p.peers_a(), p.depth - 1 + p.side - 1
        return [
            remote(src, src, self.send.at[e, base + k], self.recv.at[e, base + k], peer)
            for k, peer in enumerate(peers)
        ]

    def start(self, stage, e):
        for copy in self.copies(stage, e):
            copy.start()

    def arrive(self, stage, e):
        for copy in self.copies(stage, e):
            copy.wait_recv()

    def sent(self, e):
        for stage in range(3):
            for copy in self.copies(stage, e):
                copy.wait_send()


class Scatter:
    def __init__(self, place, buf, boxes, send, recv):
        self.p, self.buf, self.boxes, self.send, self.recv = place, buf, boxes, send, recv

    def copies(self, stage, e):
        p = self.p
        made = []
        for k in range(1, p.side if stage < 2 else p.depth):
            if stage == 0:
                a = (p.a + k) % p.side
                src = self.buf.at[e, pl.ds(p.slot_at(a, 0, 0), p.depth * p.side)]
                peer, base = p.device(a, p.b, p.z), 0
            elif stage == 1:
                b = (p.b + k) % p.side
                src = self.buf.at[e, pl.ds(p.slot_at(p.a, b, 0), p.depth)]
                peer, base = p.device(p.a, b, p.z), p.side - 1
            else:
                z = (p.z + k) % p.depth
                src = self.buf.at[e, pl.ds(p.slot_at(p.a, p.b, z), 1)]
                peer, base = p.device(p.a, p.b, z), 2 * (p.side - 1)
            at = base + k - 1
            made.append(remote(src, self.boxes[stage].at[e, k - 1], self.send.at[e, at], self.recv.at[e, at], peer))
        return made

    def start(self, stage, e):
        for copy in self.copies(stage, e):
            copy.start()

    def arrive(self, stage, e):
        for copy in self.copies(stage, e):
            copy.wait()

    def add(self, stage, e):
        p = self.p
        if stage == 0:
            first, many = p.slot_at(p.a, 0, 0), p.depth * p.side
        else:
            first, many = p.slot_at(p.a, p.b, 0), p.depth
        box = self.boxes[stage]

        def one(i, carry):
            total = self.buf[e, first + i].astype(f32)
            for k in range(p.side - 1):
                total = total + box[e, k, i].astype(f32)
            self.buf[e, first + i] = total.astype(bf16)
            return carry

        lax.fori_loop(0, many, one, 0)

    def last(self, e):
        p = self.p
        total = self.buf[e, p.slot].astype(f32)
        for k in range(p.depth - 1):
            total = total + self.boxes[2][e, k, 0].astype(f32)
        return total


def block_rows(rows):
    return (2 * rows + SUB - 1) // SUB * SUB


def pick_matrix(place, rows, lower):
    block = block_rows(rows)
    shape = (place.count * rows, place.count * block)
    feature = lax.broadcasted_iota(jnp.int32, shape, 0)
    column = lax.broadcasted_iota(jnp.int32, shape, 1)
    slot, inner = column // block, column % block - (rows if lower else 0)
    z, b, a = slot % place.depth, slot // place.depth % place.side, slot // (place.depth * place.side)
    first = jnp.where(place.mp == 0, (z * place.side + a) * place.side + b, (z * place.side + b) * place.side + a)
    hit = (inner >= 0) & (inner < rows) & (first * rows + inner == feature)
    return hit.astype(f32).astype(bf16)


def blocks_to_weights(place, rows, buf, e, up_ref, down_ref):
    if rows % 8 == 0:
        for pair in range(place.count // 2):
            one = buf[e, place.slot_of(2 * pair)].astype(f32)
            two = buf[e, place.slot_of(2 * pair + 1)].astype(f32)
            at = pl.ds(2 * pair * rows, 2 * rows)
            up_ref[at, :] = jnp.concatenate([one[:rows], two[:rows]], axis=0).astype(bf16)
            down_ref[at, :] = jnp.concatenate([one[rows : 2 * rows], two[rows : 2 * rows]], axis=0).astype(bf16)
    else:
        flat = buf[e].reshape(place.count * block_rows(rows), buf.shape[-1])
        up_ref[...] = mxu(pick_matrix(place, rows, False), flat).astype(bf16)
        down_ref[...] = mxu(pick_matrix(place, rows, True), flat).astype(bf16)


def grads_to_blocks(place, rows, up_ref, down_ref, buf, e):
    if rows % 8 == 0:
        for dp in range(place.count):
            at = pl.ds(dp * rows, rows)
            both = jnp.concatenate([up_ref[at, :], down_ref[at, :]], axis=0)
            buf[e, place.slot_of(dp)] = both.astype(bf16)
    else:
        flat = mxu(pick_matrix(place, rows, False), up_ref[...].astype(bf16), TN)
        flat = flat + mxu(pick_matrix(place, rows, True), down_ref[...].astype(bf16), TN)
        buf[e] = flat.astype(bf16).reshape(buf.shape[1:])


def expert_kernel(
    count,
    rows,
    w_ref,
    h_ref,
    d_ref,
    gate_ref,
    branch_ref,
    grad_h_ref,
    grad_gate_ref,
    total_ref,
    buf,
    box_a,
    box_b,
    box_z,
    h_all,
    d_all,
    gate_all,
    branch_acc,
    grad_h_acc,
    grad_gate_acc,
    up_w,
    down_w,
    up_grad,
    down_grad,
    share_out,
    share_in,
    gate_in,
    gather_send,
    gather_recv,
    scatter_send,
    scatter_recv,
    core_send,
    core_recv,
):
    place = Place(count)
    experts = w_ref.shape[1]
    own_tok = h_ref.shape[0]
    gather = Gather(place, buf, gather_send, gather_recv)
    scatter = Scatter(place, buf, (box_a, box_b, box_z), scatter_send, scatter_recv)
    own = pl.ds(pl.multiple_of(place.mp * own_tok, own_tok), own_tok)
    theirs = pl.ds(pl.multiple_of((1 - place.mp) * own_tok, own_tok), own_tok)

    def fill(e, carry):
        both = jnp.concatenate([w_ref[0, e], w_ref[1, e]], axis=0).astype(bf16)
        if both.shape[0] != buf.shape[2]:
            buf[e, place.slot] = jnp.zeros(buf.shape[2:], bf16)
        buf[e, place.slot, pl.ds(0, both.shape[0])] = both
        return carry

    lax.fori_loop(0, experts, fill, 0)
    loads = [
        pltpu.make_async_copy(src, dst.at[own], core_send.at[5 + i])
        for i, (src, dst) in enumerate(((h_ref, h_all), (d_ref, d_all), (gate_ref, gate_all)))
    ]
    for load in loads:
        load.start()
    place.greet()
    for e in range(3):
        gather.start(0, e)
    shared = [
        remote(ref.at[own], ref.at[own], core_send.at[i], core_recv.at[i], place.other_core())
        for i, ref in enumerate((h_all, d_all, gate_all))
    ]
    for load, copy in zip(loads, shared):
        load.wait()
        copy.start()
    gather.start(0, 3)
    branch_acc[...] = jnp.zeros_like(branch_acc)
    grad_h_acc[...] = jnp.zeros_like(grad_h_acc)
    grad_gate_acc[...] = jnp.zeros_like(grad_gate_acc)
    for e in range(2):
        gather.arrive(0, e)
        gather.start(1, e)
    gather.arrive(1, 0)
    gather.start(2, 0)
    for copy in shared:
        copy.wait()

    def compute(e):
        blocks_to_weights(place, rows, buf, e, up_w, down_w)
        up_grad[...] = jnp.zeros_like(up_grad)
        down_grad[...] = jnp.zeros_like(down_grad)

        def tile(t, carry):
            at = pl.ds(pl.multiple_of(t * TILE, TILE), TILE)
            h = h_all[at, :]
            d = d_all[at, :]
            lane = lax.broadcasted_iota(jnp.int32, (TILE, LANES), 1)
            gate = jnp.sum(jnp.where(lane == e, gate_all[at, :], 0.0), axis=1, keepdims=True)
            pre = mxu(h, up_w[...])
            back = mxu(d, down_w[...])
            act, slope = gelu_both(pre)
            inner = jnp.sum(act * back, axis=1, keepdims=True)
            grad_gate_acc[at, :] += jnp.where(lane == e, inner, 0.0)
            act_low = (gate * act).astype(bf16)
            pre_low = (gate * back * slope).astype(bf16)
            branch_acc[at, :] += mxu(act_low, down_w[...], NT)
            grad_h_acc[at, :] += mxu(pre_low, up_w[...], NT)
            up_grad[...] += mxu(h, pre_low, TN)
            down_grad[...] += mxu(d, act_low, TN)
            return carry

        lax.fori_loop(0, h_all.shape[0] // TILE, tile, 0)

    def step(e, carry):
        @pl.when(e + 4 < experts)
        def _():
            gather.start(0, e + 4)

        @pl.when(e + 2 < experts)
        def _():
            gather.arrive(0, e + 2)
            gather.start(1, e + 2)

        @pl.when(e + 1 < experts)
        def _():
            gather.arrive(1, e + 1)
            gather.start(2, e + 1)

        gather.arrive(2, e)
        compute(e)
        gather.sent(e)
        grads_to_blocks(place, rows, up_grad, down_grad, buf, e)
        scatter.start(0, e)

        @pl.when(e >= 1)
        def _():
            scatter.arrive(0, e - 1)
            scatter.add(0, e - 1)
            scatter.start(1, e - 1)

        @pl.when(e >= 2)
        def _():
            scatter.arrive(1, e - 2)
            scatter.add(1, e - 2)
            scatter.start(2, e - 2)

        @pl.when(e >= 3)
        def _():
            scatter.arrive(2, e - 3)
            total_ref[e - 3] = scatter.last(e - 3)

        return carry

    lax.fori_loop(0, experts, step, 0)
    share_out[0] = branch_acc[theirs, :].astype(bf16)
    share_out[1] = grad_h_acc[theirs, :].astype(bf16)
    shares = [
        remote(share_out, share_in, core_send.at[3], core_recv.at[3], place.other_core()),
        remote(grad_gate_acc.at[theirs], gate_in, core_send.at[4], core_recv.at[4], place.other_core()),
    ]
    shares[0].start()
    shares[1].start()
    scatter.arrive(0, experts - 1)
    scatter.add(0, experts - 1)
    scatter.start(1, experts - 1)
    scatter.arrive(1, experts - 2)
    scatter.add(1, experts - 2)
    scatter.start(2, experts - 2)
    shares[0].wait()
    shares[1].wait()
    branch_ref[...] = branch_acc[own, :] + share_in[0].astype(f32)
    grad_h_ref[...] = grad_h_acc[own, :] + share_in[1].astype(f32)
    grad_gate_ref[...] = grad_gate_acc[own, :] + gate_in[...]
    scatter.arrive(1, experts - 1)
    scatter.add(1, experts - 1)
    scatter.start(2, experts - 1)
    for e in range(experts - 3, experts):
        scatter.arrive(2, e)
        total_ref[e] = scatter.last(e)


def expert_call(count, w_expert, h_own, d_own, gates):
    _, experts, rows, hidden = w_expert.shape
    own_tok, width = h_own.shape
    depth, side = dp_sizes(count)
    block = block_rows(rows)
    tok = 2 * own_tok
    vmem = pl.BlockSpec(memory_space=pltpu.VMEM)
    gather_sems = depth + 2 * side - 3
    return pl.pallas_call(
        functools.partial(expert_kernel, count, rows),
        out_shape=(
            jax.ShapeDtypeStruct((own_tok, width), f32),
            jax.ShapeDtypeStruct((own_tok, width), f32),
            jax.ShapeDtypeStruct((own_tok, LANES), f32),
            jax.ShapeDtypeStruct((experts, block, hidden), f32),
        ),
        in_specs=[vmem] + [pl.BlockSpec(memory_space=pl.ANY)] * 3,
        out_specs=(vmem,) * 4,
        scratch_shapes=[
            pltpu.VMEM((experts, count, block, hidden), bf16),
            pltpu.VMEM((experts, side - 1, side * depth, block, hidden), bf16),
            pltpu.VMEM((experts, side - 1, depth, block, hidden), bf16),
            pltpu.VMEM((experts, depth - 1, 1, block, hidden), bf16),
            pltpu.VMEM((tok, width), bf16),
            pltpu.VMEM((tok, width), bf16),
            pltpu.VMEM((tok, LANES), f32),
            pltpu.VMEM((tok, width), f32),
            pltpu.VMEM((tok, width), f32),
            pltpu.VMEM((tok, LANES), f32),
            pltpu.VMEM((width, hidden), bf16),
            pltpu.VMEM((width, hidden), bf16),
            pltpu.VMEM((width, hidden), f32),
            pltpu.VMEM((width, hidden), f32),
            pltpu.VMEM((2, own_tok, width), bf16),
            pltpu.VMEM((2, own_tok, width), bf16),
            pltpu.VMEM((own_tok, LANES), f32),
            pltpu.SemaphoreType.DMA((experts, gather_sems)),
            pltpu.SemaphoreType.DMA((experts, gather_sems)),
            pltpu.SemaphoreType.DMA((experts, gather_sems)),
            pltpu.SemaphoreType.DMA((experts, gather_sems)),
            pltpu.SemaphoreType.DMA((8,)),
            pltpu.SemaphoreType.DMA((5,)),
        ],
        compiler_params=pltpu.CompilerParams(
            collective_id=1, has_side_effects=True, vmem_limit_bytes=VMEM_BYTES
        ),
        cost_estimate=pl.CostEstimate(
            flops=12 * tok * width * hidden * experts, bytes_accessed=8 * w_expert.size, transcendentals=0
        ),
        name="experts",
    )(w_expert, h_own, d_own, gates)


def per_device(
    tokens,
    condition,
    cotangent,
    routes,
    w_ada,
    ada_first,
    ada_second,
    w_gate,
    gate_first,
    gate_second,
    w_attn,
    attn_first,
    attn_second,
    w_expert,
    expert_first,
    expert_second,
):
    tok_dev, width = tokens.shape
    img_own = tok_dev // PATCH
    heads = width // HD
    experts = w_gate.shape[1]
    rows = w_expert.shape[2]
    count = lax.axis_size("dp")
    mp_index = lax.axis_index("mp")
    ada_low = lax.all_gather(w_ada.astype(bf16), "dp", axis=0, tiled=True)
    gate_low = lax.all_gather(w_gate.astype(bf16), "dp", axis=0, tiled=True)
    attn_low = lax.all_gather(w_attn.astype(bf16), "dp", axis=1, tiled=True)
    attn_low = lax.all_gather(attn_low, "mp", axis=2, tiled=True)
    cond_low = jax.nn.silu(condition).astype(bf16)
    cond_own = lax.dynamic_slice_in_dim(cond_low, mp_index * img_own, img_own, 0)
    modulation = jnp.dot(cond_own, ada_low, preferred_element_type=f32).reshape(img_own, 6, 1, width)
    shift_one = modulation[:, 0]
    scale_one = modulation[:, 1]
    gate_one = modulation[:, 2]
    shift_two = modulation[:, 3]
    scale_two = modulation[:, 4]
    gate_two = modulation[:, 5]
    x_img = tokens.reshape(img_own, PATCH, width)
    normed_one, inverse_one = layer_norm(x_img)
    h_one = (normed_one * (1.0 + scale_one) + shift_one).astype(bf16).reshape(tok_dev, width)
    triple = jnp.einsum("td,jdc->jtc", h_one, attn_low[:3], preferred_element_type=f32).astype(bf16)
    head_shape = (img_own, PATCH, heads, HD)
    query = triple[0].reshape(head_shape)
    keys = triple[1].reshape(head_shape)
    values = triple[2].reshape(head_shape)
    scale = HD ** (-0.5)
    scores = jnp.einsum("iqhc,ikhc->ihqk", query, keys, preferred_element_type=f32) * scale
    top = jax.nn.logsumexp(scores, axis=-1, keepdims=True)
    soft_low = jnp.exp(scores - top).astype(bf16)
    mixed = (
        jnp.einsum("ihqk,ikhc->iqhc", soft_low, values, preferred_element_type=f32)
        .astype(bf16)
        .reshape(tok_dev, width)
    )
    out_weight = attn_low[3]
    attention = jnp.einsum("tc,jc->tj", mixed, out_weight, preferred_element_type=f32)
    attention_img = attention.reshape(img_own, PATCH, width)
    x_one = x_img + gate_one * attention_img
    normed_two, inverse_two = layer_norm(x_one)
    h_two = (normed_two * (1.0 + scale_two) + shift_two).astype(bf16).reshape(tok_dev, width)
    grad_out = cotangent.reshape(img_own, PATCH, width)
    grad_branch = (grad_out * gate_two).astype(bf16).reshape(tok_dev, width)
    logits = jnp.dot(h_two, gate_low, preferred_element_type=f32)
    router = jax.nn.softmax(logits, axis=-1)
    own_routes = lax.dynamic_slice_in_dim(routes, mp_index * tok_dev, tok_dev, 0)
    iota = jnp.arange(experts, dtype=jnp.int32)
    chosen = jnp.sum((own_routes[:, :, None] == iota[None, None, :]).astype(f32), axis=1)
    gate_table = router * chosen
    shared = w_expert.shape[1] - experts
    gate_table = jnp.concatenate(
        [gate_table, jnp.ones((tok_dev, shared), f32), jnp.zeros((tok_dev, LANES - experts - shared), f32)],
        axis=1,
    )
    branch, grad_h_own, grad_gates, expert_blocks = expert_call(count, w_expert, h_two, grad_branch, gate_table)
    branch_img = branch.reshape(img_own, PATCH, width)
    output = (x_one + gate_two * branch_img).reshape(tok_dev, width)
    grad_gate_two = jnp.sum(grad_out * branch_img, axis=1, keepdims=True)
    grad_router = grad_gates[:, :experts] * chosen
    grad_logits = (
        router * (grad_router - jnp.sum(router * grad_router, axis=-1, keepdims=True))
    ).astype(bf16)
    grad_gate_w = jnp.einsum("td,te->de", h_two, grad_logits, preferred_element_type=f32)
    grad_h_two = grad_h_own + jnp.einsum("te,de->td", grad_logits, gate_low, preferred_element_type=f32)
    grad_h_two = grad_h_two.reshape(img_own, PATCH, width)
    grad_shift_two = jnp.sum(grad_h_two, axis=1, keepdims=True)
    grad_scale_two = jnp.sum(grad_h_two * normed_two, axis=1, keepdims=True)
    grad_x_one = grad_out + norm_back(grad_h_two * (1.0 + scale_two), normed_two, inverse_two)
    grad_gate_one = jnp.sum(grad_x_one * attention_img, axis=1, keepdims=True)
    grad_attention = (grad_x_one * gate_one).astype(bf16).reshape(tok_dev, width)
    grad_mixed = jnp.einsum("tj,jc->tc", grad_attention, out_weight, preferred_element_type=f32).astype(bf16)
    grad_out_weight = jnp.einsum("tj,tc->jc", grad_attention, mixed, preferred_element_type=f32)
    grad_mixed_heads = grad_mixed.reshape(head_shape)
    scores_back = jnp.einsum("iqhc,ikhc->ihqk", query, keys, preferred_element_type=f32) * scale
    soft_back = jnp.exp(scores_back - top)
    grad_soft = jnp.einsum("iqhc,ikhc->ihqk", grad_mixed_heads, values, preferred_element_type=f32)
    delta = jnp.sum(soft_back * grad_soft, axis=-1, keepdims=True)
    grad_scores = (soft_back * (grad_soft - delta)).astype(bf16)
    grad_query = jnp.einsum("ihqk,ikhc->iqhc", grad_scores, keys, preferred_element_type=f32) * scale
    grad_keys = jnp.einsum("ihqk,iqhc->ikhc", grad_scores, query, preferred_element_type=f32) * scale
    grad_values = jnp.einsum("ihqk,iqhc->ikhc", soft_low, grad_mixed_heads, preferred_element_type=f32)
    grad_triple = jnp.stack([grad_query, grad_keys, grad_values]).reshape(3, tok_dev, width).astype(bf16)
    grad_triple_w = jnp.einsum("td,jtc->jdc", h_one, grad_triple, preferred_element_type=f32)
    grad_h_one = jnp.einsum(
        "jtc,jdc->td", grad_triple, attn_low[:3], preferred_element_type=f32
    ).reshape(img_own, PATCH, width)
    grad_shift_one = jnp.sum(grad_h_one, axis=1, keepdims=True)
    grad_scale_one = jnp.sum(grad_h_one * normed_one, axis=1, keepdims=True)
    grad_tokens = (
        grad_x_one + norm_back(grad_h_one * (1.0 + scale_one), normed_one, inverse_one)
    ).reshape(tok_dev, width)
    grad_modulation = jnp.concatenate(
        [grad_shift_one, grad_scale_one, grad_gate_one, grad_shift_two, grad_scale_two, grad_gate_two],
        axis=1,
    )
    grad_modulation = grad_modulation.reshape(img_own, 6 * width).astype(bf16)
    grad_ada_w = jnp.einsum("id,ie->de", cond_own, grad_modulation, preferred_element_type=f32)
    grad_attn_w = jnp.concatenate([grad_triple_w, grad_out_weight[None]], axis=0)
    half = width // 2
    small = jnp.concatenate(
        [
            grad_ada_w.reshape(width, 2, 3 * width).transpose(1, 0, 2),
            grad_attn_w.reshape(4, width, 2, half).transpose(2, 1, 0, 3).reshape(2, width, 2 * width),
        ],
        axis=2,
    ).astype(bf16)
    small = lax.psum_scatter(small, "mp", scatter_dimension=0, tiled=False)
    small = lax.psum_scatter(small, "dp", scatter_dimension=0, tiled=True).astype(f32)
    ada_half = small[:, : 3 * width]
    attn_total = small[:, 3 * width :].reshape(-1, 4, half).transpose(1, 0, 2)
    ada_total = lax.all_gather(ada_half, "mp", axis=1, tiled=True)
    gate_total = lax.psum(grad_gate_w, ("dp", "mp"))
    gate_total = lax.dynamic_slice_in_dim(gate_total, lax.axis_index("dp") * rows, rows, 0)
    expert_total = expert_blocks[:, : 2 * rows].reshape(-1, 2, rows, w_expert.shape[3]).transpose(1, 0, 2, 3)
    squares = 0.5 * (jnp.sum(ada_total * ada_total) + jnp.sum(gate_total * gate_total))
    squares = squares + jnp.sum(attn_total * attn_total) + jnp.sum(expert_total * expert_total)
    grad_norm = jnp.sqrt(lax.psum(squares, ("dp", "mp")))
    factor = jnp.minimum(1.0, CLIP_NORM / (grad_norm + 1e-06))
    ada_new, ada_first_new, ada_second_new = adam(w_ada, ada_first, ada_second, ada_total * factor)
    gate_new, gate_first_new, gate_second_new = adam(
        w_gate, gate_first, gate_second, gate_total * factor
    )
    attn_new, attn_first_new, attn_second_new = adam(
        w_attn, attn_first, attn_second, attn_total * factor
    )
    expert_new, expert_first_new, expert_second_new = adam(
        w_expert, expert_first, expert_second, expert_total * factor
    )
    return (
        output,
        grad_tokens,
        grad_norm,
        ada_new,
        ada_first_new,
        ada_second_new,
        gate_new,
        gate_first_new,
        gate_second_new,
        attn_new,
        attn_first_new,
        attn_second_new,
        expert_new,
        expert_first_new,
        expert_second_new,
    )


def solution(mesh):
    placed = (
        P(("dp", "mp"), None),
        P("dp", None),
        P(("dp", "mp"), None),
        P("dp", None),
        P("dp", None),
        P("dp", None),
        P("dp", None),
        P("dp", None),
        P("dp", None),
        P("dp", None),
        P(None, "dp", "mp"),
        P(None, "dp", "mp"),
        P(None, "dp", "mp"),
        P(None, None, "dp", "mp"),
        P(None, None, "dp", "mp"),
        P(None, None, "dp", "mp"),
    )
    return jax.shard_map(
        per_device,
        mesh=mesh,
        in_specs=placed,
        out_specs=(
            P(("dp", "mp"), None),
            P(("dp", "mp"), None),
            P(),
            P("dp", None),
            P("dp", None),
            P("dp", None),
            P("dp", None),
            P("dp", None),
            P("dp", None),
            P(None, "dp", "mp"),
            P(None, "dp", "mp"),
            P(None, "dp", "mp"),
            P(None, None, "dp", "mp"),
            P(None, None, "dp", "mp"),
            P(None, None, "dp", "mp"),
        ),
        check_vma=False,
    )
```

```python
import functools

import jax
import jax.numpy as jnp
from jax import lax
from jax.experimental import pallas as pl
from jax.experimental.pallas import tpu as pltpu
from jax.sharding import PartitionSpec as P

HD = 64
PATCH = 256
STEP = 10
LANES = 128
SUB = 16
TILE = 512
SLOTS = 4

EPS_NORM = 1e-06
CLIP_NORM = 0.1
RATE = 0.08
BETA_ONE = 0.9
BETA_TWO = 0.95
ADAM_EPS = 1e-08
DECAY = 0.01
GELU_LIN = 0.7978845608
GELU_CUBE = 0.7978845608 * 0.044715

MESH = pl.DeviceIdType.MESH
VMEM_BYTES = 62 * 1024 * 1024
bf16 = jnp.bfloat16
f32 = jnp.float32
NN = (((1,), (0,)), ((), ()))
NT = (((1,), (1,)), ((), ()))
TN = (((0,), (0,)), ((), ()))


def mxu(left, right, dims=NN):
    return lax.dot_general(left, right, dims, preferred_element_type=f32)


def layer_norm(value):
    center = value - jnp.mean(value, axis=-1, keepdims=True)
    inverse = lax.rsqrt(jnp.mean(center * center, axis=-1, keepdims=True) + EPS_NORM)
    return (center * inverse, inverse)


def norm_back(grad, normed, inverse):
    mean_grad = jnp.mean(grad, axis=-1, keepdims=True)
    mean_proj = jnp.mean(grad * normed, axis=-1, keepdims=True)
    return inverse * (grad - mean_grad - normed * mean_proj)


def adam(master, first, second, grad):
    first_new = BETA_ONE * first + (1.0 - BETA_ONE) * grad
    second_new = BETA_TWO * second + (1.0 - BETA_TWO) * grad * grad
    fix_one = 1.0 - BETA_ONE**STEP
    fix_two = 1.0 - BETA_TWO**STEP
    update = first_new / fix_one / (jnp.sqrt(second_new / fix_two) + ADAM_EPS) + DECAY * master
    return (master - RATE * update, first_new, second_new)


def gelu_both(value):
    square = value * value
    tanh = jnp.tanh(value * (GELU_CUBE * square + GELU_LIN))
    half = 0.5 * tanh + 0.5
    act = value * half
    slope = half + act * (1.0 - tanh) * (3.0 * GELU_CUBE * square + GELU_LIN)
    return act, slope


def dp_sizes(count):
    side = 4 if count >= 64 else 2
    return count // (side * side), side


class Place:
    def __init__(self, count):
        self.count = count
        self.depth, self.side = dp_sizes(count)
        self.dp = lax.axis_index("dp")
        self.mp = lax.axis_index("mp")
        side = self.side
        self.z = self.dp // (side * side)
        y = (self.dp // side) % side
        x = self.dp % side
        self.a = jnp.where(self.mp == 0, y, x)
        self.b = jnp.where(self.mp == 0, x, y)
        self.slot = self.slot_at(self.a, self.b, self.z)

    def slot_at(self, a, b, z):
        return (a * self.side + b) * self.depth + z

    def device(self, a, b, z):
        side = self.side
        dp = jnp.where(self.mp == 0, (z * side + a) * side + b, (z * side + b) * side + a)
        return (dp, self.mp)

    def slot_of(self, dp, core=None):
        side = self.side
        z, y, x = dp // (side * side), (dp // side) % side, dp % side
        core = self.mp if core is None else core
        return jnp.where(core == 0, self.slot_at(y, x, z), self.slot_at(x, y, z))

    def peers_z(self):
        return [self.device(self.a, self.b, (self.z + k) % self.depth) for k in range(1, self.depth)]

    def peers_b(self):
        return [self.device(self.a, (self.b + k) % self.side, self.z) for k in range(1, self.side)]

    def peers_a(self):
        return [self.device((self.a + k) % self.side, self.b, self.z) for k in range(1, self.side)]

    def other_core(self):
        return (self.dp, 1 - self.mp)

    def greet(self):
        peers = self.peers_z() + self.peers_b() + self.peers_a() + [self.other_core()]
        barrier = pltpu.get_barrier_semaphore()
        for peer in peers:
            pl.semaphore_signal(barrier, inc=1, device_id=peer, device_id_type=MESH)
        pl.semaphore_wait(barrier, len(peers))


def remote(src, dst, send, recv, peer):
    return pltpu.make_async_remote_copy(
        src_ref=src, dst_ref=dst, send_sem=send, recv_sem=recv, device_id=peer, device_id_type=MESH
    )


class Gather:
    def __init__(self, place, buf, send, recv):
        self.p, self.buf, self.send, self.recv = place, buf, send, recv

    def copies(self, stage, e):
        p = self.p
        if stage == 0:
            src = self.buf.at[e, pl.ds(p.slot, 1)]
            peers, base = p.peers_z(), 0
        elif stage == 1:
            src = self.buf.at[e, pl.ds(p.slot_at(p.a, p.b, 0), p.depth)]
            peers, base = p.peers_b(), p.depth - 1
        else:
            src = self.buf.at[e, pl.ds(p.slot_at(p.a, 0, 0), p.depth * p.side)]
            peers, base = p.peers_a(), p.depth - 1 + p.side - 1
        return [
            remote(src, src, self.send.at[e, base + k], self.recv.at[e, base + k], peer)
            for k, peer in enumerate(peers)
        ]

    def start(self, stage, e):
        for copy in self.copies(stage, e):
            copy.start()

    def arrive(self, stage, e):
        for copy in self.copies(stage, e):
            copy.wait_recv()

    def sent(self, e):
        for stage in range(3):
            for copy in self.copies(stage, e):
                copy.wait_send()


class Scatter:
    def __init__(self, place, buf, boxes, send, recv):
        self.p, self.buf, self.boxes, self.send, self.recv = place, buf, boxes, send, recv

    def copies(self, stage, e):
        p = self.p
        made = []
        for k in range(1, p.side if stage < 2 else p.depth):
            if stage == 0:
                a = (p.a + k) % p.side
                src = self.buf.at[e, pl.ds(p.slot_at(a, 0, 0), p.depth * p.side)]
                peer, base = p.device(a, p.b, p.z), 0
            elif stage == 1:
                b = (p.b + k) % p.side
                src = self.buf.at[e, pl.ds(p.slot_at(p.a, b, 0), p.depth)]
                peer, base = p.device(p.a, b, p.z), p.side - 1
            else:
                z = (p.z + k) % p.depth
                src = self.buf.at[e, pl.ds(p.slot_at(p.a, p.b, z), 1)]
                peer, base = p.device(p.a, p.b, z), 2 * (p.side - 1)
            at = base + k - 1
            made.append(remote(src, self.boxes[stage].at[e % SLOTS, k - 1], self.send.at[e, at], self.recv.at[e, at], peer))
        return made

    def start(self, stage, e):
        for copy in self.copies(stage, e):
            copy.start()

    def arrive(self, stage, e):
        for copy in self.copies(stage, e):
            copy.wait()

    def add(self, stage, e):
        p = self.p
        if stage == 0:
            first, many = p.slot_at(p.a, 0, 0), p.depth * p.side
        else:
            first, many = p.slot_at(p.a, p.b, 0), p.depth
        box = self.boxes[stage]

        def one(i, carry):
            total = self.buf[e, first + i].astype(f32)
            for k in range(p.side - 1):
                total = total + box[e % SLOTS, k, i].astype(f32)
            self.buf[e, first + i] = total.astype(bf16)
            return carry

        lax.fori_loop(0, many, one, 0)

    def last(self, e):
        p = self.p
        total = self.buf[e, p.slot].astype(f32)
        for k in range(p.depth - 1):
            total = total + self.boxes[2][e % SLOTS, k, 0].astype(f32)
        return total


def block_rows(rows, parts):
    return (parts * rows + SUB - 1) // SUB * SUB


def pick_matrix(place, rows, parts, part, core):
    block = block_rows(rows, parts)
    shape = (place.count * rows, place.count * block)
    feature = lax.broadcasted_iota(jnp.int32, shape, 0)
    column = lax.broadcasted_iota(jnp.int32, shape, 1)
    slot, inner = column // block, column % block - rows * part
    z, b, a = slot % place.depth, slot // place.depth % place.side, slot // (place.depth * place.side)
    first = jnp.where(core == 0, (z * place.side + a) * place.side + b, (z * place.side + b) * place.side + a)
    hit = (inner >= 0) & (inner < rows) & (first * rows + inner == feature)
    return hit.astype(f32).astype(bf16)


def blocks_to_weights(place, rows, buf, core, outs):
    parts = len(outs)
    if rows % 8 == 0:
        for pair in range(place.count // 2):
            one = buf[place.slot_of(2 * pair, core)].astype(f32)
            two = buf[place.slot_of(2 * pair + 1, core)].astype(f32)
            at = pl.ds(2 * pair * rows, 2 * rows)
            for part, out in enumerate(outs):
                mine = slice(part * rows, (part + 1) * rows)
                out[at, :] = jnp.concatenate([one[mine], two[mine]], axis=0).astype(bf16)
    else:
        flat = buf[...].reshape(place.count * block_rows(rows, parts), buf.shape[-1])
        for part, out in enumerate(outs):
            out[...] = mxu(pick_matrix(place, rows, parts, part, core), flat).astype(bf16)


def grads_to_blocks(place, rows, grads, buf):
    parts = len(grads)
    if rows % 8 == 0:
        for dp in range(place.count):
            at = pl.ds(dp * rows, rows)
            buf[place.slot_of(dp)] = jnp.concatenate([grad[at, :] for grad in grads], axis=0).astype(bf16)
    else:
        flat = 0.0
        for part, grad in enumerate(grads):
            flat = flat + mxu(pick_matrix(place, rows, parts, part, place.mp), grad[...].astype(bf16), TN)
        buf[...] = flat.astype(bf16).reshape(buf.shape)


def expert_kernel(
    count,
    rows,
    w_ref,
    h_ref,
    d_ref,
    gate_ref,
    branch_ref,
    grad_h_ref,
    grad_gate_ref,
    total_ref,
    buf,
    box_a,
    box_b,
    box_z,
    h_all,
    d_all,
    gate_all,
    branch_acc,
    grad_h_acc,
    grad_gate_acc,
    up_w,
    down_w,
    up_grad,
    down_grad,
    share_out,
    share_in,
    gate_in,
    gather_send,
    gather_recv,
    scatter_send,
    scatter_recv,
    core_send,
    core_recv,
):
    place = Place(count)
    experts = w_ref.shape[1]
    own_tok = h_ref.shape[0]
    gather = Gather(place, buf, gather_send, gather_recv)
    scatter = Scatter(place, buf, (box_a, box_b, box_z), scatter_send, scatter_recv)
    own = pl.ds(pl.multiple_of(place.mp * own_tok, own_tok), own_tok)
    theirs = pl.ds(pl.multiple_of((1 - place.mp) * own_tok, own_tok), own_tok)

    def fill(e, carry):
        both = jnp.concatenate([w_ref[0, e], w_ref[1, e]], axis=0).astype(bf16)
        if both.shape[0] != buf.shape[2]:
            buf[e, place.slot] = jnp.zeros(buf.shape[2:], bf16)
        buf[e, place.slot, pl.ds(0, both.shape[0])] = both
        return carry

    lax.fori_loop(0, experts, fill, 0)
    loads = [
        pltpu.make_async_copy(src, dst.at[own], core_send.at[5 + i])
        for i, (src, dst) in enumerate(((h_ref, h_all), (d_ref, d_all), (gate_ref, gate_all)))
    ]
    for load in loads:
        load.start()
    place.greet()
    for e in range(3):
        gather.start(0, e)
    shared = [
        remote(ref.at[own], ref.at[own], core_send.at[i], core_recv.at[i], place.other_core())
        for i, ref in enumerate((h_all, d_all, gate_all))
    ]
    for load, copy in zip(loads, shared):
        load.wait()
        copy.start()
    gather.start(0, 3)
    branch_acc[...] = jnp.zeros_like(branch_acc)
    grad_h_acc[...] = jnp.zeros_like(grad_h_acc)
    grad_gate_acc[...] = jnp.zeros_like(grad_gate_acc)
    for e in range(2):
        gather.arrive(0, e)
        gather.start(1, e)
    gather.arrive(1, 0)
    gather.start(2, 0)
    for copy in shared:
        copy.wait()

    def compute(e):
        blocks_to_weights(place, rows, buf.at[e], place.mp, (up_w, down_w))
        up_grad[...] = jnp.zeros_like(up_grad)
        down_grad[...] = jnp.zeros_like(down_grad)

        def tile(t, carry):
            at = pl.ds(pl.multiple_of(t * TILE, TILE), TILE)
            h = h_all[at, :]
            d = d_all[at, :]
            lane = lax.broadcasted_iota(jnp.int32, (TILE, LANES), 1)
            gate = jnp.sum(jnp.where(lane == e, gate_all[at, :], 0.0), axis=1, keepdims=True)
            pre = mxu(h, up_w[...])
            back = mxu(d, down_w[...])
            act, slope = gelu_both(pre)
            inner = jnp.sum(act * back, axis=1, keepdims=True)
            grad_gate_acc[at, :] += jnp.where(lane == e, inner, 0.0)
            act_low = (gate * act).astype(bf16)
            pre_low = (gate * back * slope).astype(bf16)
            branch_acc[at, :] += mxu(act_low, down_w[...], NT)
            grad_h_acc[at, :] += mxu(pre_low, up_w[...], NT)
            up_grad[...] += mxu(h, pre_low, TN)
            down_grad[...] += mxu(d, act_low, TN)
            return carry

        lax.fori_loop(0, h_all.shape[0] // TILE, tile, 0)

    def step(e, carry):
        @pl.when(e + 4 < experts)
        def _():
            gather.start(0, e + 4)

        @pl.when(e + 2 < experts)
        def _():
            gather.arrive(0, e + 2)
            gather.start(1, e + 2)

        @pl.when(e + 1 < experts)
        def _():
            gather.arrive(1, e + 1)
            gather.start(2, e + 1)

        gather.arrive(2, e)
        compute(e)
        gather.sent(e)
        grads_to_blocks(place, rows, (up_grad, down_grad), buf.at[e])
        scatter.start(0, e)

        @pl.when(e >= 1)
        def _():
            scatter.arrive(0, e - 1)
            scatter.add(0, e - 1)
            scatter.start(1, e - 1)

        @pl.when(e >= 2)
        def _():
            scatter.arrive(1, e - 2)
            scatter.add(1, e - 2)
            scatter.start(2, e - 2)

        @pl.when(e >= 3)
        def _():
            scatter.arrive(2, e - 3)
            total_ref[e - 3] = scatter.last(e - 3)

        return carry

    lax.fori_loop(0, experts, step, 0)
    share_out[0] = branch_acc[theirs, :].astype(bf16)
    share_out[1] = grad_h_acc[theirs, :].astype(bf16)
    shares = [
        remote(share_out, share_in, core_send.at[3], core_recv.at[3], place.other_core()),
        remote(grad_gate_acc.at[theirs], gate_in, core_send.at[4], core_recv.at[4], place.other_core()),
    ]
    shares[0].start()
    shares[1].start()
    scatter.arrive(0, experts - 1)
    scatter.add(0, experts - 1)
    scatter.start(1, experts - 1)
    scatter.arrive(1, experts - 2)
    scatter.add(1, experts - 2)
    scatter.start(2, experts - 2)
    scatter.arrive(2, experts - 3)
    total_ref[experts - 3] = scatter.last(experts - 3)
    shares[0].wait()
    shares[1].wait()
    branch_ref[...] = branch_acc[own, :] + share_in[0].astype(f32)
    grad_h_ref[...] = grad_h_acc[own, :] + share_in[1].astype(f32)
    grad_gate_ref[...] = grad_gate_acc[own, :] + gate_in[...]
    scatter.arrive(1, experts - 1)
    scatter.add(1, experts - 1)
    scatter.start(2, experts - 1)
    for e in range(experts - 2, experts):
        scatter.arrive(2, e)
        total_ref[e] = scatter.last(e)


def expert_call(count, w_expert, h_own, d_own, gates):
    _, experts, rows, hidden = w_expert.shape
    own_tok, width = h_own.shape
    depth, side = dp_sizes(count)
    block = block_rows(rows, 2)
    tok = 2 * own_tok
    vmem = pl.BlockSpec(memory_space=pltpu.VMEM)
    gather_sems = depth + 2 * side - 3
    return pl.pallas_call(
        functools.partial(expert_kernel, count, rows),
        out_shape=(
            jax.ShapeDtypeStruct((own_tok, width), f32),
            jax.ShapeDtypeStruct((own_tok, width), f32),
            jax.ShapeDtypeStruct((own_tok, LANES), f32),
            jax.ShapeDtypeStruct((experts, block, hidden), f32),
        ),
        in_specs=[vmem] + [pl.BlockSpec(memory_space=pl.ANY)] * 3,
        out_specs=(vmem,) * 4,
        scratch_shapes=[
            pltpu.VMEM((experts, count, block, hidden), bf16),
            pltpu.VMEM((SLOTS, side - 1, side * depth, block, hidden), bf16),
            pltpu.VMEM((SLOTS, side - 1, depth, block, hidden), bf16),
            pltpu.VMEM((SLOTS, depth - 1, 1, block, hidden), bf16),
            pltpu.VMEM((tok, width), bf16),
            pltpu.VMEM((tok, width), bf16),
            pltpu.VMEM((tok, LANES), f32),
            pltpu.VMEM((tok, width), f32),
            pltpu.VMEM((tok, width), f32),
            pltpu.VMEM((tok, LANES), f32),
            pltpu.VMEM((width, hidden), bf16),
            pltpu.VMEM((width, hidden), bf16),
            pltpu.VMEM((width, hidden), f32),
            pltpu.VMEM((width, hidden), f32),
            pltpu.VMEM((2, own_tok, width), bf16),
            pltpu.VMEM((2, own_tok, width), bf16),
            pltpu.VMEM((own_tok, LANES), f32),
            pltpu.SemaphoreType.DMA((experts, gather_sems)),
            pltpu.SemaphoreType.DMA((experts, gather_sems)),
            pltpu.SemaphoreType.DMA((experts, gather_sems)),
            pltpu.SemaphoreType.DMA((experts, gather_sems)),
            pltpu.SemaphoreType.DMA((8,)),
            pltpu.SemaphoreType.DMA((5,)),
        ],
        compiler_params=pltpu.CompilerParams(
            collective_id=1, has_side_effects=True, vmem_limit_bytes=VMEM_BYTES
        ),
        cost_estimate=pl.CostEstimate(
            flops=12 * tok * width * hidden * experts, bytes_accessed=8 * w_expert.size, transcendentals=0
        ),
        name="experts",
    )(w_expert, h_own, d_own, gates)


def front_kernel(
    count, rows, ada_ref, gate_ref, attn_ref, ada_out, attn_out, ada_buf, attn_buf, ada_far, attn_far,
    ada_send, ada_recv, attn_send, attn_recv, core_send, core_recv
):
    place = Place(count)
    half = ada_ref.shape[1] // 2
    cut = ada_buf.shape[3]
    pad = 2 * cut - half
    cols = ada_ref[:, pl.ds(pl.multiple_of(place.mp * half, LANES), half)]
    gate = jnp.concatenate([gate_ref[...], jnp.zeros((rows, pad - gate_ref.shape[1]), f32)], axis=1)
    tail = jnp.concatenate([cols[:, cut:], gate], axis=1)
    block = jnp.concatenate([cols[:, :cut], tail], axis=0).astype(bf16)
    if block.shape[0] != ada_buf.shape[2]:
        ada_buf[0, place.slot] = jnp.zeros(ada_buf.shape[2:], bf16)
    ada_buf[0, place.slot, pl.ds(0, block.shape[0])] = block
    block = jnp.concatenate([attn_ref[j] for j in range(attn_ref.shape[0])], axis=0).astype(bf16)
    if block.shape[0] != attn_buf.shape[2]:
        attn_buf[0, place.slot] = jnp.zeros(attn_buf.shape[2:], bf16)
    attn_buf[0, place.slot, pl.ds(0, block.shape[0])] = block
    place.greet()
    gathers = (Gather(place, ada_buf, ada_send, ada_recv), Gather(place, attn_buf, attn_send, attn_recv))
    for gather in gathers:
        gather.start(0, 0)
    for stage in range(3):
        for gather in gathers:
            gather.arrive(stage, 0)
            if stage < 2:
                gather.start(stage + 1, 0)
    cross = [
        remote(ada_buf.at[0], ada_far, core_send.at[0], core_recv.at[0], place.other_core()),
        remote(attn_buf.at[0], attn_far, core_send.at[1], core_recv.at[1], place.other_core()),
    ]
    for copy in cross:
        copy.start()
    parts = attn_ref.shape[0]

    def unpack(core, ada, attn):
        blocks_to_weights(place, rows, ada, core, [ada_out.at[core, i] for i in range(2)])
        blocks_to_weights(place, rows, attn, core, [attn_out.at[core, j] for j in range(parts)])

    unpack(place.mp, ada_buf.at[0], attn_buf.at[0])
    for gather in gathers:
        gather.sent(0)
    for copy in cross:
        copy.wait()
    unpack(1 - place.mp, ada_far, attn_far)


def front_call(count, w_ada, w_gate, w_attn):
    rows, wide = w_ada.shape
    parts, _, half = w_attn.shape
    width = count * rows
    depth, side = dp_sizes(count)
    cut = (wide // 2 + LANES) // 2
    ada_block, attn_block = block_rows(rows, 2), block_rows(rows, parts)
    vmem = pl.BlockSpec(memory_space=pltpu.VMEM)
    sems = pltpu.SemaphoreType.DMA((1, depth + 2 * side - 3))
    return pl.pallas_call(
        functools.partial(front_kernel, count, rows),
        out_shape=(
            jax.ShapeDtypeStruct((2, 2, width, cut), bf16),
            jax.ShapeDtypeStruct((2, parts, width, half), bf16),
        ),
        in_specs=[vmem] * 3,
        out_specs=(vmem, vmem),
        scratch_shapes=[
            pltpu.VMEM((1, count, ada_block, cut), bf16),
            pltpu.VMEM((1, count, attn_block, half), bf16),
            pltpu.VMEM((count, ada_block, cut), bf16),
            pltpu.VMEM((count, attn_block, half), bf16),
            sems, sems, sems, sems,
            pltpu.SemaphoreType.DMA((2,)),
            pltpu.SemaphoreType.DMA((2,)),
        ],
        compiler_params=pltpu.CompilerParams(collective_id=2, has_side_effects=True, vmem_limit_bytes=VMEM_BYTES),
        name="front",
    )(w_ada, w_gate, w_attn)


def all_sum(place, value, src, box, send, recv):
    stages = (
        (place.depth, place.z, lambda i: place.device(place.a, place.b, i)),
        (place.side, place.b, lambda i: place.device(place.a, i, place.z)),
        (place.side, place.a, lambda i: place.device(i, place.b, place.z)),
        (2, place.mp, lambda i: (place.dp, i)),
    )
    at = 0
    for stage, (many, mine, device) in enumerate(stages):
        src[stage] = value
        box[stage, mine] = value
        copies = []
        for k in range(1, many):
            peer = device((mine + k) % many)
            copies.append(remote(src.at[stage], box.at[stage, mine], send.at[at], recv.at[at], peer))
            at += 1
        for copy in copies:
            copy.start()
        for copy in copies:
            copy.wait()
        value = box[stage, 0]
        for i in range(1, many):
            value = value + box[stage, i]
    return value


def back_kernel(
    count, rows, experts, ada_ref, attn_ref, square_ref, ada_out, attn_out, norm_out,
    ada_acc, attn_acc, ada_buf, attn_buf, ada_a, ada_b, ada_z, attn_a, attn_b, attn_z,
    ada_share, attn_share, ada_far, attn_far, norm_src, norm_box,
    ada_send, ada_recv, attn_send, attn_recv, core_send, core_recv, norm_send, norm_recv
):
    place = Place(count)
    parts = attn_ref.shape[1]
    place.greet()
    ada_share[...] = ada_ref[1 - place.mp].astype(bf16)
    attn_share[...] = attn_ref[1 - place.mp].astype(bf16)
    cross = [
        remote(ada_share, ada_far, core_send.at[0], core_recv.at[0], place.other_core()),
        remote(attn_share, attn_far, core_send.at[1], core_recv.at[1], place.other_core()),
    ]
    for copy in cross:
        copy.start()
    scatters = (
        Scatter(place, ada_buf, (ada_a, ada_b, ada_z), ada_send, ada_recv),
        Scatter(place, attn_buf, (attn_a, attn_b, attn_z), attn_send, attn_recv),
    )
    cross[0].wait()
    ada_acc[...] = ada_ref[place.mp] + ada_far[...].astype(f32)
    grads_to_blocks(place, rows, [ada_acc.at[i] for i in range(2)], ada_buf.at[0])
    scatters[0].start(0, 0)
    cross[1].wait()
    attn_acc[...] = attn_ref[place.mp] + attn_far[...].astype(f32)
    grads_to_blocks(place, rows, [attn_acc.at[j] for j in range(parts)], attn_buf.at[0])
    scatters[1].start(0, 0)
    for stage in range(2):
        for scatter in scatters:
            scatter.arrive(stage, 0)
            scatter.add(stage, 0)
            scatter.start(stage + 1, 0)
    for scatter in scatters:
        scatter.arrive(2, 0)
    ada = scatters[0].last(0)
    attn = scatters[1].last(0)
    ada_out[...] = ada
    attn_out[...] = attn
    shape = ada.shape
    row = lax.broadcasted_iota(jnp.int32, shape, 0)
    lane = lax.broadcasted_iota(jnp.int32, shape, 1)
    twice = (row >= rows) & (lane >= shape[1] - LANES)
    total = jnp.sum(jnp.where(twice, 0.5, 1.0) * ada * ada) + jnp.sum(attn * attn) + jnp.sum(square_ref[...])
    value = jnp.full(norm_out.shape, total, f32)
    norm_out[...] = all_sum(place, value, norm_src, norm_box, norm_send, norm_recv)


def back_call(count, rows, ada_grad, attn_grad, squares):
    _, _, width, cut = ada_grad.shape
    _, parts, _, half = attn_grad.shape
    depth, side = dp_sizes(count)
    ada_block, attn_block = block_rows(rows, 2), block_rows(rows, parts)
    vmem = pl.BlockSpec(memory_space=pltpu.VMEM)
    sems = pltpu.SemaphoreType.DMA((1, depth + 2 * side - 3))
    norm_sems = pltpu.SemaphoreType.DMA((depth + 2 * side - 2,))

    def boxes(block, lanes):
        return [
            pltpu.VMEM((1, side - 1, side * depth, block, lanes), bf16),
            pltpu.VMEM((1, side - 1, depth, block, lanes), bf16),
            pltpu.VMEM((1, depth - 1, 1, block, lanes), bf16),
        ]

    return pl.pallas_call(
        functools.partial(back_kernel, count, rows, 0),
        out_shape=(
            jax.ShapeDtypeStruct((ada_block, cut), f32),
            jax.ShapeDtypeStruct((attn_block, half), f32),
            jax.ShapeDtypeStruct((8, LANES), f32),
        ),
        in_specs=[vmem] * 3,
        out_specs=(vmem,) * 3,
        scratch_shapes=[
            pltpu.VMEM((2, width, cut), f32),
            pltpu.VMEM((parts, width, half), f32),
            pltpu.VMEM((1, count, ada_block, cut), bf16),
            pltpu.VMEM((1, count, attn_block, half), bf16),
            *boxes(ada_block, cut),
            *boxes(attn_block, half),
            pltpu.VMEM((2, width, cut), bf16),
            pltpu.VMEM((parts, width, half), bf16),
            pltpu.VMEM((2, width, cut), bf16),
            pltpu.VMEM((parts, width, half), bf16),
            pltpu.VMEM((4, 8, LANES), f32),
            pltpu.VMEM((4, max(depth, side), 8, LANES), f32),
            sems, sems, sems, sems,
            pltpu.SemaphoreType.DMA((2,)),
            pltpu.SemaphoreType.DMA((2,)),
            norm_sems, norm_sems,
        ],
        compiler_params=pltpu.CompilerParams(collective_id=3, has_side_effects=True, vmem_limit_bytes=VMEM_BYTES),
        name="back",
    )(ada_grad, attn_grad, squares)


def per_device(
    tokens,
    condition,
    cotangent,
    routes,
    w_ada,
    ada_first,
    ada_second,
    w_gate,
    gate_first,
    gate_second,
    w_attn,
    attn_first,
    attn_second,
    w_expert,
    expert_first,
    expert_second,
):
    tok_dev, width = tokens.shape
    img_own = tok_dev // PATCH
    heads = width // HD
    experts = w_gate.shape[1]
    rows = w_expert.shape[2]
    count = lax.axis_size("dp")
    mp_index = lax.axis_index("mp")
    half = width // 2
    wide = w_ada.shape[1] // 2
    ada_parts, attn_parts = front_call(count, w_ada, w_gate, w_attn)
    ada_halves = [jnp.concatenate([ada_parts[c, 0], ada_parts[c, 1]], axis=1) for c in range(2)]
    ada_low = jnp.concatenate([ada_halves[c][:, :wide] for c in range(2)], axis=1)
    gate_low = ada_halves[0][:, wide : wide + experts]
    attn_low = jnp.concatenate([attn_parts[0], attn_parts[1]], axis=2)
    cond_low = jax.nn.silu(condition).astype(bf16)
    cond_own = lax.dynamic_slice_in_dim(cond_low, mp_index * img_own, img_own, 0)
    modulation = jnp.dot(cond_own, ada_low, preferred_element_type=f32).reshape(img_own, 6, 1, width)
    shift_one = modulation[:, 0]
    scale_one = modulation[:, 1]
    gate_one = modulation[:, 2]
    shift_two = modulation[:, 3]
    scale_two = modulation[:, 4]
    gate_two = modulation[:, 5]
    x_img = tokens.reshape(img_own, PATCH, width)
    normed_one, inverse_one = layer_norm(x_img)
    h_one = (normed_one * (1.0 + scale_one) + shift_one).astype(bf16).reshape(tok_dev, width)
    triple = jnp.einsum("td,jdc->jtc", h_one, attn_low[:3], preferred_element_type=f32).astype(bf16)
    head_shape = (img_own, PATCH, heads, HD)
    query = triple[0].reshape(head_shape)
    keys = triple[1].reshape(head_shape)
    values = triple[2].reshape(head_shape)
    scale = HD ** (-0.5)
    scores = jnp.einsum("iqhc,ikhc->ihqk", query, keys, preferred_element_type=f32) * scale
    top = jax.nn.logsumexp(scores, axis=-1, keepdims=True)
    soft_low = jnp.exp(scores - top).astype(bf16)
    mixed = (
        jnp.einsum("ihqk,ikhc->iqhc", soft_low, values, preferred_element_type=f32)
        .astype(bf16)
        .reshape(tok_dev, width)
    )
    out_weight = attn_low[3]
    attention = jnp.einsum("tc,jc->tj", mixed, out_weight, preferred_element_type=f32)
    attention_img = attention.reshape(img_own, PATCH, width)
    x_one = x_img + gate_one * attention_img
    normed_two, inverse_two = layer_norm(x_one)
    h_two = (normed_two * (1.0 + scale_two) + shift_two).astype(bf16).reshape(tok_dev, width)
    grad_out = cotangent.reshape(img_own, PATCH, width)
    grad_branch = (grad_out * gate_two).astype(bf16).reshape(tok_dev, width)
    logits = jnp.dot(h_two, gate_low, preferred_element_type=f32)
    router = jax.nn.softmax(logits, axis=-1)
    own_routes = lax.dynamic_slice_in_dim(routes, mp_index * tok_dev, tok_dev, 0)
    iota = jnp.arange(experts, dtype=jnp.int32)
    chosen = jnp.sum((own_routes[:, :, None] == iota[None, None, :]).astype(f32), axis=1)
    gate_table = router * chosen
    shared = w_expert.shape[1] - experts
    gate_table = jnp.concatenate(
        [gate_table, jnp.ones((tok_dev, shared), f32), jnp.zeros((tok_dev, LANES - experts - shared), f32)],
        axis=1,
    )
    branch, grad_h_own, grad_gates, expert_blocks = expert_call(count, w_expert, h_two, grad_branch, gate_table)
    branch_img = branch.reshape(img_own, PATCH, width)
    output = (x_one + gate_two * branch_img).reshape(tok_dev, width)
    grad_gate_two = jnp.sum(grad_out * branch_img, axis=1, keepdims=True)
    grad_router = grad_gates[:, :experts] * chosen
    grad_logits = (
        router * (grad_router - jnp.sum(router * grad_router, axis=-1, keepdims=True))
    ).astype(bf16)
    grad_gate_w = jnp.einsum("td,te->de", h_two, grad_logits, preferred_element_type=f32)
    grad_h_two = grad_h_own + jnp.einsum("te,de->td", grad_logits, gate_low, preferred_element_type=f32)
    grad_h_two = grad_h_two.reshape(img_own, PATCH, width)
    grad_shift_two = jnp.sum(grad_h_two, axis=1, keepdims=True)
    grad_scale_two = jnp.sum(grad_h_two * normed_two, axis=1, keepdims=True)
    grad_x_one = grad_out + norm_back(grad_h_two * (1.0 + scale_two), normed_two, inverse_two)
    grad_gate_one = jnp.sum(grad_x_one * attention_img, axis=1, keepdims=True)
    grad_attention = (grad_x_one * gate_one).astype(bf16).reshape(tok_dev, width)
    grad_mixed = jnp.einsum("tj,jc->tc", grad_attention, out_weight, preferred_element_type=f32).astype(bf16)
    grad_out_weight = jnp.einsum("tj,tc->jc", grad_attention, mixed, preferred_element_type=f32)
    grad_mixed_heads = grad_mixed.reshape(head_shape)
    scores_back = jnp.einsum("iqhc,ikhc->ihqk", query, keys, preferred_element_type=f32) * scale
    soft_back = jnp.exp(scores_back - top)
    grad_soft = jnp.einsum("iqhc,ikhc->ihqk", grad_mixed_heads, values, preferred_element_type=f32)
    delta = jnp.sum(soft_back * grad_soft, axis=-1, keepdims=True)
    grad_scores = (soft_back * (grad_soft - delta)).astype(bf16)
    grad_query = jnp.einsum("ihqk,ikhc->iqhc", grad_scores, keys, preferred_element_type=f32) * scale
    grad_keys = jnp.einsum("ihqk,iqhc->ikhc", grad_scores, query, preferred_element_type=f32) * scale
    grad_values = jnp.einsum("ihqk,iqhc->ikhc", soft_low, grad_mixed_heads, preferred_element_type=f32)
    grad_triple = jnp.stack([grad_query, grad_keys, grad_values]).reshape(3, tok_dev, width).astype(bf16)
    grad_triple_w = jnp.einsum("td,jtc->jdc", h_one, grad_triple, preferred_element_type=f32)
    grad_h_one = jnp.einsum(
        "jtc,jdc->td", grad_triple, attn_low[:3], preferred_element_type=f32
    ).reshape(img_own, PATCH, width)
    grad_shift_one = jnp.sum(grad_h_one, axis=1, keepdims=True)
    grad_scale_one = jnp.sum(grad_h_one * normed_one, axis=1, keepdims=True)
    grad_tokens = (
        grad_x_one + norm_back(grad_h_one * (1.0 + scale_one), normed_one, inverse_one)
    ).reshape(tok_dev, width)
    grad_modulation = jnp.concatenate(
        [grad_shift_one, grad_scale_one, grad_gate_one, grad_shift_two, grad_scale_two, grad_gate_two],
        axis=1,
    )
    grad_modulation = grad_modulation.reshape(img_own, 6 * width).astype(bf16)
    grad_ada_w = jnp.einsum("id,ie->de", cond_own, grad_modulation, preferred_element_type=f32)
    attn_grad = jnp.stack([grad_triple_w[:, :, :half], grad_triple_w[:, :, half:]])
    out_grad = jnp.stack([grad_out_weight[None, :, :half], grad_out_weight[None, :, half:]])
    attn_grad = jnp.concatenate([attn_grad, out_grad], axis=1)
    gate_pad = jnp.pad(grad_gate_w, ((0, 0), (0, LANES - experts)))
    ada_grad = []
    for core in range(2):
        whole = jnp.concatenate([grad_ada_w[:, core * wide : (core + 1) * wide], gate_pad], axis=1)
        cut = whole.shape[1] // 2
        ada_grad.append(jnp.stack([whole[:, :cut], whole[:, cut:]]))
    ada_grad = jnp.stack(ada_grad)
    expert_total = expert_blocks[:, : 2 * rows].reshape(-1, 2, rows, w_expert.shape[3]).transpose(1, 0, 2, 3)
    squares = jnp.pad(jnp.sum(expert_total * expert_total).reshape(1, 1), ((0, 7), (0, LANES - 1)))
    ada_block, attn_block, square_sum = back_call(count, rows, ada_grad, attn_grad, squares)
    ada_half = jnp.concatenate([ada_block[:rows], ada_block[rows : 2 * rows]], axis=1)
    gate_total = ada_half[:, wide : wide + experts]
    ada_total = lax.all_gather(ada_half[:, :wide], "mp", axis=1, tiled=True)
    attn_total = attn_block[: 4 * rows].reshape(4, rows, half)
    grad_norm = jnp.sqrt(square_sum[0, 0])
    factor = jnp.minimum(1.0, CLIP_NORM / (grad_norm + 1e-06))
    ada_new, ada_first_new, ada_second_new = adam(w_ada, ada_first, ada_second, ada_total * factor)
    gate_new, gate_first_new, gate_second_new = adam(
        w_gate, gate_first, gate_second, gate_total * factor
    )
    attn_new, attn_first_new, attn_second_new = adam(
        w_attn, attn_first, attn_second, attn_total * factor
    )
    expert_new, expert_first_new, expert_second_new = adam(
        w_expert, expert_first, expert_second, expert_total * factor
    )
    return (
        output,
        grad_tokens,
        grad_norm,
        ada_new,
        ada_first_new,
        ada_second_new,
        gate_new,
        gate_first_new,
        gate_second_new,
        attn_new,
        attn_first_new,
        attn_second_new,
        expert_new,
        expert_first_new,
        expert_second_new,
    )


def solution(mesh):
    placed = (
        P(("dp", "mp"), None),
        P("dp", None),
        P(("dp", "mp"), None),
        P("dp", None),
        P("dp", None),
        P("dp", None),
        P("dp", None),
        P("dp", None),
        P("dp", None),
        P("dp", None),
        P(None, "dp", "mp"),
        P(None, "dp", "mp"),
        P(None, "dp", "mp"),
        P(None, None, "dp", "mp"),
        P(None, None, "dp", "mp"),
        P(None, None, "dp", "mp"),
    )
    return jax.shard_map(
        per_device,
        mesh=mesh,
        in_specs=placed,
        out_specs=(
            P(("dp", "mp"), None),
            P(("dp", "mp"), None),
            P(),
            P("dp", None),
            P("dp", None),
            P("dp", None),
            P("dp", None),
            P("dp", None),
            P("dp", None),
            P(None, "dp", "mp"),
            P(None, "dp", "mp"),
            P(None, "dp", "mp"),
            P(None, None, "dp", "mp"),
            P(None, None, "dp", "mp"),
            P(None, None, "dp", "mp"),
        ),
        check_vma=False,
    )
```

```python
import functools
import math

import jax
import jax.numpy as jnp
from jax import lax
from jax.experimental import pallas as pl
from jax.experimental.pallas import tpu as pltpu
from jax.sharding import PartitionSpec as P

HD = 64
PATCH = 256
STEP = 10
LANES = 128
SUB = 16
TILE = 512
SLOTS = 4

EPS_NORM = 1e-06
CLIP_NORM = 0.1
RATE = 0.08
BETA_ONE = 0.9
BETA_TWO = 0.95
ADAM_EPS = 1e-08
DECAY = 0.01
GELU_LIN = 0.7978845608
GELU_CUBE = 0.7978845608 * 0.044715

MESH = pl.DeviceIdType.MESH
VMEM_BYTES = 127 * 512 * 1024
bf16 = jnp.bfloat16
f32 = jnp.float32
NN = (((1,), (0,)), ((), ()))
NT = (((1,), (1,)), ((), ()))
TN = (((0,), (0,)), ((), ()))


def mxu(left, right, dims=NN):
    return lax.dot_general(left, right, dims, preferred_element_type=f32)


def layer_norm(value):
    center = value - jnp.mean(value, axis=-1, keepdims=True)
    inverse = lax.rsqrt(jnp.mean(center * center, axis=-1, keepdims=True) + EPS_NORM)
    return (center * inverse, inverse)


def norm_back(grad, normed, inverse):
    mean_grad = jnp.mean(grad, axis=-1, keepdims=True)
    mean_proj = jnp.mean(grad * normed, axis=-1, keepdims=True)
    return inverse * (grad - mean_grad - normed * mean_proj)


def adam(master, first, second, grad):
    first_new = BETA_ONE * first + (1.0 - BETA_ONE) * grad
    second_new = BETA_TWO * second + (1.0 - BETA_TWO) * grad * grad
    fix_one = 1.0 - BETA_ONE**STEP
    fix_two = 1.0 - BETA_TWO**STEP
    update = first_new / fix_one / (jnp.sqrt(second_new / fix_two) + ADAM_EPS) + DECAY * master
    return (master - RATE * update, first_new, second_new)


def gelu_both(value):
    square = value * value
    tanh = jnp.tanh(value * (GELU_CUBE * square + GELU_LIN))
    half = 0.5 * tanh + 0.5
    act = value * half
    slope = half + act * (1.0 - tanh) * (3.0 * GELU_CUBE * square + GELU_LIN)
    return act, slope


def dp_sizes(count):
    side = 4 if count >= 64 else 2
    return count // (side * side), side


class Place:
    def __init__(self, count):
        self.count = count
        self.depth, self.side = dp_sizes(count)
        self.dp = lax.axis_index("dp")
        self.mp = lax.axis_index("mp")
        side = self.side
        self.z = self.dp // (side * side)
        y = (self.dp // side) % side
        x = self.dp % side
        self.a = jnp.where(self.mp == 0, y, x)
        self.b = jnp.where(self.mp == 0, x, y)
        self.slot = self.slot_at(self.a, self.b, self.z)

    def slot_at(self, a, b, z):
        return (a * self.side + b) * self.depth + z

    def device(self, a, b, z):
        side = self.side
        dp = jnp.where(self.mp == 0, (z * side + a) * side + b, (z * side + b) * side + a)
        return (dp, self.mp)

    def slot_of(self, dp, core=None):
        side = self.side
        z, y, x = dp // (side * side), (dp // side) % side, dp % side
        core = self.mp if core is None else core
        return jnp.where(core == 0, self.slot_at(y, x, z), self.slot_at(x, y, z))

    def peers_z(self):
        return [self.device(self.a, self.b, (self.z + k) % self.depth) for k in range(1, self.depth)]

    def peers_b(self):
        return [self.device(self.a, (self.b + k) % self.side, self.z) for k in range(1, self.side)]

    def peers_a(self):
        return [self.device((self.a + k) % self.side, self.b, self.z) for k in range(1, self.side)]

    def other_core(self):
        return (self.dp, 1 - self.mp)

    def greet(self):
        peers = self.peers_z() + self.peers_b() + self.peers_a() + [self.other_core()]
        barrier = pltpu.get_barrier_semaphore()
        for peer in peers:
            pl.semaphore_signal(barrier, inc=1, device_id=peer, device_id_type=MESH)
        pl.semaphore_wait(barrier, len(peers))


def remote(src, dst, send, recv, peer):
    return pltpu.make_async_remote_copy(
        src_ref=src, dst_ref=dst, send_sem=send, recv_sem=recv, device_id=peer, device_id_type=MESH
    )


class Gather:
    def __init__(self, place, buf, send, recv):
        self.p, self.buf, self.send, self.recv = place, buf, send, recv

    def copies(self, stage, e):
        p = self.p
        if stage == 0:
            src = self.buf.at[e, pl.ds(p.slot, 1)]
            peers, base = p.peers_z(), 0
        elif stage == 1:
            src = self.buf.at[e, pl.ds(p.slot_at(p.a, p.b, 0), p.depth)]
            peers, base = p.peers_b(), p.depth - 1
        else:
            src = self.buf.at[e, pl.ds(p.slot_at(p.a, 0, 0), p.depth * p.side)]
            peers, base = p.peers_a(), p.depth - 1 + p.side - 1
        return [
            remote(src, src, self.send.at[e, base + k], self.recv.at[e, base + k], peer)
            for k, peer in enumerate(peers)
        ]

    def start(self, stage, e):
        for copy in self.copies(stage, e):
            copy.start()

    def arrive(self, stage, e):
        for copy in self.copies(stage, e):
            copy.wait_recv()

    def sent(self, e):
        for stage in range(3):
            for copy in self.copies(stage, e):
                copy.wait_send()


class Scatter:
    def __init__(self, place, buf, boxes, send, recv):
        self.p, self.buf, self.boxes, self.send, self.recv = place, buf, boxes, send, recv

    def copies(self, stage, e):
        p = self.p
        made = []
        for k in range(1, p.side if stage < 2 else p.depth):
            if stage == 0:
                a = (p.a + k) % p.side
                src = self.buf.at[e, pl.ds(p.slot_at(a, 0, 0), p.depth * p.side)]
                peer, base = p.device(a, p.b, p.z), 0
            elif stage == 1:
                b = (p.b + k) % p.side
                src = self.buf.at[e, pl.ds(p.slot_at(p.a, b, 0), p.depth)]
                peer, base = p.device(p.a, b, p.z), p.side - 1
            else:
                z = (p.z + k) % p.depth
                src = self.buf.at[e, pl.ds(p.slot_at(p.a, p.b, z), 1)]
                peer, base = p.device(p.a, p.b, z), 2 * (p.side - 1)
            at = base + k - 1
            made.append(remote(src, self.boxes[stage].at[e % SLOTS, k - 1], self.send.at[e, at], self.recv.at[e, at], peer))
        return made

    def start(self, stage, e):
        for copy in self.copies(stage, e):
            copy.start()

    def arrive(self, stage, e):
        for copy in self.copies(stage, e):
            copy.wait()

    def add(self, stage, e):
        p = self.p
        if stage == 0:
            first, many = p.slot_at(p.a, 0, 0), p.depth * p.side
        else:
            first, many = p.slot_at(p.a, p.b, 0), p.depth
        box = self.boxes[stage]

        def one(i, carry):
            total = self.buf[e, first + i].astype(f32)
            for k in range(p.side - 1):
                total = total + box[e % SLOTS, k, i].astype(f32)
            self.buf[e, first + i] = total.astype(bf16)
            return carry

        lax.fori_loop(0, many, one, 0)

    def last(self, e):
        p = self.p
        total = self.buf[e, p.slot].astype(f32)
        for k in range(p.depth - 1):
            total = total + self.boxes[2][e % SLOTS, k, 0].astype(f32)
        return total


def block_rows(rows, parts):
    return (parts * rows + SUB - 1) // SUB * SUB


def blocks_to_weights(place, rows, buf, core, outs):
    many = SUB // math.gcd(SUB, rows)
    for first in range(0, place.count, many):
        blocks = [buf[place.slot_of(first + i, core)].astype(f32) for i in range(many)]
        for part, out in enumerate(outs):
            pieces = [block[part * rows : (part + 1) * rows] for block in blocks]
            out[pl.ds(first * rows, many * rows), :] = jnp.concatenate(pieces, axis=0).astype(bf16)


def grads_to_blocks(place, rows, grads, buf):
    block = buf.shape[1]
    for dp in range(place.count):
        pieces = [grad[dp * rows : (dp + 1) * rows, :] for grad in grads]
        if block > rows * len(grads):
            pieces.append(jnp.zeros((block - rows * len(grads), buf.shape[2]), f32))
        buf[place.slot_of(dp)] = jnp.concatenate(pieces, axis=0).astype(bf16)


def all_sum(place, value, src, box, send, recv):
    stages = (
        (place.depth, place.z, lambda i: place.device(place.a, place.b, i)),
        (place.side, place.b, lambda i: place.device(place.a, i, place.z)),
        (place.side, place.a, lambda i: place.device(i, place.b, place.z)),
        (2, place.mp, lambda i: (place.dp, i)),
    )
    at = 0
    for stage, (many, mine, device) in enumerate(stages):
        src[stage] = value
        box[stage, mine] = value
        copies = []
        for k in range(1, many):
            peer = device((mine + k) % many)
            copies.append(remote(src.at[stage], box.at[stage, mine], send.at[at], recv.at[at], peer))
            at += 1
        for copy in copies:
            copy.start()
        for copy in copies:
            copy.wait()
        value = box[stage, 0]
        for i in range(1, many):
            value = value + box[stage, i]
    return value


def block_kernel(
    count, rows, experts, tile,
    tok_ref, cot_ref, cond_ref, route_ref, ada_ref, gate_ref, attn_ref, w_ref,
    output_ref, grad_tok_ref, ada_out, attn_out, total_ref, norm_out,
    buf, box_a, box_b, box_z,
    ada_buf, ada_a, ada_b, ada_z, attn_buf, attn_a, attn_b, attn_z, attn_far, attn_w, gate_w,
    cond_low, mod, grad_mod, grad_mod_in, triple, mixed, h_one, soft,
    h_all, d_all, gate_all, branch_acc, grad_h_acc, grad_gate_acc, gate_in, share_in,
    up_w, down_w, up_grad, down_grad, gate_grad, gate_grad_in, attn_share, attn_in, norm_src, norm_box,
    load_sem, gather_send, gather_recv, scatter_send, scatter_recv,
    ada_send, ada_recv, attn_send, attn_recv, ada_back_send, ada_back_recv, attn_back_send, attn_back_recv,
    core_send, core_recv, token_send, token_recv, norm_send, norm_recv,
):
    place = Place(count)
    mp = place.mp
    wide_experts = w_ref.shape[1]
    own_tok, width = tok_ref.shape
    images = own_tok // PATCH
    half = attn_ref.shape[2]
    heads = half // HD
    wide = ada_ref.shape[1] // 2
    cut = ada_buf.shape[3]
    scale = HD ** (-0.5)
    own_at = pl.multiple_of(mp * own_tok, own_tok)
    their_at = pl.multiple_of((1 - mp) * own_tok, own_tok)
    own, theirs = pl.ds(own_at, own_tok), pl.ds(their_at, own_tok)
    other = place.other_core()

    loads = [
        pltpu.make_async_copy(tok_ref, branch_acc.at[pl.ds(0, own_tok)], load_sem.at[0]),
        pltpu.make_async_copy(cot_ref, branch_acc.at[pl.ds(own_tok, own_tok)], load_sem.at[1]),
    ]
    for load in loads:
        load.start()

    def put(target, block):
        if block.shape[0] != target.shape[1]:
            target[place.slot] = jnp.zeros(target.shape[1:], bf16)
        target[place.slot, pl.ds(0, block.shape[0])] = block

    cols = ada_ref[:, pl.ds(pl.multiple_of(mp * wide, LANES), wide)]
    gate = jnp.concatenate([gate_ref[...], jnp.zeros((rows, 2 * cut - wide - experts), f32)], axis=1)
    tail = jnp.concatenate([cols[:, cut:], gate], axis=1)
    put(ada_buf.at[0], jnp.concatenate([cols[:, :cut], tail], axis=0).astype(bf16))
    parts = attn_ref.shape[0]
    put(attn_buf.at[0], jnp.concatenate([attn_ref[j] for j in range(parts)], axis=0).astype(bf16))
    place.greet()
    ada_gather = Gather(place, ada_buf, ada_send, ada_recv)
    attn_gather = Gather(place, attn_buf, attn_send, attn_recv)
    gather = Gather(place, buf, gather_send, gather_recv)
    scatter = Scatter(place, buf, (box_a, box_b, box_z), scatter_send, scatter_recv)
    ada_gather.start(0, 0)
    attn_gather.start(0, 0)

    def fill(e, carry):
        put(buf.at[e], jnp.concatenate([w_ref[0, e], w_ref[1, e]], axis=0).astype(bf16))
        return carry

    lax.fori_loop(0, wide_experts, fill, 0)

    def tick(k):
        @pl.when(k + 4 < wide_experts)
        def _():
            gather.start(0, k + 4)

        @pl.when((k + 2 >= 0) & (k + 2 < wide_experts))
        def _():
            gather.arrive(0, k + 2)
            gather.start(1, k + 2)

        @pl.when((k + 1 >= 0) & (k + 1 < wide_experts))
        def _():
            gather.arrive(1, k + 1)
            gather.start(2, k + 1)

    cond = cond_ref[...]
    cond_low[...] = (cond / (1.0 + jnp.exp(-cond))).astype(bf16)
    grad_mod[...] = jnp.zeros_like(grad_mod)
    for stage in range(3):
        for small in (ada_gather, attn_gather):
            small.arrive(stage, 0)
            if stage < 2:
                small.start(stage + 1, 0)
        if stage == 0:
            for e in range(3):
                gather.start(0, e)
    attn_cross = remote(attn_buf.at[0], attn_far, core_send.at[0], core_recv.at[0], other)
    attn_cross.start()

    low_cut = pl.ds(0, cut)
    blocks_to_weights(place, rows, ada_buf.at[0], mp, (up_w.at[:, low_cut], down_w.at[:, low_cut]))
    mod[mp, :, pl.ds(0, cut)] = mxu(cond_low[...], up_w[:, low_cut])
    mod[mp, :, pl.ds(cut, cut)] = mxu(cond_low[...], down_w[:, low_cut])
    gate_w[...] = down_w[:, pl.ds(cut - LANES, LANES)]
    mod_cross = remote(mod.at[mp], mod.at[mp], core_send.at[1], core_recv.at[1], other)
    mod_cross.start()
    blocks_to_weights(place, rows, attn_buf.at[0], mp, [attn_w.at[mp, j] for j in range(parts)])
    for load in loads:
        load.wait()
    ada_gather.sent(0)
    attn_gather.sent(0)
    gather.arrive(0, 0)
    gather.start(1, 0)
    attn_cross.wait()
    blocks_to_weights(place, rows, attn_far, 1 - mp, [attn_w.at[1 - mp, j] for j in range(parts)])
    mod_cross.wait()

    lane_pair = lax.broadcasted_iota(jnp.int32, (PATCH, 2 * HD), 1)
    masks = [(lane_pair < HD).astype(f32).astype(bf16), (lane_pair >= HD).astype(f32).astype(bf16)]
    groups = [(at, min(2, heads - at)) for at in range(0, heads, 2)]
    expert_lane = lax.broadcasted_iota(jnp.int32, (PATCH, LANES), 1)

    def mod_row(image, vector):
        flat = vector % 3 * width
        return mod[vector // 3, pl.ds(mp * images + image, 1), pl.ds(flat, width)]

    def add_grad_mod(image, vector, value):
        grad_mod[vector // 3, pl.ds(mp * images + image, 1), pl.ds(vector % 3 * width, width)] = value

    def one_head(value, group, head):
        return value if group[1] == 1 else value * masks[head]

    def route(h, image):
        logits = jnp.where(expert_lane < experts, mxu(h, gate_w[...]), -jnp.inf)
        power = jnp.exp(logits - jnp.max(logits, axis=1, keepdims=True))
        router = power / jnp.sum(power, axis=1, keepdims=True)
        picks = route_ref[pl.ds(image * PATCH, PATCH), :]
        chosen = jnp.where((picks[:, 0:1] == expert_lane) | (picks[:, 1:2] == expert_lane), 1.0, 0.0)
        return router, chosen

    def attend(at):
        return mxu(mixed[0, at, :], attn_w[0, 3], NT) + mxu(mixed[1, at, :], attn_w[1, 3], NT)

    def token_copies(image):
        at = pl.ds(pl.multiple_of(own_at + image * PATCH, PATCH), PATCH)
        return [
            remote(ref.at[at], ref.at[at], token_send.at[image, i], token_recv.at[image, i], other)
            for i, ref in enumerate((h_all, d_all, gate_all))
        ]

    def forward(image, carry):
        at = pl.ds(pl.multiple_of(image * PATCH, PATCH), PATCH)
        cot_at = pl.ds(pl.multiple_of(own_tok + image * PATCH, PATCH), PATCH)
        all_at = pl.ds(pl.multiple_of(own_at + image * PATCH, PATCH), PATCH)
        normed, _ = layer_norm(branch_acc[at, :])
        h = (normed * (1.0 + mod_row(image, 1)) + mod_row(image, 0)).astype(bf16)
        h_one[at, :] = h
        for core in range(2):
            for j in range(3):
                triple[core, j, at, :] = mxu(h, attn_w[core, j]).astype(bf16)
            for group in groups:
                lanes = pl.ds(group[0] * HD, group[1] * HD)
                query, key, value = (triple[core, j, at, lanes] for j in range(3))
                total = 0.0
                for head in range(group[1]):
                    scores = mxu(one_head(query, group, head), key, NT) * scale
                    power = jnp.exp(scores - jnp.max(scores, axis=1, keepdims=True))
                    low = (power * (1.0 / jnp.sum(power, axis=1, keepdims=True))).astype(bf16)
                    soft[image, core * heads + group[0] + head] = low
                    total = total + mxu(low, one_head(value, group, head))
                mixed[core, at, lanes] = total.astype(bf16)
        x_one = branch_acc[at, :] + mod_row(image, 2) * attend(at)
        normed, _ = layer_norm(x_one)
        h = (normed * (1.0 + mod_row(image, 4)) + mod_row(image, 3)).astype(bf16)
        h_all[all_at, :] = h
        router, chosen = route(h, image)
        shared = (expert_lane >= experts) & (expert_lane < wide_experts)
        gate_all[all_at, :] = jnp.where(shared, 1.0, router * chosen)
        d_all[all_at, :] = (branch_acc[cot_at, :] * mod_row(image, 5)).astype(bf16)
        for copy in token_copies(image):
            copy.start()

        @pl.when(image % 2 == 1)
        def _():
            tick(image // 2 - 1)

        return carry

    lax.fori_loop(0, images, forward, 0)
    ahead = images // 2 - 1

    branch_acc[...] = jnp.zeros_like(branch_acc)
    grad_h_acc[...] = jnp.zeros_like(grad_h_acc)
    grad_gate_acc[...] = jnp.zeros_like(grad_gate_acc)

    def all_tokens(image, carry):
        for copy in token_copies(image):
            copy.wait()
        return carry

    lax.fori_loop(0, images, all_tokens, 0)

    def compute(e):
        blocks_to_weights(place, rows, buf.at[e], mp, (up_w, down_w))
        up_grad[...] = jnp.zeros_like(up_grad)
        down_grad[...] = jnp.zeros_like(down_grad)

        def one_tile(t, carry):
            at = pl.ds(pl.multiple_of(t * tile, tile), tile)
            h = h_all[at, :]
            d = d_all[at, :]
            lane = lax.broadcasted_iota(jnp.int32, (tile, LANES), 1)
            gate = jnp.sum(jnp.where(lane == e, gate_all[at, :], 0.0), axis=1, keepdims=True)
            pre = mxu(h, up_w[...])
            back = mxu(d, down_w[...])
            act, slope = gelu_both(pre)
            inner = jnp.sum(act * back, axis=1, keepdims=True)
            grad_gate_acc[at, :] += jnp.where(lane == e, inner, 0.0)
            act_low = (gate * act).astype(bf16)
            pre_low = (gate * back * slope).astype(bf16)
            branch_acc[at, :] += mxu(act_low, down_w[...], NT)
            grad_h_acc[at, :] += mxu(pre_low, up_w[...], NT)
            up_grad[...] += mxu(h, pre_low, TN)
            down_grad[...] += mxu(d, act_low, TN)
            return carry

        lax.fori_loop(0, h_all.shape[0] // tile, one_tile, 0)

    def collect(k):
        @pl.when((k >= 1) & (k - 1 < wide_experts))
        def _():
            scatter.arrive(0, k - 1)
            scatter.add(0, k - 1)
            scatter.start(1, k - 1)

        @pl.when((k >= 2) & (k - 2 < wide_experts))
        def _():
            scatter.arrive(1, k - 2)
            scatter.add(1, k - 2)
            scatter.start(2, k - 2)

        @pl.when((k >= 3) & (k - 3 < wide_experts))
        def _():
            scatter.arrive(2, k - 3)
            total_ref[k - 3] = scatter.last(k - 3)

    def step(e, carry):
        tick(e + ahead)
        gather.arrive(2, e)
        compute(e)
        gather.sent(e)
        grads_to_blocks(place, rows, (up_grad, down_grad), buf.at[e])
        scatter.start(0, e)
        collect(e)
        return carry

    lax.fori_loop(0, wide_experts, step, 0)

    h_all[theirs, :] = branch_acc[theirs, :].astype(bf16)
    d_all[theirs, :] = grad_h_acc[theirs, :].astype(bf16)
    shares = [
        remote(h_all.at[theirs], share_in.at[0], core_send.at[2], core_recv.at[2], other),
        remote(d_all.at[theirs], share_in.at[1], core_send.at[3], core_recv.at[3], other),
        remote(grad_gate_acc.at[theirs], gate_in, core_send.at[4], core_recv.at[4], other),
    ]
    loads = [
        pltpu.make_async_copy(tok_ref, branch_acc.at[theirs], load_sem.at[0]),
        pltpu.make_async_copy(cot_ref, grad_h_acc.at[theirs], load_sem.at[1]),
    ]
    for copy in shares + loads:
        copy.start()
    gate_grad[...] = jnp.zeros_like(gate_grad)
    for copy in shares + loads:
        copy.wait()

    def backward(image, carry):
        at = pl.ds(pl.multiple_of(image * PATCH, PATCH), PATCH)
        own_rows = pl.ds(pl.multiple_of(own_at + image * PATCH, PATCH), PATCH)
        load_rows = pl.ds(pl.multiple_of(their_at + image * PATCH, PATCH), PATCH)
        tok, cot = branch_acc[load_rows, :], grad_h_acc[load_rows, :]
        branch = branch_acc[own_rows, :] + share_in[0, at, :].astype(f32)
        attention = attend(at)
        x_one = tok + mod_row(image, 2) * attention
        normed, inverse = layer_norm(x_one)
        branch_acc[own_rows, :] = x_one + mod_row(image, 5) * branch
        add_grad_mod(image, 5, jnp.sum(cot * branch, axis=0, keepdims=True))
        h = h_all[own_rows, :]
        router, chosen = route(h, image)
        grad_router = (grad_gate_acc[own_rows, :] + gate_in[at, :]) * chosen
        grad_logits = (router * (grad_router - jnp.sum(router * grad_router, axis=1, keepdims=True))).astype(bf16)
        gate_grad[...] += mxu(h, grad_logits, TN)
        grad_h = grad_h_acc[own_rows, :] + share_in[1, at, :].astype(f32) + mxu(grad_logits, gate_w[...], NT)
        add_grad_mod(image, 3, jnp.sum(grad_h, axis=0, keepdims=True))
        add_grad_mod(image, 4, jnp.sum(grad_h * normed, axis=0, keepdims=True))
        grad_x = cot + norm_back(grad_h * (1.0 + mod_row(image, 4)), normed, inverse)
        add_grad_mod(image, 2, jnp.sum(grad_x * attention, axis=0, keepdims=True))
        grad_att = (grad_x * mod_row(image, 2)).astype(bf16)
        d_all[own_rows, :] = grad_att
        grad_h_one = 0.0
        for core in range(2):
            grad_mixed = mxu(grad_att, attn_w[core, 3]).astype(bf16)
            for group in groups:
                lanes = pl.ds(group[0] * HD, group[1] * HD)
                query, key, value = (triple[core, j, at, lanes] for j in range(3))
                back = grad_mixed[:, group[0] * HD : (group[0] + group[1]) * HD]
                grads = [0.0, 0.0, 0.0]
                for head in range(group[1]):
                    low = soft[image, core * heads + group[0] + head]
                    prob = low.astype(f32)
                    head_back = one_head(back, group, head)
                    grad_soft = mxu(head_back, value, NT)
                    delta = jnp.sum(prob * grad_soft, axis=1, keepdims=True)
                    grad_scores = (prob * (grad_soft - delta) * scale).astype(bf16)
                    grads[0] = grads[0] + mxu(grad_scores, one_head(key, group, head))
                    grads[1] = grads[1] + mxu(grad_scores, one_head(query, group, head), TN)
                    grads[2] = grads[2] + mxu(low, head_back, TN)
                for j in range(3):
                    triple[core, j, at, lanes] = grads[j].astype(bf16)
            for j in range(3):
                grad_h_one = grad_h_one + mxu(triple[core, j, at, :], attn_w[core, j], NT)
        normed, inverse = layer_norm(tok)
        add_grad_mod(image, 0, jnp.sum(grad_h_one, axis=0, keepdims=True))
        add_grad_mod(image, 1, jnp.sum(grad_h_one * normed, axis=0, keepdims=True))
        grad_h_acc[own_rows, :] = grad_x + norm_back(grad_h_one * (1.0 + mod_row(image, 1)), normed, inverse)
        collect(wide_experts + image)
        return carry

    lax.fori_loop(0, images, backward, 0)
    for k in range(images, 3):
        collect(wide_experts + k)
    stores = [
        pltpu.make_async_copy(branch_acc.at[own], output_ref, load_sem.at[2]),
        pltpu.make_async_copy(grad_h_acc.at[own], grad_tok_ref, load_sem.at[3]),
    ]
    for copy in stores:
        copy.start()

    crosses = [
        remote(grad_mod.at[1 - mp], grad_mod_in, core_send.at[5], core_recv.at[5], other),
        remote(gate_grad, gate_grad_in, core_send.at[6], core_recv.at[6], other),
        remote(attn_share, attn_in, core_send.at[7], core_recv.at[7], other),
    ]
    crosses[0].start()
    crosses[1].start()

    def attn_grad(core, j):
        if j == parts - 1:
            return mxu(d_all[own, :], mixed[core], TN)
        return mxu(h_one[...], triple[core, j], TN)

    for j in range(parts):
        attn_share[j] = attn_grad(1 - mp, j).astype(bf16)

    crosses[2].start()
    ada_scatter = Scatter(place, ada_buf, (ada_a, ada_b, ada_z), ada_back_send, ada_back_recv)
    attn_scatter = Scatter(place, attn_buf, (attn_a, attn_b, attn_z), attn_back_send, attn_back_recv)
    crosses[0].wait()
    crosses[1].wait()
    grad_low = (grad_mod[mp] + grad_mod_in[...]).astype(bf16)
    up_grad[:, low_cut] = mxu(cond_low[...], grad_low[:, :cut], TN)
    down_grad[:, low_cut] = mxu(cond_low[...], grad_low[:, cut:], TN)
    down_grad[:, pl.ds(cut - LANES, LANES)] = gate_grad[...] + gate_grad_in[...]
    grads_to_blocks(place, rows, (up_grad[:, low_cut], down_grad[:, low_cut]), ada_buf.at[0])
    ada_scatter.start(0, 0)
    crosses[2].wait()
    grads = [attn_grad(mp, j) + attn_in[j].astype(f32) for j in range(parts)]
    grads_to_blocks(place, rows, grads, attn_buf.at[0])
    attn_scatter.start(0, 0)
    scatters = (ada_scatter, attn_scatter)
    for stage in range(2):
        for small in scatters:
            small.arrive(stage, 0)
            small.add(stage, 0)
            small.start(stage + 1, 0)
    square = jnp.zeros((1, 1), f32)
    for e in range(wide_experts):
        square = square + jnp.sum(total_ref[e] * total_ref[e])
    for small in scatters:
        small.arrive(2, 0)
    ada, attn = ada_scatter.last(0), attn_scatter.last(0)
    ada_out[...] = ada
    attn_out[...] = attn
    row = lax.broadcasted_iota(jnp.int32, ada.shape, 0)
    lane = lax.broadcasted_iota(jnp.int32, ada.shape, 1)
    twice = (row >= rows) & (lane >= cut - LANES)
    square = square + jnp.sum(jnp.where(twice, 0.5, 1.0) * ada * ada) + jnp.sum(attn * attn)
    value = jnp.broadcast_to(square, norm_out.shape)
    norm_out[...] = all_sum(place, value, norm_src, norm_box, norm_send, norm_recv)
    for copy in stores:
        copy.wait()


def block_call(tokens, condition, cotangent, routes, w_ada, w_gate, w_attn, w_expert):
    count = lax.axis_size("dp")
    own_tok, width = tokens.shape
    rows, wide = w_ada.shape
    experts = w_gate.shape[1]
    parts, _, half = w_attn.shape
    _, wide_experts, _, hidden = w_expert.shape
    depth, side = dp_sizes(count)
    images = own_tok // PATCH
    cut = (wide // 2 + LANES) // 2
    block, ada_block, attn_block = block_rows(rows, 2), block_rows(rows, 2), block_rows(rows, parts)
    tok = 2 * own_tok
    tile = TILE if count <= 16 else TILE // 2
    vmem = pl.BlockSpec(memory_space=pltpu.VMEM)
    hbm = pl.BlockSpec(memory_space=pl.ANY)
    hops = depth + 2 * side - 3

    def sems(*shape):
        return pltpu.SemaphoreType.DMA(shape)

    def boxes(slots, height, lanes):
        return [
            pltpu.VMEM((slots, side - 1, side * depth, height, lanes), bf16),
            pltpu.VMEM((slots, side - 1, depth, height, lanes), bf16),
            pltpu.VMEM((slots, depth - 1, 1, height, lanes), bf16),
        ]

    return pl.pallas_call(
        functools.partial(block_kernel, count, rows, experts, tile),
        out_shape=(
            jax.ShapeDtypeStruct((own_tok, width), f32),
            jax.ShapeDtypeStruct((own_tok, width), f32),
            jax.ShapeDtypeStruct((ada_block, cut), f32),
            jax.ShapeDtypeStruct((attn_block, half), f32),
            jax.ShapeDtypeStruct((wide_experts, block, hidden), f32),
            jax.ShapeDtypeStruct((8, LANES), f32),
        ),
        in_specs=[hbm, hbm] + [vmem] * 6,
        out_specs=(hbm, hbm) + (vmem,) * 4,
        scratch_shapes=[
            pltpu.VMEM((wide_experts, count, block, hidden), bf16),
            *boxes(SLOTS, block, hidden),
            pltpu.VMEM((1, count, ada_block, cut), bf16),
            *boxes(1, ada_block, cut),
            pltpu.VMEM((1, count, attn_block, half), bf16),
            *boxes(1, attn_block, half),
            pltpu.VMEM((count, attn_block, half), bf16),
            pltpu.VMEM((2, parts, width, half), bf16),
            pltpu.VMEM((width, LANES), bf16),
            pltpu.VMEM(condition.shape, bf16),
            pltpu.VMEM((2, condition.shape[0], 2 * cut), f32),
            pltpu.VMEM((2, condition.shape[0], 2 * cut), f32),
            pltpu.VMEM((condition.shape[0], 2 * cut), f32),
            pltpu.VMEM((2, 3, own_tok, half), bf16),
            pltpu.VMEM((2, own_tok, half), bf16),
            pltpu.VMEM((own_tok, width), bf16),
            pltpu.VMEM((images, width // HD, PATCH, PATCH), bf16),
            pltpu.VMEM((tok, width), bf16),
            pltpu.VMEM((tok, width), bf16),
            pltpu.VMEM((tok, LANES), f32),
            pltpu.VMEM((tok, width), f32),
            pltpu.VMEM((tok, width), f32),
            pltpu.VMEM((tok, LANES), f32),
            pltpu.VMEM((own_tok, LANES), f32),
            pltpu.VMEM((2, own_tok, width), bf16),
            pltpu.VMEM((width, hidden), bf16),
            pltpu.VMEM((width, hidden), bf16),
            pltpu.VMEM((width, hidden), f32),
            pltpu.VMEM((width, hidden), f32),
            pltpu.VMEM((width, LANES), f32),
            pltpu.VMEM((width, LANES), f32),
            pltpu.VMEM((parts, width, half), bf16),
            pltpu.VMEM((parts, width, half), bf16),
            pltpu.VMEM((4, 8, LANES), f32),
            pltpu.VMEM((4, max(depth, side), 8, LANES), f32),
            sems(4),
            *[sems(wide_experts, hops)] * 4,
            *[sems(1, hops)] * 8,
            sems(8),
            sems(8),
            sems(images, 3),
            sems(images, 3),
            sems(hops + 1),
            sems(hops + 1),
        ],
        compiler_params=pltpu.CompilerParams(collective_id=1, has_side_effects=True, vmem_limit_bytes=VMEM_BYTES),
        cost_estimate=pl.CostEstimate(
            flops=12 * tok * width * hidden * wide_experts, bytes_accessed=16 * w_expert.size, transcendentals=0
        ),
        name="block",
    )(tokens, cotangent, condition, routes, w_ada, w_gate, w_attn, w_expert)


def per_device(
    tokens,
    condition,
    cotangent,
    routes,
    w_ada,
    ada_first,
    ada_second,
    w_gate,
    gate_first,
    gate_second,
    w_attn,
    attn_first,
    attn_second,
    w_expert,
    expert_first,
    expert_second,
):
    tok_dev, width = tokens.shape
    experts = w_gate.shape[1]
    rows = w_expert.shape[2]
    half = w_attn.shape[2]
    wide = w_ada.shape[1] // 2
    own_routes = lax.dynamic_slice_in_dim(routes, lax.axis_index("mp") * tok_dev, tok_dev, 0)
    output, grad_tokens, ada_block, attn_block, expert_blocks, square_sum = block_call(
        tokens, condition, cotangent, own_routes, w_ada, w_gate, w_attn, w_expert
    )
    expert_total = expert_blocks[:, : 2 * rows].reshape(-1, 2, rows, w_expert.shape[3]).transpose(1, 0, 2, 3)
    ada_half = jnp.concatenate([ada_block[:rows], ada_block[rows : 2 * rows]], axis=1)
    gate_total = ada_half[:, wide : wide + experts]
    ada_total = lax.all_gather(ada_half[:, :wide], "mp", axis=1, tiled=True)
    attn_total = attn_block[: 4 * rows].reshape(4, rows, half)
    grad_norm = jnp.sqrt(square_sum[0, 0])
    factor = jnp.minimum(1.0, CLIP_NORM / (grad_norm + 1e-06))
    ada_new, ada_first_new, ada_second_new = adam(w_ada, ada_first, ada_second, ada_total * factor)
    gate_new, gate_first_new, gate_second_new = adam(
        w_gate, gate_first, gate_second, gate_total * factor
    )
    attn_new, attn_first_new, attn_second_new = adam(
        w_attn, attn_first, attn_second, attn_total * factor
    )
    expert_new, expert_first_new, expert_second_new = adam(
        w_expert, expert_first, expert_second, expert_total * factor
    )
    return (
        output,
        grad_tokens,
        grad_norm,
        ada_new,
        ada_first_new,
        ada_second_new,
        gate_new,
        gate_first_new,
        gate_second_new,
        attn_new,
        attn_first_new,
        attn_second_new,
        expert_new,
        expert_first_new,
        expert_second_new,
    )


def solution(mesh):
    placed = (
        P(("dp", "mp"), None),
        P("dp", None),
        P(("dp", "mp"), None),
        P("dp", None),
        P("dp", None),
        P("dp", None),
        P("dp", None),
        P("dp", None),
        P("dp", None),
        P("dp", None),
        P(None, "dp", "mp"),
        P(None, "dp", "mp"),
        P(None, "dp", "mp"),
        P(None, None, "dp", "mp"),
        P(None, None, "dp", "mp"),
        P(None, None, "dp", "mp"),
    )
    return jax.shard_map(
        per_device,
        mesh=mesh,
        in_specs=placed,
        out_specs=(
            P(("dp", "mp"), None),
            P(("dp", "mp"), None),
            P(),
            P("dp", None),
            P("dp", None),
            P("dp", None),
            P("dp", None),
            P("dp", None),
            P("dp", None),
            P(None, "dp", "mp"),
            P(None, "dp", "mp"),
            P(None, "dp", "mp"),
            P(None, None, "dp", "mp"),
            P(None, None, "dp", "mp"),
            P(None, None, "dp", "mp"),
        ),
        check_vma=False,
    )
```

```python
import functools
import math

import jax
import jax.numpy as jnp
from jax import lax
from jax.experimental import pallas as pl
from jax.experimental.pallas import tpu as pltpu
from jax.sharding import PartitionSpec as P

HD = 64
PATCH = 256
STEP = 10
LANES = 128
SUB = 16
TILE = 512
SLOTS = 4
ZBA, BZA = "zba", "bza"
CUT_ONE, CUT_ALL = 2, 3

EPS_NORM = 1e-06
CLIP_NORM = 0.1
RATE = 0.08
BETA_ONE = 0.9
BETA_TWO = 0.95
ADAM_EPS = 1e-08
DECAY = 0.01
GELU_LIN = 0.7978845608
GELU_CUBE = 0.7978845608 * 0.044715

MESH = pl.DeviceIdType.MESH
VMEM_BYTES = 127 * 512 * 1024
bf16 = jnp.bfloat16
f32 = jnp.float32
NN = (((1,), (0,)), ((), ()))
NT = (((1,), (1,)), ((), ()))
TN = (((0,), (0,)), ((), ()))


def mxu(left, right, dims=NN):
    return lax.dot_general(left, right, dims, preferred_element_type=f32)


def layer_norm(value):
    center = value - jnp.mean(value, axis=-1, keepdims=True)
    inverse = lax.rsqrt(jnp.mean(center * center, axis=-1, keepdims=True) + EPS_NORM)
    return (center * inverse, inverse)


def norm_back(grad, normed, inverse):
    mean_grad = jnp.mean(grad, axis=-1, keepdims=True)
    mean_proj = jnp.mean(grad * normed, axis=-1, keepdims=True)
    return inverse * (grad - mean_grad - normed * mean_proj)


def adam(master, first, second, grad):
    first_new = BETA_ONE * first + (1.0 - BETA_ONE) * grad
    second_new = BETA_TWO * second + (1.0 - BETA_TWO) * grad * grad
    fix_one = 1.0 - BETA_ONE**STEP
    fix_two = 1.0 - BETA_TWO**STEP
    update = first_new / fix_one / (jnp.sqrt(second_new / fix_two) + ADAM_EPS) + DECAY * master
    return (master - RATE * update, first_new, second_new)


def gelu_both(value):
    square = value * value
    tanh = jnp.tanh(value * (GELU_CUBE * square + GELU_LIN))
    half = 0.5 * tanh + 0.5
    act = value * half
    slope = half + act * (1.0 - tanh) * (3.0 * GELU_CUBE * square + GELU_LIN)
    return act, slope


def dp_sizes(count):
    side = 4 if count >= 64 else 2
    return count // (side * side), side


class Place:
    def __init__(self, count):
        self.count = count
        self.depth, self.side = dp_sizes(count)
        self.dp = lax.axis_index("dp")
        self.mp = lax.axis_index("mp")
        side = self.side
        y = (self.dp // side) % side
        x = self.dp % side
        self.at = {
            "z": self.dp // (side * side),
            "a": jnp.where(self.mp == 0, y, x),
            "b": jnp.where(self.mp == 0, x, y),
        }
        self.size = {"z": self.depth, "a": side, "b": side}

    def slot_at(self, order, at):
        slot = 0
        for axis in reversed(order):
            slot = slot * self.size[axis] + at.get(axis, 0)
        return slot

    def slot(self, order=ZBA):
        return self.slot_at(order, self.at)

    def slot_of(self, dp, core, order=ZBA):
        side = self.side
        z, y, x = dp // (side * side), (dp // side) % side, dp % side
        one = self.slot_at(order, {"z": z, "a": y, "b": x})
        two = self.slot_at(order, {"z": z, "a": x, "b": y})
        return jnp.where(core == 0, one, two)

    def device(self, at):
        z, a, b = at["z"], at["a"], at["b"]
        side = self.side
        dp = jnp.where(self.mp == 0, (z * side + a) * side + b, (z * side + b) * side + a)
        return (dp, self.mp)

    def along(self, axis, step):
        return (self.at[axis] + step) % self.size[axis]

    def peers(self, axis):
        return [self.device({**self.at, axis: self.along(axis, k)}) for k in range(1, self.size[axis])]

    def other_core(self):
        return (self.dp, 1 - self.mp)

    def peers_layer(self):
        layer = self.side * self.side
        first = self.dp - self.dp % layer
        peers = []
        for k in range(1, 2 * layer):
            spot = (self.dp % layer * 2 + self.mp + k) % (2 * layer)
            peers.append((first + spot // 2, spot % 2))
        return peers

    def greet(self):
        peers = self.peers("z") + self.peers_layer()
        barrier = pltpu.get_barrier_semaphore()
        for peer in peers:
            pl.semaphore_signal(barrier, inc=1, device_id=peer, device_id_type=MESH)
        pl.semaphore_wait(barrier, len(peers))


def remote(src, dst, send, recv, peer):
    return pltpu.make_async_remote_copy(
        src_ref=src, dst_ref=dst, send_sem=send, recv_sem=recv, device_id=peer, device_id_type=MESH
    )


def span(place, order, stage):
    return math.prod(place.size[axis] for axis in order[:stage])


class Gather:
    def __init__(self, place, buf, send, recv, order=ZBA):
        self.p, self.buf, self.send, self.recv, self.order = place, buf, send, recv, order

    def copies(self, stage, e):
        p, order = self.p, self.order
        fixed = {axis: p.at[axis] for axis in order[stage:]}
        src = self.buf.at[e, pl.ds(p.slot_at(order, fixed), span(p, order, stage))]
        base = sum(p.size[axis] - 1 for axis in order[:stage])
        return [
            remote(src, src, self.send.at[e, base + k], self.recv.at[e, base + k], peer)
            for k, peer in enumerate(p.peers(order[stage]))
        ]

    def start(self, stage, e):
        for copy in self.copies(stage, e):
            copy.start()

    def arrive(self, stage, e):
        for copy in self.copies(stage, e):
            copy.wait_recv()

    def sent(self, e):
        for stage in range(3):
            for copy in self.copies(stage, e):
                copy.wait_send()


class Scatter:
    def __init__(self, place, buf, box, send, recv, order=ZBA):
        self.p, self.buf, self.box, self.send, self.recv, self.order = place, buf, box, send, recv, order

    def parts(self, stage):
        p, order = self.p, self.order
        base = 0
        for before in range(3 - 1, 2 - stage, -1):
            base += (p.size[order[before]] - 1) * span(p, order, before)
        return order[2 - stage], span(p, order, 2 - stage), base

    def copies(self, stage, e):
        p, order = self.p, self.order
        axis, many, base = self.parts(stage)
        sem = sum(p.size[order[2 - before]] - 1 for before in range(stage))
        made = []
        for k, peer in enumerate(p.peers(axis)):
            fixed = {name: p.at[name] for name in order[2 - stage :]}
            fixed[axis] = p.along(axis, k + 1)
            src = self.buf.at[e, pl.ds(p.slot_at(order, fixed), many)]
            dst = self.box.at[e % SLOTS, pl.ds(base + k * many, many)]
            made.append(remote(src, dst, self.send.at[e, sem + k], self.recv.at[e, sem + k], peer))
        return made

    def start(self, stage, e):
        for copy in self.copies(stage, e):
            copy.start()

    def arrive(self, stage, e):
        for copy in self.copies(stage, e):
            copy.wait()

    def add(self, stage, e):
        p, order = self.p, self.order
        axis, many, base = self.parts(stage)
        first = p.slot_at(order, {name: p.at[name] for name in order[2 - stage :]})

        def one(i, carry):
            total = self.buf[e, first + i].astype(f32)
            for k in range(p.size[axis] - 1):
                total = total + self.box[e % SLOTS, base + k * many + i].astype(f32)
            self.buf[e, first + i] = total.astype(bf16)
            return carry

        lax.fori_loop(0, many, one, 0)

    def last(self, e):
        p, order = self.p, self.order
        axis, many, base = self.parts(2)
        total = self.buf[e, p.slot(order)].astype(f32)
        for k in range(p.size[axis] - 1):
            total = total + self.box[e % SLOTS, base + k].astype(f32)
        return total


def block_rows(rows, parts):
    return (parts * rows + SUB - 1) // SUB * SUB


def blocks_to_weights(place, rows, buf, core, outs, order=ZBA):
    many = SUB // math.gcd(SUB, rows)
    for first in range(0, place.count, many):
        blocks = [buf[place.slot_of(first + i, core, order)].astype(f32) for i in range(many)]
        for part, out in enumerate(outs):
            pieces = [block[part * rows : (part + 1) * rows] for block in blocks]
            out[pl.ds(first * rows, many * rows), :] = jnp.concatenate(pieces, axis=0).astype(bf16)


def grads_to_blocks(place, rows, grads, buf, order=ZBA):
    block = buf.shape[1]
    for dp in range(place.count):
        pieces = [grad[dp * rows : (dp + 1) * rows, :] for grad in grads]
        if block > rows * len(grads):
            pieces.append(jnp.zeros((block - rows * len(grads), buf.shape[2]), f32))
        buf[place.slot_of(dp, place.mp, order)] = jnp.concatenate(pieces, axis=0).astype(bf16)


def all_sum(place, value, src, box, send, recv):
    layer = place.side * place.side
    spot = place.dp % layer
    z = place.at["z"]
    src[0] = value
    box[z] = value
    copies = [
        remote(src.at[0], box.at[z], send.at[k], recv.at[k], peer) for k, peer in enumerate(place.peers("z"))
    ]
    for copy in copies:
        copy.start()
    for copy in copies:
        copy.wait()
    total = box[0]
    for i in range(1, place.depth):
        total = total + box[i]
    mine = spot * 2 + place.mp
    base = place.depth
    src[1] = total
    box[base + mine] = total
    at = place.depth - 1
    copies = [
        remote(src.at[1], box.at[base + mine], send.at[at + k], recv.at[at + k], peer)
        for k, peer in enumerate(place.peers_layer())
    ]
    for copy in copies:
        copy.start()
    for copy in copies:
        copy.wait()
    total = box[base]
    for i in range(1, 2 * layer):
        total = total + box[base + i]
    return total


class Both:
    def __init__(self, *both):
        self.both = both

    def start(self, stage, e):
        for one in self.both:
            one.start(stage, e)

    def arrive(self, stage, e):
        for one in self.both:
            one.arrive(stage, e)

    def add(self, stage, e):
        for one in self.both:
            one.add(stage, e)

    def sent(self, e):
        for one in self.both:
            one.sent(e)


def block_kernel(
    count, rows, experts, tile,
    tok_ref, cot_ref, cond_ref, route_ref, ada_ref, gate_ref, attn_ref, w_ref,
    output_ref, grad_tok_ref, ada_out, attn_out, total_ref, norm_out,
    buf_one, buf_two, box_one, box_two,
    ada_buf, sc_buf, mod_buf, mod_far, attn_buf, attn_box, attn_far, attn_w,
    cond_low, mod, grad_mod, grad_mod_in, triple, mixed, h_one, soft,
    h_all, d_all, gate_all, branch_acc, grad_h_acc, grad_gate_acc, gate_in, share_in,
    up_w, down_w, up_grad, down_grad, gate_grad, attn_share, attn_in, norm_src, norm_box,
    load_sem, gather_send, gather_recv, gather_send_two, gather_recv_two,
    scatter_send, scatter_recv, scatter_send_two, scatter_recv_two,
    ada_send, ada_recv, sc_send, sc_recv, mod_send, mod_recv, attn_send, attn_recv, attn_back_send, attn_back_recv,
    core_send, core_recv, token_send, token_recv, norm_send, norm_recv,
):
    place = Place(count)
    mp = place.mp
    wide_experts = w_ref.shape[1]
    own_tok, width = tok_ref.shape
    images = own_tok // PATCH
    half = attn_ref.shape[2]
    first = half // LANES * LANES
    heads = half // HD
    wide = ada_ref.shape[1] // 2
    cut = ada_buf.shape[3]
    scale = HD ** (-0.5)
    own_at = pl.multiple_of(mp * own_tok, own_tok)
    their_at = pl.multiple_of((1 - mp) * own_tok, own_tok)
    own, theirs = pl.ds(own_at, own_tok), pl.ds(their_at, own_tok)
    other = place.other_core()

    loads = [
        pltpu.make_async_copy(tok_ref, branch_acc.at[pl.ds(0, own_tok)], load_sem.at[0]),
        pltpu.make_async_copy(cot_ref, branch_acc.at[pl.ds(own_tok, own_tok)], load_sem.at[1]),
    ]
    for load in loads:
        load.start()

    def put(target, block, order=ZBA):
        if block.shape[0] != target.shape[1]:
            target[place.slot(order)] = jnp.zeros(target.shape[1:], bf16)
        target[place.slot(order), pl.ds(0, block.shape[0])] = block

    cols = ada_ref[:, pl.ds(pl.multiple_of(mp * wide, LANES), wide)]
    tail = jnp.concatenate([cols[:, cut:], jnp.zeros((rows, 2 * cut - wide), f32)], axis=1)
    put(ada_buf.at[0], jnp.concatenate([cols[:, :cut], tail], axis=0).astype(bf16))
    parts = attn_ref.shape[0]
    side_by = lax.broadcasted_iota(jnp.int32, (experts, LANES), 1) == lax.broadcasted_iota(
        jnp.int32, (experts, LANES), 0
    )
    gate = mxu(gate_ref[...].astype(bf16), side_by.astype(f32).astype(bf16), TN)[:, : 2 * LANES - half]
    spare = [gate] + [jnp.zeros_like(gate)] * (parts - 1)
    both = [jnp.concatenate([attn_ref[j], spare[j]], axis=1) for j in range(parts)]
    put(attn_buf.at[0], jnp.concatenate(both, axis=0).astype(bf16))
    cond = cond_ref[...]
    cond = cond / (1.0 + jnp.exp(-cond))
    cond_low[...] = cond.astype(bf16)
    sc_buf[0, place.slot()] = jnp.concatenate([cond, jnp.zeros((SUB - cond.shape[0], width), f32)], axis=0).astype(bf16)
    place.greet()
    ada_gather = Gather(place, ada_buf, ada_send, ada_recv)
    attn_gather = Gather(place, attn_buf, attn_send, attn_recv)
    cuts = (pl.ds(0, buf_one.shape[3]), pl.ds(buf_one.shape[3], buf_two.shape[3]))
    streams = tuple(zip((buf_one, buf_two), cuts, (ZBA, BZA)))
    gather = Both(
        Gather(place, buf_one, gather_send, gather_recv, ZBA),
        Gather(place, buf_two, gather_send_two, gather_recv_two, BZA),
    )
    scatter = Both(
        Scatter(place, buf_one, box_one, scatter_send, scatter_recv, ZBA),
        Scatter(place, buf_two, box_two, scatter_send_two, scatter_recv_two, BZA),
    )
    sc_gather = Gather(place, sc_buf, sc_send, sc_recv)
    ada_gather.start(0, 0)
    attn_gather.start(0, 0)
    sc_gather.start(0, 0)

    def fill(e, carry):
        both = jnp.concatenate([w_ref[0, e], w_ref[1, e]], axis=0).astype(bf16)
        for buf, lanes, order in streams:
            put(buf.at[e], both[:, lanes.start : lanes.start + lanes.size], order)
        return carry

    lax.fori_loop(0, wide_experts, fill, 0)

    def tick(k):
        @pl.when(k + 4 < wide_experts)
        def _():
            gather.start(0, k + 4)

        @pl.when((k + 2 >= 0) & (k + 2 < wide_experts))
        def _():
            gather.arrive(0, k + 2)
            gather.start(1, k + 2)

        @pl.when((k + 1 >= 0) & (k + 1 < wide_experts))
        def _():
            gather.arrive(1, k + 1)
            gather.start(2, k + 1)

    grad_mod[...] = jnp.zeros_like(grad_mod)
    gather.start(0, 0)
    gather.start(0, 1)
    for stage in range(2):
        for small in (ada_gather, attn_gather):
            small.arrive(stage, 0)
            small.start(stage + 1, 0)
    gather.start(0, 2)
    gather.arrive(0, 0)
    gather.start(1, 0)
    ada_gather.arrive(2, 0)

    low_cut = pl.ds(0, cut)
    blocks_to_weights(place, rows, ada_buf.at[0], mp, (up_w.at[:, low_cut], down_w.at[:, low_cut]))
    mod[mp, :, pl.ds(0, cut)] = mxu(cond_low[...], up_w[:, low_cut])
    mod[mp, :, pl.ds(cut, cut)] = mxu(cond_low[...], down_w[:, low_cut])
    mod_cross = remote(mod.at[mp], mod.at[mp], core_send.at[1], core_recv.at[1], other)
    mod_cross.start()
    attn_gather.arrive(2, 0)
    attn_cross = remote(attn_buf.at[0], attn_far, core_send.at[0], core_recv.at[0], other)
    attn_cross.start()
    blocks_to_weights(place, rows, attn_buf.at[0], mp, [attn_w.at[mp, j] for j in range(parts)])
    for load in loads:
        load.wait()
    ada_gather.sent(0)
    attn_gather.sent(0)
    sc_gather.arrive(0, 0)
    sc_gather.start(1, 0)
    attn_cross.wait()
    blocks_to_weights(place, rows, attn_far, 1 - mp, [attn_w.at[1 - mp, j] for j in range(parts)])
    mod_cross.wait()
    gate_lanes = pl.ds(first, LANES)
    half_lanes = pl.ds(0, half)

    def weight(core, j):
        return attn_w[core, j, :, half_lanes]

    lane_pair = lax.broadcasted_iota(jnp.int32, (PATCH, 2 * HD), 1)
    masks = [(lane_pair < HD).astype(f32).astype(bf16), (lane_pair >= HD).astype(f32).astype(bf16)]
    groups = [(at, min(2, heads - at)) for at in range(0, heads, 2)]
    expert_lane = lax.broadcasted_iota(jnp.int32, (PATCH, LANES), 1) - (half - first)

    def mod_row(image, vector):
        flat = vector % 3 * width
        return mod[vector // 3, pl.ds(mp * images + image, 1), pl.ds(flat, width)]

    def add_grad_mod(image, vector, value):
        grad_mod[vector // 3, pl.ds(mp * images + image, 1), pl.ds(vector % 3 * width, width)] = value

    def one_head(value, group, head):
        return value if group[1] == 1 else value * masks[head]

    def route(h, image):
        valid = (expert_lane >= 0) & (expert_lane < experts)
        logits = jnp.where(valid, mxu(h, attn_w[0, 0, :, gate_lanes]), -jnp.inf)
        power = jnp.exp(logits - jnp.max(logits, axis=1, keepdims=True))
        router = power / jnp.sum(power, axis=1, keepdims=True)
        picks = route_ref[:, pl.ds(pl.multiple_of(own_at + image * PATCH, PATCH), PATCH)]
        spot = lax.broadcasted_iota(jnp.int32, (LANES, PATCH), 0) - (half - first)
        picked = jnp.where((picks[0:1, :] == spot) | (picks[1:2, :] == spot), 1.0, 0.0)
        return router, picked.T

    def attend(at):
        return mxu(mixed[0, at, :], weight(0, 3), NT) + mxu(mixed[1, at, :], weight(1, 3), NT)

    def token_copies(image):
        at = pl.ds(pl.multiple_of(own_at + image * PATCH, PATCH), PATCH)
        return [
            remote(ref.at[at], ref.at[at], token_send.at[image, i], token_recv.at[image, i], other)
            for i, ref in enumerate((h_all, d_all, gate_all))
        ]

    def forward(image, carry):
        at = pl.ds(pl.multiple_of(image * PATCH, PATCH), PATCH)
        cot_at = pl.ds(pl.multiple_of(own_tok + image * PATCH, PATCH), PATCH)
        all_at = pl.ds(pl.multiple_of(own_at + image * PATCH, PATCH), PATCH)
        normed, _ = layer_norm(branch_acc[at, :])
        h = (normed * (1.0 + mod_row(image, 1)) + mod_row(image, 0)).astype(bf16)
        h_one[at, :] = h
        for core in range(2):
            for j in range(3):
                triple[core, j, at, :] = mxu(h, weight(core, j)).astype(bf16)
            for group in groups:
                lanes = pl.ds(group[0] * HD, group[1] * HD)
                query, key, value = (triple[core, j, at, lanes] for j in range(3))
                total = 0.0
                for head in range(group[1]):
                    scores = mxu(one_head(query, group, head), key, NT) * scale
                    power = jnp.exp(scores - jnp.max(scores, axis=1, keepdims=True))
                    low = (power * (1.0 / jnp.sum(power, axis=1, keepdims=True))).astype(bf16)
                    soft[image, core * heads + group[0] + head] = low
                    total = total + mxu(low, one_head(value, group, head))
                mixed[core, at, lanes] = total.astype(bf16)
        x_one = branch_acc[at, :] + mod_row(image, 2) * attend(at)
        normed, _ = layer_norm(x_one)
        h = (normed * (1.0 + mod_row(image, 4)) + mod_row(image, 3)).astype(bf16)
        h_all[all_at, :] = h
        router, chosen = route(h, image)
        shared = (expert_lane >= experts) & (expert_lane < wide_experts)
        gate_all[all_at, :] = jnp.where(shared, 1.0, router * chosen)
        d_all[all_at, :] = (branch_acc[cot_at, :] * mod_row(image, 5)).astype(bf16)
        for copy in token_copies(image):
            copy.start()

        @pl.when(image % 2 == 1)
        def _():
            tick(image // 2 - 1)

        @pl.when(image == 0)
        def _():
            sc_gather.arrive(1, 0)
            sc_gather.start(2, 0)

        return carry

    lax.fori_loop(0, images, forward, 0)
    ahead = images // 2 - 1
    sc_gather.arrive(2, 0)
    sc_gather.sent(0)

    branch_acc[...] = jnp.zeros_like(branch_acc)
    grad_h_acc[...] = jnp.zeros_like(grad_h_acc)
    grad_gate_acc[...] = jnp.zeros_like(grad_gate_acc)

    def all_tokens(image, carry):
        for copy in token_copies(image):
            copy.wait()
        return carry

    lax.fori_loop(0, images, all_tokens, 0)

    def compute(e):
        for buf, lanes, order in streams:
            blocks_to_weights(place, rows, buf.at[e], mp, (up_w.at[:, lanes], down_w.at[:, lanes]), order)
        up_grad[...] = jnp.zeros_like(up_grad)
        down_grad[...] = jnp.zeros_like(down_grad)

        def one_tile(t, carry):
            at = pl.ds(pl.multiple_of(t * tile, tile), tile)
            h = h_all[at, :]
            d = d_all[at, :]
            lane = lax.broadcasted_iota(jnp.int32, (tile, LANES), 1) - (half - first)
            gate = jnp.sum(jnp.where(lane == e, gate_all[at, :], 0.0), axis=1, keepdims=True)
            pre = mxu(h, up_w[...])
            back = mxu(d, down_w[...])
            act, slope = gelu_both(pre)
            inner = jnp.sum(act * back, axis=1, keepdims=True)
            grad_gate_acc[at, :] += jnp.where(lane == e, inner, 0.0)
            act_low = (gate * act).astype(bf16)
            pre_low = (gate * back * slope).astype(bf16)
            branch_acc[at, :] += mxu(act_low, down_w[...], NT)
            grad_h_acc[at, :] += mxu(pre_low, up_w[...], NT)
            up_grad[...] += mxu(h, pre_low, TN)
            down_grad[...] += mxu(d, act_low, TN)
            return carry

        lax.fori_loop(0, h_all.shape[0] // tile, one_tile, 0)

    def put_total(e):
        for part, (_, lanes, _) in zip(scatter.both, streams):
            total_ref[e, :, lanes] = part.last(e)

    def collect(k):
        @pl.when((k >= 1) & (k - 1 < wide_experts))
        def _():
            scatter.arrive(0, k - 1)
            scatter.add(0, k - 1)
            scatter.start(1, k - 1)

        @pl.when((k >= 2) & (k - 2 < wide_experts))
        def _():
            scatter.arrive(1, k - 2)
            scatter.add(1, k - 2)
            scatter.start(2, k - 2)

        @pl.when((k >= 3) & (k - 3 < wide_experts))
        def _():
            scatter.arrive(2, k - 3)
            put_total(k - 3)

    def step(e, carry):
        tick(e + ahead)
        gather.arrive(2, e)
        compute(e)
        gather.sent(e)
        for buf, lanes, order in streams:
            grads_to_blocks(place, rows, (up_grad.at[:, lanes], down_grad.at[:, lanes]), buf.at[e], order)
        scatter.start(0, e)
        collect(e)
        return carry

    lax.fori_loop(0, wide_experts, step, 0)

    h_all[theirs, :] = branch_acc[theirs, :].astype(bf16)
    d_all[theirs, :] = grad_h_acc[theirs, :].astype(bf16)
    shares = [
        remote(h_all.at[theirs], share_in.at[0], core_send.at[2], core_recv.at[2], other),
        remote(d_all.at[theirs], share_in.at[1], core_send.at[3], core_recv.at[3], other),
        remote(grad_gate_acc.at[theirs], gate_in, core_send.at[4], core_recv.at[4], other),
    ]
    loads = [
        pltpu.make_async_copy(tok_ref, branch_acc.at[theirs], load_sem.at[0]),
        pltpu.make_async_copy(cot_ref, grad_h_acc.at[theirs], load_sem.at[1]),
    ]
    for copy in shares + loads:
        copy.start()
    gate_grad[...] = jnp.zeros_like(gate_grad)
    for copy in shares + loads:
        copy.wait()

    def backward(image, carry):
        at = pl.ds(pl.multiple_of(image * PATCH, PATCH), PATCH)
        own_rows = pl.ds(pl.multiple_of(own_at + image * PATCH, PATCH), PATCH)
        load_rows = pl.ds(pl.multiple_of(their_at + image * PATCH, PATCH), PATCH)
        tok, cot = branch_acc[load_rows, :], grad_h_acc[load_rows, :]
        branch = branch_acc[own_rows, :] + share_in[0, at, :].astype(f32)
        attention = attend(at)
        x_one = tok + mod_row(image, 2) * attention
        normed, inverse = layer_norm(x_one)
        branch_acc[own_rows, :] = x_one + mod_row(image, 5) * branch
        add_grad_mod(image, 5, jnp.sum(cot * branch, axis=0, keepdims=True))
        h = h_all[own_rows, :]
        router, chosen = route(h, image)
        grad_router = (grad_gate_acc[own_rows, :] + gate_in[at, :]) * chosen
        grad_logits = (router * (grad_router - jnp.sum(router * grad_router, axis=1, keepdims=True))).astype(bf16)
        gate_grad[...] += mxu(h, grad_logits, TN)
        grad_h = grad_h_acc[own_rows, :] + share_in[1, at, :].astype(f32) + mxu(grad_logits, attn_w[0, 0, :, gate_lanes], NT)
        add_grad_mod(image, 3, jnp.sum(grad_h, axis=0, keepdims=True))
        add_grad_mod(image, 4, jnp.sum(grad_h * normed, axis=0, keepdims=True))
        grad_x = cot + norm_back(grad_h * (1.0 + mod_row(image, 4)), normed, inverse)
        add_grad_mod(image, 2, jnp.sum(grad_x * attention, axis=0, keepdims=True))
        grad_att = (grad_x * mod_row(image, 2)).astype(bf16)
        d_all[own_rows, :] = grad_att
        grad_h_one = 0.0
        for core in range(2):
            grad_mixed = mxu(grad_att, weight(core, 3)).astype(bf16)
            for group in groups:
                lanes = pl.ds(group[0] * HD, group[1] * HD)
                query, key, value = (triple[core, j, at, lanes] for j in range(3))
                back = grad_mixed[:, group[0] * HD : (group[0] + group[1]) * HD]
                grads = [0.0, 0.0, 0.0]
                for head in range(group[1]):
                    low = soft[image, core * heads + group[0] + head]
                    prob = low.astype(f32)
                    head_back = one_head(back, group, head)
                    grad_soft = mxu(head_back, value, NT)
                    delta = jnp.sum(prob * grad_soft, axis=1, keepdims=True)
                    grad_scores = (prob * (grad_soft - delta) * scale).astype(bf16)
                    grads[0] = grads[0] + mxu(grad_scores, one_head(key, group, head))
                    grads[1] = grads[1] + mxu(grad_scores, one_head(query, group, head), TN)
                    grads[2] = grads[2] + mxu(low, head_back, TN)
                for j in range(3):
                    triple[core, j, at, lanes] = grads[j].astype(bf16)
            for j in range(3):
                grad_h_one = grad_h_one + mxu(triple[core, j, at, :], weight(core, j), NT)
        normed, inverse = layer_norm(tok)
        add_grad_mod(image, 0, jnp.sum(grad_h_one, axis=0, keepdims=True))
        add_grad_mod(image, 1, jnp.sum(grad_h_one * normed, axis=0, keepdims=True))
        grad_h_acc[own_rows, :] = grad_x + norm_back(grad_h_one * (1.0 + mod_row(image, 1)), normed, inverse)
        collect(wide_experts + image)
        return carry

    lax.fori_loop(0, images, backward, 0)
    for k in range(images, 3):
        collect(wide_experts + k)
    stores = [
        pltpu.make_async_copy(branch_acc.at[own], output_ref, load_sem.at[2]),
        pltpu.make_async_copy(grad_h_acc.at[own], grad_tok_ref, load_sem.at[3]),
    ]
    for copy in stores:
        copy.start()

    crosses = [
        remote(grad_mod.at[1 - mp], grad_mod_in, core_send.at[5], core_recv.at[5], other),
        remote(attn_share, attn_in, core_send.at[6], core_recv.at[6], other),
        remote(mod_buf.at[0], mod_far, core_send.at[7], core_recv.at[7], other),
    ]
    crosses[0].start()

    def attn_grad(core, j):
        if j == parts - 1:
            return mxu(d_all[own, :], mixed[core], TN)
        return mxu(h_one[...], triple[core, j], TN)

    spare = pl.ds(half, 2 * LANES - half)
    for j in range(parts):
        attn_share[j, :, half_lanes] = attn_grad(1 - mp, j).astype(bf16)
        if j > 0:
            attn_share[j, :, spare] = jnp.zeros((width, 2 * LANES - half), bf16)
    attn_share[0, :, spare] = gate_grad[:, pl.ds(half - first, 2 * LANES - half)].astype(bf16)
    crosses[1].start()
    crosses[0].wait()
    grad_low = grad_mod[mp] + grad_mod_in[...]
    mod_buf[0, place.slot()] = jnp.concatenate([grad_low[:, :cut], grad_low[:, cut:]], axis=0).astype(bf16)
    mod_gather = Gather(place, mod_buf, mod_send, mod_recv)
    mod_gather.start(0, 0)
    crosses[1].wait()
    places = [(up_grad, 0), (up_grad, 1), (up_grad, 2), (down_grad, 0)]
    for j in range(parts):
        ref, at = places[j]
        ref[:, pl.ds(at * 2 * LANES, half)] = attn_grad(mp, j) + attn_in[j, :, half_lanes].astype(f32)
        if j > 0:
            ref[:, pl.ds(at * 2 * LANES + half, 2 * LANES - half)] = jnp.zeros((width, 2 * LANES - half), f32)
    up_grad[:, spare] = gate_grad[:, pl.ds(half - first, 2 * LANES - half)] + attn_in[0, :, spare].astype(f32)
    grads = [ref[:, pl.ds(at * 2 * LANES, 2 * LANES)] for ref, at in places]
    grads_to_blocks(place, rows, grads, attn_buf.at[0])
    attn_scatter = Scatter(place, attn_buf, attn_box, attn_back_send, attn_back_recv)
    attn_scatter.start(0, 0)
    for stage in range(2):
        mod_gather.arrive(stage, 0)
        mod_gather.start(stage + 1, 0)
        attn_scatter.arrive(stage, 0)
        attn_scatter.add(stage, 0)
        attn_scatter.start(stage + 1, 0)
    square = jnp.zeros((1, 1), f32)
    for e in range(wide_experts):
        square = square + jnp.sum(total_ref[e] * total_ref[e])
    mod_gather.arrive(2, 0)
    crosses[2].start()
    row = lax.broadcasted_iota(jnp.int32, (width, LANES), 0)
    lane = lax.broadcasted_iota(jnp.int32, (width, LANES), 1)
    pick = ((row == place.dp * rows + lane) & (lane < rows)).astype(f32).astype(bf16)
    group = cond_ref.shape[0]

    def in_order(ref, core, at):
        pieces = [ref[place.slot_of(dp, core)].astype(f32)[at : at + group] for dp in range(count)]
        return jnp.concatenate(pieces, axis=0).astype(bf16)

    conds = mxu(in_order(sc_buf.at[0], mp, 0), pick).astype(bf16)

    def ada_grad(ref, core):
        low = mxu(conds, in_order(ref, core, 0), TN)[:rows]
        high = mxu(conds, in_order(ref, core, group), TN)[:rows, : wide - cut]
        start = pl.multiple_of(core * wide, LANES)
        ada_out[:, pl.ds(start, cut)] = low
        ada_out[:, pl.ds(pl.multiple_of(start + cut, LANES), wide - cut)] = high
        return jnp.sum(low * low) + jnp.sum(high * high)

    small = ada_grad(mod_buf.at[0], mp)
    mod_gather.sent(0)
    crosses[2].wait()
    small = small + ada_grad(mod_far, 1 - mp)
    attn_scatter.arrive(2, 0)
    attn = attn_scatter.last(0)
    attn_out[...] = attn
    lane = lax.broadcasted_iota(jnp.int32, attn.shape, 1)
    square = square + 0.5 * small + jnp.sum(jnp.where(lane < half, 1.0, 0.5) * attn * attn)
    value = jnp.broadcast_to(square, norm_out.shape)
    norm_out[...] = all_sum(place, value, norm_src, norm_box, norm_send, norm_recv)
    for copy in stores:
        copy.wait()


def block_call(tokens, condition, cotangent, routes, w_ada, w_gate, w_attn, w_expert):
    count = lax.axis_size("dp")
    own_tok, width = tokens.shape
    rows, wide = w_ada.shape
    experts = w_gate.shape[0]
    parts, _, half = w_attn.shape
    _, wide_experts, _, hidden = w_expert.shape
    depth, side = dp_sizes(count)
    images = own_tok // PATCH
    cut = (wide // 4 + LANES - 1) // LANES * LANES
    spare = 2 * LANES
    block, ada_block, attn_block = block_rows(rows, 2), block_rows(rows, 2), block_rows(rows, parts)
    tok = 2 * own_tok
    tile = TILE if count <= 16 else TILE // 2
    vmem = pl.BlockSpec(memory_space=pltpu.VMEM)
    hbm = pl.BlockSpec(memory_space=pl.ANY)
    hops = depth + 2 * side - 3

    def sems(*shape):
        return pltpu.SemaphoreType.DMA(shape)

    def box(slots, height, lanes):
        return pltpu.VMEM((slots, count - 1, height, lanes), bf16)

    one = hidden * CUT_ONE // CUT_ALL // LANES * LANES
    two = hidden - one

    return pl.pallas_call(
        functools.partial(block_kernel, count, rows, experts, tile),
        out_shape=(
            jax.ShapeDtypeStruct((own_tok, width), f32),
            jax.ShapeDtypeStruct((own_tok, width), f32),
            jax.ShapeDtypeStruct((rows, wide), f32),
            jax.ShapeDtypeStruct((attn_block, spare), f32),
            jax.ShapeDtypeStruct((wide_experts, block, hidden), f32),
            jax.ShapeDtypeStruct((8, LANES), f32),
        ),
        in_specs=[hbm, hbm] + [vmem] * 6,
        out_specs=(hbm, hbm) + (vmem,) * 4,
        scratch_shapes=[
            pltpu.VMEM((wide_experts, count, block, one), bf16),
            pltpu.VMEM((wide_experts, count, block, two), bf16),
            box(SLOTS, block, one),
            box(SLOTS, block, two),
            pltpu.VMEM((1, count, ada_block, cut), bf16),
            pltpu.VMEM((1, count, SUB, width), bf16),
            pltpu.VMEM((1, count, SUB, cut), bf16),
            pltpu.VMEM((count, SUB, cut), bf16),
            pltpu.VMEM((1, count, attn_block, spare), bf16),
            box(1, attn_block, spare),
            pltpu.VMEM((count, attn_block, spare), bf16),
            pltpu.VMEM((2, parts, width, spare), bf16),
            pltpu.VMEM(condition.shape, bf16),
            pltpu.VMEM((2, condition.shape[0], 2 * cut), f32),
            pltpu.VMEM((2, condition.shape[0], 2 * cut), f32),
            pltpu.VMEM((condition.shape[0], 2 * cut), f32),
            pltpu.VMEM((2, 3, own_tok, half), bf16),
            pltpu.VMEM((2, own_tok, half), bf16),
            pltpu.VMEM((own_tok, width), bf16),
            pltpu.VMEM((images, width // HD, PATCH, PATCH), bf16),
            pltpu.VMEM((tok, width), bf16),
            pltpu.VMEM((tok, width), bf16),
            pltpu.VMEM((tok, LANES), f32),
            pltpu.VMEM((tok, width), f32),
            pltpu.VMEM((tok, width), f32),
            pltpu.VMEM((tok, LANES), f32),
            pltpu.VMEM((own_tok, LANES), f32),
            pltpu.VMEM((2, own_tok, width), bf16),
            pltpu.VMEM((width, hidden), bf16),
            pltpu.VMEM((width, hidden), bf16),
            pltpu.VMEM((width, hidden), f32),
            pltpu.VMEM((width, hidden), f32),
            pltpu.VMEM((width, LANES), f32),
            pltpu.VMEM((parts, width, spare), bf16),
            pltpu.VMEM((parts, width, spare), bf16),
            pltpu.VMEM((2, 8, LANES), f32),
            pltpu.VMEM((depth + 2 * side * side, 8, LANES), f32),
            sems(4),
            *[sems(wide_experts, hops)] * 8,
            *[sems(1, hops)] * 10,
            sems(8),
            sems(8),
            sems(images, 3),
            sems(images, 3),
            sems(depth + 2 * side * side),
            sems(depth + 2 * side * side),
        ],
        compiler_params=pltpu.CompilerParams(collective_id=1, has_side_effects=True, vmem_limit_bytes=VMEM_BYTES),
        cost_estimate=pl.CostEstimate(
            flops=12 * tok * width * hidden * wide_experts, bytes_accessed=16 * w_expert.size, transcendentals=0
        ),
        name="block",
    )(tokens, cotangent, condition, routes, w_ada, w_gate, w_attn, w_expert)
def update_kernel(rows, half, output_ref, grad_tok_ref, norm_ref, expert_ref, attn_ref, ada_ref, *refs):
    ada, gate, attn, expert = (refs[3 * i : 3 * i + 3] for i in range(4))
    outs, hold, sem = refs[12:-2], refs[-2], refs[-1]
    ada_new, gate_new, attn_new, expert_new = (outs[3 * i : 3 * i + 3] for i in range(4))
    loads = [pltpu.make_async_copy(ref, hold.at[i], sem.at[i]) for i, ref in enumerate((output_ref, grad_tok_ref))]
    stores = [pltpu.make_async_copy(hold.at[i], outs[13 + i], sem.at[2 + i]) for i in range(2)]
    for copy in loads:
        copy.start()
    total = jnp.sqrt(norm_ref[...])
    outs[12][0, 0] = jnp.max(total)
    factor = jnp.minimum(1.0, CLIP_NORM / (total[0:1, 0:1] + 1e-06))

    def write(ins, news, at, grad):
        for new, value in zip(news, adam(ins[0][at], ins[1][at], ins[2][at], grad * factor)):
            new[at] = value

    everything = (slice(None), slice(None))
    write(ada, ada_new, everything, ada_ref[...])
    for load, store in zip(loads, stores):
        load.wait()
        store.start()
    first = half // LANES * LANES
    small = attn_ref[pl.ds(0, rows), pl.ds(first, LANES)]
    square = jnp.concatenate([small, jnp.zeros((LANES - rows, LANES), f32)], axis=0).T
    experts = gate[0].shape[0]
    write(gate, gate_new, everything, square[half - first : half - first + experts, :rows])
    for j in range(attn[0].shape[0]):
        write(attn, attn_new, (j,), attn_ref[pl.ds(j * rows, rows), pl.ds(0, half)])

    def one(e, carry):
        for part in range(2):
            write(expert, expert_new, (part, e), expert_ref[e, pl.ds(part * rows, rows), :])
        return carry

    lax.fori_loop(0, expert[0].shape[1], one, 0)
    for copy in stores:
        copy.wait()


def update_call(rows, half, output, grad_tokens, norm, expert, attn, ada, weights):
    vmem = pl.BlockSpec(memory_space=pltpu.VMEM)
    hbm = pl.BlockSpec(memory_space=pl.ANY)
    shapes = [jax.ShapeDtypeStruct(w.shape, f32) for w in weights]
    return pl.pallas_call(
        functools.partial(update_kernel, rows, half),
        out_shape=shapes
        + [jax.ShapeDtypeStruct((1, 1), f32)]
        + [jax.ShapeDtypeStruct(output.shape, f32), jax.ShapeDtypeStruct(grad_tokens.shape, f32)],
        in_specs=[hbm, hbm] + [vmem] * (4 + len(weights)),
        out_specs=[vmem] * len(weights) + [pl.BlockSpec(memory_space=pltpu.SMEM), hbm, hbm],
        scratch_shapes=[pltpu.VMEM((2, *output.shape), f32), pltpu.SemaphoreType.DMA((4,))],
        compiler_params=pltpu.CompilerParams(vmem_limit_bytes=VMEM_BYTES),
        name="update",
    )(output, grad_tokens, norm, expert, attn, ada, *weights)


def per_device(
    tokens,
    condition,
    cotangent,
    routes,
    w_ada,
    ada_first,
    ada_second,
    w_gate,
    gate_first,
    gate_second,
    w_attn,
    attn_first,
    attn_second,
    w_expert,
    expert_first,
    expert_second,
):
    output, grad_tokens, ada_total, attn_total, expert_total, square_sum = block_call(
        tokens, condition, cotangent, routes.T, w_ada, w_gate.T, w_attn, w_expert
    )
    updated = update_call(
        w_ada.shape[0], w_attn.shape[2], output, grad_tokens, square_sum, expert_total, attn_total, ada_total,
        (
            w_ada, ada_first, ada_second,
            w_gate.T, gate_first.T, gate_second.T,
            w_attn, attn_first, attn_second,
            w_expert, expert_first, expert_second,
        ),
    )
    gates = [gate.T for gate in updated[3:6]]
    return (*updated[13:], updated[12].reshape(()), *updated[:3], *gates, *updated[6:12])


def solution(mesh):
    placed = (
        P(("dp", "mp"), None),
        P("dp", None),
        P(("dp", "mp"), None),
        P("dp", None),
        P("dp", None),
        P("dp", None),
        P("dp", None),
        P("dp", None),
        P("dp", None),
        P("dp", None),
        P(None, "dp", "mp"),
        P(None, "dp", "mp"),
        P(None, "dp", "mp"),
        P(None, None, "dp", "mp"),
        P(None, None, "dp", "mp"),
        P(None, None, "dp", "mp"),
    )
    return jax.shard_map(
        per_device,
        mesh=mesh,
        in_specs=placed,
        out_specs=(
            P(("dp", "mp"), None),
            P(("dp", "mp"), None),
            P(),
            P("dp", None),
            P("dp", None),
            P("dp", None),
            P("dp", None),
            P("dp", None),
            P("dp", None),
            P(None, "dp", "mp"),
            P(None, "dp", "mp"),
            P(None, "dp", "mp"),
            P(None, None, "dp", "mp"),
            P(None, None, "dp", "mp"),
            P(None, None, "dp", "mp"),
        ),
        check_vma=False,
    )
```

```python
import functools
import math

import jax
import jax.numpy as jnp
from jax import lax
from jax.experimental import pallas as pl
from jax.experimental.pallas import tpu as pltpu
from jax.sharding import PartitionSpec as P

HD = 64
PATCH = 256
STEP = 10
LANES = 128
SUB = 16
TILE = 512
SLOTS = 4
ZBA, BZA = "zba", "bza"
CUT_ONE, CUT_ALL = 2, 3

EPS_NORM = 1e-06
CLIP_NORM = 0.1
RATE = 0.08
BETA_ONE = 0.9
BETA_TWO = 0.95
ADAM_EPS = 1e-08
DECAY = 0.01
GELU_LIN = 0.7978845608
GELU_CUBE = 0.7978845608 * 0.044715

MESH = pl.DeviceIdType.MESH
VMEM_BYTES = 127 * 512 * 1024
bf16 = jnp.bfloat16
f32 = jnp.float32
NN = (((1,), (0,)), ((), ()))
NT = (((1,), (1,)), ((), ()))
TN = (((0,), (0,)), ((), ()))


def mxu(left, right, dims=NN):
    return lax.dot_general(left, right, dims, preferred_element_type=f32)


def layer_norm(value):
    center = value - jnp.mean(value, axis=-1, keepdims=True)
    inverse = lax.rsqrt(jnp.mean(center * center, axis=-1, keepdims=True) + EPS_NORM)
    return (center * inverse, inverse)


def norm_back(grad, normed, inverse):
    mean_grad = jnp.mean(grad, axis=-1, keepdims=True)
    mean_proj = jnp.mean(grad * normed, axis=-1, keepdims=True)
    return inverse * (grad - mean_grad - normed * mean_proj)


def adam(master, first, second, grad):
    first_new = BETA_ONE * first + (1.0 - BETA_ONE) * grad
    second_new = BETA_TWO * second + (1.0 - BETA_TWO) * grad * grad
    fix_one = 1.0 - BETA_ONE**STEP
    fix_two = 1.0 - BETA_TWO**STEP
    update = first_new / fix_one / (jnp.sqrt(second_new / fix_two) + ADAM_EPS) + DECAY * master
    return (master - RATE * update, first_new, second_new)


def gelu_both(value):
    square = value * value
    tanh = jnp.tanh(value * (GELU_CUBE * square + GELU_LIN))
    half = 0.5 * tanh + 0.5
    act = value * half
    slope = half + act * (1.0 - tanh) * (3.0 * GELU_CUBE * square + GELU_LIN)
    return act, slope


def dp_sizes(count):
    side = 4 if count >= 64 else 2
    return count // (side * side), side


class Place:
    def __init__(self, count):
        self.count = count
        self.depth, self.side = dp_sizes(count)
        self.dp = lax.axis_index("dp")
        self.mp = lax.axis_index("mp")
        side = self.side
        y = (self.dp // side) % side
        x = self.dp % side
        self.at = {
            "z": self.dp // (side * side),
            "a": jnp.where(self.mp == 0, y, x),
            "b": jnp.where(self.mp == 0, x, y),
        }
        self.size = {"z": self.depth, "a": side, "b": side}
        self.near = {axis: self.peers(axis) for axis in "zab"}
        self.first, self.others = {}, {}
        for order in (ZBA, BZA):
            for stage, axis in enumerate(order):
                fixed = {name: self.at[name] for name in order[stage:]}
                self.first[order, stage] = self.slot_at(order, fixed)
                self.others[order, stage] = [
                    self.slot_at(order, {**fixed, axis: self.along(axis, k)}) for k in range(1, self.size[axis])
                ]

    def slot_at(self, order, at):
        slot = 0
        for axis in reversed(order):
            slot = slot * self.size[axis] + at.get(axis, 0)
        return slot

    def slot(self, order=ZBA):
        return self.first[order, 0]

    def slot_of(self, dp, core, order=ZBA):
        side = self.side
        z, y, x = dp // (side * side), (dp // side) % side, dp % side
        one = self.slot_at(order, {"z": z, "a": y, "b": x})
        two = self.slot_at(order, {"z": z, "a": x, "b": y})
        return jnp.where(core == 0, one, two)

    def device(self, at):
        z, a, b = at["z"], at["a"], at["b"]
        side = self.side
        dp = jnp.where(self.mp == 0, (z * side + a) * side + b, (z * side + b) * side + a)
        return (dp, self.mp)

    def along(self, axis, step):
        return (self.at[axis] + step) % self.size[axis]

    def peers(self, axis):
        return [self.device({**self.at, axis: self.along(axis, k)}) for k in range(1, self.size[axis])]

    def other_core(self):
        return (self.dp, 1 - self.mp)

    def peers_layer(self):
        layer = self.side * self.side
        first = self.dp - self.dp % layer
        peers = []
        for k in range(1, 2 * layer):
            spot = (self.dp % layer * 2 + self.mp + k) % (2 * layer)
            peers.append((first + spot // 2, spot % 2))
        return peers

    def greet(self):
        peers = self.peers("z") + self.peers_layer()
        barrier = pltpu.get_barrier_semaphore()
        for peer in peers:
            pl.semaphore_signal(barrier, inc=1, device_id=peer, device_id_type=MESH)
        pl.semaphore_wait(barrier, len(peers))


def remote(src, dst, send, recv, peer):
    return pltpu.make_async_remote_copy(
        src_ref=src, dst_ref=dst, send_sem=send, recv_sem=recv, device_id=peer, device_id_type=MESH
    )


def span(place, order, stage):
    return math.prod(place.size[axis] for axis in order[:stage])


class Gather:
    def __init__(self, place, buf, send, recv, order=ZBA):
        self.p, self.buf, self.send, self.recv, self.order = place, buf, send, recv, order

    def copies(self, stage, e):
        p, order = self.p, self.order
        src = self.buf.at[e, pl.ds(p.first[order, stage], span(p, order, stage))]
        base = sum(p.size[axis] - 1 for axis in order[:stage])
        return [
            remote(src, src, self.send.at[e, base + k], self.recv.at[e, base + k], peer)
            for k, peer in enumerate(p.near[order[stage]])
        ]

    def start(self, stage, e):
        for copy in self.copies(stage, e):
            copy.start()

    def arrive(self, stage, e):
        for copy in self.copies(stage, e):
            copy.wait_recv()

    def sent(self, e):
        for stage in range(3):
            for copy in self.copies(stage, e):
                copy.wait_send()


class Scatter:
    def __init__(self, place, buf, boxes, send, recv, order=ZBA):
        self.p, self.buf, self.boxes, self.send, self.recv, self.order = place, buf, boxes, send, recv, order

    def box(self, stage, e, block, many):
        box = self.boxes[min(stage, 1)]
        if stage == 2:
            order = self.order
            block = block + (self.p.size[order[1]] - 1) * span(self.p, order, 1)
        return box.at[e % box.shape[0], pl.ds(block, many)]

    def copies(self, stage, e):
        p, order = self.p, self.order
        axis, many = order[2 - stage], span(p, order, 2 - stage)
        sem = sum(p.size[order[2 - before]] - 1 for before in range(stage))
        made = []
        for k, peer in enumerate(p.near[axis]):
            src = self.buf.at[e, pl.ds(p.others[order, 2 - stage][k], many)]
            dst = self.box(stage, e, k * many, many)
            made.append(remote(src, dst, self.send.at[e, sem + k], self.recv.at[e, sem + k], peer))
        return made

    def start(self, stage, e):
        for copy in self.copies(stage, e):
            copy.start()

    def arrive(self, stage, e):
        for copy in self.copies(stage, e):
            copy.wait()

    def total(self, stage, e, i):
        p, order = self.p, self.order
        many = span(p, order, 2 - stage)
        total = self.buf[e, p.first[order, 2 - stage] + i].astype(f32)
        for k in range(p.size[order[2 - stage]] - 1):
            total = total + self.box(stage, e, k * many + i, 1)[0].astype(f32)
        return total

    def add(self, stage, e):
        def one(i, carry):
            self.buf[e, self.p.first[self.order, 2 - stage] + i] = self.total(stage, e, i).astype(bf16)
            return carry

        lax.fori_loop(0, span(self.p, self.order, 2 - stage), one, 0)

    def last(self, e):
        return self.total(2, e, 0)


def block_rows(rows, parts):
    return (parts * rows + SUB - 1) // SUB * SUB


def blocks_to_weights(place, rows, buf, core, outs, order=ZBA):
    many = SUB // math.gcd(SUB, rows)
    for first in range(0, place.count, many):
        blocks = [buf[place.slot_of(first + i, core, order)].astype(f32) for i in range(many)]
        for part, out in enumerate(outs):
            pieces = [block[part * rows : (part + 1) * rows] for block in blocks]
            out[pl.ds(first * rows, many * rows), :] = jnp.concatenate(pieces, axis=0).astype(bf16)


def grads_to_blocks(place, rows, grads, buf, order=ZBA):
    block = buf.shape[1]
    for dp in range(place.count):
        pieces = [grad[dp * rows : (dp + 1) * rows, :] for grad in grads]
        if block > rows * len(grads):
            pieces.append(jnp.zeros((block - rows * len(grads), buf.shape[2]), f32))
        buf[place.slot_of(dp, place.mp, order)] = jnp.concatenate(pieces, axis=0).astype(bf16)


def all_sum(place, value, src, box, send, recv):
    layer = place.side * place.side
    spot = place.dp % layer
    z = place.at["z"]
    src[0] = value
    box[z] = value
    copies = [
        remote(src.at[0], box.at[z], send.at[k], recv.at[k], peer) for k, peer in enumerate(place.near["z"])
    ]
    for copy in copies:
        copy.start()
    for copy in copies:
        copy.wait()
    total = box[0]
    for i in range(1, place.depth):
        total = total + box[i]
    mine = spot * 2 + place.mp
    base = place.depth
    src[1] = total
    box[base + mine] = total
    at = place.depth - 1
    copies = [
        remote(src.at[1], box.at[base + mine], send.at[at + k], recv.at[at + k], peer)
        for k, peer in enumerate(place.peers_layer())
    ]
    for copy in copies:
        copy.start()
    for copy in copies:
        copy.wait()
    total = box[base]
    for i in range(1, 2 * layer):
        total = total + box[base + i]
    return total


class Both:
    def __init__(self, *both):
        self.both = both

    def start(self, stage, e):
        for one in self.both:
            one.start(stage, e)

    def arrive(self, stage, e):
        for one in self.both:
            one.arrive(stage, e)

    def add(self, stage, e):
        for one in self.both:
            one.add(stage, e)

    def sent(self, e):
        for one in self.both:
            one.sent(e)


def block_kernel(
    count, rows, experts, tile, lag,
    tok_ref, cot_ref, cond_ref, route_ref, ada_ref, gate_ref, attn_ref, w_ref,
    output_ref, grad_tok_ref, ada_out, attn_out, total_ref, norm_out,
    buf_one, buf_two, box_one, rest_one, box_two, rest_two,
    ada_buf, sc_buf, mod_buf, mod_far, attn_buf, attn_box, attn_rest, attn_far, attn_w,
    cond_low, mod, grad_mod, grad_mod_in, triple, mixed, h_one, soft,
    h_all, d_all, gate_all, branch_acc, grad_h_acc, grad_gate_acc, gate_in, share_in,
    up_w, down_w, up_grad, down_grad, gate_grad, attn_share, attn_in, norm_src, norm_box,
    load_sem, gather_send, gather_recv, gather_send_two, gather_recv_two,
    scatter_send, scatter_recv, scatter_send_two, scatter_recv_two,
    ada_send, ada_recv, sc_send, sc_recv, mod_send, mod_recv, attn_send, attn_recv, attn_back_send, attn_back_recv,
    core_send, core_recv, token_send, token_recv, norm_send, norm_recv,
):
    place = Place(count)
    mp = place.mp
    wide_experts = w_ref.shape[1]
    own_tok, width = tok_ref.shape
    images = own_tok // PATCH
    half = attn_ref.shape[2]
    first = half // LANES * LANES
    heads = half // HD
    wide = ada_ref.shape[1] // 2
    cut = ada_buf.shape[3]
    scale = HD ** (-0.5)
    own_at = pl.multiple_of(mp * own_tok, own_tok)
    their_at = pl.multiple_of((1 - mp) * own_tok, own_tok)
    own, theirs = pl.ds(own_at, own_tok), pl.ds(their_at, own_tok)
    other = place.other_core()

    loads = [
        pltpu.make_async_copy(tok_ref, branch_acc.at[pl.ds(0, own_tok)], load_sem.at[0]),
        pltpu.make_async_copy(cot_ref, branch_acc.at[pl.ds(own_tok, own_tok)], load_sem.at[1]),
    ]
    for load in loads:
        load.start()

    def put(target, block, order=ZBA):
        if block.shape[0] != target.shape[1]:
            target[place.slot(order)] = jnp.zeros(target.shape[1:], bf16)
        target[place.slot(order), pl.ds(0, block.shape[0])] = block

    cols = ada_ref[:, pl.ds(pl.multiple_of(mp * wide, LANES), wide)]
    tail = jnp.concatenate([cols[:, cut:], jnp.zeros((rows, 2 * cut - wide), f32)], axis=1)
    put(ada_buf.at[0], jnp.concatenate([cols[:, :cut], tail], axis=0).astype(bf16))
    parts = attn_ref.shape[0]
    side_by = lax.broadcasted_iota(jnp.int32, (experts, LANES), 1) == lax.broadcasted_iota(
        jnp.int32, (experts, LANES), 0
    )
    gate = mxu(gate_ref[...].astype(bf16), side_by.astype(f32).astype(bf16), TN)[:, : 2 * LANES - half]
    spare = [gate] + [jnp.zeros_like(gate)] * (parts - 1)
    both = [jnp.concatenate([attn_ref[j], spare[j]], axis=1) for j in range(parts)]
    pair = parts // 2
    for i in range(2):
        put(attn_buf.at[i], jnp.concatenate(both[i * pair : (i + 1) * pair], axis=0).astype(bf16))
    cond = cond_ref[...]
    cond = cond / (1.0 + jnp.exp(-cond))
    cond_low[...] = cond.astype(bf16)
    sc_buf[0, place.slot()] = jnp.concatenate([cond, jnp.zeros((SUB - cond.shape[0], width), f32)], axis=0).astype(bf16)
    place.greet()
    ada_gather = Gather(place, ada_buf, ada_send, ada_recv)
    attn_gather = Gather(place, attn_buf, attn_send, attn_recv)
    cuts = (pl.ds(0, buf_one.shape[3]), pl.ds(buf_one.shape[3], buf_two.shape[3]))
    streams = tuple(zip((buf_one, buf_two), cuts, (ZBA, BZA)))
    gather = Both(
        Gather(place, buf_one, gather_send, gather_recv, ZBA),
        Gather(place, buf_two, gather_send_two, gather_recv_two, BZA),
    )
    scatter = Both(
        Scatter(place, buf_one, (box_one, rest_one), scatter_send, scatter_recv, ZBA),
        Scatter(place, buf_two, (box_two, rest_two), scatter_send_two, scatter_recv_two, BZA),
    )
    sc_gather = Gather(place, sc_buf, sc_send, sc_recv)
    ada_gather.start(0, 0)
    attn_gather.start(0, 0)
    attn_gather.start(0, 1)
    sc_gather.start(0, 0)

    def fill(e, carry):
        both = jnp.concatenate([w_ref[0, e], w_ref[1, e]], axis=0).astype(bf16)
        for buf, lanes, order in streams:
            put(buf.at[e], both[:, lanes.start : lanes.start + lanes.size], order)
        return carry

    lax.fori_loop(0, wide_experts, fill, 0)

    def tick(k):
        @pl.when(k + 5 < wide_experts)
        def _():
            gather.start(0, k + 5)

        @pl.when(k + 3 < wide_experts)
        def _():
            gather.arrive(0, k + 3)
            gather.start(1, k + 3)

        @pl.when(k + 1 < wide_experts)
        def _():
            gather.arrive(1, k + 1)
            gather.start(2, k + 1)

    grad_mod[...] = jnp.zeros_like(grad_mod)
    gather.start(0, 0)
    gather.start(0, 1)
    for stage in range(2):
        for small, i in ((ada_gather, 0), (attn_gather, 0), (attn_gather, 1)):
            small.arrive(stage, i)
            small.start(stage + 1, i)
    gather.start(0, 2)
    gather.start(0, 3)
    gather.arrive(0, 0)
    gather.start(1, 0)
    ada_gather.arrive(2, 0)

    low_cut = pl.ds(0, cut)
    blocks_to_weights(place, rows, ada_buf.at[0], mp, (up_w.at[:, low_cut], down_w.at[:, low_cut]))
    mod[mp, :, pl.ds(0, cut)] = mxu(cond_low[...], up_w[:, low_cut])
    mod[mp, :, pl.ds(cut, cut)] = mxu(cond_low[...], down_w[:, low_cut])
    mod_cross = remote(mod.at[mp], mod.at[mp], core_send.at[1], core_recv.at[1], other)
    mod_cross.start()
    attn_cross = []
    for i in range(2):
        attn_gather.arrive(2, i)
        attn_cross.append(
            remote(attn_buf.at[i], attn_far.at[i], core_send.at[8 + i], core_recv.at[8 + i], other)
        )
        attn_cross[i].start()
        outs = [attn_w.at[mp, j] for j in range(i * pair, (i + 1) * pair)]
        blocks_to_weights(place, rows, attn_buf.at[i], mp, outs)
    for load in loads:
        load.wait()
    ada_gather.sent(0)
    attn_gather.sent(0)
    attn_gather.sent(1)
    sc_gather.arrive(0, 0)
    sc_gather.start(1, 0)
    for i in range(2):
        attn_cross[i].wait()
        outs = [attn_w.at[1 - mp, j] for j in range(i * pair, (i + 1) * pair)]
        blocks_to_weights(place, rows, attn_far.at[i], 1 - mp, outs)
    mod_cross.wait()
    gather.arrive(0, 1)
    gather.start(1, 1)
    gate_lanes = pl.ds(first, LANES)
    half_lanes = pl.ds(0, half)

    def weight(core, j):
        return attn_w[core, j, :, half_lanes]

    lane_pair = lax.broadcasted_iota(jnp.int32, (PATCH, 2 * HD), 1)
    masks = [(lane_pair < HD).astype(f32).astype(bf16), (lane_pair >= HD).astype(f32).astype(bf16)]
    groups = [(at, min(2, heads - at)) for at in range(0, heads, 2)]
    expert_lane = lax.broadcasted_iota(jnp.int32, (PATCH, LANES), 1) - (half - first)

    def mod_row(image, vector):
        flat = vector % 3 * width
        return mod[vector // 3, pl.ds(mp * images + image, 1), pl.ds(flat, width)]

    def add_grad_mod(image, vector, value):
        grad_mod[vector // 3, pl.ds(mp * images + image, 1), pl.ds(vector % 3 * width, width)] = value

    def one_head(value, group, head):
        return value if group[1] == 1 else value * masks[head]

    def route(h, image):
        valid = (expert_lane >= 0) & (expert_lane < experts)
        logits = jnp.where(valid, mxu(h, attn_w[0, 0, :, gate_lanes]), -jnp.inf)
        power = jnp.exp(logits - jnp.max(logits, axis=1, keepdims=True))
        router = power / jnp.sum(power, axis=1, keepdims=True)
        picks = route_ref[:, pl.ds(pl.multiple_of(own_at + image * PATCH, PATCH), PATCH)]
        spot = lax.broadcasted_iota(jnp.int32, (LANES, PATCH), 0) - (half - first)
        picked = jnp.where((picks[0:1, :] == spot) | (picks[1:2, :] == spot), 1.0, 0.0)
        return router, picked.T

    def attend(at):
        return mxu(mixed[0, at, :], weight(0, 3), NT) + mxu(mixed[1, at, :], weight(1, 3), NT)

    def token_copies(image):
        at = pl.ds(pl.multiple_of(own_at + image * PATCH, PATCH), PATCH)
        return [
            remote(ref.at[at], ref.at[at], token_send.at[image, i], token_recv.at[image, i], other)
            for i, ref in enumerate((h_all, d_all, gate_all))
        ]

    def forward(image, carry):
        at = pl.ds(pl.multiple_of(image * PATCH, PATCH), PATCH)
        cot_at = pl.ds(pl.multiple_of(own_tok + image * PATCH, PATCH), PATCH)
        all_at = pl.ds(pl.multiple_of(own_at + image * PATCH, PATCH), PATCH)
        normed, _ = layer_norm(branch_acc[at, :])
        h = (normed * (1.0 + mod_row(image, 1)) + mod_row(image, 0)).astype(bf16)
        h_one[at, :] = h
        for core in range(2):
            for j in range(3):
                triple[core, j, at, :] = mxu(h, weight(core, j)).astype(bf16)
            for group in groups:
                lanes = pl.ds(group[0] * HD, group[1] * HD)
                query, key, value = (triple[core, j, at, lanes] for j in range(3))
                total = 0.0
                for head in range(group[1]):
                    scores = mxu(one_head(query, group, head), key, NT) * scale
                    power = jnp.exp(scores - jnp.max(scores, axis=1, keepdims=True))
                    low = (power * (1.0 / jnp.sum(power, axis=1, keepdims=True))).astype(bf16)
                    soft[image, core * heads + group[0] + head] = low
                    total = total + mxu(low, one_head(value, group, head))
                mixed[core, at, lanes] = total.astype(bf16)
        x_one = branch_acc[at, :] + mod_row(image, 2) * attend(at)
        normed, _ = layer_norm(x_one)
        h = (normed * (1.0 + mod_row(image, 4)) + mod_row(image, 3)).astype(bf16)
        h_all[all_at, :] = h
        router, chosen = route(h, image)
        shared = (expert_lane >= experts) & (expert_lane < wide_experts)
        gate_all[all_at, :] = jnp.where(shared, 1.0, router * chosen)
        d_all[all_at, :] = (branch_acc[cot_at, :] * mod_row(image, 5)).astype(bf16)
        for copy in token_copies(image):
            copy.start()

        tick(image - 1)

        @pl.when(image == 0)
        def _():
            sc_gather.arrive(1, 0)
            sc_gather.start(2, 0)

        return carry

    lax.fori_loop(0, images, forward, 0)
    ahead = images - 1
    sc_gather.arrive(2, 0)
    sc_gather.sent(0)

    branch_acc[...] = jnp.zeros_like(branch_acc)
    grad_h_acc[...] = jnp.zeros_like(grad_h_acc)
    grad_gate_acc[...] = jnp.zeros_like(grad_gate_acc)

    def all_tokens(image, carry):
        for copy in token_copies(image):
            copy.wait()
        return carry

    lax.fori_loop(0, images, all_tokens, 0)

    shares = [
        remote(h_all.at[theirs], share_in.at[0], core_send.at[2], core_recv.at[2], other),
        remote(d_all.at[theirs], share_in.at[1], core_send.at[3], core_recv.at[3], other),
        remote(grad_gate_acc.at[theirs], gate_in, core_send.at[4], core_recv.at[4], other),
    ]
    loads = [
        pltpu.make_async_copy(tok_ref, branch_acc.at[theirs], load_sem.at[0]),
        pltpu.make_async_copy(cot_ref, grad_h_acc.at[theirs], load_sem.at[1]),
    ]
    tiles = h_all.shape[0] // tile

    def compute(e):
        for buf, lanes, order in streams:
            blocks_to_weights(place, rows, buf.at[e], mp, (up_w.at[:, lanes], down_w.at[:, lanes]), order)
        up_grad[...] = jnp.zeros_like(up_grad)
        down_grad[...] = jnp.zeros_like(down_grad)

        def one_tile(t, carry):
            @pl.when((e == wide_experts - 1) & (t == tiles // 2))
            def _():
                h_all[theirs, :] = branch_acc[theirs, :].astype(bf16)
                d_all[theirs, :] = grad_h_acc[theirs, :].astype(bf16)
                for copy in shares:
                    copy.start()
                for copy in loads:
                    copy.start()

            at = pl.ds(pl.multiple_of((t + (1 - mp) * (tiles // 2)) % tiles * tile, tile), tile)
            h = h_all[at, :]
            d = d_all[at, :]
            lane = lax.broadcasted_iota(jnp.int32, (tile, LANES), 1) - (half - first)
            gate = jnp.sum(jnp.where(lane == e, gate_all[at, :], 0.0), axis=1, keepdims=True)
            pre = mxu(h, up_w[...])
            back = mxu(d, down_w[...])
            act, slope = gelu_both(pre)
            inner = jnp.sum(act * back, axis=1, keepdims=True)
            grad_gate_acc[at, :] += jnp.where(lane == e, inner, 0.0)
            act_low = (gate * act).astype(bf16)
            pre_low = (gate * back * slope).astype(bf16)
            branch_acc[at, :] += mxu(act_low, down_w[...], NT)
            grad_h_acc[at, :] += mxu(pre_low, up_w[...], NT)
            up_grad[...] += mxu(h, pre_low, TN)
            down_grad[...] += mxu(d, act_low, TN)
            return carry

        lax.fori_loop(0, tiles, one_tile, 0)

    def put_total(e):
        for part, (_, lanes, _) in zip(scatter.both, streams):
            total_ref[e, :, lanes] = part.last(e)

    def collect(k):
        @pl.when((k >= 1) & (k - 1 < wide_experts))
        def _():
            scatter.arrive(0, k - 1)
            scatter.add(0, k - 1)
            scatter.start(1, k - 1)

        @pl.when((k >= 2) & (k - 2 < wide_experts))
        def _():
            scatter.arrive(1, k - 2)
            scatter.add(1, k - 2)
            scatter.start(2, k - 2)

        @pl.when((k >= 3) & (k - 3 < wide_experts))
        def _():
            scatter.arrive(2, k - 3)
            put_total(k - 3)

    def step(e, carry):
        tick(e + ahead)
        gather.arrive(2, e)
        compute(e)
        gather.sent(e)
        for buf, lanes, order in streams:
            grads_to_blocks(place, rows, (up_grad.at[:, lanes], down_grad.at[:, lanes]), buf.at[e], order)
        scatter.start(0, e)
        collect(e - lag)
        return carry

    lax.fori_loop(0, wide_experts, step, 0)

    gate_grad[...] = jnp.zeros_like(gate_grad)
    for copy in shares + loads:
        copy.wait()

    def backward(image, carry):
        at = pl.ds(pl.multiple_of(image * PATCH, PATCH), PATCH)
        own_rows = pl.ds(pl.multiple_of(own_at + image * PATCH, PATCH), PATCH)
        load_rows = pl.ds(pl.multiple_of(their_at + image * PATCH, PATCH), PATCH)
        tok, cot = branch_acc[load_rows, :], grad_h_acc[load_rows, :]
        branch = branch_acc[own_rows, :] + share_in[0, at, :].astype(f32)
        attention = attend(at)
        x_one = tok + mod_row(image, 2) * attention
        normed, inverse = layer_norm(x_one)
        branch_acc[own_rows, :] = x_one + mod_row(image, 5) * branch
        add_grad_mod(image, 5, jnp.sum(cot * branch, axis=0, keepdims=True))
        h = h_all[own_rows, :]
        router, chosen = route(h, image)
        grad_router = (grad_gate_acc[own_rows, :] + gate_in[at, :]) * chosen
        grad_logits = (router * (grad_router - jnp.sum(router * grad_router, axis=1, keepdims=True))).astype(bf16)
        gate_grad[...] += mxu(h, grad_logits, TN)
        grad_h = grad_h_acc[own_rows, :] + share_in[1, at, :].astype(f32) + mxu(grad_logits, attn_w[0, 0, :, gate_lanes], NT)
        add_grad_mod(image, 3, jnp.sum(grad_h, axis=0, keepdims=True))
        add_grad_mod(image, 4, jnp.sum(grad_h * normed, axis=0, keepdims=True))
        grad_x = cot + norm_back(grad_h * (1.0 + mod_row(image, 4)), normed, inverse)
        add_grad_mod(image, 2, jnp.sum(grad_x * attention, axis=0, keepdims=True))
        grad_att = (grad_x * mod_row(image, 2)).astype(bf16)
        d_all[own_rows, :] = grad_att
        grad_h_one = 0.0
        for core in range(2):
            grad_mixed = mxu(grad_att, weight(core, 3)).astype(bf16)
            for group in groups:
                lanes = pl.ds(group[0] * HD, group[1] * HD)
                query, key, value = (triple[core, j, at, lanes] for j in range(3))
                back = grad_mixed[:, group[0] * HD : (group[0] + group[1]) * HD]
                grads = [0.0, 0.0, 0.0]
                for head in range(group[1]):
                    low = soft[image, core * heads + group[0] + head]
                    prob = low.astype(f32)
                    head_back = one_head(back, group, head)
                    grad_soft = mxu(head_back, value, NT)
                    delta = jnp.sum(prob * grad_soft, axis=1, keepdims=True)
                    grad_scores = (prob * (grad_soft - delta) * scale).astype(bf16)
                    grads[0] = grads[0] + mxu(grad_scores, one_head(key, group, head))
                    grads[1] = grads[1] + mxu(grad_scores, one_head(query, group, head), TN)
                    grads[2] = grads[2] + mxu(low, head_back, TN)
                for j in range(3):
                    triple[core, j, at, lanes] = grads[j].astype(bf16)
            for j in range(3):
                grad_h_one = grad_h_one + mxu(triple[core, j, at, :], weight(core, j), NT)
        normed, inverse = layer_norm(tok)
        add_grad_mod(image, 0, jnp.sum(grad_h_one, axis=0, keepdims=True))
        add_grad_mod(image, 1, jnp.sum(grad_h_one * normed, axis=0, keepdims=True))
        grad_h_acc[own_rows, :] = grad_x + norm_back(grad_h_one * (1.0 + mod_row(image, 1)), normed, inverse)
        collect(wide_experts - lag + image)
        return carry

    lax.fori_loop(0, images, backward, 0)
    for k in range(images, 3 + lag):
        collect(wide_experts - lag + k)
    stores = [
        pltpu.make_async_copy(branch_acc.at[own], output_ref, load_sem.at[2]),
        pltpu.make_async_copy(grad_h_acc.at[own], grad_tok_ref, load_sem.at[3]),
    ]
    for copy in stores:
        copy.start()

    crosses = [
        remote(grad_mod.at[1 - mp], grad_mod_in, core_send.at[5], core_recv.at[5], other),
        *[
            remote(
                attn_share.at[pl.ds(i * pair, pair)], attn_in.at[pl.ds(i * pair, pair)],
                core_send.at[6 + i], core_recv.at[6 + i], other,
            )
            for i in range(2)
        ],
        remote(mod_buf.at[0], mod_far, core_send.at[0], core_recv.at[0], other),
    ]
    crosses[0].start()

    def attn_grad(core, j):
        if j == parts - 1:
            return mxu(d_all[own, :], mixed[core], TN)
        return mxu(h_one[...], triple[core, j], TN)

    spare = pl.ds(half, 2 * LANES - half)
    places = [(up_grad, 0), (up_grad, 1), (up_grad, 2), (down_grad, 0)]
    attn_scatter = Scatter(place, attn_buf, (attn_box, attn_rest), attn_back_send, attn_back_recv)
    for i in range(2):
        for j in range(i * pair, (i + 1) * pair):
            attn_share[j, :, half_lanes] = attn_grad(1 - mp, j).astype(bf16)
            extra = gate_grad[:, pl.ds(half - first, 2 * LANES - half)].astype(bf16)
            attn_share[j, :, spare] = extra if j == 0 else jnp.zeros_like(extra)
        crosses[1 + i].start()
    crosses[0].wait()
    grad_low = grad_mod[mp] + grad_mod_in[...]
    mod_buf[0, place.slot()] = jnp.concatenate([grad_low[:, :cut], grad_low[:, cut:]], axis=0).astype(bf16)
    mod_gather = Gather(place, mod_buf, mod_send, mod_recv)
    for i in range(2):
        for j in range(i * pair, (i + 1) * pair):
            ref, at = places[j]
            ref[:, pl.ds(at * 2 * LANES, half)] = attn_grad(mp, j)
        crosses[1 + i].wait()
        grads = []
        for j in range(i * pair, (i + 1) * pair):
            ref, at = places[j]
            lanes = pl.ds(at * 2 * LANES, half)
            ref[:, lanes] += attn_in[j, :, half_lanes].astype(f32)
            extra = gate_grad[:, pl.ds(half - first, 2 * LANES - half)] + attn_in[0, :, spare].astype(f32)
            ref[:, pl.ds(at * 2 * LANES + half, 2 * LANES - half)] = extra if j == 0 else jnp.zeros_like(extra)
            grads.append(ref[:, pl.ds(at * 2 * LANES, 2 * LANES)])
        grads_to_blocks(place, rows, grads, attn_buf.at[i])
        attn_scatter.start(0, i)
    mod_gather.start(0, 0)
    for stage in range(2):
        for i in range(2):
            attn_scatter.arrive(stage, i)
            attn_scatter.add(stage, i)
            attn_scatter.start(stage + 1, i)
        mod_gather.arrive(stage, 0)
        mod_gather.start(stage + 1, 0)
    square = jnp.zeros((1, 1), f32)
    for e in range(wide_experts):
        square = square + jnp.sum(total_ref[e] * total_ref[e])
    mod_gather.arrive(2, 0)
    crosses[3].start()
    row = lax.broadcasted_iota(jnp.int32, (width, LANES), 0)
    lane = lax.broadcasted_iota(jnp.int32, (width, LANES), 1)
    pick = ((row == place.dp * rows + lane) & (lane < rows)).astype(f32).astype(bf16)
    group = cond_ref.shape[0]

    def in_order(ref, core, at):
        pieces = [ref[place.slot_of(dp, core)].astype(f32)[at : at + group] for dp in range(count)]
        return jnp.concatenate(pieces, axis=0).astype(bf16)

    conds = mxu(in_order(sc_buf.at[0], mp, 0), pick).astype(bf16)

    def ada_grad(ref, core):
        low = mxu(conds, in_order(ref, core, 0), TN)[:rows]
        high = mxu(conds, in_order(ref, core, group), TN)[:rows, : wide - cut]
        start = pl.multiple_of(core * wide, LANES)
        ada_out[:, pl.ds(start, cut)] = low
        ada_out[:, pl.ds(pl.multiple_of(start + cut, LANES), wide - cut)] = high
        return jnp.sum(low * low) + jnp.sum(high * high)

    small = ada_grad(mod_buf.at[0], mp)
    mod_gather.sent(0)
    crosses[3].wait()
    small = small + ada_grad(mod_far, 1 - mp)
    square = square + 0.5 * small
    for i in range(2):
        attn_scatter.arrive(2, i)
        attn = attn_scatter.last(i)
        attn_out[i] = attn
        lane = lax.broadcasted_iota(jnp.int32, attn.shape, 1)
        square = square + jnp.sum(jnp.where(lane < half, 1.0, 0.5) * attn * attn)
    value = jnp.broadcast_to(square, norm_out.shape)
    norm_out[...] = all_sum(place, value, norm_src, norm_box, norm_send, norm_recv)
    for copy in stores:
        copy.wait()


def block_call(tokens, condition, cotangent, routes, w_ada, w_gate, w_attn, w_expert):
    count = lax.axis_size("dp")
    own_tok, width = tokens.shape
    rows, wide = w_ada.shape
    experts = w_gate.shape[0]
    parts, _, half = w_attn.shape
    _, wide_experts, _, hidden = w_expert.shape
    depth, side = dp_sizes(count)
    images = own_tok // PATCH
    cut = (wide // 4 + LANES - 1) // LANES * LANES
    spare = 2 * LANES
    block, ada_block, attn_block = block_rows(rows, 2), block_rows(rows, 2), block_rows(rows, parts // 2)
    tok = 2 * own_tok
    tile, lag = (TILE, 2) if count <= 16 else (TILE // 2, 0)
    vmem = pl.BlockSpec(memory_space=pltpu.VMEM)
    hbm = pl.BlockSpec(memory_space=pl.ANY)
    hops = depth + 2 * side - 3

    def sems(*shape):
        return pltpu.SemaphoreType.DMA(shape)

    def boxes(slots, order, height, lanes):
        size = {"z": depth, "a": side, "b": side}
        span = size[order[0]] * size[order[1]]
        first = (size[order[2]] - 1) * span
        return [
            pltpu.VMEM((slots, first, height, lanes), bf16),
            pltpu.VMEM((min(slots, SLOTS), span - 1, height, lanes), bf16),
        ]

    one = hidden * CUT_ONE // CUT_ALL // LANES * LANES
    two = hidden - one

    return pl.pallas_call(
        functools.partial(block_kernel, count, rows, experts, tile, lag),
        out_shape=(
            jax.ShapeDtypeStruct((own_tok, width), f32),
            jax.ShapeDtypeStruct((own_tok, width), f32),
            jax.ShapeDtypeStruct((rows, wide), f32),
            jax.ShapeDtypeStruct((2, attn_block, spare), f32),
            jax.ShapeDtypeStruct((wide_experts, block, hidden), f32),
            jax.ShapeDtypeStruct((8, LANES), f32),
        ),
        in_specs=[hbm, hbm] + [vmem] * 6,
        out_specs=(hbm, hbm) + (vmem,) * 4,
        scratch_shapes=[
            pltpu.VMEM((wide_experts, count, block, one), bf16),
            pltpu.VMEM((wide_experts, count, block, two), bf16),
            *boxes(SLOTS + 2 * lag, ZBA, block, one),
            *boxes(SLOTS + 2 * lag, BZA, block, two),
            pltpu.VMEM((1, count, ada_block, cut), bf16),
            pltpu.VMEM((1, count, SUB, width), bf16),
            pltpu.VMEM((1, count, SUB, cut), bf16),
            pltpu.VMEM((count, SUB, cut), bf16),
            pltpu.VMEM((2, count, attn_block, spare), bf16),
            *boxes(2, ZBA, attn_block, spare),
            pltpu.VMEM((2, count, attn_block, spare), bf16),
            pltpu.VMEM((2, parts, width, spare), bf16),
            pltpu.VMEM(condition.shape, bf16),
            pltpu.VMEM((2, condition.shape[0], 2 * cut), f32),
            pltpu.VMEM((2, condition.shape[0], 2 * cut), f32),
            pltpu.VMEM((condition.shape[0], 2 * cut), f32),
            pltpu.VMEM((2, 3, own_tok, half), bf16),
            pltpu.VMEM((2, own_tok, half), bf16),
            pltpu.VMEM((own_tok, width), bf16),
            pltpu.VMEM((images, width // HD, PATCH, PATCH), bf16),
            pltpu.VMEM((tok, width), bf16),
            pltpu.VMEM((tok, width), bf16),
            pltpu.VMEM((tok, LANES), f32),
            pltpu.VMEM((tok, width), f32),
            pltpu.VMEM((tok, width), f32),
            pltpu.VMEM((tok, LANES), f32),
            pltpu.VMEM((own_tok, LANES), f32),
            pltpu.VMEM((2, own_tok, width), bf16),
            pltpu.VMEM((width, hidden), bf16),
            pltpu.VMEM((width, hidden), bf16),
            pltpu.VMEM((width, hidden), f32),
            pltpu.VMEM((width, hidden), f32),
            pltpu.VMEM((width, LANES), f32),
            pltpu.VMEM((parts, width, spare), bf16),
            pltpu.VMEM((parts, width, spare), bf16),
            pltpu.VMEM((2, 8, LANES), f32),
            pltpu.VMEM((depth + 2 * side * side, 8, LANES), f32),
            sems(4),
            *[sems(wide_experts, hops)] * 8,
            *[sems(1, hops)] * 6,
            *[sems(2, hops)] * 4,
            sems(10),
            sems(10),
            sems(images, 3),
            sems(images, 3),
            sems(depth + 2 * side * side),
            sems(depth + 2 * side * side),
        ],
        compiler_params=pltpu.CompilerParams(collective_id=1, has_side_effects=True, vmem_limit_bytes=VMEM_BYTES),
        cost_estimate=pl.CostEstimate(
            flops=12 * tok * width * hidden * wide_experts, bytes_accessed=16 * w_expert.size, transcendentals=0
        ),
        name="block",
    )(tokens, cotangent, condition, routes, w_ada, w_gate, w_attn, w_expert)
def update_kernel(rows, half, output_ref, grad_tok_ref, expert_w, expert_m, expert_v, expert_ref, norm_ref, attn_ref, ada_ref, *refs):
    ada, gate, attn = (refs[3 * i : 3 * i + 3] for i in range(3))
    outs, (hold, held, grads, sem, token_sem) = refs[9:-5], refs[-5:]
    ada_new, gate_new, attn_new, expert_new = (outs[3 * i : 3 * i + 3] for i in range(4))
    expert = (expert_w, expert_m, expert_v)
    many = expert_w.shape[1] // 2
    chunks = [(part, h) for h in range(2) for part in range(2)]
    grad_loads = [
        pltpu.make_async_copy(expert_ref.at[pl.ds(h * many, many)], grads.at[pl.ds(h * many, many)], token_sem.at[4 + h])
        for h in range(2)
    ]

    def moves(c, refs, back):
        part, h = chunks[c]
        made = []
        for i, ref in enumerate(refs):
            far, near = ref.at[part, pl.ds(h * many, many)], held.at[i, part, pl.ds(h * many, many)]
            made.append(pltpu.make_async_copy(*((near, far) if back else (far, near)), sem.at[int(back), c, i]))
        return made

    for c in range(4):
        if chunks[c][0] == 0:
            grad_loads[chunks[c][1]].start()
        for copy in moves(c, expert, False):
            copy.start()
    token_loads = [pltpu.make_async_copy(ref, hold.at[i], token_sem.at[i]) for i, ref in enumerate((output_ref, grad_tok_ref))]
    token_stores = [pltpu.make_async_copy(hold.at[i], outs[13 + i], token_sem.at[2 + i]) for i in range(2)]
    for copy in token_loads:
        copy.start()
    total = jnp.sqrt(norm_ref[...])
    outs[12][0, 0] = jnp.max(total)
    factor = jnp.minimum(1.0, CLIP_NORM / (total[0:1, 0:1] + 1e-06))

    def write(ins, news, at, grad):
        for new, value in zip(news, adam(ins[0][at], ins[1][at], ins[2][at], grad * factor)):
            new[at] = value

    everything = (slice(None), slice(None))
    write(ada, ada_new, everything, ada_ref[...])
    first = half // LANES * LANES
    small = attn_ref[0, pl.ds(0, rows), pl.ds(first, LANES)]
    square = jnp.concatenate([small, jnp.zeros((LANES - rows, LANES), f32)], axis=0).T
    experts = gate[0].shape[0]
    write(gate, gate_new, everything, square[half - first : half - first + experts, :rows])
    parts = attn[0].shape[0]
    for j in range(parts):
        grad = attn_ref[j // (parts // 2), pl.ds(j % (parts // 2) * rows, rows), pl.ds(0, half)]
        write(attn, attn_new, (j,), grad)
    here = [held.at[i] for i in range(3)]
    for c, (part, h) in enumerate(chunks):
        if part == 0:
            grad_loads[h].wait()
        for copy in moves(c, expert, False):
            copy.wait()

        def one(e, carry):
            write(here, here, (part, e), grads[e, pl.ds(part * rows, rows), :])
            return carry

        lax.fori_loop(h * many, (h + 1) * many, one, 0)
        for copy in moves(c, expert_new, True):
            copy.start()
    for load, store in zip(token_loads, token_stores):
        load.wait()
        store.start()
    for c in range(4):
        for copy in moves(c, expert_new, True):
            copy.wait()
    for copy in token_stores:
        copy.wait()


def update_call(rows, half, output, grad_tokens, norm, expert, attn, ada, weights):
    vmem = pl.BlockSpec(memory_space=pltpu.VMEM)
    hbm = pl.BlockSpec(memory_space=pl.ANY)
    shapes = [jax.ShapeDtypeStruct(w.shape, f32) for w in weights]
    return pl.pallas_call(
        functools.partial(update_kernel, rows, half),
        out_shape=shapes
        + [jax.ShapeDtypeStruct((1, 1), f32)]
        + [jax.ShapeDtypeStruct(output.shape, f32), jax.ShapeDtypeStruct(grad_tokens.shape, f32)],
        in_specs=[hbm] * 6 + [vmem] * (3 + 9),
        out_specs=[vmem] * 9 + [hbm] * 3 + [pl.BlockSpec(memory_space=pltpu.SMEM), hbm, hbm],
        scratch_shapes=[
            pltpu.VMEM((2, *output.shape), f32),
            pltpu.VMEM((3, *weights[9].shape), f32),
            pltpu.VMEM(expert.shape, f32),
            pltpu.SemaphoreType.DMA((2, 4, 3)),
            pltpu.SemaphoreType.DMA((6,)),
        ],
        compiler_params=pltpu.CompilerParams(vmem_limit_bytes=VMEM_BYTES),
        name="update",
    )(output, grad_tokens, *weights[9:], expert, norm, attn, ada, *weights[:9])


def per_device(
    tokens,
    condition,
    cotangent,
    routes,
    w_ada,
    ada_first,
    ada_second,
    w_gate,
    gate_first,
    gate_second,
    w_attn,
    attn_first,
    attn_second,
    w_expert,
    expert_first,
    expert_second,
):
    output, grad_tokens, ada_total, attn_total, expert_total, square_sum = block_call(
        tokens, condition, cotangent, routes.T, w_ada, w_gate.T, w_attn, w_expert
    )
    updated = update_call(
        w_ada.shape[0], w_attn.shape[2], output, grad_tokens, square_sum, expert_total, attn_total, ada_total,
        (
            w_ada, ada_first, ada_second,
            w_gate.T, gate_first.T, gate_second.T,
            w_attn, attn_first, attn_second,
            w_expert, expert_first, expert_second,
        ),
    )
    gates = [gate.T for gate in updated[3:6]]
    return (*updated[13:], updated[12].reshape(()), *updated[:3], *gates, *updated[6:12])


def solution(mesh):
    placed = (
        P(("dp", "mp"), None),
        P("dp", None),
        P(("dp", "mp"), None),
        P("dp", None),
        P("dp", None),
        P("dp", None),
        P("dp", None),
        P("dp", None),
        P("dp", None),
        P("dp", None),
        P(None, "dp", "mp"),
        P(None, "dp", "mp"),
        P(None, "dp", "mp"),
        P(None, None, "dp", "mp"),
        P(None, None, "dp", "mp"),
        P(None, None, "dp", "mp"),
    )
    return jax.shard_map(
        per_device,
        mesh=mesh,
        in_specs=placed,
        out_specs=(
            P(("dp", "mp"), None),
            P(("dp", "mp"), None),
            P(),
            P("dp", None),
            P("dp", None),
            P("dp", None),
            P("dp", None),
            P("dp", None),
            P("dp", None),
            P(None, "dp", "mp"),
            P(None, "dp", "mp"),
            P(None, "dp", "mp"),
            P(None, None, "dp", "mp"),
            P(None, None, "dp", "mp"),
            P(None, None, "dp", "mp"),
        ),
        check_vma=False,
    )
```

```python
import functools
import math

import jax
import jax.numpy as jnp
from jax import lax
from jax.experimental import pallas as pl
from jax.experimental.pallas import tpu as pltpu
from jax.sharding import PartitionSpec as P

HD = 64
PATCH = 256
STEP = 10
LANES = 128
SUB = 16
TILE = 512
SLOTS, REST = 4, 4
ZBA, BZA = "zba", "bza"
CUT_ONE, CUT_ALL = 2, 3

EPS_NORM = 1e-06
CLIP_NORM = 0.1
RATE = 0.08
BETA_ONE = 0.9
BETA_TWO = 0.95
ADAM_EPS = 1e-08
DECAY = 0.01
GELU_LIN = 0.7978845608
GELU_CUBE = 0.7978845608 * 0.044715

MESH = pl.DeviceIdType.MESH
VMEM_BYTES = 127 * 512 * 1024
bf16 = jnp.bfloat16
f32 = jnp.float32
NN = (((1,), (0,)), ((), ()))
NT = (((1,), (1,)), ((), ()))
TN = (((0,), (0,)), ((), ()))


def mxu(left, right, dims=NN):
    return lax.dot_general(left, right, dims, preferred_element_type=f32)


def layer_norm(value):
    center = value - jnp.mean(value, axis=-1, keepdims=True)
    inverse = lax.rsqrt(jnp.mean(center * center, axis=-1, keepdims=True) + EPS_NORM)
    return (center * inverse, inverse)


def norm_back(grad, normed, inverse):
    mean_grad = jnp.mean(grad, axis=-1, keepdims=True)
    mean_proj = jnp.mean(grad * normed, axis=-1, keepdims=True)
    return inverse * (grad - mean_grad - normed * mean_proj)


def adam(master, first, second, grad):
    first_new = BETA_ONE * first + (1.0 - BETA_ONE) * grad
    second_new = BETA_TWO * second + (1.0 - BETA_TWO) * grad * grad
    fix_one = 1.0 - BETA_ONE**STEP
    fix_two = 1.0 - BETA_TWO**STEP
    update = first_new / fix_one / (jnp.sqrt(second_new / fix_two) + ADAM_EPS) + DECAY * master
    return (master - RATE * update, first_new, second_new)


def gelu_both(value):
    square = value * value
    tanh = jnp.tanh(value * (GELU_CUBE * square + GELU_LIN))
    half = 0.5 * tanh + 0.5
    act = value * half
    slope = half + act * (1.0 - tanh) * (3.0 * GELU_CUBE * square + GELU_LIN)
    return act, slope


def dp_sizes(count):
    side = 4 if count >= 64 else 2
    return count // (side * side), side


class Place:
    def __init__(self, count):
        self.count = count
        self.depth, self.side = dp_sizes(count)
        self.dp = lax.axis_index("dp")
        self.mp = lax.axis_index("mp")
        side = self.side
        y = (self.dp // side) % side
        x = self.dp % side
        self.at = {
            "z": self.dp // (side * side),
            "a": jnp.where(self.mp == 0, y, x),
            "b": jnp.where(self.mp == 0, x, y),
        }
        self.size = {"z": self.depth, "a": side, "b": side}
        self.near = {axis: self.peers(axis) for axis in "zab"}
        self.first, self.others = {}, {}
        for order in (ZBA, BZA):
            for stage, axis in enumerate(order):
                fixed = {name: self.at[name] for name in order[stage:]}
                self.first[order, stage] = self.slot_at(order, fixed)
                self.others[order, stage] = [
                    self.slot_at(order, {**fixed, axis: self.along(axis, k)}) for k in range(1, self.size[axis])
                ]
        z = self.at["z"]
        self.line = self.depth == 4
        self.end = (z == 0) | (z == 3)
        self.next_end = jnp.where(z < 2, 0, 3)
        self.inside = jnp.where(z < 2, 1, 2)
        self.far_end = 3 - self.next_end

    def slot_at(self, order, at):
        slot = 0
        for axis in reversed(order):
            slot = slot * self.size[axis] + at.get(axis, 0)
        return slot

    def slot(self, order=ZBA):
        return self.first[order, 0]

    def slot_of(self, dp, core, order=ZBA):
        side = self.side
        z, y, x = dp // (side * side), (dp // side) % side, dp % side
        one = self.slot_at(order, {"z": z, "a": y, "b": x})
        two = self.slot_at(order, {"z": z, "a": x, "b": y})
        return jnp.where(core == 0, one, two)

    def device(self, at):
        z, a, b = at["z"], at["a"], at["b"]
        side = self.side
        dp = jnp.where(self.mp == 0, (z * side + a) * side + b, (z * side + b) * side + a)
        return (dp, self.mp)

    def along(self, axis, step):
        return (self.at[axis] + step) % self.size[axis]

    def peers(self, axis):
        return [self.device({**self.at, axis: self.along(axis, k)}) for k in range(1, self.size[axis])]

    def other_core(self):
        return (self.dp, 1 - self.mp)

    def peers_layer(self):
        layer = self.side * self.side
        first = self.dp - self.dp % layer
        peers = []
        for k in range(1, 2 * layer):
            spot = (self.dp % layer * 2 + self.mp + k) % (2 * layer)
            peers.append((first + spot // 2, spot % 2))
        return peers

    def greet(self):
        peers = self.peers("z") + self.peers_layer()
        barrier = pltpu.get_barrier_semaphore()
        for peer in peers:
            pl.semaphore_signal(barrier, inc=1, device_id=peer, device_id_type=MESH)
        pl.semaphore_wait(barrier, len(peers))


def remote(src, dst, send, recv, peer):
    return pltpu.make_async_remote_copy(
        src_ref=src, dst_ref=dst, send_sem=send, recv_sem=recv, device_id=peer, device_id_type=MESH
    )


def span(place, order, stage):
    return math.prod(place.size[axis] for axis in order[:stage])


class Gather:
    def __init__(self, place, buf, send, recv, order=ZBA, relay=False):
        self.p, self.buf, self.send, self.recv, self.order = place, buf, send, recv, order
        self.relayed = relay and place.line

    def copies(self, stage, e):
        p, order = self.p, self.order
        src = self.buf.at[e, pl.ds(p.first[order, stage], span(p, order, stage))]
        base = sum(p.size[axis] - 1 for axis in order[:stage])
        return [
            remote(src, src, self.send.at[e, base + k], self.recv.at[e, base + k], peer)
            for k, peer in enumerate(p.near[order[stage]])
        ]

    def passed(self, e):
        p, order = self.p, self.order
        stage = order.index("z")
        base = sum(p.size[axis] - 1 for axis in order[:stage])
        fixed = {name: p.at[name] for name in order[stage:]}
        src = self.buf.at[e, pl.ds(p.slot_at(order, {**fixed, "z": p.far_end}), span(p, order, stage))]
        extra = sum(size - 1 for size in p.size.values())
        recv = self.recv.at[e, base + jnp.where(p.next_end == 0, 0, 2)]
        return remote(src, src, self.send.at[e, extra], recv, p.device({**p.at, "z": p.next_end}))

    def each(self, stage, e, act):
        for k, copy in enumerate(self.copies(stage, e)):
            if self.relayed and self.order[stage] == "z" and k != 1:
                pl.when(self.p.at["z"] != (3 if k == 0 else 0))(functools.partial(act, copy))
            else:
                act(copy)

    def start(self, stage, e):
        self.each(stage, e, lambda copy: copy.start())

    def relay(self, e):
        if self.relayed:

            @pl.when(~self.p.end)
            def _():
                self.copies(self.order.index("z"), e)[1].wait_recv()
                self.passed(e).start()

    def arrive(self, stage, e):
        for k, copy in enumerate(self.copies(stage, e)):
            if self.relayed and self.order[stage] == "z" and k == 1:
                pl.when(self.p.end)(copy.wait_recv)
            else:
                copy.wait_recv()

    def sent(self, e):
        for stage in range(3):
            self.each(stage, e, lambda copy: copy.wait_send())
        if self.relayed:
            pl.when(~self.p.end)(lambda: self.passed(e).wait_send())


class Scatter:
    def __init__(self, place, buf, boxes, send, recv, order=ZBA, relay=False):
        self.p, self.buf, self.boxes, self.send, self.recv, self.order = place, buf, boxes, send, recv, order
        self.relayed = relay and place.line

    def box(self, stage, e, block, many):
        box = self.boxes[min(stage, 1)]
        if stage >= 2:
            order = self.order
            block = block + (self.p.size[order[1]] - 1) * span(self.p, order, 1)
        if stage == 3:
            block = block + self.p.size[self.order[0]] - 1
        return box.at[e % box.shape[0], pl.ds(block, many)]

    def copies(self, stage, e):
        p, order = self.p, self.order
        axis, many = order[2 - stage], span(p, order, 2 - stage)
        sem = sum(p.size[order[2 - before]] - 1 for before in range(stage))
        made = []
        for k, peer in enumerate(p.near[axis]):
            src = self.buf.at[e, pl.ds(p.others[order, 2 - stage][k], many)]
            dst = self.box(stage, e, k * many, many)
            made.append(remote(src, dst, self.send.at[e, sem + k], self.recv.at[e, sem + k], peer))
        return made

    def passed(self, e):
        p, order = self.p, self.order
        at = order.index("z")
        many = span(p, order, at)
        fixed = {name: p.at[name] for name in order[at:]}
        src = self.buf.at[e, pl.ds(p.slot_at(order, {**fixed, "z": p.far_end}), many)]
        extra = sum(size - 1 for size in p.size.values())
        peer = p.device({**p.at, "z": p.inside})
        return remote(src, self.box(3, e, 0, many), self.send.at[e, extra], self.recv.at[e, extra], peer)

    def on_line(self, stage):
        return self.relayed and self.order[2 - stage] == "z"

    def start(self, stage, e):
        for k, copy in enumerate(self.copies(stage, e)):
            if self.on_line(stage):
                here = self.p.end if k == 1 else self.p.at["z"] != (3 if k == 0 else 0)
                pl.when(here)(copy.start)
            else:
                copy.start()
        if self.on_line(stage):
            pl.when(self.p.end)(lambda: self.passed(e).start())

    def relay(self, e):
        if self.relayed:
            stage = 2 - self.order.index("z")
            many = span(self.p, self.order, 2 - stage)

            @pl.when(~self.p.end)
            def _():
                self.passed(e).wait_recv()
                to = self.p.others[self.order, 2 - stage][1]
                for i in range(many):
                    total = self.buf[e, to + i].astype(f32) + self.box(3, e, i, 1)[0].astype(f32)
                    self.buf[e, to + i] = total.astype(bf16)
                self.copies(stage, e)[1].start()

    def arrive(self, stage, e):
        for k, copy in enumerate(self.copies(stage, e)):
            if self.on_line(stage) and k != 1:
                pl.when(self.p.at["z"] != (3 if k == 0 else 0))(copy.wait_send)
                pl.when(self.p.at["z"] != (0 if k == 0 else 3))(copy.wait_recv)
            else:
                copy.wait()
        if self.on_line(stage):
            pl.when(self.p.end)(lambda: self.passed(e).wait_send())

    def total(self, stage, e, i):
        p, order = self.p, self.order
        many = span(p, order, 2 - stage)
        total = self.buf[e, p.first[order, 2 - stage] + i].astype(f32)
        for k in range(p.size[order[2 - stage]] - 1):
            term = self.box(stage, e, k * many + i, 1)[0].astype(f32)
            if self.on_line(stage) and k != 1:
                term = jnp.where(p.at["z"] != (0 if k == 0 else 3), term, 0.0)
            total = total + term
        return total

    def add(self, stage, e):
        def one(i, carry):
            self.buf[e, self.p.first[self.order, 2 - stage] + i] = self.total(stage, e, i).astype(bf16)
            return carry

        lax.fori_loop(0, span(self.p, self.order, 2 - stage), one, 0)

    def last(self, e):
        return self.total(2, e, 0)


def block_rows(rows, parts):
    return (parts * rows + SUB - 1) // SUB * SUB


def blocks_to_weights(place, rows, buf, core, outs, order=ZBA):
    many = SUB // math.gcd(SUB, rows)
    for first in range(0, place.count, many):
        blocks = [buf[place.slot_of(first + i, core, order)].astype(f32) for i in range(many)]
        for part, out in enumerate(outs):
            pieces = [block[part * rows : (part + 1) * rows] for block in blocks]
            out[pl.ds(first * rows, many * rows), :] = jnp.concatenate(pieces, axis=0).astype(bf16)


def grads_to_blocks(place, rows, grads, buf, order=ZBA):
    block = buf.shape[1]
    for dp in range(place.count):
        pieces = [grad[dp * rows : (dp + 1) * rows, :] for grad in grads]
        if block > rows * len(grads):
            pieces.append(jnp.zeros((block - rows * len(grads), buf.shape[2]), f32))
        buf[place.slot_of(dp, place.mp, order)] = jnp.concatenate(pieces, axis=0).astype(bf16)


def all_sum(place, value, src, box, send, recv):
    layer = place.side * place.side
    spot = place.dp % layer
    z = place.at["z"]
    src[0] = value
    box[z] = value
    copies = [
        remote(src.at[0], box.at[z], send.at[k], recv.at[k], peer) for k, peer in enumerate(place.near["z"])
    ]
    for copy in copies:
        copy.start()
    for copy in copies:
        copy.wait()
    total = box[0]
    for i in range(1, place.depth):
        total = total + box[i]
    mine = spot * 2 + place.mp
    base = place.depth
    src[1] = total
    box[base + mine] = total
    at = place.depth - 1
    copies = [
        remote(src.at[1], box.at[base + mine], send.at[at + k], recv.at[at + k], peer)
        for k, peer in enumerate(place.peers_layer())
    ]
    for copy in copies:
        copy.start()
    for copy in copies:
        copy.wait()
    total = box[base]
    for i in range(1, 2 * layer):
        total = total + box[base + i]
    return total


def block_kernel(
    count, rows, experts, tile, lag,
    tok_ref, cot_ref, cond_ref, route_ref, ada_ref, gate_ref, attn_ref, w_ref,
    output_ref, grad_tok_ref, ada_out, attn_out, total_ref, norm_out,
    buf_one, buf_two, box_one, rest_one, box_two, rest_two,
    ada_buf, sc_buf, mod_buf, mod_far, attn_buf, attn_box, attn_rest, attn_far, attn_w,
    cond_low, mod, grad_mod, grad_mod_in, triple, mixed, h_one, soft,
    h_all, d_all, gate_all, branch_acc, grad_h_acc, grad_gate_acc, gate_in, share_in,
    up_w, down_w, up_grad, down_grad, gate_grad, attn_share, attn_in, norm_src, norm_box,
    load_sem, gather_send, gather_recv, gather_send_two, gather_recv_two,
    scatter_send, scatter_recv, scatter_send_two, scatter_recv_two,
    ada_send, ada_recv, sc_send, sc_recv, mod_send, mod_recv, attn_send, attn_recv, attn_back_send, attn_back_recv,
    core_send, core_recv, token_send, token_recv, norm_send, norm_recv,
):
    place = Place(count)
    mp = place.mp
    wide_experts = w_ref.shape[1]
    own_tok, width = tok_ref.shape
    images = own_tok // PATCH
    half = attn_ref.shape[2]
    first = half // LANES * LANES
    heads = half // HD
    wide = ada_ref.shape[1] // 2
    cut = ada_buf.shape[3]
    scale = HD ** (-0.5)
    own_at = pl.multiple_of(mp * own_tok, own_tok)
    their_at = pl.multiple_of((1 - mp) * own_tok, own_tok)
    own, theirs = pl.ds(own_at, own_tok), pl.ds(their_at, own_tok)
    other = place.other_core()

    loads = [
        pltpu.make_async_copy(tok_ref, branch_acc.at[pl.ds(0, own_tok)], load_sem.at[0]),
        pltpu.make_async_copy(cot_ref, branch_acc.at[pl.ds(own_tok, own_tok)], load_sem.at[1]),
    ]
    for load in loads:
        load.start()

    def put(target, block, order=ZBA):
        if block.shape[0] != target.shape[1]:
            target[place.slot(order)] = jnp.zeros(target.shape[1:], bf16)
        target[place.slot(order), pl.ds(0, block.shape[0])] = block

    cols = ada_ref[:, pl.ds(pl.multiple_of(mp * wide, LANES), wide)]
    tail = jnp.concatenate([cols[:, cut:], jnp.zeros((rows, 2 * cut - wide), f32)], axis=1)
    put(ada_buf.at[0], jnp.concatenate([cols[:, :cut], tail], axis=0).astype(bf16))
    parts = attn_ref.shape[0]
    side_by = lax.broadcasted_iota(jnp.int32, (experts, LANES), 1) == lax.broadcasted_iota(
        jnp.int32, (experts, LANES), 0
    )
    gate = mxu(gate_ref[...].astype(bf16), side_by.astype(f32).astype(bf16), TN)[:, : 2 * LANES - half]
    spare = [gate] + [jnp.zeros_like(gate)] * (parts - 1)
    both = [jnp.concatenate([attn_ref[j], spare[j]], axis=1) for j in range(parts)]
    pair = parts // 2
    for i in range(2):
        put(attn_buf.at[i], jnp.concatenate(both[i * pair : (i + 1) * pair], axis=0).astype(bf16))
    cond = cond_ref[...]
    cond = cond / (1.0 + jnp.exp(-cond))
    cond_low[...] = cond.astype(bf16)
    sc_buf[0, place.slot()] = jnp.concatenate([cond, jnp.zeros((SUB - cond.shape[0], width), f32)], axis=0).astype(bf16)
    place.greet()
    ada_gather = Gather(place, ada_buf, ada_send, ada_recv)
    attn_gather = Gather(place, attn_buf, attn_send, attn_recv)
    cuts = (pl.ds(0, buf_one.shape[3]), pl.ds(buf_one.shape[3], buf_two.shape[3]))
    streams = tuple(zip((buf_one, buf_two), cuts, (ZBA, BZA)))
    gathers = (
        Gather(place, buf_one, gather_send, gather_recv, ZBA, True),
        Gather(place, buf_two, gather_send_two, gather_recv_two, BZA, True),
    )
    scatters = (
        Scatter(place, buf_one, (box_one, rest_one), scatter_send, scatter_recv, ZBA, True),
        Scatter(place, buf_two, (box_two, rest_two), scatter_send_two, scatter_recv_two, BZA, True),
    )
    sc_gather = Gather(place, sc_buf, sc_send, sc_recv)
    ada_gather.start(0, 0)
    attn_gather.start(0, 0)
    attn_gather.start(0, 1)
    sc_gather.start(0, 0)

    def fill(e, carry):
        both = jnp.concatenate([w_ref[0, e], w_ref[1, e]], axis=0).astype(bf16)
        for buf, lanes, order in streams:
            put(buf.at[e], both[:, lanes.start : lanes.start + lanes.size], order)
        return carry

    lax.fori_loop(0, wide_experts, fill, 0)

    def begin(e):
        for one in gathers:
            one.start(0, e)

    def onward(stage, e):
        for one in gathers:
            one.arrive(stage, e)
            one.start(stage + 1, e)

    def tick(k):
        pl.when(k + 5 < wide_experts)(lambda: begin(k + 5))
        pl.when(k + 4 < wide_experts)(lambda: gathers[0].relay(k + 4))
        pl.when(k + 3 < wide_experts)(lambda: onward(0, k + 3))
        pl.when(k + 2 < wide_experts)(lambda: gathers[1].relay(k + 2))
        pl.when(k + 1 < wide_experts)(lambda: onward(1, k + 1))

    grad_mod[...] = jnp.zeros_like(grad_mod)
    for stage in range(2):
        for small, i in ((ada_gather, 0), (attn_gather, 0), (attn_gather, 1)):
            small.arrive(stage, i)
            small.start(stage + 1, i)
        if stage == 0:
            begin(0)
            begin(1)
    begin(2)
    begin(3)
    gathers[0].relay(0)
    onward(0, 0)
    ada_gather.arrive(2, 0)

    low_cut = pl.ds(0, cut)
    blocks_to_weights(place, rows, ada_buf.at[0], mp, (up_w.at[:, low_cut], down_w.at[:, low_cut]))
    mod[mp, :, pl.ds(0, cut)] = mxu(cond_low[...], up_w[:, low_cut])
    mod[mp, :, pl.ds(cut, cut)] = mxu(cond_low[...], down_w[:, low_cut])
    mod_cross = remote(mod.at[mp], mod.at[mp], core_send.at[1], core_recv.at[1], other)
    mod_cross.start()
    attn_cross = []
    for i in range(2):
        attn_gather.arrive(2, i)
        attn_cross.append(
            remote(attn_buf.at[i], attn_far.at[i], core_send.at[8 + i], core_recv.at[8 + i], other)
        )
        attn_cross[i].start()
        outs = [attn_w.at[mp, j] for j in range(i * pair, (i + 1) * pair)]
        blocks_to_weights(place, rows, attn_buf.at[i], mp, outs)
    for load in loads:
        load.wait()
    ada_gather.sent(0)
    attn_gather.sent(0)
    attn_gather.sent(1)
    sc_gather.arrive(0, 0)
    sc_gather.start(1, 0)
    for i in range(2):
        attn_cross[i].wait()
        outs = [attn_w.at[1 - mp, j] for j in range(i * pair, (i + 1) * pair)]
        blocks_to_weights(place, rows, attn_far.at[i], 1 - mp, outs)
    mod_cross.wait()
    gathers[0].relay(1)
    onward(0, 1)
    gathers[0].relay(2)
    gathers[1].relay(0)
    gate_lanes = pl.ds(first, LANES)
    half_lanes = pl.ds(0, half)

    def weight(core, j):
        return attn_w[core, j, :, half_lanes]

    lane_pair = lax.broadcasted_iota(jnp.int32, (PATCH, 2 * HD), 1)
    masks = [(lane_pair < HD).astype(f32).astype(bf16), (lane_pair >= HD).astype(f32).astype(bf16)]
    groups = [(at, min(2, heads - at)) for at in range(0, heads, 2)]
    expert_lane = lax.broadcasted_iota(jnp.int32, (PATCH, LANES), 1) - (half - first)

    def mod_row(image, vector):
        flat = vector % 3 * width
        return mod[vector // 3, pl.ds(mp * images + image, 1), pl.ds(flat, width)]

    def add_grad_mod(image, vector, value):
        grad_mod[vector // 3, pl.ds(mp * images + image, 1), pl.ds(vector % 3 * width, width)] = value

    def one_head(value, group, head):
        return value if group[1] == 1 else value * masks[head]

    def route(h, image):
        valid = (expert_lane >= 0) & (expert_lane < experts)
        logits = jnp.where(valid, mxu(h, attn_w[0, 0, :, gate_lanes]), -jnp.inf)
        power = jnp.exp(logits - jnp.max(logits, axis=1, keepdims=True))
        router = power / jnp.sum(power, axis=1, keepdims=True)
        picks = route_ref[:, pl.ds(pl.multiple_of(own_at + image * PATCH, PATCH), PATCH)]
        spot = lax.broadcasted_iota(jnp.int32, (LANES, PATCH), 0) - (half - first)
        picked = jnp.where((picks[0:1, :] == spot) | (picks[1:2, :] == spot), 1.0, 0.0)
        return router, picked.T

    def attend(at):
        return mxu(mixed[0, at, :], weight(0, 3), NT) + mxu(mixed[1, at, :], weight(1, 3), NT)

    def token_copies(image):
        at = pl.ds(pl.multiple_of(own_at + image * PATCH, PATCH), PATCH)
        return [
            remote(ref.at[at], ref.at[at], token_send.at[image, i], token_recv.at[image, i], other)
            for i, ref in enumerate((h_all, d_all, gate_all))
        ]

    def forward(image, carry):
        at = pl.ds(pl.multiple_of(image * PATCH, PATCH), PATCH)
        cot_at = pl.ds(pl.multiple_of(own_tok + image * PATCH, PATCH), PATCH)
        all_at = pl.ds(pl.multiple_of(own_at + image * PATCH, PATCH), PATCH)
        normed, _ = layer_norm(branch_acc[at, :])
        h = (normed * (1.0 + mod_row(image, 1)) + mod_row(image, 0)).astype(bf16)
        h_one[at, :] = h
        for core in range(2):
            for j in range(3):
                triple[core, j, at, :] = mxu(h, weight(core, j)).astype(bf16)
            for group in groups:
                lanes = pl.ds(group[0] * HD, group[1] * HD)
                query, key, value = (triple[core, j, at, lanes] for j in range(3))
                total = 0.0
                for head in range(group[1]):
                    scores = mxu(one_head(query, group, head), key, NT) * scale
                    power = jnp.exp(scores - jnp.max(scores, axis=1, keepdims=True))
                    low = (power * (1.0 / jnp.sum(power, axis=1, keepdims=True))).astype(bf16)
                    soft[image, core * heads + group[0] + head] = low
                    total = total + mxu(low, one_head(value, group, head))
                mixed[core, at, lanes] = total.astype(bf16)
        x_one = branch_acc[at, :] + mod_row(image, 2) * attend(at)
        normed, _ = layer_norm(x_one)
        h = (normed * (1.0 + mod_row(image, 4)) + mod_row(image, 3)).astype(bf16)
        h_all[all_at, :] = h
        router, chosen = route(h, image)
        shared = (expert_lane >= experts) & (expert_lane < wide_experts)
        gate_all[all_at, :] = jnp.where(shared, 1.0, router * chosen)
        d_all[all_at, :] = (branch_acc[cot_at, :] * mod_row(image, 5)).astype(bf16)
        for copy in token_copies(image):
            copy.start()

        tick(image - 1)

        @pl.when(image == 0)
        def _():
            sc_gather.arrive(1, 0)
            sc_gather.start(2, 0)

        return carry

    lax.fori_loop(0, images, forward, 0)
    ahead = images - 1
    sc_gather.arrive(2, 0)
    sc_gather.sent(0)

    branch_acc[...] = jnp.zeros_like(branch_acc)
    grad_h_acc[...] = jnp.zeros_like(grad_h_acc)
    grad_gate_acc[...] = jnp.zeros_like(grad_gate_acc)

    def all_tokens(image, carry):
        for copy in token_copies(image):
            copy.wait()
        return carry

    lax.fori_loop(0, images, all_tokens, 0)

    shares = [
        remote(h_all.at[theirs], share_in.at[0], core_send.at[2], core_recv.at[2], other),
        remote(d_all.at[theirs], share_in.at[1], core_send.at[3], core_recv.at[3], other),
        remote(grad_gate_acc.at[theirs], gate_in, core_send.at[4], core_recv.at[4], other),
    ]
    loads = [
        pltpu.make_async_copy(tok_ref, branch_acc.at[theirs], load_sem.at[0]),
        pltpu.make_async_copy(cot_ref, grad_h_acc.at[theirs], load_sem.at[1]),
    ]
    tiles = h_all.shape[0] // tile

    def compute(e):
        for buf, lanes, order in streams:
            blocks_to_weights(place, rows, buf.at[e], mp, (up_w.at[:, lanes], down_w.at[:, lanes]), order)
        up_grad[...] = jnp.zeros_like(up_grad)
        down_grad[...] = jnp.zeros_like(down_grad)

        def one_tile(t, carry):
            @pl.when((e == wide_experts - 1) & (t == tiles // 2))
            def _():
                h_all[theirs, :] = branch_acc[theirs, :].astype(bf16)
                d_all[theirs, :] = grad_h_acc[theirs, :].astype(bf16)
                for copy in shares:
                    copy.start()
                for copy in loads:
                    copy.start()

            at = pl.ds(pl.multiple_of((t + (1 - mp) * (tiles // 2)) % tiles * tile, tile), tile)
            h = h_all[at, :]
            d = d_all[at, :]
            lane = lax.broadcasted_iota(jnp.int32, (tile, LANES), 1) - (half - first)
            gate = jnp.sum(jnp.where(lane == e, gate_all[at, :], 0.0), axis=1, keepdims=True)
            pre = mxu(h, up_w[...])
            back = mxu(d, down_w[...])
            act, slope = gelu_both(pre)
            inner = jnp.sum(act * back, axis=1, keepdims=True)
            grad_gate_acc[at, :] += jnp.where(lane == e, inner, 0.0)
            act_low = (gate * act).astype(bf16)
            pre_low = (gate * back * slope).astype(bf16)
            branch_acc[at, :] += mxu(act_low, down_w[...], NT)
            grad_h_acc[at, :] += mxu(pre_low, up_w[...], NT)
            up_grad[...] += mxu(h, pre_low, TN)
            down_grad[...] += mxu(d, act_low, TN)
            return carry

        lax.fori_loop(0, tiles, one_tile, 0)

    def follow(one, stage, e):
        one.arrive(stage, e)
        one.add(stage, e)
        one.start(stage + 1, e)

    def finish(e):
        for one, (_, lanes, _) in zip(scatters, streams):
            one.arrive(2, e)
            total_ref[e, :, lanes] = one.last(e)

    def collect(k):
        def at(late, act):
            pl.when((k >= late) & (k - late < wide_experts))(lambda: act(k - late))

        at(4, finish)
        at(3, scatters[0].relay)
        at(3, lambda e: follow(scatters[1], 1, e))
        at(2, lambda e: follow(scatters[0], 1, e))
        at(2, scatters[1].relay)
        at(1, lambda e: [follow(one, 0, e) for one in scatters] and None)

    def step(e, carry):
        tick(e + ahead)
        for one in gathers:
            one.arrive(2, e)
        compute(e)
        for one in gathers:
            one.sent(e)
        for buf, lanes, order in streams:
            grads_to_blocks(place, rows, (up_grad.at[:, lanes], down_grad.at[:, lanes]), buf.at[e], order)
        for one in scatters:
            one.start(0, e)
        collect(e - lag)
        return carry

    lax.fori_loop(0, wide_experts, step, 0)

    gate_grad[...] = jnp.zeros_like(gate_grad)
    for copy in shares + loads:
        copy.wait()

    def backward(image, carry):
        at = pl.ds(pl.multiple_of(image * PATCH, PATCH), PATCH)
        own_rows = pl.ds(pl.multiple_of(own_at + image * PATCH, PATCH), PATCH)
        load_rows = pl.ds(pl.multiple_of(their_at + image * PATCH, PATCH), PATCH)
        tok, cot = branch_acc[load_rows, :], grad_h_acc[load_rows, :]
        branch = branch_acc[own_rows, :] + share_in[0, at, :].astype(f32)
        attention = attend(at)
        x_one = tok + mod_row(image, 2) * attention
        normed, inverse = layer_norm(x_one)
        branch_acc[own_rows, :] = x_one + mod_row(image, 5) * branch
        add_grad_mod(image, 5, jnp.sum(cot * branch, axis=0, keepdims=True))
        h = h_all[own_rows, :]
        router, chosen = route(h, image)
        grad_router = (grad_gate_acc[own_rows, :] + gate_in[at, :]) * chosen
        grad_logits = (router * (grad_router - jnp.sum(router * grad_router, axis=1, keepdims=True))).astype(bf16)
        gate_grad[...] += mxu(h, grad_logits, TN)
        grad_h = grad_h_acc[own_rows, :] + share_in[1, at, :].astype(f32) + mxu(grad_logits, attn_w[0, 0, :, gate_lanes], NT)
        add_grad_mod(image, 3, jnp.sum(grad_h, axis=0, keepdims=True))
        add_grad_mod(image, 4, jnp.sum(grad_h * normed, axis=0, keepdims=True))
        grad_x = cot + norm_back(grad_h * (1.0 + mod_row(image, 4)), normed, inverse)
        add_grad_mod(image, 2, jnp.sum(grad_x * attention, axis=0, keepdims=True))
        grad_att = (grad_x * mod_row(image, 2)).astype(bf16)
        d_all[own_rows, :] = grad_att
        grad_h_one = 0.0
        for core in range(2):
            grad_mixed = mxu(grad_att, weight(core, 3)).astype(bf16)
            for group in groups:
                lanes = pl.ds(group[0] * HD, group[1] * HD)
                query, key, value = (triple[core, j, at, lanes] for j in range(3))
                back = grad_mixed[:, group[0] * HD : (group[0] + group[1]) * HD]
                grads = [0.0, 0.0, 0.0]
                for head in range(group[1]):
                    low = soft[image, core * heads + group[0] + head]
                    prob = low.astype(f32)
                    head_back = one_head(back, group, head)
                    grad_soft = mxu(head_back, value, NT)
                    delta = jnp.sum(prob * grad_soft, axis=1, keepdims=True)
                    grad_scores = (prob * (grad_soft - delta) * scale).astype(bf16)
                    grads[0] = grads[0] + mxu(grad_scores, one_head(key, group, head))
                    grads[1] = grads[1] + mxu(grad_scores, one_head(query, group, head), TN)
                    grads[2] = grads[2] + mxu(low, head_back, TN)
                for j in range(3):
                    triple[core, j, at, lanes] = grads[j].astype(bf16)
            for j in range(3):
                grad_h_one = grad_h_one + mxu(triple[core, j, at, :], weight(core, j), NT)
        normed, inverse = layer_norm(tok)
        add_grad_mod(image, 0, jnp.sum(grad_h_one, axis=0, keepdims=True))
        add_grad_mod(image, 1, jnp.sum(grad_h_one * normed, axis=0, keepdims=True))
        grad_h_acc[own_rows, :] = grad_x + norm_back(grad_h_one * (1.0 + mod_row(image, 1)), normed, inverse)

        @pl.when(image > 0)
        def _():
            collect(wide_experts - lag + image - 1)

        return carry

    lax.fori_loop(0, images, backward, 0)
    stores = [
        pltpu.make_async_copy(branch_acc.at[own], output_ref, load_sem.at[2]),
        pltpu.make_async_copy(grad_h_acc.at[own], grad_tok_ref, load_sem.at[3]),
    ]
    for copy in stores:
        copy.start()

    crosses = [
        remote(grad_mod.at[1 - mp], grad_mod_in, core_send.at[5], core_recv.at[5], other),
        *[
            remote(
                attn_share.at[pl.ds(i * pair, pair)], attn_in.at[pl.ds(i * pair, pair)],
                core_send.at[6 + i], core_recv.at[6 + i], other,
            )
            for i in range(2)
        ],
        remote(mod_buf.at[0], mod_far, core_send.at[0], core_recv.at[0], other),
    ]
    crosses[0].start()

    def attn_grad(core, j):
        if j == parts - 1:
            return mxu(d_all[own, :], mixed[core], TN)
        return mxu(h_one[...], triple[core, j], TN)

    spare = pl.ds(half, 2 * LANES - half)
    places = [(up_grad, 0), (up_grad, 1), (up_grad, 2), (down_grad, 0)]
    attn_scatter = Scatter(place, attn_buf, (attn_box, attn_rest), attn_back_send, attn_back_recv)
    for i in range(2):
        for j in range(i * pair, (i + 1) * pair):
            attn_share[j, :, half_lanes] = attn_grad(1 - mp, j).astype(bf16)
            extra = gate_grad[:, pl.ds(half - first, 2 * LANES - half)].astype(bf16)
            attn_share[j, :, spare] = extra if j == 0 else jnp.zeros_like(extra)
        crosses[1 + i].start()
    crosses[0].wait()
    grad_low = grad_mod[mp] + grad_mod_in[...]
    mod_buf[0, place.slot()] = jnp.concatenate([grad_low[:, :cut], grad_low[:, cut:]], axis=0).astype(bf16)
    mod_gather = Gather(place, mod_buf, mod_send, mod_recv)
    for i in range(2):
        for j in range(i * pair, (i + 1) * pair):
            ref, at = places[j]
            ref[:, pl.ds(at * 2 * LANES, half)] = attn_grad(mp, j)
        crosses[1 + i].wait()
        grads = []
        for j in range(i * pair, (i + 1) * pair):
            ref, at = places[j]
            lanes = pl.ds(at * 2 * LANES, half)
            ref[:, lanes] += attn_in[j, :, half_lanes].astype(f32)
            extra = gate_grad[:, pl.ds(half - first, 2 * LANES - half)] + attn_in[0, :, spare].astype(f32)
            ref[:, pl.ds(at * 2 * LANES + half, 2 * LANES - half)] = extra if j == 0 else jnp.zeros_like(extra)
            grads.append(ref[:, pl.ds(at * 2 * LANES, 2 * LANES)])
        grads_to_blocks(place, rows, grads, attn_buf.at[i])
        attn_scatter.start(0, i)
    mod_gather.start(0, 0)
    left = list(range(wide_experts - lag + images - 1, wide_experts + 4))
    for stage in range(2):
        if len(left) > 1:
            collect(left.pop(0))
        for i in range(2):
            attn_scatter.arrive(stage, i)
            attn_scatter.add(stage, i)
            attn_scatter.start(stage + 1, i)
        mod_gather.arrive(stage, 0)
        mod_gather.start(stage + 1, 0)
    for k in left:
        collect(k)
    square = jnp.zeros((1, 1), f32)
    for e in range(wide_experts):
        square = square + jnp.sum(total_ref[e] * total_ref[e])
    mod_gather.arrive(2, 0)
    crosses[3].start()
    row = lax.broadcasted_iota(jnp.int32, (width, LANES), 0)
    lane = lax.broadcasted_iota(jnp.int32, (width, LANES), 1)
    pick = ((row == place.dp * rows + lane) & (lane < rows)).astype(f32).astype(bf16)
    group = cond_ref.shape[0]

    def in_order(ref, core, at):
        pieces = [ref[place.slot_of(dp, core)].astype(f32)[at : at + group] for dp in range(count)]
        return jnp.concatenate(pieces, axis=0).astype(bf16)

    conds = mxu(in_order(sc_buf.at[0], mp, 0), pick).astype(bf16)

    def ada_grad(ref, core):
        low = mxu(conds, in_order(ref, core, 0), TN)[:rows]
        high = mxu(conds, in_order(ref, core, group), TN)[:rows, : wide - cut]
        start = pl.multiple_of(core * wide, LANES)
        ada_out[:, pl.ds(start, cut)] = low
        ada_out[:, pl.ds(pl.multiple_of(start + cut, LANES), wide - cut)] = high
        return jnp.sum(low * low) + jnp.sum(high * high)

    small = ada_grad(mod_buf.at[0], mp)
    mod_gather.sent(0)
    crosses[3].wait()
    small = small + ada_grad(mod_far, 1 - mp)
    square = square + 0.5 * small
    for i in range(2):
        attn_scatter.arrive(2, i)
        attn = attn_scatter.last(i)
        attn_out[i] = attn
        lane = lax.broadcasted_iota(jnp.int32, attn.shape, 1)
        square = square + jnp.sum(jnp.where(lane < half, 1.0, 0.5) * attn * attn)
    value = jnp.broadcast_to(square, norm_out.shape)
    norm_out[...] = all_sum(place, value, norm_src, norm_box, norm_send, norm_recv)
    for copy in stores:
        copy.wait()


def block_call(tokens, condition, cotangent, routes, w_ada, w_gate, w_attn, w_expert):
    count = lax.axis_size("dp")
    own_tok, width = tokens.shape
    rows, wide = w_ada.shape
    experts = w_gate.shape[0]
    parts, _, half = w_attn.shape
    _, wide_experts, _, hidden = w_expert.shape
    depth, side = dp_sizes(count)
    images = own_tok // PATCH
    cut = (wide // 4 + LANES - 1) // LANES * LANES
    spare = 2 * LANES
    block, ada_block, attn_block = block_rows(rows, 2), block_rows(rows, 2), block_rows(rows, parts // 2)
    tok = 2 * own_tok
    tile, lag = (TILE, 2) if count <= 16 else (TILE // 2, 0)
    vmem = pl.BlockSpec(memory_space=pltpu.VMEM)
    hbm = pl.BlockSpec(memory_space=pl.ANY)
    hops = depth + 2 * side - 3

    def sems(*shape):
        return pltpu.SemaphoreType.DMA(shape)

    def boxes(slots, order, height, lanes):
        size = {"z": depth, "a": side, "b": side}
        span = size[order[0]] * size[order[1]]
        first = (size[order[2]] - 1) * span
        extra = 0 if slots <= 2 else math.prod(size[axis] for axis in order[: order.index("z")])
        return [
            pltpu.VMEM((slots, first, height, lanes), bf16),
            pltpu.VMEM((min(slots, REST), span - 1 + extra, height, lanes), bf16),
        ]

    one = hidden * CUT_ONE // CUT_ALL // LANES * LANES
    two = hidden - one

    return pl.pallas_call(
        functools.partial(block_kernel, count, rows, experts, tile, lag),
        out_shape=(
            jax.ShapeDtypeStruct((own_tok, width), f32),
            jax.ShapeDtypeStruct((own_tok, width), f32),
            jax.ShapeDtypeStruct((rows, wide), f32),
            jax.ShapeDtypeStruct((2, attn_block, spare), f32),
            jax.ShapeDtypeStruct((wide_experts, block, hidden), f32),
            jax.ShapeDtypeStruct((8, LANES), f32),
        ),
        in_specs=[hbm, hbm] + [vmem] * 6,
        out_specs=(hbm, hbm) + (vmem,) * 4,
        scratch_shapes=[
            pltpu.VMEM((wide_experts, count, block, one), bf16),
            pltpu.VMEM((wide_experts, count, block, two), bf16),
            *boxes(SLOTS + 2 * lag, ZBA, block, one),
            *boxes(SLOTS + 2 * lag, BZA, block, two),
            pltpu.VMEM((1, count, ada_block, cut), bf16),
            pltpu.VMEM((1, count, SUB, width), bf16),
            pltpu.VMEM((1, count, SUB, cut), bf16),
            pltpu.VMEM((count, SUB, cut), bf16),
            pltpu.VMEM((2, count, attn_block, spare), bf16),
            *boxes(2, ZBA, attn_block, spare),
            pltpu.VMEM((2, count, attn_block, spare), bf16),
            pltpu.VMEM((2, parts, width, spare), bf16),
            pltpu.VMEM(condition.shape, bf16),
            pltpu.VMEM((2, condition.shape[0], 2 * cut), f32),
            pltpu.VMEM((2, condition.shape[0], 2 * cut), f32),
            pltpu.VMEM((condition.shape[0], 2 * cut), f32),
            pltpu.VMEM((2, 3, own_tok, half), bf16),
            pltpu.VMEM((2, own_tok, half), bf16),
            pltpu.VMEM((own_tok, width), bf16),
            pltpu.VMEM((images, width // HD, PATCH, PATCH), bf16),
            pltpu.VMEM((tok, width), bf16),
            pltpu.VMEM((tok, width), bf16),
            pltpu.VMEM((tok, LANES), f32),
            pltpu.VMEM((tok, width), f32),
            pltpu.VMEM((tok, width), f32),
            pltpu.VMEM((tok, LANES), f32),
            pltpu.VMEM((own_tok, LANES), f32),
            pltpu.VMEM((2, own_tok, width), bf16),
            pltpu.VMEM((width, hidden), bf16),
            pltpu.VMEM((width, hidden), bf16),
            pltpu.VMEM((width, hidden), f32),
            pltpu.VMEM((width, hidden), f32),
            pltpu.VMEM((width, LANES), f32),
            pltpu.VMEM((parts, width, spare), bf16),
            pltpu.VMEM((parts, width, spare), bf16),
            pltpu.VMEM((2, 8, LANES), f32),
            pltpu.VMEM((depth + 2 * side * side, 8, LANES), f32),
            sems(4),
            *[sems(wide_experts, hops + 1)] * 8,
            *[sems(1, hops)] * 6,
            *[sems(2, hops)] * 4,
            sems(10),
            sems(10),
            sems(images, 3),
            sems(images, 3),
            sems(depth + 2 * side * side),
            sems(depth + 2 * side * side),
        ],
        compiler_params=pltpu.CompilerParams(collective_id=1, has_side_effects=True, vmem_limit_bytes=VMEM_BYTES),
        cost_estimate=pl.CostEstimate(
            flops=12 * tok * width * hidden * wide_experts, bytes_accessed=16 * w_expert.size, transcendentals=0
        ),
        name="block",
    )(tokens, cotangent, condition, routes, w_ada, w_gate, w_attn, w_expert)
def update_kernel(rows, half, output_ref, grad_tok_ref, expert_w, expert_m, expert_v, expert_ref, norm_ref, attn_ref, ada_ref, *refs):
    ada, gate, attn = (refs[3 * i : 3 * i + 3] for i in range(3))
    outs, (hold, held, grads, sem, token_sem) = refs[9:-5], refs[-5:]
    ada_new, gate_new, attn_new, expert_new = (outs[3 * i : 3 * i + 3] for i in range(4))
    expert = (expert_w, expert_m, expert_v)
    many = expert_w.shape[1] // 2
    chunks = [(part, h) for h in range(2) for part in range(2)]
    grad_loads = [
        pltpu.make_async_copy(expert_ref.at[pl.ds(h * many, many)], grads.at[pl.ds(h * many, many)], token_sem.at[4 + h])
        for h in range(2)
    ]

    def moves(c, refs, back):
        part, h = chunks[c]
        made = []
        for i, ref in enumerate(refs):
            far, near = ref.at[part, pl.ds(h * many, many)], held.at[i, part, pl.ds(h * many, many)]
            made.append(pltpu.make_async_copy(*((near, far) if back else (far, near)), sem.at[int(back), c, i]))
        return made

    for c in range(4):
        if chunks[c][0] == 0:
            grad_loads[chunks[c][1]].start()
        for copy in moves(c, expert, False):
            copy.start()
    token_loads = [pltpu.make_async_copy(ref, hold.at[i], token_sem.at[i]) for i, ref in enumerate((output_ref, grad_tok_ref))]
    token_stores = [pltpu.make_async_copy(hold.at[i], outs[13 + i], token_sem.at[2 + i]) for i in range(2)]
    for copy in token_loads:
        copy.start()
    total = jnp.sqrt(norm_ref[...])
    outs[12][0, 0] = jnp.max(total)
    factor = jnp.minimum(1.0, CLIP_NORM / (total[0:1, 0:1] + 1e-06))

    def write(ins, news, at, grad):
        for new, value in zip(news, adam(ins[0][at], ins[1][at], ins[2][at], grad * factor)):
            new[at] = value

    everything = (slice(None), slice(None))
    write(ada, ada_new, everything, ada_ref[...])
    first = half // LANES * LANES
    small = attn_ref[0, pl.ds(0, rows), pl.ds(first, LANES)]
    square = jnp.concatenate([small, jnp.zeros((LANES - rows, LANES), f32)], axis=0).T
    experts = gate[0].shape[0]
    write(gate, gate_new, everything, square[half - first : half - first + experts, :rows])
    parts = attn[0].shape[0]
    for j in range(parts):
        grad = attn_ref[j // (parts // 2), pl.ds(j % (parts // 2) * rows, rows), pl.ds(0, half)]
        write(attn, attn_new, (j,), grad)
    here = [held.at[i] for i in range(3)]
    for c, (part, h) in enumerate(chunks):
        if part == 0:
            grad_loads[h].wait()
        for copy in moves(c, expert, False):
            copy.wait()

        def one(e, carry):
            write(here, here, (part, e), grads[e, pl.ds(part * rows, rows), :])
            return carry

        lax.fori_loop(h * many, (h + 1) * many, one, 0)
        for copy in moves(c, expert_new, True):
            copy.start()
    for load, store in zip(token_loads, token_stores):
        load.wait()
        store.start()
    for c in range(4):
        for copy in moves(c, expert_new, True):
            copy.wait()
    for copy in token_stores:
        copy.wait()


def update_call(rows, half, output, grad_tokens, norm, expert, attn, ada, weights):
    vmem = pl.BlockSpec(memory_space=pltpu.VMEM)
    hbm = pl.BlockSpec(memory_space=pl.ANY)
    shapes = [jax.ShapeDtypeStruct(w.shape, f32) for w in weights]
    return pl.pallas_call(
        functools.partial(update_kernel, rows, half),
        out_shape=shapes
        + [jax.ShapeDtypeStruct((1, 1), f32)]
        + [jax.ShapeDtypeStruct(output.shape, f32), jax.ShapeDtypeStruct(grad_tokens.shape, f32)],
        in_specs=[hbm] * 6 + [vmem] * (3 + 9),
        out_specs=[vmem] * 9 + [hbm] * 3 + [pl.BlockSpec(memory_space=pltpu.SMEM), hbm, hbm],
        scratch_shapes=[
            pltpu.VMEM((2, *output.shape), f32),
            pltpu.VMEM((3, *weights[9].shape), f32),
            pltpu.VMEM(expert.shape, f32),
            pltpu.SemaphoreType.DMA((2, 4, 3)),
            pltpu.SemaphoreType.DMA((6,)),
        ],
        compiler_params=pltpu.CompilerParams(vmem_limit_bytes=VMEM_BYTES),
        name="update",
    )(output, grad_tokens, *weights[9:], expert, norm, attn, ada, *weights[:9])


def per_device(
    tokens,
    condition,
    cotangent,
    routes,
    w_ada,
    ada_first,
    ada_second,
    w_gate,
    gate_first,
    gate_second,
    w_attn,
    attn_first,
    attn_second,
    w_expert,
    expert_first,
    expert_second,
):
    output, grad_tokens, ada_total, attn_total, expert_total, square_sum = block_call(
        tokens, condition, cotangent, routes.T, w_ada, w_gate.T, w_attn, w_expert
    )
    updated = update_call(
        w_ada.shape[0], w_attn.shape[2], output, grad_tokens, square_sum, expert_total, attn_total, ada_total,
        (
            w_ada, ada_first, ada_second,
            w_gate.T, gate_first.T, gate_second.T,
            w_attn, attn_first, attn_second,
            w_expert, expert_first, expert_second,
        ),
    )
    gates = [gate.T for gate in updated[3:6]]
    return (*updated[13:], updated[12].reshape(()), *updated[:3], *gates, *updated[6:12])


def solution(mesh):
    placed = (
        P(("dp", "mp"), None),
        P("dp", None),
        P(("dp", "mp"), None),
        P("dp", None),
        P("dp", None),
        P("dp", None),
        P("dp", None),
        P("dp", None),
        P("dp", None),
        P("dp", None),
        P(None, "dp", "mp"),
        P(None, "dp", "mp"),
        P(None, "dp", "mp"),
        P(None, None, "dp", "mp"),
        P(None, None, "dp", "mp"),
        P(None, None, "dp", "mp"),
    )
    return jax.shard_map(
        per_device,
        mesh=mesh,
        in_specs=placed,
        out_specs=(
            P(("dp", "mp"), None),
            P(("dp", "mp"), None),
            P(),
            P("dp", None),
            P("dp", None),
            P("dp", None),
            P("dp", None),
            P("dp", None),
            P("dp", None),
            P(None, "dp", "mp"),
            P(None, "dp", "mp"),
            P(None, "dp", "mp"),
            P(None, None, "dp", "mp"),
            P(None, None, "dp", "mp"),
            P(None, None, "dp", "mp"),
        ),
        check_vma=False,
    )
```

```python
import functools
import math

import jax
import jax.numpy as jnp
from jax import lax
from jax.experimental import pallas as pl
from jax.experimental.pallas import tpu as pltpu
from jax.sharding import PartitionSpec as P

HD = 64
PATCH = 256
STEP = 10
LANES = 128
SUB = 16
TILE = 512
SLOTS, REST = 4, 4
ZBA, BZA = "zba", "bza"
CUT_ONE, CUT_ALL = 1, 2

EPS_NORM = 1e-06
CLIP_NORM = 0.1
RATE = 0.08
BETA_ONE = 0.9
BETA_TWO = 0.95
ADAM_EPS = 1e-08
DECAY = 0.01
GELU_LIN = 0.7978845608
GELU_CUBE = 0.7978845608 * 0.044715

MESH = pl.DeviceIdType.MESH
VMEM_BYTES = 127 * 512 * 1024
bf16 = jnp.bfloat16
f32 = jnp.float32
NN = (((1,), (0,)), ((), ()))
NT = (((1,), (1,)), ((), ()))
TN = (((0,), (0,)), ((), ()))


def mxu(left, right, dims=NN):
    return lax.dot_general(left, right, dims, preferred_element_type=f32)


def layer_norm(value):
    center = value - jnp.mean(value, axis=-1, keepdims=True)
    inverse = lax.rsqrt(jnp.mean(center * center, axis=-1, keepdims=True) + EPS_NORM)
    return (center * inverse, inverse)


def norm_back(grad, normed, inverse):
    mean_grad = jnp.mean(grad, axis=-1, keepdims=True)
    mean_proj = jnp.mean(grad * normed, axis=-1, keepdims=True)
    return inverse * (grad - mean_grad - normed * mean_proj)


def adam(master, first, second, grad):
    first_new = BETA_ONE * first + (1.0 - BETA_ONE) * grad
    second_new = BETA_TWO * second + (1.0 - BETA_TWO) * grad * grad
    fix_one = 1.0 - BETA_ONE**STEP
    fix_two = 1.0 - BETA_TWO**STEP
    update = first_new * (1.0 / fix_one) / (jnp.sqrt(second_new * (1.0 / fix_two)) + ADAM_EPS) + DECAY * master
    return (master - RATE * update, first_new, second_new)


def gelu_both(value):
    square = value * value
    tanh = jnp.tanh(value * (GELU_CUBE * square + GELU_LIN))
    half = 0.5 * tanh + 0.5
    act = value * half
    slope = half + act * (1.0 - tanh) * (3.0 * GELU_CUBE * square + GELU_LIN)
    return act, slope


def dp_sizes(count):
    side = 4 if count >= 64 else 2
    return count // (side * side), side


class Place:
    def __init__(self, count):
        self.count = count
        self.depth, self.side = dp_sizes(count)
        self.dp = lax.axis_index("dp")
        self.mp = lax.axis_index("mp")
        side = self.side
        y = (self.dp // side) % side
        x = self.dp % side
        self.at = {
            "z": self.dp // (side * side),
            "a": jnp.where(self.mp == 0, y, x),
            "b": jnp.where(self.mp == 0, x, y),
        }
        self.size = {"z": self.depth, "a": side, "b": side}
        self.near = {axis: self.peers(axis) for axis in "zab"}
        self.first, self.others = {}, {}
        for order in (ZBA, BZA):
            for stage, axis in enumerate(order):
                fixed = {name: self.at[name] for name in order[stage:]}
                self.first[order, stage] = self.slot_at(order, fixed)
                self.others[order, stage] = [
                    self.slot_at(order, {**fixed, axis: self.along(axis, k)}) for k in range(1, self.size[axis])
                ]
        z = self.at["z"]
        self.line = self.depth == 4
        self.end = (z == 0) | (z == 3)
        self.next_end = jnp.where(z < 2, 0, 3)
        self.inside = jnp.where(z < 2, 1, 2)
        self.far_end = 3 - self.next_end

    def slot_at(self, order, at):
        slot = 0
        for axis in reversed(order):
            slot = slot * self.size[axis] + at.get(axis, 0)
        return slot

    def slot(self, order=ZBA):
        return self.first[order, 0]

    def slot_of(self, dp, core, order=ZBA):
        side = self.side
        z, y, x = dp // (side * side), (dp // side) % side, dp % side
        one = self.slot_at(order, {"z": z, "a": y, "b": x})
        two = self.slot_at(order, {"z": z, "a": x, "b": y})
        return jnp.where(core == 0, one, two)

    def device(self, at):
        z, a, b = at["z"], at["a"], at["b"]
        side = self.side
        dp = jnp.where(self.mp == 0, (z * side + a) * side + b, (z * side + b) * side + a)
        return (dp, self.mp)

    def along(self, axis, step):
        return (self.at[axis] + step) % self.size[axis]

    def peers(self, axis):
        return [self.device({**self.at, axis: self.along(axis, k)}) for k in range(1, self.size[axis])]

    def other_core(self):
        return (self.dp, 1 - self.mp)

    def peers_layer(self):
        layer = self.side * self.side
        first = self.dp - self.dp % layer
        peers = []
        for k in range(1, 2 * layer):
            spot = (self.dp % layer * 2 + self.mp + k) % (2 * layer)
            peers.append((first + spot // 2, spot % 2))
        return peers

    def greet(self):
        peers = self.near["z"] + self.peers_layer()
        barrier = pltpu.get_barrier_semaphore()
        for peer in peers:
            pl.semaphore_signal(barrier, inc=1, device_id=peer, device_id_type=MESH)
        return lambda: pl.semaphore_wait(barrier, len(peers))


def remote(src, dst, send, recv, peer):
    return pltpu.make_async_remote_copy(
        src_ref=src, dst_ref=dst, send_sem=send, recv_sem=recv, device_id=peer, device_id_type=MESH
    )


def span(place, order, stage):
    return math.prod(place.size[axis] for axis in order[:stage])


class Gather:
    def __init__(self, place, buf, send, recv, order=ZBA, relay=False):
        self.p, self.buf, self.send, self.recv, self.order = place, buf, send, recv, order
        self.relayed = relay and place.line

    def copies(self, stage, e):
        p, order = self.p, self.order
        src = self.buf.at[e, pl.ds(p.first[order, stage], span(p, order, stage))]
        base = sum(p.size[axis] - 1 for axis in order[:stage])
        return [
            remote(src, src, self.send.at[e, base + k], self.recv.at[e, base + k], peer)
            for k, peer in enumerate(p.near[order[stage]])
        ]

    def passed(self, e):
        p, order = self.p, self.order
        stage = order.index("z")
        base = sum(p.size[axis] - 1 for axis in order[:stage])
        fixed = {name: p.at[name] for name in order[stage:]}
        src = self.buf.at[e, pl.ds(p.slot_at(order, {**fixed, "z": p.far_end}), span(p, order, stage))]
        extra = sum(size - 1 for size in p.size.values())
        recv = self.recv.at[e, base + jnp.where(p.next_end == 0, 0, 2)]
        return remote(src, src, self.send.at[e, extra], recv, p.device({**p.at, "z": p.next_end}))

    def each(self, stage, e, act):
        for k, copy in enumerate(self.copies(stage, e)):
            if self.relayed and self.order[stage] == "z" and k != 1:
                pl.when(self.p.at["z"] != (3 if k == 0 else 0))(functools.partial(act, copy))
            else:
                act(copy)

    def start(self, stage, e):
        self.each(stage, e, lambda copy: copy.start())

    def relay(self, e):
        if self.relayed:

            @pl.when(~self.p.end)
            def _():
                self.copies(self.order.index("z"), e)[1].wait_recv()
                self.passed(e).start()

    def arrive(self, stage, e):
        for k, copy in enumerate(self.copies(stage, e)):
            if self.relayed and self.order[stage] == "z" and k == 1:
                pl.when(self.p.end)(copy.wait_recv)
            else:
                copy.wait_recv()

    def sent(self, e):
        for stage in range(3):
            self.each(stage, e, lambda copy: copy.wait_send())
        if self.relayed:
            pl.when(~self.p.end)(lambda: self.passed(e).wait_send())


class Scatter:
    def __init__(self, place, buf, boxes, send, recv, order=ZBA, relay=False):
        self.p, self.buf, self.boxes, self.send, self.recv, self.order = place, buf, boxes, send, recv, order
        self.relayed = relay and place.line

    def box(self, stage, e, block, many):
        box = self.boxes[min(stage, 1)]
        if stage >= 2:
            order = self.order
            block = block + (self.p.size[order[1]] - 1) * span(self.p, order, 1)
        if stage == 3:
            block = block + self.p.size[self.order[0]] - 1
        return box.at[e % box.shape[0], pl.ds(block, many)]

    def copies(self, stage, e):
        p, order = self.p, self.order
        axis, many = order[2 - stage], span(p, order, 2 - stage)
        sem = sum(p.size[order[2 - before]] - 1 for before in range(stage))
        made = []
        for k, peer in enumerate(p.near[axis]):
            src = self.buf.at[e, pl.ds(p.others[order, 2 - stage][k], many)]
            dst = self.box(stage, e, k * many, many)
            made.append(remote(src, dst, self.send.at[e, sem + k], self.recv.at[e, sem + k], peer))
        return made

    def passed(self, e):
        p, order = self.p, self.order
        at = order.index("z")
        many = span(p, order, at)
        fixed = {name: p.at[name] for name in order[at:]}
        src = self.buf.at[e, pl.ds(p.slot_at(order, {**fixed, "z": p.far_end}), many)]
        extra = sum(size - 1 for size in p.size.values())
        peer = p.device({**p.at, "z": p.inside})
        return remote(src, self.box(3, e, 0, many), self.send.at[e, extra], self.recv.at[e, extra], peer)

    def on_line(self, stage):
        return self.relayed and self.order[2 - stage] == "z"

    def start(self, stage, e):
        for k, copy in enumerate(self.copies(stage, e)):
            if self.on_line(stage):
                here = self.p.end if k == 1 else self.p.at["z"] != (3 if k == 0 else 0)
                pl.when(here)(copy.start)
            else:
                copy.start()
        if self.on_line(stage):
            pl.when(self.p.end)(lambda: self.passed(e).start())

    def relay(self, e):
        if self.relayed:
            stage = 2 - self.order.index("z")
            many = span(self.p, self.order, 2 - stage)

            @pl.when(~self.p.end)
            def _():
                self.passed(e).wait_recv()
                to = self.p.others[self.order, 2 - stage][1]
                for i in range(many):
                    total = self.buf[e, to + i].astype(f32) + self.box(3, e, i, 1)[0].astype(f32)
                    self.buf[e, to + i] = total.astype(bf16)
                self.copies(stage, e)[1].start()

    def arrive(self, stage, e):
        for k, copy in enumerate(self.copies(stage, e)):
            if self.on_line(stage) and k != 1:
                pl.when(self.p.at["z"] != (3 if k == 0 else 0))(copy.wait_send)
                pl.when(self.p.at["z"] != (0 if k == 0 else 3))(copy.wait_recv)
            else:
                copy.wait()
        if self.on_line(stage):
            pl.when(self.p.end)(lambda: self.passed(e).wait_send())

    def total(self, stage, e, i):
        p, order = self.p, self.order
        many = span(p, order, 2 - stage)
        total = self.buf[e, p.first[order, 2 - stage] + i].astype(f32)
        for k in range(p.size[order[2 - stage]] - 1):
            term = self.box(stage, e, k * many + i, 1)[0].astype(f32)
            if self.on_line(stage) and k != 1:
                term = jnp.where(p.at["z"] != (0 if k == 0 else 3), term, 0.0)
            total = total + term
        return total

    def add(self, stage, e):
        def one(i, carry):
            self.buf[e, self.p.first[self.order, 2 - stage] + i] = self.total(stage, e, i).astype(bf16)
            return carry

        lax.fori_loop(0, span(self.p, self.order, 2 - stage), one, 0)

    def last(self, e):
        return self.total(2, e, 0)


def block_rows(rows, parts):
    return (parts * rows + SUB - 1) // SUB * SUB


def blocks_to_weights(place, rows, buf, core, outs, order=ZBA):
    many = SUB // math.gcd(SUB, rows)
    for first in range(0, place.count, many):
        blocks = [buf[place.slot_of(first + i, core, order)].astype(f32) for i in range(many)]
        for part, out in enumerate(outs):
            pieces = [block[part * rows : (part + 1) * rows] for block in blocks]
            out[pl.ds(first * rows, many * rows), :] = jnp.concatenate(pieces, axis=0).astype(bf16)


def grads_to_blocks(place, rows, grads, buf, order=ZBA):
    block = buf.shape[1]
    for dp in range(place.count):
        pieces = [grad[dp * rows : (dp + 1) * rows, :] for grad in grads]
        if block > rows * len(grads):
            pieces.append(jnp.zeros((block - rows * len(grads), buf.shape[2]), f32))
        buf[place.slot_of(dp, place.mp, order)] = jnp.concatenate(pieces, axis=0).astype(bf16)


def all_sum(place, value, src, box, send, recv):
    layer = place.side * place.side
    spot = place.dp % layer
    z = place.at["z"]
    src[0] = value
    box[z] = value
    copies = [
        remote(src.at[0], box.at[z], send.at[k], recv.at[k], peer) for k, peer in enumerate(place.near["z"])
    ]
    for copy in copies:
        copy.start()
    for copy in copies:
        copy.wait()
    total = box[0]
    for i in range(1, place.depth):
        total = total + box[i]
    mine = spot * 2 + place.mp
    base = place.depth
    src[1] = total
    box[base + mine] = total
    at = place.depth - 1
    copies = [
        remote(src.at[1], box.at[base + mine], send.at[at + k], recv.at[at + k], peer)
        for k, peer in enumerate(place.peers_layer())
    ]
    for copy in copies:
        copy.start()
    for copy in copies:
        copy.wait()
    total = box[base]
    for i in range(1, 2 * layer):
        total = total + box[base + i]
    return total


def block_kernel(
    count, rows, experts, tile, lag,
    tok_ref, cot_ref, cond_ref, route_ref, ada_ref, gate_ref, attn_ref, w_ref,
    output_ref, grad_tok_ref, ada_out, attn_out, total_ref, norm_out,
    buf_one, buf_two, box_one, rest_one, box_two, rest_two,
    ada_one, ada_two, sc_buf, mod_buf, mod_far, attn_buf, attn_box, attn_rest, attn_far, attn_w,
    cond_low, mod_one, mod_two, grad_mod, grad_mod_in, triple, mixed, h_one, soft,
    h_all, d_all, gate_all, branch_acc, grad_h_acc, grad_gate_acc, gate_in, share_in,
    up_w, down_w, up_grad, down_grad, gate_grad, attn_share, attn_in, norm_src, norm_box,
    load_sem, gather_send, gather_recv, gather_send_two, gather_recv_two,
    scatter_send, scatter_recv, scatter_send_two, scatter_recv_two,
    ada_send, ada_recv, more_send, more_recv, sc_send, sc_recv, mod_send, mod_recv, attn_send, attn_recv, attn_back_send, attn_back_recv,
    core_send, core_recv, token_send, token_recv, norm_send, norm_recv,
):
    place = Place(count)
    met = place.greet()
    mp = place.mp
    wide_experts = w_ref.shape[1]
    own_tok, width = tok_ref.shape
    images = own_tok // PATCH
    half = attn_ref.shape[2]
    first = half // LANES * LANES
    heads = half // HD
    wide = ada_ref.shape[1] // 2
    cut = mod_buf.shape[3]
    scale = HD ** (-0.5)
    own_at = pl.multiple_of(mp * own_tok, own_tok)
    their_at = pl.multiple_of((1 - mp) * own_tok, own_tok)
    own, theirs = pl.ds(own_at, own_tok), pl.ds(their_at, own_tok)
    other = place.other_core()

    loads = [
        pltpu.make_async_copy(tok_ref, branch_acc.at[pl.ds(0, own_tok)], load_sem.at[0]),
        pltpu.make_async_copy(cot_ref, branch_acc.at[pl.ds(own_tok, own_tok)], load_sem.at[1]),
    ]
    for load in loads:
        load.start()

    def put(target, block, order=ZBA):
        if block.shape[0] != target.shape[1]:
            target[place.slot(order)] = jnp.zeros(target.shape[1:], bf16)
        target[place.slot(order), pl.ds(0, block.shape[0])] = block

    put(ada_one.at[0], ada_ref[:, pl.ds(pl.multiple_of(mp * width, LANES), width)].astype(bf16))
    cols = ada_ref[:, pl.ds(pl.multiple_of((1 + mp) * 2 * width, LANES), 2 * width)]
    put(ada_two.at[0], jnp.concatenate([cols[:, :width], cols[:, width:]], axis=0).astype(bf16))
    parts = attn_ref.shape[0]
    side_by = lax.broadcasted_iota(jnp.int32, (experts, LANES), 1) == lax.broadcasted_iota(
        jnp.int32, (experts, LANES), 0
    )
    gate = mxu(gate_ref[...].astype(bf16), side_by.astype(f32).astype(bf16), TN)[:, : 2 * LANES - half]
    spare = [gate] + [jnp.zeros_like(gate)] * (parts - 1)
    both = [jnp.concatenate([attn_ref[j], spare[j]], axis=1) for j in range(parts)]
    pair = parts // 2
    for i in range(2):
        put(attn_buf.at[i], jnp.concatenate(both[i * pair : (i + 1) * pair], axis=0).astype(bf16))
    cond = cond_ref[...]
    cond = cond / (1.0 + jnp.exp(-cond))
    cond_low[...] = cond.astype(bf16)
    sc_buf[0, place.slot()] = jnp.concatenate([cond, jnp.zeros((SUB - cond.shape[0], width), f32)], axis=0).astype(bf16)
    met()
    ada_gather = Gather(place, ada_one, ada_send, ada_recv)
    more_gather = Gather(place, ada_two, more_send, more_recv)
    attn_gather = Gather(place, attn_buf, attn_send, attn_recv)
    cuts = (pl.ds(0, buf_one.shape[3]), pl.ds(buf_one.shape[3], buf_two.shape[3]))
    streams = tuple(zip((buf_one, buf_two), cuts, (ZBA, BZA)))
    gathers = (
        Gather(place, buf_one, gather_send, gather_recv, ZBA, True),
        Gather(place, buf_two, gather_send_two, gather_recv_two, BZA, True),
    )
    scatters = (
        Scatter(place, buf_one, (box_one, rest_one), scatter_send, scatter_recv, ZBA, True),
        Scatter(place, buf_two, (box_two, rest_two), scatter_send_two, scatter_recv_two, BZA, True),
    )
    sc_gather = Gather(place, sc_buf, sc_send, sc_recv)
    ada_gather.start(0, 0)
    attn_gather.start(0, 0)
    attn_gather.start(0, 1)
    more_gather.start(0, 0)
    sc_gather.start(0, 0)

    def fill(e, carry):
        both = jnp.concatenate([w_ref[0, e], w_ref[1, e]], axis=0).astype(bf16)
        for buf, lanes, order in streams:
            put(buf.at[e], both[:, lanes.start : lanes.start + lanes.size], order)
        return carry

    lax.fori_loop(0, wide_experts, fill, 0)

    def begin(e):
        for one in gathers:
            one.start(0, e)

    def onward(stage, e):
        for one in gathers:
            one.arrive(stage, e)
            one.start(stage + 1, e)

    def tick(k):
        pl.when(k + 6 < wide_experts)(lambda: begin(k + 6))
        pl.when(k + 4 < wide_experts)(lambda: gathers[0].relay(k + 4))
        pl.when(k + 3 < wide_experts)(lambda: onward(0, k + 3))
        pl.when(k + 1 < wide_experts)(lambda: gathers[1].relay(k + 1))
        pl.when((k >= 0) & (k < wide_experts))(lambda: onward(1, k))

    grad_mod[...] = jnp.zeros_like(grad_mod)
    items = ((ada_gather, 0), (attn_gather, 0), (attn_gather, 1), (more_gather, 0))

    def wave(w):
        for i in (w, w - 1):
            if 0 <= i < len(items):
                small, which = items[i]
                small.arrive(w - i, which)
                small.start(w - i + 1, which)

    for w in range(len(items)):
        wave(w)
    begin(0)
    begin(1)
    width_lanes = pl.ds(0, width)
    ada_gather.arrive(2, 0)

    blocks_to_weights(place, rows, ada_one.at[0], mp, (up_w.at[:, width_lanes],))
    mod_one[mp] = mxu(cond_low[...], up_w[:, width_lanes])
    mod_cross = [
        remote(ref.at[mp], ref.at[mp], core_send.at[i], core_recv.at[i], other)
        for i, ref in ((1, mod_one), (0, mod_two))
    ]
    mod_cross[0].start()
    wave(len(items))
    attn_cross = []
    for i in range(2):
        attn_gather.arrive(2, i)
        attn_cross.append(
            remote(attn_buf.at[i], attn_far.at[i], core_send.at[8 + i], core_recv.at[8 + i], other)
        )
        attn_cross[i].start()
        outs = [attn_w.at[mp, j] for j in range(i * pair, (i + 1) * pair)]
        blocks_to_weights(place, rows, attn_buf.at[i], mp, outs)
    for load in loads:
        load.wait()
    ada_gather.sent(0)
    attn_gather.sent(0)
    attn_gather.sent(1)
    begin(2)
    begin(3)
    begin(4)
    gathers[0].relay(0)
    onward(0, 0)
    sc_gather.arrive(0, 0)
    sc_gather.start(1, 0)
    for i in range(2):
        attn_cross[i].wait()
        outs = [attn_w.at[1 - mp, j] for j in range(i * pair, (i + 1) * pair)]
        blocks_to_weights(place, rows, attn_far.at[i], 1 - mp, outs)
    mod_cross[0].wait()
    gathers[0].relay(1)
    onward(0, 1)
    gathers[0].relay(2)
    gate_lanes = pl.ds(first, LANES)
    half_lanes = pl.ds(0, half)

    def weight(core, j):
        return attn_w[core, j, :, half_lanes]

    lane_pair = lax.broadcasted_iota(jnp.int32, (PATCH, 2 * HD), 1)
    masks = [(lane_pair < HD).astype(f32).astype(bf16), (lane_pair >= HD).astype(f32).astype(bf16)]
    groups = [(at, min(2, heads - at)) for at in range(0, heads, 2)]
    expert_lane = lax.broadcasted_iota(jnp.int32, (PATCH, LANES), 1) - (half - first)

    def mod_row(image, vector):
        row = pl.ds(mp * images + image, 1)
        if vector < 2:
            return mod_one[vector, row, :]
        return mod_two[vector // 2 - 1, row, pl.ds(vector % 2 * width, width)]

    def add_grad_mod(image, vector, value):
        grad_mod[vector // 3, pl.ds(mp * images + image, 1), pl.ds(vector % 3 * width, width)] = value

    def one_head(value, group, head):
        return value if group[1] == 1 else value * masks[head]

    def route(h, image):
        valid = (expert_lane >= 0) & (expert_lane < experts)
        logits = jnp.where(valid, mxu(h, attn_w[0, 0, :, gate_lanes]), -jnp.inf)
        power = jnp.exp(logits - jnp.max(logits, axis=1, keepdims=True))
        router = power / jnp.sum(power, axis=1, keepdims=True)
        picks = route_ref[:, pl.ds(pl.multiple_of(own_at + image * PATCH, PATCH), PATCH)]
        spot = lax.broadcasted_iota(jnp.int32, (LANES, PATCH), 0) - (half - first)
        picked = jnp.where((picks[0:1, :] == spot) | (picks[1:2, :] == spot), 1.0, 0.0)
        return router, picked.T

    def attend(at):
        return mxu(mixed[0, at, :], weight(0, 3), NT) + mxu(mixed[1, at, :], weight(1, 3), NT)

    def token_copies(image):
        at = pl.ds(pl.multiple_of(own_at + image * PATCH, PATCH), PATCH)
        return [
            remote(ref.at[at], ref.at[at], token_send.at[image, i], token_recv.at[image, i], other)
            for i, ref in enumerate((h_all, d_all, gate_all))
        ]

    def attention(image, carry):
        at = pl.ds(pl.multiple_of(image * PATCH, PATCH), PATCH)
        normed, _ = layer_norm(branch_acc[at, :])
        h = (normed * (1.0 + mod_row(image, 1)) + mod_row(image, 0)).astype(bf16)
        h_one[at, :] = h
        for core in range(2):
            for j in range(3):
                triple[core, j, at, :] = mxu(h, weight(core, j)).astype(bf16)
            for group in groups:
                lanes = pl.ds(group[0] * HD, group[1] * HD)
                query, key, value = (triple[core, j, at, lanes] for j in range(3))
                total = 0.0
                for head in range(group[1]):
                    scores = mxu(one_head(query, group, head), key, NT) * scale
                    power = jnp.exp(scores - jnp.max(scores, axis=1, keepdims=True))
                    low = (power * (1.0 / jnp.sum(power, axis=1, keepdims=True))).astype(bf16)
                    soft[image, core * heads + group[0] + head] = low
                    total = total + mxu(low, one_head(value, group, head))
                mixed[core, at, lanes] = total.astype(bf16)
        tick(image - 1)

        @pl.when(image == 0)
        def _():
            sc_gather.arrive(1, 0)
            sc_gather.start(2, 0)

        return carry

    lax.fori_loop(0, images, attention, 0)
    more_gather.arrive(2, 0)
    blocks_to_weights(place, rows, ada_two.at[0], mp, (up_w.at[:, width_lanes], down_w.at[:, width_lanes]))
    mod_two[mp, :, pl.ds(0, width)] = mxu(cond_low[...], up_w[:, width_lanes])
    mod_two[mp, :, pl.ds(width, width)] = mxu(cond_low[...], down_w[:, width_lanes])
    mod_cross[1].start()
    more_gather.sent(0)
    mod_cross[1].wait()

    def forward(image, carry):
        at = pl.ds(pl.multiple_of(image * PATCH, PATCH), PATCH)
        cot_at = pl.ds(pl.multiple_of(own_tok + image * PATCH, PATCH), PATCH)
        all_at = pl.ds(pl.multiple_of(own_at + image * PATCH, PATCH), PATCH)
        x_one = branch_acc[at, :] + mod_row(image, 2) * attend(at)
        normed, _ = layer_norm(x_one)
        h = (normed * (1.0 + mod_row(image, 4)) + mod_row(image, 3)).astype(bf16)
        h_all[all_at, :] = h
        router, chosen = route(h, image)
        shared = (expert_lane >= experts) & (expert_lane < wide_experts)
        gate_all[all_at, :] = jnp.where(shared, 1.0, router * chosen)
        d_all[all_at, :] = (branch_acc[cot_at, :] * mod_row(image, 5)).astype(bf16)
        for copy in token_copies(image):
            copy.start()

        return carry

    lax.fori_loop(0, images, forward, 0)
    ahead = images - 1
    sc_gather.arrive(2, 0)
    sc_gather.sent(0)

    branch_acc[...] = jnp.zeros_like(branch_acc)
    grad_h_acc[...] = jnp.zeros_like(grad_h_acc)
    grad_gate_acc[...] = jnp.zeros_like(grad_gate_acc)

    def all_tokens(image, carry):
        for copy in token_copies(image):
            copy.wait()
        return carry

    lax.fori_loop(0, images, all_tokens, 0)

    shares = [
        remote(h_all.at[theirs], share_in.at[0], core_send.at[2], core_recv.at[2], other),
        remote(d_all.at[theirs], share_in.at[1], core_send.at[3], core_recv.at[3], other),
        remote(grad_gate_acc.at[theirs], gate_in, core_send.at[4], core_recv.at[4], other),
    ]
    loads = [
        pltpu.make_async_copy(tok_ref, branch_acc.at[theirs], load_sem.at[0]),
        pltpu.make_async_copy(cot_ref, grad_h_acc.at[theirs], load_sem.at[1]),
    ]
    tiles = h_all.shape[0] // tile

    def compute(e):
        for buf, lanes, order in streams:
            blocks_to_weights(place, rows, buf.at[e], mp, (up_w.at[:, lanes], down_w.at[:, lanes]), order)
        up_grad[...] = jnp.zeros_like(up_grad)
        down_grad[...] = jnp.zeros_like(down_grad)

        def one_tile(t, carry):
            @pl.when((e == wide_experts - 1) & (t == tiles // 2))
            def _():
                h_all[theirs, :] = branch_acc[theirs, :].astype(bf16)
                d_all[theirs, :] = grad_h_acc[theirs, :].astype(bf16)
                for copy in shares:
                    copy.start()
                for copy in loads:
                    copy.start()

            at = pl.ds(pl.multiple_of((t + (1 - mp) * (tiles // 2)) % tiles * tile, tile), tile)
            h = h_all[at, :]
            d = d_all[at, :]
            lane = lax.broadcasted_iota(jnp.int32, (tile, LANES), 1) - (half - first)
            gate = jnp.sum(jnp.where(lane == e, gate_all[at, :], 0.0), axis=1, keepdims=True)
            pre = mxu(h, up_w[...])
            back = mxu(d, down_w[...])
            act, slope = gelu_both(pre)
            inner = jnp.sum(act * back, axis=1, keepdims=True)
            grad_gate_acc[at, :] += jnp.where(lane == e, inner, 0.0)
            act_low = (gate * act).astype(bf16)
            pre_low = (gate * back * slope).astype(bf16)
            branch_acc[at, :] += mxu(act_low, down_w[...], NT)
            grad_h_acc[at, :] += mxu(pre_low, up_w[...], NT)
            up_grad[...] += mxu(h, pre_low, TN)
            down_grad[...] += mxu(d, act_low, TN)
            return carry

        lax.fori_loop(0, tiles, one_tile, 0)

    def follow(one, stage, e):
        one.arrive(stage, e)
        one.add(stage, e)
        one.start(stage + 1, e)

    def finish(e):
        for one, (_, lanes, _) in zip(scatters, streams):
            one.arrive(2, e)
            total_ref[e, :, lanes] = one.last(e)

    def collect(k):
        def at(late, act):
            pl.when((k >= late) & (k - late < wide_experts))(lambda: act(k - late))

        at(4, finish)
        at(3, scatters[0].relay)
        at(3, lambda e: follow(scatters[1], 1, e))
        at(2, lambda e: follow(scatters[0], 1, e))
        at(2, scatters[1].relay)
        at(1, lambda e: [follow(one, 0, e) for one in scatters] and None)

    def step(e, carry):
        tick(e + ahead)
        for one in gathers:
            one.arrive(2, e)
        compute(e)
        for one in gathers:
            one.sent(e)
        for buf, lanes, order in streams:
            grads_to_blocks(place, rows, (up_grad.at[:, lanes], down_grad.at[:, lanes]), buf.at[e], order)
        for one in scatters:
            one.start(0, e)
        collect(e - lag)
        return carry

    lax.fori_loop(0, wide_experts, step, 0)

    gate_grad[...] = jnp.zeros_like(gate_grad)
    for copy in shares + loads:
        copy.wait()

    def backward(image, carry):
        at = pl.ds(pl.multiple_of(image * PATCH, PATCH), PATCH)
        own_rows = pl.ds(pl.multiple_of(own_at + image * PATCH, PATCH), PATCH)
        load_rows = pl.ds(pl.multiple_of(their_at + image * PATCH, PATCH), PATCH)
        tok, cot = branch_acc[load_rows, :], grad_h_acc[load_rows, :]
        branch = branch_acc[own_rows, :] + share_in[0, at, :].astype(f32)
        attention = attend(at)
        x_one = tok + mod_row(image, 2) * attention
        normed, inverse = layer_norm(x_one)
        branch_acc[own_rows, :] = x_one + mod_row(image, 5) * branch
        add_grad_mod(image, 5, jnp.sum(cot * branch, axis=0, keepdims=True))
        h = h_all[own_rows, :]
        router, chosen = route(h, image)
        grad_router = (grad_gate_acc[own_rows, :] + gate_in[at, :]) * chosen
        grad_logits = (router * (grad_router - jnp.sum(router * grad_router, axis=1, keepdims=True))).astype(bf16)
        gate_grad[...] += mxu(h, grad_logits, TN)
        grad_h = grad_h_acc[own_rows, :] + share_in[1, at, :].astype(f32) + mxu(grad_logits, attn_w[0, 0, :, gate_lanes], NT)
        add_grad_mod(image, 3, jnp.sum(grad_h, axis=0, keepdims=True))
        add_grad_mod(image, 4, jnp.sum(grad_h * normed, axis=0, keepdims=True))
        grad_x = cot + norm_back(grad_h * (1.0 + mod_row(image, 4)), normed, inverse)
        add_grad_mod(image, 2, jnp.sum(grad_x * attention, axis=0, keepdims=True))
        grad_att = (grad_x * mod_row(image, 2)).astype(bf16)
        d_all[own_rows, :] = grad_att
        grad_h_one = 0.0
        for core in range(2):
            grad_mixed = mxu(grad_att, weight(core, 3)).astype(bf16)
            for group in groups:
                lanes = pl.ds(group[0] * HD, group[1] * HD)
                query, key, value = (triple[core, j, at, lanes] for j in range(3))
                back = grad_mixed[:, group[0] * HD : (group[0] + group[1]) * HD]
                grads = [0.0, 0.0, 0.0]
                for head in range(group[1]):
                    low = soft[image, core * heads + group[0] + head]
                    prob = low.astype(f32)
                    head_back = one_head(back, group, head)
                    grad_soft = mxu(head_back, value, NT)
                    delta = jnp.sum(prob * grad_soft, axis=1, keepdims=True)
                    grad_scores = (prob * (grad_soft - delta) * scale).astype(bf16)
                    grads[0] = grads[0] + mxu(grad_scores, one_head(key, group, head))
                    grads[1] = grads[1] + mxu(grad_scores, one_head(query, group, head), TN)
                    grads[2] = grads[2] + mxu(low, head_back, TN)
                for j in range(3):
                    triple[core, j, at, lanes] = grads[j].astype(bf16)
            for j in range(3):
                grad_h_one = grad_h_one + mxu(triple[core, j, at, :], weight(core, j), NT)
        normed, inverse = layer_norm(tok)
        add_grad_mod(image, 0, jnp.sum(grad_h_one, axis=0, keepdims=True))
        add_grad_mod(image, 1, jnp.sum(grad_h_one * normed, axis=0, keepdims=True))
        grad_h_acc[own_rows, :] = grad_x + norm_back(grad_h_one * (1.0 + mod_row(image, 1)), normed, inverse)

        @pl.when(image > 0)
        def _():
            collect(wide_experts - lag + image - 1)

        return carry

    lax.fori_loop(0, images, backward, 0)
    stores = [
        pltpu.make_async_copy(branch_acc.at[own], output_ref, load_sem.at[2]),
        pltpu.make_async_copy(grad_h_acc.at[own], grad_tok_ref, load_sem.at[3]),
    ]
    for copy in stores:
        copy.start()

    crosses = [
        remote(grad_mod.at[1 - mp], grad_mod_in, core_send.at[5], core_recv.at[5], other),
        *[
            remote(
                attn_share.at[pl.ds(i * pair, pair)], attn_in.at[pl.ds(i * pair, pair)],
                core_send.at[6 + i], core_recv.at[6 + i], other,
            )
            for i in range(2)
        ],
        remote(mod_buf.at[0], mod_far, core_send.at[1], core_recv.at[1], other),
    ]
    crosses[0].start()

    def attn_grad(core, j):
        if j == parts - 1:
            return mxu(d_all[own, :], mixed[core], TN)
        return mxu(h_one[...], triple[core, j], TN)

    spare = pl.ds(half, 2 * LANES - half)
    places = [(up_grad, 0), (up_grad, 1), (up_grad, 2), (down_grad, 0)]
    attn_scatter = Scatter(place, attn_buf, (attn_box, attn_rest), attn_back_send, attn_back_recv)
    for i in range(2):
        for j in range(i * pair, (i + 1) * pair):
            attn_share[j, :, half_lanes] = attn_grad(1 - mp, j).astype(bf16)
            extra = gate_grad[:, pl.ds(half - first, 2 * LANES - half)].astype(bf16)
            attn_share[j, :, spare] = extra if j == 0 else jnp.zeros_like(extra)
        crosses[1 + i].start()
    crosses[0].wait()
    grad_low = grad_mod[mp] + grad_mod_in[...]
    mod_buf[0, place.slot()] = jnp.concatenate([grad_low[:, :cut], grad_low[:, cut:]], axis=0).astype(bf16)
    mod_gather = Gather(place, mod_buf, mod_send, mod_recv)
    for i in range(2):
        for j in range(i * pair, (i + 1) * pair):
            ref, at = places[j]
            ref[:, pl.ds(at * 2 * LANES, half)] = attn_grad(mp, j)
        crosses[1 + i].wait()
        grads = []
        for j in range(i * pair, (i + 1) * pair):
            ref, at = places[j]
            lanes = pl.ds(at * 2 * LANES, half)
            ref[:, lanes] += attn_in[j, :, half_lanes].astype(f32)
            extra = gate_grad[:, pl.ds(half - first, 2 * LANES - half)] + attn_in[0, :, spare].astype(f32)
            ref[:, pl.ds(at * 2 * LANES + half, 2 * LANES - half)] = extra if j == 0 else jnp.zeros_like(extra)
            grads.append(ref[:, pl.ds(at * 2 * LANES, 2 * LANES)])
        grads_to_blocks(place, rows, grads, attn_buf.at[i])
        attn_scatter.start(0, i)
    mod_gather.start(0, 0)
    left = list(range(wide_experts - lag + images - 1, wide_experts + 4))
    for stage in range(2):
        if len(left) > 1:
            collect(left.pop(0))
        for i in range(2):
            attn_scatter.arrive(stage, i)
            attn_scatter.add(stage, i)
            attn_scatter.start(stage + 1, i)
        mod_gather.arrive(stage, 0)
        mod_gather.start(stage + 1, 0)
    for k in left:
        collect(k)
    square = jnp.zeros((1, 1), f32)
    for e in range(wide_experts):
        square = square + jnp.sum(total_ref[e] * total_ref[e])
    mod_gather.arrive(2, 0)
    crosses[3].start()
    row = lax.broadcasted_iota(jnp.int32, (width, LANES), 0)
    lane = lax.broadcasted_iota(jnp.int32, (width, LANES), 1)
    pick = ((row == place.dp * rows + lane) & (lane < rows)).astype(f32).astype(bf16)
    group = cond_ref.shape[0]

    def in_order(ref, core, at):
        pieces = [ref[place.slot_of(dp, core)].astype(f32)[at : at + group] for dp in range(count)]
        return jnp.concatenate(pieces, axis=0).astype(bf16)

    conds = mxu(in_order(sc_buf.at[0], mp, 0), pick).astype(bf16)

    def ada_grad(ref, core):
        low = mxu(conds, in_order(ref, core, 0), TN)[:rows]
        high = mxu(conds, in_order(ref, core, group), TN)[:rows, : wide - cut]
        start = pl.multiple_of(core * wide, LANES)
        ada_out[:, pl.ds(start, cut)] = low
        ada_out[:, pl.ds(pl.multiple_of(start + cut, LANES), wide - cut)] = high
        return jnp.sum(low * low) + jnp.sum(high * high)

    small = ada_grad(mod_buf.at[0], mp)
    mod_gather.sent(0)
    crosses[3].wait()
    small = small + ada_grad(mod_far, 1 - mp)
    square = square + 0.5 * small
    for i in range(2):
        attn_scatter.arrive(2, i)
        attn = attn_scatter.last(i)
        attn_out[i] = attn
        lane = lax.broadcasted_iota(jnp.int32, attn.shape, 1)
        square = square + jnp.sum(jnp.where(lane < half, 1.0, 0.5) * attn * attn)
    value = jnp.broadcast_to(square, norm_out.shape)
    norm_out[...] = all_sum(place, value, norm_src, norm_box, norm_send, norm_recv)
    for copy in stores:
        copy.wait()


def block_call(tokens, condition, cotangent, routes, w_ada, w_gate, w_attn, w_expert):
    count = lax.axis_size("dp")
    own_tok, width = tokens.shape
    rows, wide = w_ada.shape
    experts = w_gate.shape[0]
    parts, _, half = w_attn.shape
    _, wide_experts, _, hidden = w_expert.shape
    depth, side = dp_sizes(count)
    images = own_tok // PATCH
    cut = (wide // 4 + LANES - 1) // LANES * LANES
    spare = 2 * LANES
    block, ada_block, attn_block = block_rows(rows, 2), block_rows(rows, 2), block_rows(rows, parts // 2)
    tok = 2 * own_tok
    tile, lag = (TILE, 2) if count <= 16 else (TILE // 2, 0)
    vmem = pl.BlockSpec(memory_space=pltpu.VMEM)
    hbm = pl.BlockSpec(memory_space=pl.ANY)
    hops = depth + 2 * side - 3

    def sems(*shape):
        return pltpu.SemaphoreType.DMA(shape)

    def boxes(slots, order, height, lanes):
        size = {"z": depth, "a": side, "b": side}
        span = size[order[0]] * size[order[1]]
        first = (size[order[2]] - 1) * span
        extra = 0 if slots <= 2 else math.prod(size[axis] for axis in order[: order.index("z")])
        return [
            pltpu.VMEM((slots, first, height, lanes), bf16),
            pltpu.VMEM((min(slots, REST), span - 1 + extra, height, lanes), bf16),
        ]

    one = hidden * CUT_ONE // CUT_ALL // LANES * LANES
    two = hidden - one

    return pl.pallas_call(
        functools.partial(block_kernel, count, rows, experts, tile, lag),
        out_shape=(
            jax.ShapeDtypeStruct((own_tok, width), f32),
            jax.ShapeDtypeStruct((own_tok, width), f32),
            jax.ShapeDtypeStruct((rows, wide), f32),
            jax.ShapeDtypeStruct((2, attn_block, spare), f32),
            jax.ShapeDtypeStruct((wide_experts, block, hidden), f32),
            jax.ShapeDtypeStruct((8, LANES), f32),
        ),
        in_specs=[hbm, hbm] + [vmem] * 6,
        out_specs=(hbm, hbm) + (vmem,) * 4,
        scratch_shapes=[
            pltpu.VMEM((wide_experts, count, block, one), bf16),
            pltpu.VMEM((wide_experts, count, block, two), bf16),
            *boxes(SLOTS + 2 * lag, ZBA, block, one),
            *boxes(SLOTS + 2 * lag, BZA, block, two),
            pltpu.VMEM((1, count, block_rows(rows, 1), width), bf16),
            pltpu.VMEM((1, count, ada_block, width), bf16),
            pltpu.VMEM((1, count, SUB, width), bf16),
            pltpu.VMEM((1, count, SUB, cut), bf16),
            pltpu.VMEM((count, SUB, cut), bf16),
            pltpu.VMEM((2, count, attn_block, spare), bf16),
            *boxes(2, ZBA, attn_block, spare),
            pltpu.VMEM((2, count, attn_block, spare), bf16),
            pltpu.VMEM((2, parts, width, spare), bf16),
            pltpu.VMEM(condition.shape, bf16),
            pltpu.VMEM((2, condition.shape[0], width), f32),
            pltpu.VMEM((2, condition.shape[0], 2 * width), f32),
            pltpu.VMEM((2, condition.shape[0], 2 * cut), f32),
            pltpu.VMEM((condition.shape[0], 2 * cut), f32),
            pltpu.VMEM((2, 3, own_tok, half), bf16),
            pltpu.VMEM((2, own_tok, half), bf16),
            pltpu.VMEM((own_tok, width), bf16),
            pltpu.VMEM((images, width // HD, PATCH, PATCH), bf16),
            pltpu.VMEM((tok, width), bf16),
            pltpu.VMEM((tok, width), bf16),
            pltpu.VMEM((tok, LANES), f32),
            pltpu.VMEM((tok, width), f32),
            pltpu.VMEM((tok, width), f32),
            pltpu.VMEM((tok, LANES), f32),
            pltpu.VMEM((own_tok, LANES), f32),
            pltpu.VMEM((2, own_tok, width), bf16),
            pltpu.VMEM((width, hidden), bf16),
            pltpu.VMEM((width, hidden), bf16),
            pltpu.VMEM((width, hidden), f32),
            pltpu.VMEM((width, hidden), f32),
            pltpu.VMEM((width, LANES), f32),
            pltpu.VMEM((parts, width, spare), bf16),
            pltpu.VMEM((parts, width, spare), bf16),
            pltpu.VMEM((2, 8, LANES), f32),
            pltpu.VMEM((depth + 2 * side * side, 8, LANES), f32),
            sems(4),
            *[sems(wide_experts, hops + 1)] * 8,
            *[sems(1, hops)] * 8,
            *[sems(2, hops)] * 4,
            sems(10),
            sems(10),
            sems(images, 3),
            sems(images, 3),
            sems(depth + 2 * side * side),
            sems(depth + 2 * side * side),
        ],
        compiler_params=pltpu.CompilerParams(collective_id=1, has_side_effects=True, vmem_limit_bytes=VMEM_BYTES),
        cost_estimate=pl.CostEstimate(
            flops=12 * tok * width * hidden * wide_experts, bytes_accessed=16 * w_expert.size, transcendentals=0
        ),
        name="block",
    )(tokens, cotangent, condition, routes, w_ada, w_gate, w_attn, w_expert)
def update_kernel(rows, half, output_ref, grad_tok_ref, expert_w, expert_m, expert_v, expert_ref, norm_ref, attn_ref, ada_ref, *refs):
    ada, gate, attn = (refs[3 * i : 3 * i + 3] for i in range(3))
    outs, (hold, held, grads, sem, token_sem) = refs[9:-5], refs[-5:]
    ada_new, gate_new, attn_new, expert_new = (outs[3 * i : 3 * i + 3] for i in range(4))
    expert = (expert_w, expert_m, expert_v)
    many = expert_w.shape[1] // 2
    chunks = [(part, h) for h in range(2) for part in range(2)]
    grad_loads = [
        pltpu.make_async_copy(expert_ref.at[pl.ds(h * many, many)], grads.at[pl.ds(h * many, many)], token_sem.at[4 + h])
        for h in range(2)
    ]

    def moves(c, refs, back):
        part, h = chunks[c]
        made = []
        for i, ref in enumerate(refs):
            far, near = ref.at[part, pl.ds(h * many, many)], held.at[i, part, pl.ds(h * many, many)]
            made.append(pltpu.make_async_copy(*((near, far) if back else (far, near)), sem.at[int(back), c, i]))
        return made

    for c in range(4):
        if chunks[c][0] == 0:
            grad_loads[chunks[c][1]].start()
        for copy in moves(c, expert, False):
            copy.start()
    token_loads = [pltpu.make_async_copy(ref, hold.at[i], token_sem.at[i]) for i, ref in enumerate((output_ref, grad_tok_ref))]
    token_stores = [pltpu.make_async_copy(hold.at[i], outs[13 + i], token_sem.at[2 + i]) for i in range(2)]
    for copy in token_loads:
        copy.start()
    total = jnp.sqrt(norm_ref[...])
    outs[12][0, 0] = jnp.max(total)
    factor = jnp.minimum(1.0, CLIP_NORM / (total[0:1, 0:1] + 1e-06))

    def write(ins, news, at, grad):
        for new, value in zip(news, adam(ins[0][at], ins[1][at], ins[2][at], grad * factor)):
            new[at] = value

    everything = (slice(None), slice(None))
    write(ada, ada_new, everything, ada_ref[...])
    first = half // LANES * LANES
    small = attn_ref[0, pl.ds(0, rows), pl.ds(first, LANES)]
    square = jnp.concatenate([small, jnp.zeros((LANES - rows, LANES), f32)], axis=0).T
    experts = gate[0].shape[0]
    write(gate, gate_new, everything, square[half - first : half - first + experts, :rows])
    parts = attn[0].shape[0]
    for j in range(parts):
        grad = attn_ref[j // (parts // 2), pl.ds(j % (parts // 2) * rows, rows), pl.ds(0, half)]
        write(attn, attn_new, (j,), grad)
    here = [held.at[i] for i in range(3)]
    for c, (part, h) in enumerate(chunks):
        if part == 0:
            grad_loads[h].wait()
        for copy in moves(c, expert, False):
            copy.wait()

        def one(e, carry):
            write(here, here, (part, e), grads[e, pl.ds(part * rows, rows), :])
            return carry

        lax.fori_loop(h * many, (h + 1) * many, one, 0)
        for copy in moves(c, expert_new, True):
            copy.start()
    for load, store in zip(token_loads, token_stores):
        load.wait()
        store.start()
    for c in range(4):
        for copy in moves(c, expert_new, True):
            copy.wait()
    for copy in token_stores:
        copy.wait()


def update_call(rows, half, output, grad_tokens, norm, expert, attn, ada, weights):
    vmem = pl.BlockSpec(memory_space=pltpu.VMEM)
    hbm = pl.BlockSpec(memory_space=pl.ANY)
    shapes = [jax.ShapeDtypeStruct(w.shape, f32) for w in weights]
    return pl.pallas_call(
        functools.partial(update_kernel, rows, half),
        out_shape=shapes
        + [jax.ShapeDtypeStruct((1, 1), f32)]
        + [jax.ShapeDtypeStruct(output.shape, f32), jax.ShapeDtypeStruct(grad_tokens.shape, f32)],
        in_specs=[hbm] * 6 + [vmem] * (3 + 9),
        out_specs=[vmem] * 9 + [hbm] * 3 + [pl.BlockSpec(memory_space=pltpu.SMEM), hbm, hbm],
        scratch_shapes=[
            pltpu.VMEM((2, *output.shape), f32),
            pltpu.VMEM((3, *weights[9].shape), f32),
            pltpu.VMEM(expert.shape, f32),
            pltpu.SemaphoreType.DMA((2, 4, 3)),
            pltpu.SemaphoreType.DMA((6,)),
        ],
        compiler_params=pltpu.CompilerParams(vmem_limit_bytes=VMEM_BYTES),
        name="update",
    )(output, grad_tokens, *weights[9:], expert, norm, attn, ada, *weights[:9])


def per_device(
    tokens,
    condition,
    cotangent,
    routes,
    w_ada,
    ada_first,
    ada_second,
    w_gate,
    gate_first,
    gate_second,
    w_attn,
    attn_first,
    attn_second,
    w_expert,
    expert_first,
    expert_second,
):
    output, grad_tokens, ada_total, attn_total, expert_total, square_sum = block_call(
        tokens, condition, cotangent, routes.T, w_ada, w_gate.T, w_attn, w_expert
    )
    updated = update_call(
        w_ada.shape[0], w_attn.shape[2], output, grad_tokens, square_sum, expert_total, attn_total, ada_total,
        (
            w_ada, ada_first, ada_second,
            w_gate.T, gate_first.T, gate_second.T,
            w_attn, attn_first, attn_second,
            w_expert, expert_first, expert_second,
        ),
    )
    gates = [gate.T for gate in updated[3:6]]
    return (*updated[13:], updated[12].reshape(()), *updated[:3], *gates, *updated[6:12])


def solution(mesh):
    placed = (
        P(("dp", "mp"), None),
        P("dp", None),
        P(("dp", "mp"), None),
        P("dp", None),
        P("dp", None),
        P("dp", None),
        P("dp", None),
        P("dp", None),
        P("dp", None),
        P("dp", None),
        P(None, "dp", "mp"),
        P(None, "dp", "mp"),
        P(None, "dp", "mp"),
        P(None, None, "dp", "mp"),
        P(None, None, "dp", "mp"),
        P(None, None, "dp", "mp"),
    )
    return jax.shard_map(
        per_device,
        mesh=mesh,
        in_specs=placed,
        out_specs=(
            P(("dp", "mp"), None),
            P(("dp", "mp"), None),
            P(),
            P("dp", None),
            P("dp", None),
            P("dp", None),
            P("dp", None),
            P("dp", None),
            P("dp", None),
            P(None, "dp", "mp"),
            P(None, "dp", "mp"),
            P(None, "dp", "mp"),
            P(None, None, "dp", "mp"),
            P(None, None, "dp", "mp"),
            P(None, None, "dp", "mp"),
        ),
        check_vma=False,
    )
```

```python
import functools
import math

import jax
import jax.numpy as jnp
from jax import lax
from jax.experimental import pallas as pl
from jax.experimental.pallas import tpu as pltpu
from jax.sharding import PartitionSpec as P

HD = 64
PATCH = 256
STEP = 10
LANES = 128
SUB = 16
TILE = 512
SLOTS, REST = 4, 4
ZBA, BZA = "zba", "bza"
CUT_ONE, CUT_ALL = 2, 3

EPS_NORM = 1e-06
CLIP_NORM = 0.1
RATE = 0.08
BETA_ONE = 0.9
BETA_TWO = 0.95
ADAM_EPS = 1e-08
DECAY = 0.01
GELU_LIN = 0.7978845608
GELU_CUBE = 0.7978845608 * 0.044715

MESH = pl.DeviceIdType.MESH
VMEM_BYTES = 127 * 512 * 1024
bf16 = jnp.bfloat16
f32 = jnp.float32
NN = (((1,), (0,)), ((), ()))
NT = (((1,), (1,)), ((), ()))
TN = (((0,), (0,)), ((), ()))


def mxu(left, right, dims=NN):
    return lax.dot_general(left, right, dims, preferred_element_type=f32)


def layer_norm(value):
    center = value - jnp.mean(value, axis=-1, keepdims=True)
    inverse = lax.rsqrt(jnp.mean(center * center, axis=-1, keepdims=True) + EPS_NORM)
    return (center * inverse, inverse)


def norm_back(grad, normed, inverse):
    mean_grad = jnp.mean(grad, axis=-1, keepdims=True)
    mean_proj = jnp.mean(grad * normed, axis=-1, keepdims=True)
    return inverse * (grad - mean_grad - normed * mean_proj)


def adam(master, first, second, grad):
    first_new = BETA_ONE * first + (1.0 - BETA_ONE) * grad
    second_new = BETA_TWO * second + (1.0 - BETA_TWO) * grad * grad
    fix_one = 1.0 - BETA_ONE**STEP
    fix_two = 1.0 - BETA_TWO**STEP
    update = first_new * (1.0 / fix_one) / (jnp.sqrt(second_new * (1.0 / fix_two)) + ADAM_EPS) + DECAY * master
    return (master - RATE * update, first_new, second_new)


def gelu_both(value):
    square = value * value
    tanh = jnp.tanh(value * (GELU_CUBE * square + GELU_LIN))
    half = 0.5 * tanh + 0.5
    act = value * half
    slope = half + act * (1.0 - tanh) * (3.0 * GELU_CUBE * square + GELU_LIN)
    return act, slope


def dp_sizes(count):
    side = 4 if count >= 64 else 2
    return count // (side * side), side


class Place:
    def __init__(self, count):
        self.count = count
        self.depth, self.side = dp_sizes(count)
        self.dp = lax.axis_index("dp")
        self.mp = lax.axis_index("mp")
        side = self.side
        y = (self.dp // side) % side
        x = self.dp % side
        self.at = {
            "z": self.dp // (side * side),
            "a": jnp.where(self.mp == 0, y, x),
            "b": jnp.where(self.mp == 0, x, y),
        }
        self.size = {"z": self.depth, "a": side, "b": side}
        self.near = {axis: self.peers(axis) for axis in "zab"}
        self.first, self.others = {}, {}
        for order in (ZBA, BZA):
            for stage, axis in enumerate(order):
                fixed = {name: self.at[name] for name in order[stage:]}
                self.first[order, stage] = self.slot_at(order, fixed)
                self.others[order, stage] = [
                    self.slot_at(order, {**fixed, axis: self.along(axis, k)}) for k in range(1, self.size[axis])
                ]
        z = self.at["z"]
        self.line = self.depth == 4
        self.end = (z == 0) | (z == 3)
        self.next_end = jnp.where(z < 2, 0, 3)
        self.inside = jnp.where(z < 2, 1, 2)
        self.far_end = 3 - self.next_end

    def slot_at(self, order, at):
        slot = 0
        for axis in reversed(order):
            slot = slot * self.size[axis] + at.get(axis, 0)
        return slot

    def slot(self, order=ZBA):
        return self.first[order, 0]

    def slot_of(self, dp, core, order=ZBA):
        side = self.side
        z, y, x = dp // (side * side), (dp // side) % side, dp % side
        one = self.slot_at(order, {"z": z, "a": y, "b": x})
        two = self.slot_at(order, {"z": z, "a": x, "b": y})
        return jnp.where(core == 0, one, two)

    def device(self, at):
        z, a, b = at["z"], at["a"], at["b"]
        side = self.side
        dp = jnp.where(self.mp == 0, (z * side + a) * side + b, (z * side + b) * side + a)
        return (dp, self.mp)

    def along(self, axis, step):
        return (self.at[axis] + step) % self.size[axis]

    def peers(self, axis):
        return [self.device({**self.at, axis: self.along(axis, k)}) for k in range(1, self.size[axis])]

    def other_core(self):
        return (self.dp, 1 - self.mp)

    def peers_layer(self):
        layer = self.side * self.side
        first = self.dp - self.dp % layer
        peers = []
        for k in range(1, 2 * layer):
            spot = (self.dp % layer * 2 + self.mp + k) % (2 * layer)
            peers.append((first + spot // 2, spot % 2))
        return peers

    def greet(self):
        peers = self.near["z"] + self.peers_layer()
        barrier = pltpu.get_barrier_semaphore()
        for peer in peers:
            pl.semaphore_signal(barrier, inc=1, device_id=peer, device_id_type=MESH)
        return lambda: pl.semaphore_wait(barrier, len(peers))


def remote(src, dst, send, recv, peer):
    return pltpu.make_async_remote_copy(
        src_ref=src, dst_ref=dst, send_sem=send, recv_sem=recv, device_id=peer, device_id_type=MESH
    )


def span(place, order, stage):
    return math.prod(place.size[axis] for axis in order[:stage])


class Gather:
    def __init__(self, place, buf, send, recv, order=ZBA, relay=False):
        self.p, self.buf, self.send, self.recv, self.order = place, buf, send, recv, order
        self.relayed = relay and place.line

    def copies(self, stage, e):
        p, order = self.p, self.order
        src = self.buf.at[e, pl.ds(p.first[order, stage], span(p, order, stage))]
        base = sum(p.size[axis] - 1 for axis in order[:stage])
        return [
            remote(src, src, self.send.at[e, base + k], self.recv.at[e, base + k], peer)
            for k, peer in enumerate(p.near[order[stage]])
        ]

    def passed(self, e):
        p, order = self.p, self.order
        stage = order.index("z")
        base = sum(p.size[axis] - 1 for axis in order[:stage])
        fixed = {name: p.at[name] for name in order[stage:]}
        src = self.buf.at[e, pl.ds(p.slot_at(order, {**fixed, "z": p.far_end}), span(p, order, stage))]
        extra = sum(size - 1 for size in p.size.values())
        recv = self.recv.at[e, base + jnp.where(p.next_end == 0, 0, 2)]
        return remote(src, src, self.send.at[e, extra], recv, p.device({**p.at, "z": p.next_end}))

    def each(self, stage, e, act):
        for k, copy in enumerate(self.copies(stage, e)):
            if self.relayed and self.order[stage] == "z" and k != 1:
                pl.when(self.p.at["z"] != (3 if k == 0 else 0))(functools.partial(act, copy))
            else:
                act(copy)

    def start(self, stage, e):
        self.each(stage, e, lambda copy: copy.start())

    def relay(self, e):
        if self.relayed:

            @pl.when(~self.p.end)
            def _():
                self.copies(self.order.index("z"), e)[1].wait_recv()
                self.passed(e).start()

    def arrive(self, stage, e):
        for k, copy in enumerate(self.copies(stage, e)):
            if self.relayed and self.order[stage] == "z" and k == 1:
                pl.when(self.p.end)(copy.wait_recv)
            else:
                copy.wait_recv()

    def sent(self, e):
        for stage in range(3):
            self.each(stage, e, lambda copy: copy.wait_send())
        if self.relayed:
            pl.when(~self.p.end)(lambda: self.passed(e).wait_send())


class Scatter:
    def __init__(self, place, buf, boxes, send, recv, order=ZBA, relay=False):
        self.p, self.buf, self.boxes, self.send, self.recv, self.order = place, buf, boxes, send, recv, order
        self.relayed = relay and place.line

    def box(self, stage, e, block, many):
        box = self.boxes[min(stage, 1)]
        if stage >= 2:
            order = self.order
            block = block + (self.p.size[order[1]] - 1) * span(self.p, order, 1)
        if stage == 3:
            block = block + self.p.size[self.order[0]] - 1
        return box.at[e % box.shape[0], pl.ds(block, many)]

    def copies(self, stage, e):
        p, order = self.p, self.order
        axis, many = order[2 - stage], span(p, order, 2 - stage)
        sem = sum(p.size[order[2 - before]] - 1 for before in range(stage))
        made = []
        for k, peer in enumerate(p.near[axis]):
            src = self.buf.at[e, pl.ds(p.others[order, 2 - stage][k], many)]
            dst = self.box(stage, e, k * many, many)
            made.append(remote(src, dst, self.send.at[e, sem + k], self.recv.at[e, sem + k], peer))
        return made

    def passed(self, e):
        p, order = self.p, self.order
        at = order.index("z")
        many = span(p, order, at)
        fixed = {name: p.at[name] for name in order[at:]}
        src = self.buf.at[e, pl.ds(p.slot_at(order, {**fixed, "z": p.far_end}), many)]
        extra = sum(size - 1 for size in p.size.values())
        peer = p.device({**p.at, "z": p.inside})
        return remote(src, self.box(3, e, 0, many), self.send.at[e, extra], self.recv.at[e, extra], peer)

    def on_line(self, stage):
        return self.relayed and self.order[2 - stage] == "z"

    def start(self, stage, e):
        for k, copy in enumerate(self.copies(stage, e)):
            if self.on_line(stage):
                here = self.p.end if k == 1 else self.p.at["z"] != (3 if k == 0 else 0)
                pl.when(here)(copy.start)
            else:
                copy.start()
        if self.on_line(stage):
            pl.when(self.p.end)(lambda: self.passed(e).start())

    def relay(self, e):
        if self.relayed:
            stage = 2 - self.order.index("z")
            many = span(self.p, self.order, 2 - stage)

            @pl.when(~self.p.end)
            def _():
                self.passed(e).wait_recv()
                to = self.p.others[self.order, 2 - stage][1]
                for i in range(many):
                    total = self.buf[e, to + i].astype(f32) + self.box(3, e, i, 1)[0].astype(f32)
                    self.buf[e, to + i] = total.astype(bf16)
                self.copies(stage, e)[1].start()

    def arrive(self, stage, e):
        for k, copy in enumerate(self.copies(stage, e)):
            if self.on_line(stage) and k != 1:
                pl.when(self.p.at["z"] != (3 if k == 0 else 0))(copy.wait_send)
                pl.when(self.p.at["z"] != (0 if k == 0 else 3))(copy.wait_recv)
            else:
                copy.wait()
        if self.on_line(stage):
            pl.when(self.p.end)(lambda: self.passed(e).wait_send())

    def total(self, stage, e, i):
        p, order = self.p, self.order
        many = span(p, order, 2 - stage)
        total = self.buf[e, p.first[order, 2 - stage] + i].astype(f32)
        for k in range(p.size[order[2 - stage]] - 1):
            term = self.box(stage, e, k * many + i, 1)[0].astype(f32)
            if self.on_line(stage) and k != 1:
                term = jnp.where(p.at["z"] != (0 if k == 0 else 3), term, 0.0)
            total = total + term
        return total

    def add(self, stage, e):
        def one(i, carry):
            self.buf[e, self.p.first[self.order, 2 - stage] + i] = self.total(stage, e, i).astype(bf16)
            return carry

        lax.fori_loop(0, span(self.p, self.order, 2 - stage), one, 0)

    def last(self, e):
        return self.total(2, e, 0)


def block_rows(rows, parts):
    return (parts * rows + SUB - 1) // SUB * SUB


def blocks_to_weights(place, rows, buf, core, outs, order=ZBA):
    many = SUB // math.gcd(SUB, rows)
    for first in range(0, place.count, many):
        blocks = [buf[place.slot_of(first + i, core, order)].astype(f32) for i in range(many)]
        for part, out in enumerate(outs):
            pieces = [block[part * rows : (part + 1) * rows] for block in blocks]
            out[pl.ds(first * rows, many * rows), :] = jnp.concatenate(pieces, axis=0).astype(bf16)


def grads_to_blocks(place, rows, grads, buf, order=ZBA):
    block = buf.shape[1]
    for dp in range(place.count):
        pieces = [grad[dp * rows : (dp + 1) * rows, :] for grad in grads]
        if block > rows * len(grads):
            pieces.append(jnp.zeros((block - rows * len(grads), buf.shape[2]), f32))
        buf[place.slot_of(dp, place.mp, order)] = jnp.concatenate(pieces, axis=0).astype(bf16)


def all_sum(place, value, src, box, send, recv):
    layer = place.side * place.side
    spot = place.dp % layer
    z = place.at["z"]
    src[0] = value
    box[z] = value
    copies = [
        remote(src.at[0], box.at[z], send.at[k], recv.at[k], peer) for k, peer in enumerate(place.near["z"])
    ]
    for copy in copies:
        copy.start()
    for copy in copies:
        copy.wait()
    total = box[0]
    for i in range(1, place.depth):
        total = total + box[i]
    mine = spot * 2 + place.mp
    base = place.depth
    src[1] = total
    box[base + mine] = total
    at = place.depth - 1
    copies = [
        remote(src.at[1], box.at[base + mine], send.at[at + k], recv.at[at + k], peer)
        for k, peer in enumerate(place.peers_layer())
    ]
    for copy in copies:
        copy.start()
    for copy in copies:
        copy.wait()
    total = box[base]
    for i in range(1, 2 * layer):
        total = total + box[base + i]
    return total


def block_kernel(
    count, rows, experts, tile, lag,
    tok_ref, cot_ref, cond_ref, route_ref, ada_ref, gate_ref, attn_ref, w_ref,
    output_ref, grad_tok_ref, ada_out, attn_out, total_ref, norm_out,
    buf_one, buf_two, box_one, rest_one, box_two, rest_two,
    ada_one, ada_two, sc_buf, mod_buf, mod_far, attn_buf, attn_box, attn_rest, attn_far, attn_w,
    cond_low, mod_one, mod_two, grad_mod, grad_mod_in, triple, mixed, h_one, soft,
    h_all, d_all, gate_all, branch_acc, grad_h_acc, grad_gate_acc, gate_in, share_in,
    up_w, down_w, up_grad, down_grad, gate_grad, attn_share, attn_in, norm_src, norm_box,
    w_hold, load_sem, gather_send, gather_recv, gather_send_two, gather_recv_two,
    scatter_send, scatter_recv, scatter_send_two, scatter_recv_two,
    ada_send, ada_recv, more_send, more_recv, sc_send, sc_recv, mod_send, mod_recv, attn_send, attn_recv, attn_back_send, attn_back_recv,
    core_send, core_recv, token_send, token_recv, norm_send, norm_recv,
):
    place = Place(count)
    met = place.greet()
    mp = place.mp
    wide_experts = w_ref.shape[1]
    own_tok, width = tok_ref.shape
    images = own_tok // PATCH
    half = attn_ref.shape[2]
    first = half // LANES * LANES
    heads = half // HD
    wide = ada_ref.shape[1] // 2
    cut = mod_buf.shape[3]
    scale = HD ** (-0.5)
    own_at = pl.multiple_of(mp * own_tok, own_tok)
    their_at = pl.multiple_of((1 - mp) * own_tok, own_tok)
    own, theirs = pl.ds(own_at, own_tok), pl.ds(their_at, own_tok)
    other = place.other_core()

    loads = [
        pltpu.make_async_copy(tok_ref, branch_acc.at[pl.ds(0, own_tok)], load_sem.at[0]),
        pltpu.make_async_copy(cot_ref, branch_acc.at[pl.ds(own_tok, own_tok)], load_sem.at[1]),
    ]
    w_load = pltpu.make_async_copy(w_ref, w_hold, load_sem.at[2])
    w_load.start()
    for load in loads:
        load.start()

    def put(target, block, order=ZBA):
        if block.shape[0] != target.shape[1]:
            target[place.slot(order)] = jnp.zeros(target.shape[1:], bf16)
        target[place.slot(order), pl.ds(0, block.shape[0])] = block

    put(ada_one.at[0], ada_ref[:, pl.ds(pl.multiple_of(mp * width, LANES), width)].astype(bf16))
    cols = ada_ref[:, pl.ds(pl.multiple_of((1 + mp) * 2 * width, LANES), 2 * width)]
    put(ada_two.at[0], jnp.concatenate([cols[:, :width], cols[:, width:]], axis=0).astype(bf16))
    parts = attn_ref.shape[0]
    side_by = lax.broadcasted_iota(jnp.int32, (experts, LANES), 1) == lax.broadcasted_iota(
        jnp.int32, (experts, LANES), 0
    )
    gate = mxu(gate_ref[...].astype(bf16), side_by.astype(f32).astype(bf16), TN)[:, : 2 * LANES - half]
    spare = [gate] + [jnp.zeros_like(gate)] * (parts - 1)
    both = [jnp.concatenate([attn_ref[j], spare[j]], axis=1) for j in range(parts)]
    pair = parts // 2
    for i in range(2):
        put(attn_buf.at[i], jnp.concatenate(both[i * pair : (i + 1) * pair], axis=0).astype(bf16))
    cond = cond_ref[...]
    cond = cond / (1.0 + jnp.exp(-cond))
    cond_low[...] = cond.astype(bf16)
    sc_buf[0, place.slot()] = jnp.concatenate([cond, jnp.zeros((SUB - cond.shape[0], width), f32)], axis=0).astype(bf16)
    met()
    ada_gather = Gather(place, ada_one, ada_send, ada_recv)
    more_gather = Gather(place, ada_two, more_send, more_recv)
    attn_gather = Gather(place, attn_buf, attn_send, attn_recv)
    cuts = (pl.ds(0, buf_one.shape[3]), pl.ds(buf_one.shape[3], buf_two.shape[3]))
    streams = tuple(zip((buf_one, buf_two), cuts, (ZBA, BZA)))
    gathers = (
        Gather(place, buf_one, gather_send, gather_recv, ZBA, True),
        Gather(place, buf_two, gather_send_two, gather_recv_two, BZA, True),
    )
    scatters = (
        Scatter(place, buf_one, (box_one, rest_one), scatter_send, scatter_recv, ZBA, True),
        Scatter(place, buf_two, (box_two, rest_two), scatter_send_two, scatter_recv_two, BZA, True),
    )
    sc_gather = Gather(place, sc_buf, sc_send, sc_recv)
    ada_gather.start(0, 0)
    attn_gather.start(0, 0)
    attn_gather.start(0, 1)
    more_gather.start(0, 0)
    sc_gather.start(0, 0)

    def fill(e, carry):
        both = jnp.concatenate([w_hold[0, e], w_hold[1, e]], axis=0).astype(bf16)
        for buf, lanes, order in streams:
            put(buf.at[e], both[:, lanes.start : lanes.start + lanes.size], order)
        return carry

    w_load.wait()
    lax.fori_loop(0, wide_experts, fill, 0)

    def begin(e):
        for one in gathers:
            one.start(0, e)

    def onward(stage, e):
        for one in gathers:
            one.arrive(stage, e)
            one.start(stage + 1, e)

    def tick(k):
        pl.when(k + 6 < wide_experts)(lambda: begin(k + 6))
        pl.when(k + 4 < wide_experts)(lambda: gathers[0].relay(k + 4))
        pl.when(k + 3 < wide_experts)(lambda: onward(0, k + 3))
        pl.when(k + 2 < wide_experts)(lambda: gathers[1].relay(k + 2))
        pl.when((k >= 0) & (k < wide_experts))(lambda: onward(1, k))

    grad_mod[...] = jnp.zeros_like(grad_mod)
    items = ((ada_gather, 0), (attn_gather, 0), (attn_gather, 1), (more_gather, 0))

    def wave(w):
        for i in (w, w - 1):
            if 0 <= i < len(items):
                small, which = items[i]
                small.arrive(w - i, which)
                small.start(w - i + 1, which)

    for w in range(len(items)):
        wave(w)
    begin(0)
    begin(1)
    width_lanes = pl.ds(0, width)
    ada_gather.arrive(2, 0)

    blocks_to_weights(place, rows, ada_one.at[0], mp, (up_w.at[:, width_lanes],))
    mod_one[mp] = mxu(cond_low[...], up_w[:, width_lanes])
    mod_cross = [
        remote(ref.at[mp], ref.at[mp], core_send.at[i], core_recv.at[i], other)
        for i, ref in ((1, mod_one), (0, mod_two))
    ]
    mod_cross[0].start()
    wave(len(items))
    attn_cross = []
    for i in range(2):
        attn_gather.arrive(2, i)
        attn_cross.append(
            remote(attn_buf.at[i], attn_far.at[i], core_send.at[8 + i], core_recv.at[8 + i], other)
        )
        attn_cross[i].start()
        outs = [attn_w.at[mp, j] for j in range(i * pair, (i + 1) * pair)]
        blocks_to_weights(place, rows, attn_buf.at[i], mp, outs)
    for load in loads:
        load.wait()
    ada_gather.sent(0)
    attn_gather.sent(0)
    attn_gather.sent(1)
    begin(2)
    begin(3)
    begin(4)
    gathers[0].relay(0)
    onward(0, 0)
    sc_gather.arrive(0, 0)
    sc_gather.start(1, 0)
    for i in range(2):
        attn_cross[i].wait()
        outs = [attn_w.at[1 - mp, j] for j in range(i * pair, (i + 1) * pair)]
        blocks_to_weights(place, rows, attn_far.at[i], 1 - mp, outs)
    mod_cross[0].wait()
    gathers[0].relay(1)
    onward(0, 1)
    gathers[0].relay(2)
    gathers[1].relay(0)
    gate_lanes = pl.ds(first, LANES)
    half_lanes = pl.ds(0, half)

    def weight(core, j):
        return attn_w[core, j, :, half_lanes]

    lane_pair = lax.broadcasted_iota(jnp.int32, (PATCH, 2 * HD), 1)
    masks = [(lane_pair < HD).astype(f32).astype(bf16), (lane_pair >= HD).astype(f32).astype(bf16)]
    groups = [(at, min(2, heads - at)) for at in range(0, heads, 2)]
    expert_lane = lax.broadcasted_iota(jnp.int32, (PATCH, LANES), 1) - (half - first)

    def mod_row(image, vector):
        row = pl.ds(mp * images + image, 1)
        if vector < 2:
            return mod_one[vector, row, :]
        return mod_two[vector // 2 - 1, row, pl.ds(vector % 2 * width, width)]

    def add_grad_mod(image, vector, value):
        grad_mod[vector // 3, pl.ds(mp * images + image, 1), pl.ds(vector % 3 * width, width)] = value

    def one_head(value, group, head):
        return value if group[1] == 1 else value * masks[head]

    def route(h, image):
        valid = (expert_lane >= 0) & (expert_lane < experts)
        logits = jnp.where(valid, mxu(h, attn_w[0, 0, :, gate_lanes]), -jnp.inf)
        power = jnp.exp(logits - jnp.max(logits, axis=1, keepdims=True))
        router = power / jnp.sum(power, axis=1, keepdims=True)
        picks = route_ref[:, pl.ds(pl.multiple_of(own_at + image * PATCH, PATCH), PATCH)]
        spot = lax.broadcasted_iota(jnp.int32, (LANES, PATCH), 0) - (half - first)
        picked = jnp.where((picks[0:1, :] == spot) | (picks[1:2, :] == spot), 1.0, 0.0)
        return router, picked.T

    def attend(at):
        return mxu(mixed[0, at, :], weight(0, 3), NT) + mxu(mixed[1, at, :], weight(1, 3), NT)

    def token_copies(image):
        at = pl.ds(pl.multiple_of(own_at + image * PATCH, PATCH), PATCH)
        return [
            remote(ref.at[at], ref.at[at], token_send.at[image, i], token_recv.at[image, i], other)
            for i, ref in enumerate((h_all, d_all, gate_all))
        ]

    def attention(image, carry):
        at = pl.ds(pl.multiple_of(image * PATCH, PATCH), PATCH)
        normed, _ = layer_norm(branch_acc[at, :])
        h = (normed * (1.0 + mod_row(image, 1)) + mod_row(image, 0)).astype(bf16)
        h_one[at, :] = h
        for core in range(2):
            for j in range(3):
                triple[core, j, at, :] = mxu(h, weight(core, j)).astype(bf16)
            for group in groups:
                lanes = pl.ds(group[0] * HD, group[1] * HD)
                query, key, value = (triple[core, j, at, lanes] for j in range(3))
                total = 0.0
                for head in range(group[1]):
                    scores = mxu(one_head(query, group, head), key, NT) * scale
                    power = jnp.exp(scores - jnp.max(scores, axis=1, keepdims=True))
                    low = (power * (1.0 / jnp.sum(power, axis=1, keepdims=True))).astype(bf16)
                    soft[image, core * heads + group[0] + head] = low
                    total = total + mxu(low, one_head(value, group, head))
                mixed[core, at, lanes] = total.astype(bf16)
        tick(image - 1)

        @pl.when(image == 0)
        def _():
            sc_gather.arrive(1, 0)
            sc_gather.start(2, 0)

        return carry

    lax.fori_loop(0, images, attention, 0)
    more_gather.arrive(2, 0)
    blocks_to_weights(place, rows, ada_two.at[0], mp, (up_w.at[:, width_lanes], down_w.at[:, width_lanes]))
    mod_two[mp, :, pl.ds(0, width)] = mxu(cond_low[...], up_w[:, width_lanes])
    mod_two[mp, :, pl.ds(width, width)] = mxu(cond_low[...], down_w[:, width_lanes])
    mod_cross[1].start()
    more_gather.sent(0)
    mod_cross[1].wait()

    def forward(image, carry):
        at = pl.ds(pl.multiple_of(image * PATCH, PATCH), PATCH)
        cot_at = pl.ds(pl.multiple_of(own_tok + image * PATCH, PATCH), PATCH)
        all_at = pl.ds(pl.multiple_of(own_at + image * PATCH, PATCH), PATCH)
        x_one = branch_acc[at, :] + mod_row(image, 2) * attend(at)
        normed, _ = layer_norm(x_one)
        h = (normed * (1.0 + mod_row(image, 4)) + mod_row(image, 3)).astype(bf16)
        h_all[all_at, :] = h
        router, chosen = route(h, image)
        shared = (expert_lane >= experts) & (expert_lane < wide_experts)
        gate_all[all_at, :] = jnp.where(shared, 1.0, router * chosen)
        d_all[all_at, :] = (branch_acc[cot_at, :] * mod_row(image, 5)).astype(bf16)
        for copy in token_copies(image):
            copy.start()

        return carry

    lax.fori_loop(0, images, forward, 0)
    ahead = images - 1
    sc_gather.arrive(2, 0)
    sc_gather.sent(0)

    branch_acc[...] = jnp.zeros_like(branch_acc)
    grad_h_acc[...] = jnp.zeros_like(grad_h_acc)
    grad_gate_acc[...] = jnp.zeros_like(grad_gate_acc)

    def all_tokens(image, carry):
        for copy in token_copies(image):
            copy.wait()
        return carry

    lax.fori_loop(0, images, all_tokens, 0)

    shares = [
        remote(h_all.at[theirs], share_in.at[0], core_send.at[2], core_recv.at[2], other),
        remote(d_all.at[theirs], share_in.at[1], core_send.at[3], core_recv.at[3], other),
        remote(grad_gate_acc.at[theirs], gate_in, core_send.at[4], core_recv.at[4], other),
    ]
    loads = [
        pltpu.make_async_copy(tok_ref, branch_acc.at[theirs], load_sem.at[0]),
        pltpu.make_async_copy(cot_ref, grad_h_acc.at[theirs], load_sem.at[1]),
    ]
    tiles = h_all.shape[0] // tile

    def compute(e):
        for buf, lanes, order in streams:
            blocks_to_weights(place, rows, buf.at[e], mp, (up_w.at[:, lanes], down_w.at[:, lanes]), order)
        up_grad[...] = jnp.zeros_like(up_grad)
        down_grad[...] = jnp.zeros_like(down_grad)

        def one_tile(t, carry):
            @pl.when((e == wide_experts - 1) & (t == tiles // 2))
            def _():
                h_all[theirs, :] = branch_acc[theirs, :].astype(bf16)
                d_all[theirs, :] = grad_h_acc[theirs, :].astype(bf16)
                for copy in shares:
                    copy.start()
                for copy in loads:
                    copy.start()

            at = pl.ds(pl.multiple_of((t + (1 - mp) * (tiles // 2)) % tiles * tile, tile), tile)
            h = h_all[at, :]
            d = d_all[at, :]
            lane = lax.broadcasted_iota(jnp.int32, (tile, LANES), 1) - (half - first)
            gate = jnp.sum(jnp.where(lane == e, gate_all[at, :], 0.0), axis=1, keepdims=True)
            pre = mxu(h, up_w[...])
            back = mxu(d, down_w[...])
            act, slope = gelu_both(pre)
            inner = jnp.sum(act * back, axis=1, keepdims=True)
            grad_gate_acc[at, :] += jnp.where(lane == e, inner, 0.0)
            act_low = (gate * act).astype(bf16)
            pre_low = (gate * back * slope).astype(bf16)
            branch_acc[at, :] += mxu(act_low, down_w[...], NT)
            grad_h_acc[at, :] += mxu(pre_low, up_w[...], NT)
            up_grad[...] += mxu(h, pre_low, TN)
            down_grad[...] += mxu(d, act_low, TN)
            return carry

        lax.fori_loop(0, tiles, one_tile, 0)

    def follow(one, stage, e):
        one.arrive(stage, e)
        one.add(stage, e)
        one.start(stage + 1, e)

    def finish(e):
        for one, (_, lanes, _) in zip(scatters, streams):
            one.arrive(2, e)
            total_ref[e, :, lanes] = one.last(e)

    def collect(k):
        def at(late, act):
            pl.when((k >= late) & (k - late < wide_experts))(lambda: act(k - late))

        at(4, finish)
        at(3, scatters[0].relay)
        at(3, lambda e: follow(scatters[1], 1, e))
        at(2, lambda e: follow(scatters[0], 1, e))
        at(2, scatters[1].relay)
        at(1, lambda e: [follow(one, 0, e) for one in scatters] and None)

    def step(e, carry):
        tick(e + ahead)
        for one in gathers:
            one.arrive(2, e)
        compute(e)
        for one in gathers:
            one.sent(e)
        for buf, lanes, order in streams:
            grads_to_blocks(place, rows, (up_grad.at[:, lanes], down_grad.at[:, lanes]), buf.at[e], order)
        for one in scatters:
            one.start(0, e)
        collect(e - lag)
        return carry

    lax.fori_loop(0, wide_experts, step, 0)

    row = lax.broadcasted_iota(jnp.int32, (width, LANES), 0)
    lane = lax.broadcasted_iota(jnp.int32, (width, LANES), 1)
    pick = ((row == place.dp * rows + lane) & (lane < rows)).astype(f32).astype(bf16)
    group = cond_ref.shape[0]

    def in_order(ref, core, at):
        pieces = [ref[place.slot_of(dp, core)].astype(f32)[at : at + group] for dp in range(count)]
        return jnp.concatenate(pieces, axis=0).astype(bf16)

    conds = mxu(in_order(sc_buf.at[0], mp, 0), pick).astype(bf16)

    gate_grad[...] = jnp.zeros_like(gate_grad)
    for copy in shares + loads:
        copy.wait()

    def backward(image, carry):
        at = pl.ds(pl.multiple_of(image * PATCH, PATCH), PATCH)
        own_rows = pl.ds(pl.multiple_of(own_at + image * PATCH, PATCH), PATCH)
        load_rows = pl.ds(pl.multiple_of(their_at + image * PATCH, PATCH), PATCH)
        tok, cot = branch_acc[load_rows, :], grad_h_acc[load_rows, :]
        branch = branch_acc[own_rows, :] + share_in[0, at, :].astype(f32)
        attention = attend(at)
        x_one = tok + mod_row(image, 2) * attention
        normed, inverse = layer_norm(x_one)
        branch_acc[own_rows, :] = x_one + mod_row(image, 5) * branch
        add_grad_mod(image, 5, jnp.sum(cot * branch, axis=0, keepdims=True))
        h = h_all[own_rows, :]
        router, chosen = route(h, image)
        grad_router = (grad_gate_acc[own_rows, :] + gate_in[at, :]) * chosen
        grad_logits = (router * (grad_router - jnp.sum(router * grad_router, axis=1, keepdims=True))).astype(bf16)
        gate_grad[...] += mxu(h, grad_logits, TN)
        grad_h = grad_h_acc[own_rows, :] + share_in[1, at, :].astype(f32) + mxu(grad_logits, attn_w[0, 0, :, gate_lanes], NT)
        add_grad_mod(image, 3, jnp.sum(grad_h, axis=0, keepdims=True))
        add_grad_mod(image, 4, jnp.sum(grad_h * normed, axis=0, keepdims=True))
        grad_x = cot + norm_back(grad_h * (1.0 + mod_row(image, 4)), normed, inverse)
        add_grad_mod(image, 2, jnp.sum(grad_x * attention, axis=0, keepdims=True))
        grad_att = (grad_x * mod_row(image, 2)).astype(bf16)
        d_all[own_rows, :] = grad_att
        grad_h_one = 0.0
        for core in range(2):
            grad_mixed = mxu(grad_att, weight(core, 3)).astype(bf16)
            for group in groups:
                lanes = pl.ds(group[0] * HD, group[1] * HD)
                query, key, value = (triple[core, j, at, lanes] for j in range(3))
                back = grad_mixed[:, group[0] * HD : (group[0] + group[1]) * HD]
                grads = [0.0, 0.0, 0.0]
                for head in range(group[1]):
                    low = soft[image, core * heads + group[0] + head]
                    prob = low.astype(f32)
                    head_back = one_head(back, group, head)
                    grad_soft = mxu(head_back, value, NT)
                    delta = jnp.sum(prob * grad_soft, axis=1, keepdims=True)
                    grad_scores = (prob * (grad_soft - delta) * scale).astype(bf16)
                    grads[0] = grads[0] + mxu(grad_scores, one_head(key, group, head))
                    grads[1] = grads[1] + mxu(grad_scores, one_head(query, group, head), TN)
                    grads[2] = grads[2] + mxu(low, head_back, TN)
                for j in range(3):
                    triple[core, j, at, lanes] = grads[j].astype(bf16)
            for j in range(3):
                grad_h_one = grad_h_one + mxu(triple[core, j, at, :], weight(core, j), NT)
        normed, inverse = layer_norm(tok)
        add_grad_mod(image, 0, jnp.sum(grad_h_one, axis=0, keepdims=True))
        add_grad_mod(image, 1, jnp.sum(grad_h_one * normed, axis=0, keepdims=True))
        grad_h_acc[own_rows, :] = grad_x + norm_back(grad_h_one * (1.0 + mod_row(image, 1)), normed, inverse)

        @pl.when(image > 0)
        def _():
            collect(wide_experts - lag + image - 1)

        return carry

    lax.fori_loop(0, images, backward, 0)
    stores = [
        pltpu.make_async_copy(branch_acc.at[own], output_ref, load_sem.at[2]),
        pltpu.make_async_copy(grad_h_acc.at[own], grad_tok_ref, load_sem.at[3]),
    ]
    for copy in stores:
        copy.start()

    crosses = [
        remote(grad_mod.at[1 - mp], grad_mod_in, core_send.at[5], core_recv.at[5], other),
        *[
            remote(
                attn_share.at[pl.ds(i * pair, pair)], attn_in.at[pl.ds(i * pair, pair)],
                core_send.at[6 + i], core_recv.at[6 + i], other,
            )
            for i in range(2)
        ],
        remote(mod_buf.at[0], mod_far, core_send.at[1], core_recv.at[1], other),
    ]
    crosses[0].start()

    def attn_grad(core, j):
        if j == parts - 1:
            return mxu(d_all[own, :], mixed[core], TN)
        return mxu(h_one[...], triple[core, j], TN)

    spare = pl.ds(half, 2 * LANES - half)
    places = [(up_grad, 0), (up_grad, 1), (up_grad, 2), (down_grad, 0)]
    attn_scatter = Scatter(place, attn_buf, (attn_box, attn_rest), attn_back_send, attn_back_recv)
    for i in range(2):
        for j in range(i * pair, (i + 1) * pair):
            attn_share[j, :, half_lanes] = attn_grad(1 - mp, j).astype(bf16)
            extra = gate_grad[:, pl.ds(half - first, 2 * LANES - half)].astype(bf16)
            attn_share[j, :, spare] = extra if j == 0 else jnp.zeros_like(extra)
        crosses[1 + i].start()
    crosses[0].wait()
    grad_low = grad_mod[mp] + grad_mod_in[...]
    mod_buf[0, place.slot()] = jnp.concatenate([grad_low[:, :cut], grad_low[:, cut:]], axis=0).astype(bf16)
    mod_gather = Gather(place, mod_buf, mod_send, mod_recv)
    for i in range(2):
        for j in range(i * pair, (i + 1) * pair):
            ref, at = places[j]
            ref[:, pl.ds(at * 2 * LANES, half)] = attn_grad(mp, j)
        crosses[1 + i].wait()
        grads = []
        for j in range(i * pair, (i + 1) * pair):
            ref, at = places[j]
            lanes = pl.ds(at * 2 * LANES, half)
            ref[:, lanes] += attn_in[j, :, half_lanes].astype(f32)
            extra = gate_grad[:, pl.ds(half - first, 2 * LANES - half)] + attn_in[0, :, spare].astype(f32)
            ref[:, pl.ds(at * 2 * LANES + half, 2 * LANES - half)] = extra if j == 0 else jnp.zeros_like(extra)
            grads.append(ref[:, pl.ds(at * 2 * LANES, 2 * LANES)])
        grads_to_blocks(place, rows, grads, attn_buf.at[i])
        attn_scatter.start(0, i)
    mod_gather.start(0, 0)
    left = list(range(wide_experts - lag + images - 1, wide_experts + 4))
    for stage in range(2):
        if len(left) > 1:
            collect(left.pop(0))
        for i in range(2):
            attn_scatter.arrive(stage, i)
            attn_scatter.add(stage, i)
            attn_scatter.start(stage + 1, i)
        mod_gather.arrive(stage, 0)
        mod_gather.start(stage + 1, 0)
    for k in left:
        collect(k)
    square = jnp.zeros((1, 1), f32)
    for e in range(wide_experts):
        square = square + jnp.sum(total_ref[e] * total_ref[e])
    mod_gather.arrive(2, 0)
    crosses[3].start()
    def ada_grad(ref, core):
        low = mxu(conds, in_order(ref, core, 0), TN)[:rows]
        high = mxu(conds, in_order(ref, core, group), TN)[:rows, : wide - cut]
        start = pl.multiple_of(core * wide, LANES)
        ada_out[:, pl.ds(start, cut)] = low
        ada_out[:, pl.ds(pl.multiple_of(start + cut, LANES), wide - cut)] = high
        return jnp.sum(low * low) + jnp.sum(high * high)

    small = ada_grad(mod_buf.at[0], mp)
    mod_gather.sent(0)
    crosses[3].wait()
    small = small + ada_grad(mod_far, 1 - mp)
    square = square + 0.5 * small
    for i in range(2):
        attn_scatter.arrive(2, i)
        attn = attn_scatter.last(i)
        attn_out[i] = attn
        lane = lax.broadcasted_iota(jnp.int32, attn.shape, 1)
        square = square + jnp.sum(jnp.where(lane < half, 1.0, 0.5) * attn * attn)
    value = jnp.broadcast_to(square, norm_out.shape)
    norm_out[...] = all_sum(place, value, norm_src, norm_box, norm_send, norm_recv)
    for copy in stores:
        copy.wait()


def block_call(tokens, condition, cotangent, routes, w_ada, w_gate, w_attn, w_expert):
    count = lax.axis_size("dp")
    own_tok, width = tokens.shape
    rows, wide = w_ada.shape
    experts = w_gate.shape[0]
    parts, _, half = w_attn.shape
    _, wide_experts, _, hidden = w_expert.shape
    depth, side = dp_sizes(count)
    images = own_tok // PATCH
    cut = (wide // 4 + LANES - 1) // LANES * LANES
    spare = 2 * LANES
    block, ada_block, attn_block = block_rows(rows, 2), block_rows(rows, 2), block_rows(rows, parts // 2)
    tok = 2 * own_tok
    tile, lag = (TILE, 2) if count <= 16 else (TILE // 2, 0)
    vmem = pl.BlockSpec(memory_space=pltpu.VMEM)
    hbm = pl.BlockSpec(memory_space=pl.ANY)
    hops = depth + 2 * side - 3

    def sems(*shape):
        return pltpu.SemaphoreType.DMA(shape)

    def boxes(slots, order, height, lanes):
        size = {"z": depth, "a": side, "b": side}
        span = size[order[0]] * size[order[1]]
        first = (size[order[2]] - 1) * span
        extra = 0 if slots <= 2 else math.prod(size[axis] for axis in order[: order.index("z")])
        return [
            pltpu.VMEM((slots, first, height, lanes), bf16),
            pltpu.VMEM((min(slots, REST), span - 1 + extra, height, lanes), bf16),
        ]

    one = hidden * CUT_ONE // CUT_ALL // LANES * LANES
    two = hidden - one

    return pl.pallas_call(
        functools.partial(block_kernel, count, rows, experts, tile, lag),
        out_shape=(
            jax.ShapeDtypeStruct((own_tok, width), f32),
            jax.ShapeDtypeStruct((own_tok, width), f32),
            jax.ShapeDtypeStruct((rows, wide), f32),
            jax.ShapeDtypeStruct((2, attn_block, spare), f32),
            jax.ShapeDtypeStruct((wide_experts, block, hidden), f32),
            jax.ShapeDtypeStruct((8, LANES), f32),
        ),
        in_specs=[hbm, hbm] + [vmem] * 5 + [hbm],
        out_specs=(hbm, hbm) + (vmem,) * 4,
        scratch_shapes=[
            pltpu.VMEM((wide_experts, count, block, one), bf16),
            pltpu.VMEM((wide_experts, count, block, two), bf16),
            *boxes(SLOTS + 2 * lag, ZBA, block, one),
            *boxes(SLOTS + 2 * lag, BZA, block, two),
            pltpu.VMEM((1, count, block_rows(rows, 1), width), bf16),
            pltpu.VMEM((1, count, ada_block, width), bf16),
            pltpu.VMEM((1, count, SUB, width), bf16),
            pltpu.VMEM((1, count, SUB, cut), bf16),
            pltpu.VMEM((count, SUB, cut), bf16),
            pltpu.VMEM((2, count, attn_block, spare), bf16),
            *boxes(2, ZBA, attn_block, spare),
            pltpu.VMEM((2, count, attn_block, spare), bf16),
            pltpu.VMEM((2, parts, width, spare), bf16),
            pltpu.VMEM(condition.shape, bf16),
            pltpu.VMEM((2, condition.shape[0], width), f32),
            pltpu.VMEM((2, condition.shape[0], 2 * width), f32),
            pltpu.VMEM((2, condition.shape[0], 2 * cut), f32),
            pltpu.VMEM((condition.shape[0], 2 * cut), f32),
            pltpu.VMEM((2, 3, own_tok, half), bf16),
            pltpu.VMEM((2, own_tok, half), bf16),
            pltpu.VMEM((own_tok, width), bf16),
            pltpu.VMEM((images, width // HD, PATCH, PATCH), bf16),
            pltpu.VMEM((tok, width), bf16),
            pltpu.VMEM((tok, width), bf16),
            pltpu.VMEM((tok, LANES), f32),
            pltpu.VMEM((tok, width), f32),
            pltpu.VMEM((tok, width), f32),
            pltpu.VMEM((tok, LANES), f32),
            pltpu.VMEM((own_tok, LANES), f32),
            pltpu.VMEM((2, own_tok, width), bf16),
            pltpu.VMEM((width, hidden), bf16),
            pltpu.VMEM((width, hidden), bf16),
            pltpu.VMEM((width, hidden), f32),
            pltpu.VMEM((width, hidden), f32),
            pltpu.VMEM((width, LANES), f32),
            pltpu.VMEM((parts, width, spare), bf16),
            pltpu.VMEM((parts, width, spare), bf16),
            pltpu.VMEM((2, 8, LANES), f32),
            pltpu.VMEM((depth + 2 * side * side, 8, LANES), f32),
            pltpu.VMEM(w_expert.shape, f32),
            sems(4),
            *[sems(wide_experts, hops + 1)] * 8,
            *[sems(1, hops)] * 8,
            *[sems(2, hops)] * 4,
            sems(10),
            sems(10),
            sems(images, 3),
            sems(images, 3),
            sems(depth + 2 * side * side),
            sems(depth + 2 * side * side),
        ],
        compiler_params=pltpu.CompilerParams(collective_id=1, has_side_effects=True, vmem_limit_bytes=VMEM_BYTES),
        cost_estimate=pl.CostEstimate(
            flops=12 * tok * width * hidden * wide_experts, bytes_accessed=16 * w_expert.size, transcendentals=0
        ),
        name="block",
    )(tokens, cotangent, condition, routes, w_ada, w_gate, w_attn, w_expert)
def update_kernel(rows, half, output_ref, grad_tok_ref, expert_w, expert_m, expert_v, expert_ref, norm_ref, attn_ref, ada_ref, *refs):
    ada, gate, attn = (refs[3 * i : 3 * i + 3] for i in range(3))
    outs, (hold, held, grads, sem, token_sem) = refs[9:-5], refs[-5:]
    ada_new, gate_new, attn_new, expert_new = (outs[3 * i : 3 * i + 3] for i in range(4))
    expert = (expert_w, expert_m, expert_v)
    many = expert_w.shape[1] // 2
    chunks = [(part, h) for h in range(2) for part in range(2)]
    grad_loads = [
        pltpu.make_async_copy(expert_ref.at[pl.ds(h * many, many)], grads.at[pl.ds(h * many, many)], token_sem.at[4 + h])
        for h in range(2)
    ]

    def moves(c, refs, back):
        part, h = chunks[c]
        made = []
        for i, ref in enumerate(refs):
            far, near = ref.at[part, pl.ds(h * many, many)], held.at[i, part, pl.ds(h * many, many)]
            made.append(pltpu.make_async_copy(*((near, far) if back else (far, near)), sem.at[int(back), c, i]))
        return made

    for c in range(4):
        if chunks[c][0] == 0:
            grad_loads[chunks[c][1]].start()
        for copy in moves(c, expert, False):
            copy.start()
    token_loads = [pltpu.make_async_copy(ref, hold.at[i], token_sem.at[i]) for i, ref in enumerate((output_ref, grad_tok_ref))]
    token_stores = [pltpu.make_async_copy(hold.at[i], outs[13 + i], token_sem.at[2 + i]) for i in range(2)]
    for copy in token_loads:
        copy.start()
    total = jnp.sqrt(norm_ref[...])
    outs[12][0, 0] = jnp.max(total)
    factor = jnp.minimum(1.0, CLIP_NORM / (total[0:1, 0:1] + 1e-06))

    def write(ins, news, at, grad):
        for new, value in zip(news, adam(ins[0][at], ins[1][at], ins[2][at], grad * factor)):
            new[at] = value

    everything = (slice(None), slice(None))
    write(ada, ada_new, everything, ada_ref[...])
    first = half // LANES * LANES
    small = attn_ref[0, pl.ds(0, rows), pl.ds(first, LANES)]
    square = jnp.concatenate([small, jnp.zeros((LANES - rows, LANES), f32)], axis=0).T
    experts = gate[0].shape[0]
    write(gate, gate_new, everything, square[half - first : half - first + experts, :rows])
    parts = attn[0].shape[0]
    for j in range(parts):
        grad = attn_ref[j // (parts // 2), pl.ds(j % (parts // 2) * rows, rows), pl.ds(0, half)]
        write(attn, attn_new, (j,), grad)
    here = [held.at[i] for i in range(3)]
    for c, (part, h) in enumerate(chunks):
        if part == 0:
            grad_loads[h].wait()
        for copy in moves(c, expert, False):
            copy.wait()

        def one(e, carry):
            write(here, here, (part, e), grads[e, pl.ds(part * rows, rows), :])
            return carry

        lax.fori_loop(h * many, (h + 1) * many, one, 0)
        for copy in moves(c, expert_new, True):
            copy.start()
    for load, store in zip(token_loads, token_stores):
        load.wait()
        store.start()
    for c in range(4):
        for copy in moves(c, expert_new, True):
            copy.wait()
    for copy in token_stores:
        copy.wait()


def update_call(rows, half, output, grad_tokens, norm, expert, attn, ada, weights):
    vmem = pl.BlockSpec(memory_space=pltpu.VMEM)
    hbm = pl.BlockSpec(memory_space=pl.ANY)
    shapes = [jax.ShapeDtypeStruct(w.shape, f32) for w in weights]
    return pl.pallas_call(
        functools.partial(update_kernel, rows, half),
        out_shape=shapes
        + [jax.ShapeDtypeStruct((1, 1), f32)]
        + [jax.ShapeDtypeStruct(output.shape, f32), jax.ShapeDtypeStruct(grad_tokens.shape, f32)],
        in_specs=[hbm] * 6 + [vmem] * (3 + 9),
        out_specs=[vmem] * 9 + [hbm] * 3 + [pl.BlockSpec(memory_space=pltpu.SMEM), hbm, hbm],
        scratch_shapes=[
            pltpu.VMEM((2, *output.shape), f32),
            pltpu.VMEM((3, *weights[9].shape), f32),
            pltpu.VMEM(expert.shape, f32),
            pltpu.SemaphoreType.DMA((2, 4, 3)),
            pltpu.SemaphoreType.DMA((6,)),
        ],
        compiler_params=pltpu.CompilerParams(vmem_limit_bytes=VMEM_BYTES),
        name="update",
    )(output, grad_tokens, *weights[9:], expert, norm, attn, ada, *weights[:9])


def per_device(
    tokens,
    condition,
    cotangent,
    routes,
    w_ada,
    ada_first,
    ada_second,
    w_gate,
    gate_first,
    gate_second,
    w_attn,
    attn_first,
    attn_second,
    w_expert,
    expert_first,
    expert_second,
):
    output, grad_tokens, ada_total, attn_total, expert_total, square_sum = block_call(
        tokens, condition, cotangent, routes.T, w_ada, w_gate.T, w_attn, w_expert
    )
    updated = update_call(
        w_ada.shape[0], w_attn.shape[2], output, grad_tokens, square_sum, expert_total, attn_total, ada_total,
        (
            w_ada, ada_first, ada_second,
            w_gate.T, gate_first.T, gate_second.T,
            w_attn, attn_first, attn_second,
            w_expert, expert_first, expert_second,
        ),
    )
    gates = [gate.T for gate in updated[3:6]]
    return (*updated[13:], updated[12].reshape(()), *updated[:3], *gates, *updated[6:12])


def solution(mesh):
    placed = (
        P(("dp", "mp"), None),
        P("dp", None),
        P(("dp", "mp"), None),
        P("dp", None),
        P("dp", None),
        P("dp", None),
        P("dp", None),
        P("dp", None),
        P("dp", None),
        P("dp", None),
        P(None, "dp", "mp"),
        P(None, "dp", "mp"),
        P(None, "dp", "mp"),
        P(None, None, "dp", "mp"),
        P(None, None, "dp", "mp"),
        P(None, None, "dp", "mp"),
    )
    return jax.shard_map(
        per_device,
        mesh=mesh,
        in_specs=placed,
        out_specs=(
            P(("dp", "mp"), None),
            P(("dp", "mp"), None),
            P(),
            P("dp", None),
            P("dp", None),
            P("dp", None),
            P("dp", None),
            P("dp", None),
            P("dp", None),
            P(None, "dp", "mp"),
            P(None, "dp", "mp"),
            P(None, "dp", "mp"),
            P(None, None, "dp", "mp"),
            P(None, None, "dp", "mp"),
            P(None, None, "dp", "mp"),
        ),
        check_vma=False,
    )
```

```python
import functools
import math

import jax
import jax.numpy as jnp
from jax import lax
from jax.experimental import pallas as pl
from jax.experimental.pallas import tpu as pltpu
from jax.sharding import PartitionSpec as P

HD = 64
PATCH = 256
STEP = 10
LANES = 128
SUB = 16
TILE = 512
SLOTS, REST = 4, 4
ZBA, BZA = "zba", "bza"
CUT_ONE, CUT_ALL = 2, 3

EPS_NORM = 1e-06
CLIP_NORM = 0.1
RATE = 0.08
BETA_ONE = 0.9
BETA_TWO = 0.95
ADAM_EPS = 1e-08
DECAY = 0.01
GELU_LIN = 0.7978845608
GELU_CUBE = 0.7978845608 * 0.044715

MESH = pl.DeviceIdType.MESH
VMEM_BYTES = 127 * 512 * 1024
bf16 = jnp.bfloat16
f32 = jnp.float32
NN = (((1,), (0,)), ((), ()))
NT = (((1,), (1,)), ((), ()))
TN = (((0,), (0,)), ((), ()))


def mxu(left, right, dims=NN):
    return lax.dot_general(left, right, dims, preferred_element_type=f32)


def layer_norm(value):
    center = value - jnp.mean(value, axis=-1, keepdims=True)
    inverse = lax.rsqrt(jnp.mean(center * center, axis=-1, keepdims=True) + EPS_NORM)
    return (center * inverse, inverse)


def norm_back(grad, normed, inverse):
    mean_grad = jnp.mean(grad, axis=-1, keepdims=True)
    mean_proj = jnp.mean(grad * normed, axis=-1, keepdims=True)
    return inverse * (grad - mean_grad - normed * mean_proj)


def adam(master, first, second, grad):
    first_new = BETA_ONE * first + (1.0 - BETA_ONE) * grad
    second_new = BETA_TWO * second + (1.0 - BETA_TWO) * grad * grad
    fix_one = 1.0 - BETA_ONE**STEP
    fix_two = 1.0 - BETA_TWO**STEP
    update = first_new * (1.0 / fix_one) / (jnp.sqrt(second_new * (1.0 / fix_two)) + ADAM_EPS) + DECAY * master
    return (master - RATE * update, first_new, second_new)


def gelu_both(value):
    square = value * value
    tanh = jnp.tanh(value * (GELU_CUBE * square + GELU_LIN))
    half = 0.5 * tanh + 0.5
    act = value * half
    slope = half + act * (1.0 - tanh) * (3.0 * GELU_CUBE * square + GELU_LIN)
    return act, slope


def dp_sizes(count):
    side = 4 if count >= 64 else 2
    return count // (side * side), side


class Place:
    def __init__(self, count):
        self.count = count
        self.depth, self.side = dp_sizes(count)
        self.dp = lax.axis_index("dp")
        self.mp = lax.axis_index("mp")
        side = self.side
        y = (self.dp // side) % side
        x = self.dp % side
        self.at = {
            "z": self.dp // (side * side),
            "a": jnp.where(self.mp == 0, y, x),
            "b": jnp.where(self.mp == 0, x, y),
        }
        self.size = {"z": self.depth, "a": side, "b": side}
        self.near = {axis: self.peers(axis) for axis in "zab"}
        self.first, self.others = {}, {}
        for order in (ZBA, BZA):
            for stage, axis in enumerate(order):
                fixed = {name: self.at[name] for name in order[stage:]}
                self.first[order, stage] = self.slot_at(order, fixed)
                self.others[order, stage] = [
                    self.slot_at(order, {**fixed, axis: self.along(axis, k)}) for k in range(1, self.size[axis])
                ]
        z = self.at["z"]
        self.line = self.depth == 4
        self.end = (z == 0) | (z == 3)
        self.next_end = jnp.where(z < 2, 0, 3)
        self.inside = jnp.where(z < 2, 1, 2)
        self.far_end = 3 - self.next_end

    def slot_at(self, order, at):
        slot = 0
        for axis in reversed(order):
            slot = slot * self.size[axis] + at.get(axis, 0)
        return slot

    def slot(self, order=ZBA):
        return self.first[order, 0]

    def slot_of(self, dp, core, order=ZBA):
        side = self.side
        z, y, x = dp // (side * side), (dp // side) % side, dp % side
        one = self.slot_at(order, {"z": z, "a": y, "b": x})
        two = self.slot_at(order, {"z": z, "a": x, "b": y})
        return jnp.where(core == 0, one, two)

    def device(self, at):
        z, a, b = at["z"], at["a"], at["b"]
        side = self.side
        dp = jnp.where(self.mp == 0, (z * side + a) * side + b, (z * side + b) * side + a)
        return (dp, self.mp)

    def along(self, axis, step):
        return (self.at[axis] + step) % self.size[axis]

    def peers(self, axis):
        return [self.device({**self.at, axis: self.along(axis, k)}) for k in range(1, self.size[axis])]

    def other_core(self):
        return (self.dp, 1 - self.mp)

    def peers_layer(self):
        layer = self.side * self.side
        first = self.dp - self.dp % layer
        peers = []
        for k in range(1, 2 * layer):
            spot = (self.dp % layer * 2 + self.mp + k) % (2 * layer)
            peers.append((first + spot // 2, spot % 2))
        return peers

    def greet(self):
        peers = self.near["z"] + self.peers_layer()
        barrier = pltpu.get_barrier_semaphore()
        for peer in peers:
            pl.semaphore_signal(barrier, inc=1, device_id=peer, device_id_type=MESH)
        return lambda: pl.semaphore_wait(barrier, len(peers))


def remote(src, dst, send, recv, peer):
    return pltpu.make_async_remote_copy(
        src_ref=src, dst_ref=dst, send_sem=send, recv_sem=recv, device_id=peer, device_id_type=MESH
    )


def span(place, order, stage):
    return math.prod(place.size[axis] for axis in order[:stage])


class Gather:
    def __init__(self, place, buf, send, recv, order=ZBA, relay=False):
        self.p, self.buf, self.send, self.recv, self.order = place, buf, send, recv, order
        self.relayed = relay and place.line

    def copies(self, stage, e):
        p, order = self.p, self.order
        src = self.buf.at[e, pl.ds(p.first[order, stage], span(p, order, stage))]
        base = sum(p.size[axis] - 1 for axis in order[:stage])
        return [
            remote(src, src, self.send.at[e, base + k], self.recv.at[e, base + k], peer)
            for k, peer in enumerate(p.near[order[stage]])
        ]

    def passed(self, e):
        p, order = self.p, self.order
        stage = order.index("z")
        base = sum(p.size[axis] - 1 for axis in order[:stage])
        fixed = {name: p.at[name] for name in order[stage:]}
        src = self.buf.at[e, pl.ds(p.slot_at(order, {**fixed, "z": p.far_end}), span(p, order, stage))]
        extra = sum(size - 1 for size in p.size.values())
        recv = self.recv.at[e, base + jnp.where(p.next_end == 0, 0, 2)]
        return remote(src, src, self.send.at[e, extra], recv, p.device({**p.at, "z": p.next_end}))

    def each(self, stage, e, act):
        for k, copy in enumerate(self.copies(stage, e)):
            if self.relayed and self.order[stage] == "z" and k != 1:
                pl.when(self.p.at["z"] != (3 if k == 0 else 0))(functools.partial(act, copy))
            else:
                act(copy)

    def start(self, stage, e):
        self.each(stage, e, lambda copy: copy.start())

    def relay(self, e):
        if self.relayed:

            @pl.when(~self.p.end)
            def _():
                self.copies(self.order.index("z"), e)[1].wait_recv()
                self.passed(e).start()

    def arrive(self, stage, e):
        for k, copy in enumerate(self.copies(stage, e)):
            if self.relayed and self.order[stage] == "z" and k == 1:
                pl.when(self.p.end)(copy.wait_recv)
            else:
                copy.wait_recv()

    def sent(self, e):
        for stage in range(3):
            self.each(stage, e, lambda copy: copy.wait_send())
        if self.relayed:
            pl.when(~self.p.end)(lambda: self.passed(e).wait_send())


class Scatter:
    def __init__(self, place, buf, boxes, send, recv, order=ZBA, relay=False):
        self.p, self.buf, self.boxes, self.send, self.recv, self.order = place, buf, boxes, send, recv, order
        self.relayed = relay and place.line

    def box(self, stage, e, block, many):
        box = self.boxes[min(stage, 1)]
        if stage >= 2:
            order = self.order
            block = block + (self.p.size[order[1]] - 1) * span(self.p, order, 1)
        if stage == 3:
            block = block + self.p.size[self.order[0]] - 1
        return box.at[e % box.shape[0], pl.ds(block, many)]

    def copies(self, stage, e):
        p, order = self.p, self.order
        axis, many = order[2 - stage], span(p, order, 2 - stage)
        sem = sum(p.size[order[2 - before]] - 1 for before in range(stage))
        made = []
        for k, peer in enumerate(p.near[axis]):
            src = self.buf.at[e, pl.ds(p.others[order, 2 - stage][k], many)]
            dst = self.box(stage, e, k * many, many)
            made.append(remote(src, dst, self.send.at[e, sem + k], self.recv.at[e, sem + k], peer))
        return made

    def passed(self, e):
        p, order = self.p, self.order
        at = order.index("z")
        many = span(p, order, at)
        fixed = {name: p.at[name] for name in order[at:]}
        src = self.buf.at[e, pl.ds(p.slot_at(order, {**fixed, "z": p.far_end}), many)]
        extra = sum(size - 1 for size in p.size.values())
        peer = p.device({**p.at, "z": p.inside})
        return remote(src, self.box(3, e, 0, many), self.send.at[e, extra], self.recv.at[e, extra], peer)

    def on_line(self, stage):
        return self.relayed and self.order[2 - stage] == "z"

    def start(self, stage, e):
        for k, copy in enumerate(self.copies(stage, e)):
            if self.on_line(stage):
                here = self.p.end if k == 1 else self.p.at["z"] != (3 if k == 0 else 0)
                pl.when(here)(copy.start)
            else:
                copy.start()
        if self.on_line(stage):
            pl.when(self.p.end)(lambda: self.passed(e).start())

    def relay(self, e):
        if self.relayed:
            stage = 2 - self.order.index("z")
            many = span(self.p, self.order, 2 - stage)

            @pl.when(~self.p.end)
            def _():
                self.passed(e).wait_recv()
                to = self.p.others[self.order, 2 - stage][1]
                for i in range(many):
                    total = self.buf[e, to + i].astype(f32) + self.box(3, e, i, 1)[0].astype(f32)
                    self.buf[e, to + i] = total.astype(bf16)
                self.copies(stage, e)[1].start()

    def arrive(self, stage, e):
        for k, copy in enumerate(self.copies(stage, e)):
            if self.on_line(stage) and k != 1:
                pl.when(self.p.at["z"] != (3 if k == 0 else 0))(copy.wait_send)
                pl.when(self.p.at["z"] != (0 if k == 0 else 3))(copy.wait_recv)
            else:
                copy.wait()
        if self.on_line(stage):
            pl.when(self.p.end)(lambda: self.passed(e).wait_send())

    def total(self, stage, e, i):
        p, order = self.p, self.order
        many = span(p, order, 2 - stage)
        total = self.buf[e, p.first[order, 2 - stage] + i].astype(f32)
        for k in range(p.size[order[2 - stage]] - 1):
            term = self.box(stage, e, k * many + i, 1)[0].astype(f32)
            if self.on_line(stage) and k != 1:
                term = jnp.where(p.at["z"] != (0 if k == 0 else 3), term, 0.0)
            total = total + term
        return total

    def add(self, stage, e):
        def one(i, carry):
            self.buf[e, self.p.first[self.order, 2 - stage] + i] = self.total(stage, e, i).astype(bf16)
            return carry

        lax.fori_loop(0, span(self.p, self.order, 2 - stage), one, 0)

    def last(self, e):
        return self.total(2, e, 0)


def block_rows(rows, parts):
    return (parts * rows + SUB - 1) // SUB * SUB


def blocks_to_weights(place, rows, buf, core, outs, order=ZBA):
    many = SUB // math.gcd(SUB, rows)
    for first in range(0, place.count, many):
        blocks = [buf[place.slot_of(first + i, core, order)].astype(f32) for i in range(many)]
        for part, out in enumerate(outs):
            pieces = [block[part * rows : (part + 1) * rows] for block in blocks]
            out[pl.ds(first * rows, many * rows), :] = jnp.concatenate(pieces, axis=0).astype(bf16)


def grads_to_blocks(place, rows, grads, buf, order=ZBA):
    block = buf.shape[1]
    for dp in range(place.count):
        pieces = [grad[dp * rows : (dp + 1) * rows, :] for grad in grads]
        if block > rows * len(grads):
            pieces.append(jnp.zeros((block - rows * len(grads), buf.shape[2]), f32))
        buf[place.slot_of(dp, place.mp, order)] = jnp.concatenate(pieces, axis=0).astype(bf16)


def all_sum(place, value, src, box, send, recv):
    layer = place.side * place.side
    spot = place.dp % layer
    z = place.at["z"]
    src[0] = value
    box[z] = value
    copies = [
        remote(src.at[0], box.at[z], send.at[k], recv.at[k], peer) for k, peer in enumerate(place.near["z"])
    ]
    for copy in copies:
        copy.start()
    for copy in copies:
        copy.wait()
    total = box[0]
    for i in range(1, place.depth):
        total = total + box[i]
    mine = spot * 2 + place.mp
    base = place.depth
    src[1] = total
    box[base + mine] = total
    at = place.depth - 1
    copies = [
        remote(src.at[1], box.at[base + mine], send.at[at + k], recv.at[at + k], peer)
        for k, peer in enumerate(place.peers_layer())
    ]
    for copy in copies:
        copy.start()
    for copy in copies:
        copy.wait()
    total = box[base]
    for i in range(1, 2 * layer):
        total = total + box[base + i]
    return total


def block_kernel(
    count, rows, experts, tile, lag,
    tok_ref, cot_ref, cond_ref, route_ref, ada_ref, gate_ref, attn_ref, w_ref,
    output_ref, grad_tok_ref, ada_out, attn_out, total_ref, norm_out,
    buf_one, buf_two, box_one, rest_one, box_two, rest_two,
    ada_one, ada_two, sc_buf, mod_buf, mod_far, attn_buf, attn_box, attn_rest, attn_far, attn_w,
    cond_low, mod_one, mod_two, grad_mod, grad_mod_in, triple, mixed, h_one, soft,
    h_all, d_all, gate_all, branch_acc, grad_h_acc, grad_gate_acc, gate_in, share_in,
    up_w, down_w, up_grad, down_grad, gate_grad, attn_share, attn_in, norm_src, norm_box,
    w_hold, total_hold, load_sem, gather_send, gather_recv, gather_send_two, gather_recv_two,
    scatter_send, scatter_recv, scatter_send_two, scatter_recv_two,
    ada_send, ada_recv, more_send, more_recv, sc_send, sc_recv, mod_send, mod_recv, attn_send, attn_recv, attn_back_send, attn_back_recv,
    core_send, core_recv, token_send, token_recv, norm_send, norm_recv,
):
    place = Place(count)
    met = place.greet()
    mp = place.mp
    wide_experts = w_ref.shape[1]
    own_tok, width = tok_ref.shape
    images = own_tok // PATCH
    half = attn_ref.shape[2]
    first = half // LANES * LANES
    heads = half // HD
    wide = ada_ref.shape[1] // 2
    cut = mod_buf.shape[3]
    scale = HD ** (-0.5)
    own_at = pl.multiple_of(mp * own_tok, own_tok)
    their_at = pl.multiple_of((1 - mp) * own_tok, own_tok)
    own, theirs = pl.ds(own_at, own_tok), pl.ds(their_at, own_tok)
    other = place.other_core()

    loads = [
        pltpu.make_async_copy(tok_ref, branch_acc.at[pl.ds(0, own_tok)], load_sem.at[0]),
        pltpu.make_async_copy(cot_ref, branch_acc.at[pl.ds(own_tok, own_tok)], load_sem.at[1]),
    ]
    w_load = pltpu.make_async_copy(w_ref, w_hold, load_sem.at[2])
    w_load.start()
    for load in loads:
        load.start()

    def put(target, block, order=ZBA):
        if block.shape[0] != target.shape[1]:
            target[place.slot(order)] = jnp.zeros(target.shape[1:], bf16)
        target[place.slot(order), pl.ds(0, block.shape[0])] = block

    put(ada_one.at[0], ada_ref[:, pl.ds(pl.multiple_of(mp * width, LANES), width)].astype(bf16))
    cols = ada_ref[:, pl.ds(pl.multiple_of((1 + mp) * 2 * width, LANES), 2 * width)]
    put(ada_two.at[0], jnp.concatenate([cols[:, :width], cols[:, width:]], axis=0).astype(bf16))
    parts = attn_ref.shape[0]
    side_by = lax.broadcasted_iota(jnp.int32, (experts, LANES), 1) == lax.broadcasted_iota(
        jnp.int32, (experts, LANES), 0
    )
    gate = mxu(gate_ref[...].astype(bf16), side_by.astype(f32).astype(bf16), TN)[:, : 2 * LANES - half]
    spare = [gate] + [jnp.zeros_like(gate)] * (parts - 1)
    both = [jnp.concatenate([attn_ref[j], spare[j]], axis=1) for j in range(parts)]
    pair = parts // 2
    for i in range(2):
        put(attn_buf.at[i], jnp.concatenate(both[i * pair : (i + 1) * pair], axis=0).astype(bf16))
    cond = cond_ref[...]
    cond = cond / (1.0 + jnp.exp(-cond))
    cond_low[...] = cond.astype(bf16)
    sc_buf[0, place.slot()] = jnp.concatenate([cond, jnp.zeros((SUB - cond.shape[0], width), f32)], axis=0).astype(bf16)
    met()
    ada_gather = Gather(place, ada_one, ada_send, ada_recv)
    more_gather = Gather(place, ada_two, more_send, more_recv)
    attn_gather = Gather(place, attn_buf, attn_send, attn_recv)
    cuts = (pl.ds(0, buf_one.shape[3]), pl.ds(buf_one.shape[3], buf_two.shape[3]))
    streams = tuple(zip((buf_one, buf_two), cuts, (ZBA, BZA)))
    gathers = (
        Gather(place, buf_one, gather_send, gather_recv, ZBA, True),
        Gather(place, buf_two, gather_send_two, gather_recv_two, BZA, True),
    )
    scatters = (
        Scatter(place, buf_one, (box_one, rest_one), scatter_send, scatter_recv, ZBA, True),
        Scatter(place, buf_two, (box_two, rest_two), scatter_send_two, scatter_recv_two, BZA, True),
    )
    sc_gather = Gather(place, sc_buf, sc_send, sc_recv)
    ada_gather.start(0, 0)
    attn_gather.start(0, 0)
    attn_gather.start(0, 1)
    more_gather.start(0, 0)
    sc_gather.start(0, 0)

    def fill(e, carry):
        both = jnp.concatenate([w_hold[0, e], w_hold[1, e]], axis=0).astype(bf16)
        for buf, lanes, order in streams:
            put(buf.at[e], both[:, lanes.start : lanes.start + lanes.size], order)
        return carry

    w_load.wait()
    lax.fori_loop(0, wide_experts, fill, 0)

    def begin(e):
        for one in gathers:
            one.start(0, e)

    def onward(stage, e):
        for one in gathers:
            one.arrive(stage, e)
            one.start(stage + 1, e)

    def tick(k):
        pl.when(k + 6 < wide_experts)(lambda: begin(k + 6))
        pl.when(k + 4 < wide_experts)(lambda: gathers[0].relay(k + 4))
        pl.when(k + 3 < wide_experts)(lambda: onward(0, k + 3))
        pl.when(k + 2 < wide_experts)(lambda: gathers[1].relay(k + 2))
        pl.when((k >= 0) & (k < wide_experts))(lambda: onward(1, k))

    grad_mod[...] = jnp.zeros_like(grad_mod)
    items = ((ada_gather, 0), (attn_gather, 0), (attn_gather, 1), (more_gather, 0))

    def wave(w):
        for i in (w, w - 1):
            if 0 <= i < len(items):
                small, which = items[i]
                small.arrive(w - i, which)
                small.start(w - i + 1, which)

    for w in range(len(items)):
        wave(w)
    begin(0)
    begin(1)
    width_lanes = pl.ds(0, width)
    ada_gather.arrive(2, 0)

    blocks_to_weights(place, rows, ada_one.at[0], mp, (up_w.at[:, width_lanes],))
    mod_one[mp] = mxu(cond_low[...], up_w[:, width_lanes])
    mod_cross = [
        remote(ref.at[mp], ref.at[mp], core_send.at[i], core_recv.at[i], other)
        for i, ref in ((1, mod_one), (0, mod_two))
    ]
    mod_cross[0].start()
    wave(len(items))
    attn_cross = []
    for i in range(2):
        attn_gather.arrive(2, i)
        attn_cross.append(
            remote(attn_buf.at[i], attn_far.at[i], core_send.at[8 + i], core_recv.at[8 + i], other)
        )
        attn_cross[i].start()
        outs = [attn_w.at[mp, j] for j in range(i * pair, (i + 1) * pair)]
        blocks_to_weights(place, rows, attn_buf.at[i], mp, outs)
    for load in loads:
        load.wait()
    ada_gather.sent(0)
    attn_gather.sent(0)
    attn_gather.sent(1)
    begin(2)
    begin(3)
    begin(4)
    gathers[0].relay(0)
    onward(0, 0)
    sc_gather.arrive(0, 0)
    sc_gather.start(1, 0)
    for i in range(2):
        attn_cross[i].wait()
        outs = [attn_w.at[1 - mp, j] for j in range(i * pair, (i + 1) * pair)]
        blocks_to_weights(place, rows, attn_far.at[i], 1 - mp, outs)
    mod_cross[0].wait()
    gathers[0].relay(1)
    onward(0, 1)
    gathers[0].relay(2)
    gathers[1].relay(0)
    gate_lanes = pl.ds(first, LANES)
    half_lanes = pl.ds(0, half)

    def weight(core, j):
        return attn_w[core, j, :, half_lanes]

    lane_pair = lax.broadcasted_iota(jnp.int32, (PATCH, 2 * HD), 1)
    masks = [(lane_pair < HD).astype(f32).astype(bf16), (lane_pair >= HD).astype(f32).astype(bf16)]
    groups = [(at, min(2, heads - at)) for at in range(0, heads, 2)]
    expert_lane = lax.broadcasted_iota(jnp.int32, (PATCH, LANES), 1) - (half - first)

    def mod_row(image, vector):
        row = pl.ds(mp * images + image, 1)
        if vector < 2:
            return mod_one[vector, row, :]
        return mod_two[vector // 2 - 1, row, pl.ds(vector % 2 * width, width)]

    def add_grad_mod(image, vector, value):
        grad_mod[vector // 3, pl.ds(mp * images + image, 1), pl.ds(vector % 3 * width, width)] = value

    def one_head(value, group, head):
        return value if group[1] == 1 else value * masks[head]

    def route(h, image):
        valid = (expert_lane >= 0) & (expert_lane < experts)
        logits = jnp.where(valid, mxu(h, attn_w[0, 0, :, gate_lanes]), -jnp.inf)
        power = jnp.exp(logits - jnp.max(logits, axis=1, keepdims=True))
        router = power / jnp.sum(power, axis=1, keepdims=True)
        picks = route_ref[:, pl.ds(pl.multiple_of(own_at + image * PATCH, PATCH), PATCH)]
        spot = lax.broadcasted_iota(jnp.int32, (LANES, PATCH), 0) - (half - first)
        picked = jnp.where((picks[0:1, :] == spot) | (picks[1:2, :] == spot), 1.0, 0.0)
        return router, picked.T

    def attend(at):
        return mxu(mixed[0, at, :], weight(0, 3), NT) + mxu(mixed[1, at, :], weight(1, 3), NT)

    def token_copies(image):
        at = pl.ds(pl.multiple_of(own_at + image * PATCH, PATCH), PATCH)
        return [
            remote(ref.at[at], ref.at[at], token_send.at[image, i], token_recv.at[image, i], other)
            for i, ref in enumerate((h_all, d_all, gate_all))
        ]

    def attention(image, carry):
        at = pl.ds(pl.multiple_of(image * PATCH, PATCH), PATCH)
        normed, _ = layer_norm(branch_acc[at, :])
        h = (normed * (1.0 + mod_row(image, 1)) + mod_row(image, 0)).astype(bf16)
        h_one[at, :] = h
        for core in range(2):
            for j in range(3):
                triple[core, j, at, :] = mxu(h, weight(core, j)).astype(bf16)
            for group in groups:
                lanes = pl.ds(group[0] * HD, group[1] * HD)
                query, key, value = (triple[core, j, at, lanes] for j in range(3))
                total = 0.0
                for head in range(group[1]):
                    scores = mxu(one_head(query, group, head), key, NT) * scale
                    power = jnp.exp(scores - jnp.max(scores, axis=1, keepdims=True))
                    low = (power * (1.0 / jnp.sum(power, axis=1, keepdims=True))).astype(bf16)
                    soft[image, core * heads + group[0] + head] = low
                    total = total + mxu(low, one_head(value, group, head))
                mixed[core, at, lanes] = total.astype(bf16)
        tick(image - 1)

        @pl.when(image == 0)
        def _():
            sc_gather.arrive(1, 0)
            sc_gather.start(2, 0)

        return carry

    lax.fori_loop(0, images, attention, 0)
    more_gather.arrive(2, 0)
    blocks_to_weights(place, rows, ada_two.at[0], mp, (up_w.at[:, width_lanes], down_w.at[:, width_lanes]))
    mod_two[mp, :, pl.ds(0, width)] = mxu(cond_low[...], up_w[:, width_lanes])
    mod_two[mp, :, pl.ds(width, width)] = mxu(cond_low[...], down_w[:, width_lanes])
    mod_cross[1].start()
    more_gather.sent(0)
    mod_cross[1].wait()

    def forward(image, carry):
        at = pl.ds(pl.multiple_of(image * PATCH, PATCH), PATCH)
        cot_at = pl.ds(pl.multiple_of(own_tok + image * PATCH, PATCH), PATCH)
        all_at = pl.ds(pl.multiple_of(own_at + image * PATCH, PATCH), PATCH)
        x_one = branch_acc[at, :] + mod_row(image, 2) * attend(at)
        normed, _ = layer_norm(x_one)
        h = (normed * (1.0 + mod_row(image, 4)) + mod_row(image, 3)).astype(bf16)
        h_all[all_at, :] = h
        router, chosen = route(h, image)
        shared = (expert_lane >= experts) & (expert_lane < wide_experts)
        gate_all[all_at, :] = jnp.where(shared, 1.0, router * chosen)
        d_all[all_at, :] = (branch_acc[cot_at, :] * mod_row(image, 5)).astype(bf16)
        for copy in token_copies(image):
            copy.start()

        return carry

    lax.fori_loop(0, images, forward, 0)
    ahead = images - 1
    sc_gather.arrive(2, 0)
    sc_gather.sent(0)

    branch_acc[...] = jnp.zeros_like(branch_acc)
    grad_h_acc[...] = jnp.zeros_like(grad_h_acc)
    grad_gate_acc[...] = jnp.zeros_like(grad_gate_acc)

    def all_tokens(image, carry):
        for copy in token_copies(image):
            copy.wait()
        return carry

    lax.fori_loop(0, images, all_tokens, 0)

    shares = [
        remote(h_all.at[theirs], share_in.at[0], core_send.at[2], core_recv.at[2], other),
        remote(d_all.at[theirs], share_in.at[1], core_send.at[3], core_recv.at[3], other),
        remote(grad_gate_acc.at[theirs], gate_in, core_send.at[4], core_recv.at[4], other),
    ]
    loads = [
        pltpu.make_async_copy(tok_ref, branch_acc.at[theirs], load_sem.at[0]),
        pltpu.make_async_copy(cot_ref, grad_h_acc.at[theirs], load_sem.at[1]),
    ]
    tiles = h_all.shape[0] // tile

    def compute(e):
        for buf, lanes, order in streams:
            blocks_to_weights(place, rows, buf.at[e], mp, (up_w.at[:, lanes], down_w.at[:, lanes]), order)
        up_grad[...] = jnp.zeros_like(up_grad)
        down_grad[...] = jnp.zeros_like(down_grad)

        def one_tile(t, carry):
            @pl.when((e == wide_experts - 1) & (t == tiles // 2))
            def _():
                h_all[theirs, :] = branch_acc[theirs, :].astype(bf16)
                d_all[theirs, :] = grad_h_acc[theirs, :].astype(bf16)
                for copy in shares:
                    copy.start()
                for copy in loads:
                    copy.start()

            at = pl.ds(pl.multiple_of((t + (1 - mp) * (tiles // 2)) % tiles * tile, tile), tile)
            h = h_all[at, :]
            d = d_all[at, :]
            lane = lax.broadcasted_iota(jnp.int32, (tile, LANES), 1) - (half - first)
            gate = jnp.sum(jnp.where(lane == e, gate_all[at, :], 0.0), axis=1, keepdims=True)
            pre = mxu(h, up_w[...])
            back = mxu(d, down_w[...])
            act, slope = gelu_both(pre)
            inner = jnp.sum(act * back, axis=1, keepdims=True)
            grad_gate_acc[at, :] += jnp.where(lane == e, inner, 0.0)
            act_low = (gate * act).astype(bf16)
            pre_low = (gate * back * slope).astype(bf16)
            branch_acc[at, :] += mxu(act_low, down_w[...], NT)
            grad_h_acc[at, :] += mxu(pre_low, up_w[...], NT)
            up_grad[...] += mxu(h, pre_low, TN)
            down_grad[...] += mxu(d, act_low, TN)
            return carry

        lax.fori_loop(0, tiles, one_tile, 0)

    def follow(one, stage, e):
        one.arrive(stage, e)
        one.add(stage, e)
        one.start(stage + 1, e)

    def finish(e):
        for one, (_, lanes, _) in zip(scatters, streams):
            one.arrive(2, e)
            total_hold[e, :, lanes] = one.last(e)

    def collect(k):
        def at(late, act):
            pl.when((k >= late) & (k - late < wide_experts))(lambda: act(k - late))

        at(4, finish)
        at(3, scatters[0].relay)
        at(3, lambda e: follow(scatters[1], 1, e))
        at(2, lambda e: follow(scatters[0], 1, e))
        at(2, scatters[1].relay)
        at(1, lambda e: [follow(one, 0, e) for one in scatters] and None)

    def step(e, carry):
        tick(e + ahead)
        for one in gathers:
            one.arrive(2, e)
        compute(e)
        for one in gathers:
            one.sent(e)
        for buf, lanes, order in streams:
            grads_to_blocks(place, rows, (up_grad.at[:, lanes], down_grad.at[:, lanes]), buf.at[e], order)
        for one in scatters:
            one.start(0, e)
        collect(e - lag)
        return carry

    lax.fori_loop(0, wide_experts, step, 0)

    row = lax.broadcasted_iota(jnp.int32, (width, LANES), 0)
    lane = lax.broadcasted_iota(jnp.int32, (width, LANES), 1)
    pick = ((row == place.dp * rows + lane) & (lane < rows)).astype(f32).astype(bf16)
    group = cond_ref.shape[0]

    def in_order(ref, core, at):
        pieces = [ref[place.slot_of(dp, core)].astype(f32)[at : at + group] for dp in range(count)]
        return jnp.concatenate(pieces, axis=0).astype(bf16)

    conds = mxu(in_order(sc_buf.at[0], mp, 0), pick).astype(bf16)

    gate_grad[...] = jnp.zeros_like(gate_grad)
    for copy in shares + loads:
        copy.wait()

    def backward(image, carry):
        at = pl.ds(pl.multiple_of(image * PATCH, PATCH), PATCH)
        own_rows = pl.ds(pl.multiple_of(own_at + image * PATCH, PATCH), PATCH)
        load_rows = pl.ds(pl.multiple_of(their_at + image * PATCH, PATCH), PATCH)
        tok, cot = branch_acc[load_rows, :], grad_h_acc[load_rows, :]
        branch = branch_acc[own_rows, :] + share_in[0, at, :].astype(f32)
        attention = attend(at)
        x_one = tok + mod_row(image, 2) * attention
        normed, inverse = layer_norm(x_one)
        branch_acc[own_rows, :] = x_one + mod_row(image, 5) * branch
        add_grad_mod(image, 5, jnp.sum(cot * branch, axis=0, keepdims=True))
        h = h_all[own_rows, :]
        router, chosen = route(h, image)
        grad_router = (grad_gate_acc[own_rows, :] + gate_in[at, :]) * chosen
        grad_logits = (router * (grad_router - jnp.sum(router * grad_router, axis=1, keepdims=True))).astype(bf16)
        gate_grad[...] += mxu(h, grad_logits, TN)
        grad_h = grad_h_acc[own_rows, :] + share_in[1, at, :].astype(f32) + mxu(grad_logits, attn_w[0, 0, :, gate_lanes], NT)
        add_grad_mod(image, 3, jnp.sum(grad_h, axis=0, keepdims=True))
        add_grad_mod(image, 4, jnp.sum(grad_h * normed, axis=0, keepdims=True))
        grad_x = cot + norm_back(grad_h * (1.0 + mod_row(image, 4)), normed, inverse)
        add_grad_mod(image, 2, jnp.sum(grad_x * attention, axis=0, keepdims=True))
        grad_att = (grad_x * mod_row(image, 2)).astype(bf16)
        d_all[own_rows, :] = grad_att
        grad_h_one = 0.0
        for core in range(2):
            grad_mixed = mxu(grad_att, weight(core, 3)).astype(bf16)
            for group in groups:
                lanes = pl.ds(group[0] * HD, group[1] * HD)
                query, key, value = (triple[core, j, at, lanes] for j in range(3))
                back = grad_mixed[:, group[0] * HD : (group[0] + group[1]) * HD]
                grads = [0.0, 0.0, 0.0]
                for head in range(group[1]):
                    low = soft[image, core * heads + group[0] + head]
                    prob = low.astype(f32)
                    head_back = one_head(back, group, head)
                    grad_soft = mxu(head_back, value, NT)
                    delta = jnp.sum(prob * grad_soft, axis=1, keepdims=True)
                    grad_scores = (prob * (grad_soft - delta) * scale).astype(bf16)
                    grads[0] = grads[0] + mxu(grad_scores, one_head(key, group, head))
                    grads[1] = grads[1] + mxu(grad_scores, one_head(query, group, head), TN)
                    grads[2] = grads[2] + mxu(low, head_back, TN)
                for j in range(3):
                    triple[core, j, at, lanes] = grads[j].astype(bf16)
            for j in range(3):
                grad_h_one = grad_h_one + mxu(triple[core, j, at, :], weight(core, j), NT)
        normed, inverse = layer_norm(tok)
        add_grad_mod(image, 0, jnp.sum(grad_h_one, axis=0, keepdims=True))
        add_grad_mod(image, 1, jnp.sum(grad_h_one * normed, axis=0, keepdims=True))
        grad_h_acc[own_rows, :] = grad_x + norm_back(grad_h_one * (1.0 + mod_row(image, 1)), normed, inverse)

        @pl.when(image > 0)
        def _():
            collect(wide_experts - lag + image - 1)

        return carry

    lax.fori_loop(0, images, backward, 0)
    stores = [
        pltpu.make_async_copy(branch_acc.at[own], output_ref, load_sem.at[2]),
        pltpu.make_async_copy(grad_h_acc.at[own], grad_tok_ref, load_sem.at[3]),
    ]
    for copy in stores:
        copy.start()

    crosses = [
        remote(grad_mod.at[1 - mp], grad_mod_in, core_send.at[5], core_recv.at[5], other),
        *[
            remote(
                attn_share.at[pl.ds(i * pair, pair)], attn_in.at[pl.ds(i * pair, pair)],
                core_send.at[6 + i], core_recv.at[6 + i], other,
            )
            for i in range(2)
        ],
        remote(mod_buf.at[0], mod_far, core_send.at[1], core_recv.at[1], other),
    ]
    crosses[0].start()

    def attn_grad(core, j):
        if j == parts - 1:
            return mxu(d_all[own, :], mixed[core], TN)
        return mxu(h_one[...], triple[core, j], TN)

    spare = pl.ds(half, 2 * LANES - half)
    places = [(up_grad, 0), (up_grad, 1), (up_grad, 2), (down_grad, 0)]
    attn_scatter = Scatter(place, attn_buf, (attn_box, attn_rest), attn_back_send, attn_back_recv)
    for i in range(2):
        for j in range(i * pair, (i + 1) * pair):
            attn_share[j, :, half_lanes] = attn_grad(1 - mp, j).astype(bf16)
            extra = gate_grad[:, pl.ds(half - first, 2 * LANES - half)].astype(bf16)
            attn_share[j, :, spare] = extra if j == 0 else jnp.zeros_like(extra)
        crosses[1 + i].start()
    crosses[0].wait()
    grad_low = grad_mod[mp] + grad_mod_in[...]
    mod_buf[0, place.slot()] = jnp.concatenate([grad_low[:, :cut], grad_low[:, cut:]], axis=0).astype(bf16)
    mod_gather = Gather(place, mod_buf, mod_send, mod_recv)
    for i in range(2):
        for j in range(i * pair, (i + 1) * pair):
            ref, at = places[j]
            ref[:, pl.ds(at * 2 * LANES, half)] = attn_grad(mp, j)
        crosses[1 + i].wait()
        grads = []
        for j in range(i * pair, (i + 1) * pair):
            ref, at = places[j]
            lanes = pl.ds(at * 2 * LANES, half)
            ref[:, lanes] += attn_in[j, :, half_lanes].astype(f32)
            extra = gate_grad[:, pl.ds(half - first, 2 * LANES - half)] + attn_in[0, :, spare].astype(f32)
            ref[:, pl.ds(at * 2 * LANES + half, 2 * LANES - half)] = extra if j == 0 else jnp.zeros_like(extra)
            grads.append(ref[:, pl.ds(at * 2 * LANES, 2 * LANES)])
        grads_to_blocks(place, rows, grads, attn_buf.at[i])
        attn_scatter.start(0, i)
    mod_gather.start(0, 0)
    left = list(range(wide_experts - lag + images - 1, wide_experts + 4))
    for stage in range(2):
        if len(left) > 1:
            collect(left.pop(0))
        for i in range(2):
            attn_scatter.arrive(stage, i)
            attn_scatter.add(stage, i)
            attn_scatter.start(stage + 1, i)
        mod_gather.arrive(stage, 0)
        mod_gather.start(stage + 1, 0)
    for k in left:
        collect(k)
    stores.append(pltpu.make_async_copy(total_hold, total_ref, load_sem.at[4]))
    stores[-1].start()
    square = jnp.zeros((1, 1), f32)
    for e in range(wide_experts):
        square = square + jnp.sum(total_hold[e] * total_hold[e])
    mod_gather.arrive(2, 0)
    crosses[3].start()
    def ada_grad(ref, core):
        low = mxu(conds, in_order(ref, core, 0), TN)[:rows]
        high = mxu(conds, in_order(ref, core, group), TN)[:rows, : wide - cut]
        start = pl.multiple_of(core * wide, LANES)
        ada_out[:, pl.ds(start, cut)] = low
        ada_out[:, pl.ds(pl.multiple_of(start + cut, LANES), wide - cut)] = high
        return jnp.sum(low * low) + jnp.sum(high * high)

    small = ada_grad(mod_buf.at[0], mp)
    mod_gather.sent(0)
    crosses[3].wait()
    small = small + ada_grad(mod_far, 1 - mp)
    square = square + 0.5 * small
    for i in range(2):
        attn_scatter.arrive(2, i)
        attn = attn_scatter.last(i)
        attn_out[i] = attn
        lane = lax.broadcasted_iota(jnp.int32, attn.shape, 1)
        square = square + jnp.sum(jnp.where(lane < half, 1.0, 0.5) * attn * attn)
    value = jnp.broadcast_to(square, norm_out.shape)
    norm_out[...] = all_sum(place, value, norm_src, norm_box, norm_send, norm_recv)
    for copy in stores:
        copy.wait()


def block_call(tokens, condition, cotangent, routes, w_ada, w_gate, w_attn, w_expert):
    count = lax.axis_size("dp")
    own_tok, width = tokens.shape
    rows, wide = w_ada.shape
    experts = w_gate.shape[0]
    parts, _, half = w_attn.shape
    _, wide_experts, _, hidden = w_expert.shape
    depth, side = dp_sizes(count)
    images = own_tok // PATCH
    cut = (wide // 4 + LANES - 1) // LANES * LANES
    spare = 2 * LANES
    block, ada_block, attn_block = block_rows(rows, 2), block_rows(rows, 2), block_rows(rows, parts // 2)
    tok = 2 * own_tok
    tile, lag = (TILE, 2) if count <= 16 else (TILE // 2, 0)
    vmem = pl.BlockSpec(memory_space=pltpu.VMEM)
    hbm = pl.BlockSpec(memory_space=pl.ANY)
    hops = depth + 2 * side - 3

    def sems(*shape):
        return pltpu.SemaphoreType.DMA(shape)

    def boxes(slots, order, height, lanes):
        size = {"z": depth, "a": side, "b": side}
        span = size[order[0]] * size[order[1]]
        first = (size[order[2]] - 1) * span
        extra = 0 if slots <= 2 else math.prod(size[axis] for axis in order[: order.index("z")])
        return [
            pltpu.VMEM((slots, first, height, lanes), bf16),
            pltpu.VMEM((min(slots, REST), span - 1 + extra, height, lanes), bf16),
        ]

    one = hidden * CUT_ONE // CUT_ALL // LANES * LANES
    two = hidden - one

    return pl.pallas_call(
        functools.partial(block_kernel, count, rows, experts, tile, lag),
        out_shape=(
            jax.ShapeDtypeStruct((own_tok, width), f32),
            jax.ShapeDtypeStruct((own_tok, width), f32),
            jax.ShapeDtypeStruct((rows, wide), f32),
            jax.ShapeDtypeStruct((2, attn_block, spare), f32),
            jax.ShapeDtypeStruct((wide_experts, block, hidden), f32),
            jax.ShapeDtypeStruct((8, LANES), f32),
        ),
        in_specs=[hbm, hbm] + [vmem] * 5 + [hbm],
        out_specs=(hbm, hbm, vmem, vmem, hbm, vmem),
        scratch_shapes=[
            pltpu.VMEM((wide_experts, count, block, one), bf16),
            pltpu.VMEM((wide_experts, count, block, two), bf16),
            *boxes(SLOTS + 2 * lag, ZBA, block, one),
            *boxes(SLOTS + 2 * lag, BZA, block, two),
            pltpu.VMEM((1, count, block_rows(rows, 1), width), bf16),
            pltpu.VMEM((1, count, ada_block, width), bf16),
            pltpu.VMEM((1, count, SUB, width), bf16),
            pltpu.VMEM((1, count, SUB, cut), bf16),
            pltpu.VMEM((count, SUB, cut), bf16),
            pltpu.VMEM((2, count, attn_block, spare), bf16),
            *boxes(2, ZBA, attn_block, spare),
            pltpu.VMEM((2, count, attn_block, spare), bf16),
            pltpu.VMEM((2, parts, width, spare), bf16),
            pltpu.VMEM(condition.shape, bf16),
            pltpu.VMEM((2, condition.shape[0], width), f32),
            pltpu.VMEM((2, condition.shape[0], 2 * width), f32),
            pltpu.VMEM((2, condition.shape[0], 2 * cut), f32),
            pltpu.VMEM((condition.shape[0], 2 * cut), f32),
            pltpu.VMEM((2, 3, own_tok, half), bf16),
            pltpu.VMEM((2, own_tok, half), bf16),
            pltpu.VMEM((own_tok, width), bf16),
            pltpu.VMEM((images, width // HD, PATCH, PATCH), bf16),
            pltpu.VMEM((tok, width), bf16),
            pltpu.VMEM((tok, width), bf16),
            pltpu.VMEM((tok, LANES), f32),
            pltpu.VMEM((tok, width), f32),
            pltpu.VMEM((tok, width), f32),
            pltpu.VMEM((tok, LANES), f32),
            pltpu.VMEM((own_tok, LANES), f32),
            pltpu.VMEM((2, own_tok, width), bf16),
            pltpu.VMEM((width, hidden), bf16),
            pltpu.VMEM((width, hidden), bf16),
            pltpu.VMEM((width, hidden), f32),
            pltpu.VMEM((width, hidden), f32),
            pltpu.VMEM((width, LANES), f32),
            pltpu.VMEM((parts, width, spare), bf16),
            pltpu.VMEM((parts, width, spare), bf16),
            pltpu.VMEM((2, 8, LANES), f32),
            pltpu.VMEM((depth + 2 * side * side, 8, LANES), f32),
            pltpu.VMEM(w_expert.shape, f32),
            pltpu.VMEM((wide_experts, block, hidden), f32),
            sems(5),
            *[sems(wide_experts, hops + 1)] * 8,
            *[sems(1, hops)] * 8,
            *[sems(2, hops)] * 4,
            sems(10),
            sems(10),
            sems(images, 3),
            sems(images, 3),
            sems(depth + 2 * side * side),
            sems(depth + 2 * side * side),
        ],
        compiler_params=pltpu.CompilerParams(collective_id=1, has_side_effects=True, vmem_limit_bytes=VMEM_BYTES),
        cost_estimate=pl.CostEstimate(
            flops=12 * tok * width * hidden * wide_experts, bytes_accessed=16 * w_expert.size, transcendentals=0
        ),
        name="block",
    )(tokens, cotangent, condition, routes, w_ada, w_gate, w_attn, w_expert)
def update_kernel(rows, half, output_ref, grad_tok_ref, expert_w, expert_m, expert_v, expert_ref, norm_ref, attn_ref, ada_ref, *refs):
    ada, gate, attn = (refs[3 * i : 3 * i + 3] for i in range(3))
    outs, (hold, held, grads, sem, token_sem) = refs[9:-5], refs[-5:]
    ada_new, gate_new, attn_new, expert_new = (outs[3 * i : 3 * i + 3] for i in range(4))
    expert = (expert_w, expert_m, expert_v)
    many = expert_w.shape[1] // 2
    chunks = [(part, h) for h in range(2) for part in range(2)]
    grad_loads = [
        pltpu.make_async_copy(expert_ref.at[pl.ds(h * many, many)], grads.at[pl.ds(h * many, many)], token_sem.at[4 + h])
        for h in range(2)
    ]

    def moves(c, refs, back):
        part, h = chunks[c]
        made = []
        for i, ref in enumerate(refs):
            far, near = ref.at[part, pl.ds(h * many, many)], held.at[i, part, pl.ds(h * many, many)]
            made.append(pltpu.make_async_copy(*((near, far) if back else (far, near)), sem.at[int(back), c, i]))
        return made

    for c in range(4):
        if chunks[c][0] == 0:
            grad_loads[chunks[c][1]].start()
        for copy in moves(c, expert, False):
            copy.start()
    token_loads = [pltpu.make_async_copy(ref, hold.at[i], token_sem.at[i]) for i, ref in enumerate((output_ref, grad_tok_ref))]
    token_stores = [pltpu.make_async_copy(hold.at[i], outs[13 + i], token_sem.at[2 + i]) for i in range(2)]
    for copy in token_loads:
        copy.start()
    total = jnp.sqrt(norm_ref[...])
    outs[12][0, 0] = jnp.max(total)
    factor = jnp.minimum(1.0, CLIP_NORM / (total[0:1, 0:1] + 1e-06))

    def write(ins, news, at, grad):
        for new, value in zip(news, adam(ins[0][at], ins[1][at], ins[2][at], grad * factor)):
            new[at] = value

    everything = (slice(None), slice(None))
    write(ada, ada_new, everything, ada_ref[...])
    first = half // LANES * LANES
    small = attn_ref[0, pl.ds(0, rows), pl.ds(first, LANES)]
    square = jnp.concatenate([small, jnp.zeros((LANES - rows, LANES), f32)], axis=0).T
    experts = gate[0].shape[0]
    write(gate, gate_new, everything, square[half - first : half - first + experts, :rows])
    parts = attn[0].shape[0]
    for j in range(parts):
        grad = attn_ref[j // (parts // 2), pl.ds(j % (parts // 2) * rows, rows), pl.ds(0, half)]
        write(attn, attn_new, (j,), grad)
    here = [held.at[i] for i in range(3)]
    for c, (part, h) in enumerate(chunks):
        if part == 0:
            grad_loads[h].wait()
        for copy in moves(c, expert, False):
            copy.wait()

        def one(e, carry):
            write(here, here, (part, e), grads[e, pl.ds(part * rows, rows), :])
            return carry

        lax.fori_loop(h * many, (h + 1) * many, one, 0)
        for copy in moves(c, expert_new, True):
            copy.start()
    for load, store in zip(token_loads, token_stores):
        load.wait()
        store.start()
    for c in range(4):
        for copy in moves(c, expert_new, True):
            copy.wait()
    for copy in token_stores:
        copy.wait()


def update_call(rows, half, output, grad_tokens, norm, expert, attn, ada, weights):
    vmem = pl.BlockSpec(memory_space=pltpu.VMEM)
    hbm = pl.BlockSpec(memory_space=pl.ANY)
    shapes = [jax.ShapeDtypeStruct(w.shape, f32) for w in weights]
    return pl.pallas_call(
        functools.partial(update_kernel, rows, half),
        out_shape=shapes
        + [jax.ShapeDtypeStruct((1, 1), f32)]
        + [jax.ShapeDtypeStruct(output.shape, f32), jax.ShapeDtypeStruct(grad_tokens.shape, f32)],
        in_specs=[hbm] * 6 + [vmem] * (3 + 9),
        out_specs=[vmem] * 9 + [hbm] * 3 + [pl.BlockSpec(memory_space=pltpu.SMEM), hbm, hbm],
        scratch_shapes=[
            pltpu.VMEM((2, *output.shape), f32),
            pltpu.VMEM((3, *weights[9].shape), f32),
            pltpu.VMEM(expert.shape, f32),
            pltpu.SemaphoreType.DMA((2, 4, 3)),
            pltpu.SemaphoreType.DMA((6,)),
        ],
        compiler_params=pltpu.CompilerParams(vmem_limit_bytes=VMEM_BYTES),
        name="update",
    )(output, grad_tokens, *weights[9:], expert, norm, attn, ada, *weights[:9])


def per_device(
    tokens,
    condition,
    cotangent,
    routes,
    w_ada,
    ada_first,
    ada_second,
    w_gate,
    gate_first,
    gate_second,
    w_attn,
    attn_first,
    attn_second,
    w_expert,
    expert_first,
    expert_second,
):
    output, grad_tokens, ada_total, attn_total, expert_total, square_sum = block_call(
        tokens, condition, cotangent, routes.T, w_ada, w_gate.T, w_attn, w_expert
    )
    updated = update_call(
        w_ada.shape[0], w_attn.shape[2], output, grad_tokens, square_sum, expert_total, attn_total, ada_total,
        (
            w_ada, ada_first, ada_second,
            w_gate.T, gate_first.T, gate_second.T,
            w_attn, attn_first, attn_second,
            w_expert, expert_first, expert_second,
        ),
    )
    gates = [gate.T for gate in updated[3:6]]
    return (*updated[13:], updated[12].reshape(()), *updated[:3], *gates, *updated[6:12])


def solution(mesh):
    placed = (
        P(("dp", "mp"), None),
        P("dp", None),
        P(("dp", "mp"), None),
        P("dp", None),
        P("dp", None),
        P("dp", None),
        P("dp", None),
        P("dp", None),
        P("dp", None),
        P("dp", None),
        P(None, "dp", "mp"),
        P(None, "dp", "mp"),
        P(None, "dp", "mp"),
        P(None, None, "dp", "mp"),
        P(None, None, "dp", "mp"),
        P(None, None, "dp", "mp"),
    )
    return jax.shard_map(
        per_device,
        mesh=mesh,
        in_specs=placed,
        out_specs=(
            P(("dp", "mp"), None),
            P(("dp", "mp"), None),
            P(),
            P("dp", None),
            P("dp", None),
            P("dp", None),
            P("dp", None),
            P("dp", None),
            P("dp", None),
            P(None, "dp", "mp"),
            P(None, "dp", "mp"),
            P(None, "dp", "mp"),
            P(None, None, "dp", "mp"),
            P(None, None, "dp", "mp"),
            P(None, None, "dp", "mp"),
        ),
        check_vma=False,
    )
```
